32 devices in a mesh: dev: 32 (over z, y, x, core).
Axes of the slice: x: 2, y: 2, z: 4, core: 2. Of those that a mesh axis runs over, the one named last changes fastest.
Arguments:
- token_ids: int32 [2, 8192], P(None, 'dev'), may hold values from 0 to 16383
- lengths: int32 [2, 30], replicated, may hold values from 128 to 1024, as said below
- embedding: bfloat16 [16384, 768], P('dev'), may hold values from -6 to 6
- norm1_gain: bfloat16 [768], P('dev'), may hold values from 0.099609375 to 1.8984375
- w_query: bfloat16 [768, 768], P('dev'), may hold values from -0.21875 to 0.21875
- w_key: bfloat16 [768, 768], P('dev'), may hold values from -0.21875 to 0.21875
- w_value: bfloat16 [768, 768], P('dev'), may hold values from -0.21875 to 0.21875
- w_out: bfloat16 [768, 768], P('dev'), may hold values from -2 to 2
- mix_logits: bfloat16 [12, 12], replicated, may hold values from -3.5 to 3.5
- mix_weights: bfloat16 [12, 12], replicated, may hold values from -1.75 to 1.75
- norm2_gain: bfloat16 [768], P('dev'), may hold values from 0.099609375 to 1.8984375
- w_up: bfloat16 [768, 3072], P('dev'), may hold values from -0.21875 to 0.21875
- w_down: bfloat16 [3072, 768], P('dev'), may hold values from -0.109375 to 0.109375
- cotangent: bfloat16 [2, 8192, 768], P(None, 'dev'), may hold values from -6 to 6
Outputs:
- layer_out: bfloat16 [2, 8192, 768], P(None, 'dev')
- grad_input: float32 [2, 8192, 768], P(None, 'dev')
- grad_embedding: float32 [16384, 768], P('dev')
- grad_norm1: float32 [768], P('dev')
- grad_query: float32 [768, 768], P('dev')
- grad_key: float32 [768, 768], P('dev')
- grad_value: float32 [768, 768], P('dev')
- grad_out: float32 [768, 768], P('dev')
- grad_mix_logits: float32 [12, 12], replicated
- grad_mix_weights: float32 [12, 12], replicated
- grad_norm2: float32 [768], P('dev')
- grad_up: float32 [768, 3072], P('dev')
- grad_down: float32 [3072, 768], P('dev')
The draws below stay inside these ranges and needn't reach their ends.
Inputs may be any that keep to these rules, and one draw needn't show every extreme that they name: Each row of lengths sums to 8192; in each row 8/15 of the entries are 128, 4/15 are 256, 2/15 are 512 and 1/15 are 1024, in a drawn order.
All inputs are finite; a program needn't handle non-finite values.
Results may differ from the reference program's by a relative error of at most 0.012.
The reference program's roundings to bfloat16 on the way count: a program that leaves them out, or rounds other values in their place, can miss the bound.
Values may be sent and summed in bfloat16 or wider, within the bound.
No kernel may reach another device: no remote copies, remote signals or barrier semaphores. Data moves between devices by JAX's collectives and lax.ppermute only.
A program may use at most 384 MiB of HBM per device.

```python
import math
import jax
import jax.numpy as jnp
import numpy as np
from jax import lax

D = 768
HEADS = 12
FF = 3072
VOCAB = 16384
ROWS = 256
MICRO = 2
UNIT = 128
HD = 768
TOK_MB = 8192
NSEQ = 30


def draw_lengths(key, part):
    key = jax.random.fold_in(key, 11)
    group_base = NSEQ // 15
    spans = jnp.concatenate([jnp.full((8 * group_base,), 1, jnp.int32), jnp.full((4 * group_base,), 2, jnp.int32), jnp.full((2 * group_base,), 4, jnp.int32), jnp.full((group_base,), 8, jnp.int32)])
    shuffled = [jax.random.permutation(jax.random.fold_in(key, micro_idx), spans) for micro_idx in range(MICRO)]
    return (jnp.stack(shuffled) * UNIT).astype(jnp.int32)


def with_ends(entries, stream_key, least, high):
    place = [jax.random.randint(jax.random.fold_in(stream_key, axis), (), 0, length) for axis, length in enumerate(entries.shape)]
    widest = entries.shape.index(max(entries.shape))
    next_to = place[:widest] + [(place[widest] + 1) % entries.shape[widest]] + place[widest + 1:]
    return entries.at[tuple(place)].set(least).at[tuple(next_to)].set(high)


def steps_of(own_key, shape, split, smallest, high):
    level = 1.0
    for position, parts in split:
        draws = jax.random.uniform(jax.random.fold_in(jax.random.fold_in(own_key, 6), position), (parts,), jnp.float32, smallest / len(split), high / len(split))
        level = level * jnp.repeat(jnp.exp(draws), shape[position] // parts).reshape((-1,) + (1,) * (len(shape) - 1 - position))
    return level


def rank_table(amount, lean):
    loads = [(1 << 20) // math.isqrt(standing ** lean) + 1 for standing in range(1, amount + 1)]
    deviation = 1 + sum(loads) // (1 << 30)
    return np.cumsum(np.array([max(1, weight // deviation) for weight in loads]))


def skewed_ids(stream_key, shape, count, lean):
    table = rank_table(count, lean)
    ticket = jax.random.randint(jax.random.fold_in(stream_key, 1), shape, 0, int(table[count - 1]))
    standing = jnp.searchsorted(jnp.asarray(table, jnp.int32), ticket, side="right")
    return jax.random.permutation(jax.random.fold_in(stream_key, 2), count)[standing].astype(jnp.int32)


def bell_draw(key, dims, deviation, limit, shards=(), kind=jnp.bfloat16):
    array = jax.random.normal(key, dims, jnp.float32) * deviation
    if len(shards) > 0:
        array = steps_of(key, dims, shards, -0.22, 0.18) * array
    return jnp.clip(array, min=-limit, max=limit).astype(kind)


def setup_inputs(seed: int = 0) -> dict:
    seeds = jax.random.split(jax.random.key(seed), 15)
    return {
        "token_ids": with_ends(skewed_ids(seeds[0], (MICRO, TOK_MB), VOCAB, 2), jax.random.fold_in(seeds[0], 3), 0, VOCAB - 1).astype(jnp.int32),
        "lengths": draw_lengths(jax.random.fold_in(seeds[14], 71), 0),
        "embedding": bell_draw(seeds[2], (VOCAB, D), 1.0, 6.0, ((0, 32),)),
        "norm1_gain": jnp.clip(1.0 + 0.18 * jax.random.normal(seeds[3], (D,), jnp.float32), 0.099609375, 1.8984375).astype(jnp.bfloat16),
        "w_query": bell_draw(seeds[4], (D, HD), D ** -0.5, 0.21875, ((0, 32),)),
        "w_key": bell_draw(seeds[5], (D, HD), D ** -0.5, 0.21875, ((0, 32),)),
        "w_value": bell_draw(seeds[6], (D, HD), D ** -0.5, 0.21875, ((0, 32),)),
        "w_out": bell_draw(seeds[7], (HD, D), (max(HD // 96, 2)) ** -0.5, 2.0, ((0, 32),)),
        "mix_logits": bell_draw(seeds[8], (HEADS, HEADS), (max(HEADS // 4, 1)) ** -0.5, 3.5),
        "mix_weights": bell_draw(seeds[9], (HEADS, HEADS), HEADS ** -0.5, 1.75),
        "norm2_gain": jnp.clip(1.0 + 0.18 * jax.random.normal(seeds[10], (D,), jnp.float32), 0.099609375, 1.8984375).astype(jnp.bfloat16),
        "w_up": bell_draw(seeds[11], (D, FF), D ** -0.5, 0.21875, ((0, 32),)),
        "w_down": bell_draw(seeds[12], (FF, D), FF ** -0.5, 0.109375, ((0, 32),)),
        "cotangent": bell_draw(seeds[13], (MICRO, TOK_MB, D), 1.0, 6.0, ((1, 32),)),
    }


norm_eps = 1e-06
score_scale = 0.125
masked = -1e+30
highest = lax.Precision.HIGHEST

@jax.custom_vjp
def low(v):
    return lax.optimization_barrier(v.astype(jnp.bfloat16)).astype(jnp.float32)

@jax.custom_vjp
def low_back(v):
    return v

def low_keep(v):
    return (low(v), None)

def low_pass(kept, grad):
    return (grad,)

def back_keep(v):
    return (v, None)

def back_low(kept, grad):
    return (low(grad),)
low.defvjp(low_keep, low_pass)
low_back.defvjp(back_keep, back_low)

def matmul(left, right):
    return jnp.dot(left, right, precision=highest, preferred_element_type=jnp.float32)

def rms_norm(values, gain_vec):
    inv_rms = lax.rsqrt(lax.optimization_barrier(jnp.mean(values * values, axis=-1, keepdims=True)) + norm_eps)
    return values * inv_rms * gain_vec

def seq_starts(lengths_row, query_rows):
    seq_ends = jnp.cumsum(lengths_row).astype(jnp.int32)
    starts = (seq_ends - lengths_row).astype(jnp.int32)
    return lax.optimization_barrier(jnp.max(jnp.where(starts[None, :] <= query_rows[:, None], starts[None, :], 0), axis=1)).astype(jnp.int32)

def attention(query_vecs, key_vecs, value_vecs, mix_logit, mix_prob, seq_begin):
    total_rows = query_vecs.shape[0]
    head_count = mix_logit.shape[0]
    block_rows = 4 * ROWS
    zero_pad = jnp.zeros((block_rows, key_vecs.shape[1]), key_vecs.dtype)
    key_pad = jnp.concatenate([zero_pad, key_vecs], axis=0)
    value_pad = jnp.concatenate([zero_pad, value_vecs], axis=0)

    def one_block(block_idx):
        anchor = (block_idx * block_rows).astype(jnp.int32)
        q_blk = lax.dynamic_slice_in_dim(query_vecs, anchor, block_rows, 0).reshape(block_rows, head_count, -1)
        k_blk = lax.dynamic_slice_in_dim(key_pad, anchor, 2 * block_rows, 0).reshape(2 * block_rows, head_count, -1)
        v_blk = lax.dynamic_slice_in_dim(value_pad, anchor, 2 * block_rows, 0).reshape(2 * block_rows, head_count, -1)
        begin_blk = lax.dynamic_slice_in_dim(seq_begin, anchor, block_rows, 0)
        query_rows = anchor + jnp.arange(block_rows, dtype=jnp.int32)
        key_rows = anchor - block_rows + jnp.arange(2 * block_rows, dtype=jnp.int32)
        scores = low_back(jnp.einsum('qhd,thd->hqt', q_blk, k_blk, precision=highest) * score_scale)
        logits = jnp.einsum('hj,hqt->jqt', mix_logit, scores, precision=highest)
        allowed = (key_rows[None, :] >= begin_blk[:, None]) & (key_rows[None, :] <= query_rows[:, None])
        logits = jnp.where(allowed[None], logits, masked)
        probabilities = jax.nn.softmax(logits, axis=-1)
        mixed_p = low(jnp.einsum('jk,jqt->kqt', mix_prob, probabilities, precision=highest))
        return jnp.einsum('kqt,tkd->qkd', mixed_p, v_blk, precision=highest).reshape(block_rows, -1)
    blocks = lax.map(jax.checkpoint(one_block), jnp.arange(total_rows // block_rows, dtype=jnp.int32))
    return blocks.reshape(total_rows, -1)

def layer(seq_begin, inputs, gain_one, w_query, w_key, w_value, w_out, mix_logit, mix_prob, gain_two, w_up, w_down):
    hidden_one = low(rms_norm(inputs, gain_one))
    query_vecs = low(low_back(matmul(hidden_one, w_query)))
    key_vecs = low(low_back(matmul(hidden_one, w_key)))
    value_vecs = low(low_back(matmul(hidden_one, w_value)))
    attended = low(low_back(attention(query_vecs, key_vecs, value_vecs, mix_logit, mix_prob, seq_begin)))
    branch_one = low_back(matmul(attended, w_out))
    middle = inputs + branch_one
    hidden_two = low(rms_norm(middle, gain_two))
    up_proj = low_back(matmul(hidden_two, w_up))
    activated = low(jax.nn.gelu(up_proj))
    branch_two = low_back(matmul(activated, w_down))
    return middle + branch_two

def reference(token_ids, lengths, embedding, norm1_gain, w_query, w_key, w_value, w_out, mix_logits, mix_weights, norm2_gain, w_up, w_down, cotangent):
    table_full = embedding.astype(jnp.float32)
    weights = tuple((matrix.astype(jnp.float32) for matrix in (norm1_gain, w_query, w_key, w_value, w_out, mix_logits, mix_weights, norm2_gain, w_up, w_down)))
    outputs, grad_inputs = ([], [])
    grad_table = jnp.zeros_like(table_full)
    grad_weights = tuple((jnp.zeros_like(matrix) for matrix in weights))
    all_rows = jnp.arange(TOK_MB, dtype=jnp.int32)
    for micro_idx in range(MICRO):
        tok_ids = token_ids[micro_idx]
        seq_begin = seq_starts(lengths[micro_idx], all_rows)
        inputs, pick_rows = jax.vjp(lambda table_arg: jnp.take(table_arg, tok_ids, axis=0), table_full)
        result, pull_back = jax.vjp(lambda *operands: layer(seq_begin, *operands), inputs, *weights)
        pulled = pull_back(cotangent[micro_idx].astype(jnp.float32))
        outputs.append(result.astype(jnp.bfloat16))
        grad_inputs.append(pulled[0])
        grad_table = grad_table + pick_rows(pulled[0])[0]
        grad_weights = tuple((running + addend for running, addend in zip(grad_weights, pulled[1:])))
    return (jnp.stack(outputs), jnp.stack(grad_inputs), grad_table, grad_weights[0], grad_weights[1], grad_weights[2], grad_weights[3], grad_weights[4], grad_weights[5], grad_weights[6], grad_weights[7], grad_weights[8], grad_weights[9])
```

```python
from functools import partial

import jax
import jax.numpy as jnp
from jax import lax
from jax.experimental import pallas as pl
from jax.experimental.pallas import tpu as pltpu
from jax.sharding import PartitionSpec as P

norm_eps = 1e-06

masked = -1e30
UNIT = 128
CHUNK = 256
GROUP = 16
MAX_CHUNKS = 4


def dot_nn(left, right):
    return lax.dot_general(left, right, (((1,), (0,)), ((), ())), preferred_element_type=jnp.float32)


def dot_nt(left, right):
    return lax.dot_general(left, right, (((1,), (1,)), ((), ())), preferred_element_type=jnp.float32)


def spread_heads(rows, lane_head, quad, heads_per_quad):
    part = rows[:, quad * CHUNK : (quad + 1) * CHUNK]
    zero = jnp.zeros_like(part)
    return jnp.concatenate([jnp.where(lane_head == head, part, zero) for head in range(heads_per_quad)], axis=0)


def own_lanes(wide, lane_head, heads_per_quad):
    total = jnp.where(lane_head == 0, wide[:UNIT], 0.0)
    for head in range(1, heads_per_quad):
        total = total + jnp.where(lane_head == head, wide[head * UNIT : (head + 1) * UNIT], 0.0)
    return total


def group_rows(ref, chunk, group, heads):
    rows = ref[chunk, :, GROUP * group : GROUP * (group + 1), :]
    return rows.reshape(heads * GROUP, rows.shape[-1])


def allowed_keys(chunk, group, blocks):
    key = lax.broadcasted_iota(jnp.int32, (GROUP, CHUNK), 1) - (UNIT + CHUNK * chunk)
    row = lax.broadcasted_iota(jnp.int32, (GROUP, CHUNK), 0) + GROUP * group
    return (key <= row) & (key >= (1 - blocks) * UNIT)


def fwd_kernel(heads, units_per_row, blocks_ref, q_ref, k_ref, v_ref, mixl_ref, mixp_ref, att_ref, lse_ref, qx, score, logit, mixed, total, top, row_sum):
    unit = pl.program_id(0)
    blocks = blocks_ref[unit]
    chunks = (blocks + 1) // 2
    last_key = k_ref.shape[1] - units_per_row * UNIT + UNIT * (unit % units_per_row + 1)
    quads = q_ref.shape[2] // CHUNK
    per_quad = heads // quads
    groups = UNIT // GROUP
    lane_head = lax.broadcasted_iota(jnp.int32, (UNIT, CHUNK), 1) // (CHUNK // per_quad)
    for quad in range(quads):
        qx[quad] = spread_heads(q_ref[0], lane_head, quad, per_quad)
        total[quad] = jnp.zeros_like(total[quad])
    top[...] = jnp.full_like(top, masked)
    row_sum[...] = jnp.zeros_like(row_sum)

    def keys_of(chunk):
        return pl.ds(pl.multiple_of(last_key - CHUNK * (chunk + 1), UNIT), CHUNK)

    @pl.loop(0, chunks)
    def _(chunk):
        for quad in range(quads):
            s = dot_nt(qx[quad], k_ref[0, keys_of(chunk), quad * CHUNK : (quad + 1) * CHUNK])
            score[0, quad * per_quad : (quad + 1) * per_quad] = s.reshape(per_quad, UNIT, CHUNK).astype(jnp.bfloat16)
        for group in range(groups):
            rows = slice(GROUP * group, GROUP * (group + 1))
            l = dot_nn(mixl_ref[...], group_rows(score, 0, group, heads)).reshape(heads, GROUP, CHUNK)
            l = jnp.where(allowed_keys(chunk, group, blocks)[None], l, masked)
            logit[chunk, :, rows, :] = l
            top[:, rows, :] = jnp.maximum(top[:, rows, :], jnp.maximum(l[:, :, :UNIT], l[:, :, UNIT:]))

    for head in range(heads):
        top[head] = jnp.broadcast_to(jnp.max(top[head], axis=-1, keepdims=True), (UNIT, UNIT))

    @pl.loop(0, chunks)
    def _(chunk):
        for head in range(heads):
            row_top = top[head]
            left = jnp.exp(logit[chunk, head, :, :UNIT] - row_top)
            right = jnp.exp(logit[chunk, head, :, UNIT:] - row_top)
            logit[chunk, head, :, :UNIT] = left
            logit[chunk, head, :, UNIT:] = right
            row_sum[head] += left + right

    for head in range(heads):
        norm = jnp.broadcast_to(jnp.sum(row_sum[head], axis=-1, keepdims=True), (UNIT, UNIT))
        lse_ref[0, head] = top[head] + jnp.log(norm)
        row_sum[head] = 1.0 / norm

    @pl.loop(0, chunks)
    def _(chunk):
        for group in range(groups):
            rows = slice(GROUP * group, GROUP * (group + 1))
            scale = row_sum[:, rows, :]
            p = logit[chunk, :, rows, :]
            p = jnp.concatenate([p[:, :, :UNIT] * scale, p[:, :, UNIT:] * scale], axis=-1)
            p = p.astype(jnp.bfloat16).reshape(heads * GROUP, CHUNK)
            a = dot_nn(mixp_ref[...], p)
            mixed[:, rows, :] = a.astype(jnp.bfloat16).reshape(heads, GROUP, CHUNK)
        for quad in range(quads):
            a = mixed[quad * per_quad : (quad + 1) * per_quad].reshape(per_quad * UNIT, CHUNK)
            total[quad] += dot_nn(a, v_ref[0, keys_of(chunk), quad * CHUNK : (quad + 1) * CHUNK])

    for quad in range(quads):
        att_ref[0, :, quad * CHUNK : (quad + 1) * CHUNK] = own_lanes(total[quad], lane_head, per_quad).astype(jnp.bfloat16)


def attention_fwd(blocks, q, k, v, mixl, mixp, heads):
    units, _, width = q.shape
    per_row = units // k.shape[0]
    quads = width // CHUNK
    per_quad = heads // quads
    wide = heads * GROUP
    whole = pl.BlockSpec((wide, wide), lambda u, _: (0, 0))
    kv_spec = pl.BlockSpec((1,) + k.shape[1:], lambda u, _: (u // per_row, 0, 0))
    return pl.pallas_call(
        partial(fwd_kernel, heads, per_row),
        grid_spec=pltpu.PrefetchScalarGridSpec(
            num_scalar_prefetch=1,
            grid=(units,),
            in_specs=[
                pl.BlockSpec((1, UNIT, width), lambda u, _: (u, 0, 0)),
                kv_spec,
                kv_spec,
                whole,
                whole,
            ],
            out_specs=[
                pl.BlockSpec((1, UNIT, width), lambda u, _: (u, 0, 0)),
                pl.BlockSpec((1, heads, UNIT, UNIT), lambda u, _: (u, 0, 0, 0)),
            ],
            scratch_shapes=[
                pltpu.VMEM((quads, per_quad * UNIT, CHUNK), jnp.bfloat16),
                pltpu.VMEM((1, heads, UNIT, CHUNK), jnp.bfloat16),
                pltpu.VMEM((MAX_CHUNKS, heads, UNIT, CHUNK), jnp.float32),
                pltpu.VMEM((heads, UNIT, CHUNK), jnp.bfloat16),
                pltpu.VMEM((quads, per_quad * UNIT, CHUNK), jnp.float32),
                pltpu.VMEM((heads, UNIT, UNIT), jnp.float32),
                pltpu.VMEM((heads, UNIT, UNIT), jnp.float32),
            ],
        ),
        out_shape=[
            jax.ShapeDtypeStruct((units, UNIT, width), jnp.bfloat16),
            jax.ShapeDtypeStruct((units, heads, UNIT, UNIT), jnp.float32),
        ],
        compiler_params=pltpu.CompilerParams(vmem_limit_bytes=48 * 1024 * 1024),
        name="attention_fwd",
    )(blocks, q, k, v, mixl, mixp)


def bwd_kernel(heads, units_per_row, blocks_ref, q_ref, k_ref, v_ref, do_ref, lse_ref, mixl_ref, mixlt_ref, mixp_ref, mixpt_ref,
               dq_ref, dk_ref, dv_ref, gl_ref, gp_ref,
               qx, qxt, dox, doxt, score, prob, grad_prob, grad_mixed, mixed, delta, dq_total, dk_total, dv_total):
    unit = pl.program_id(0)
    blocks = blocks_ref[unit]
    chunks = (blocks + 1) // 2
    key_units = k_ref.shape[1] // UNIT
    inner = unit % units_per_row
    last_unit = key_units - units_per_row + inner + 1
    quads = q_ref.shape[2] // CHUNK
    per_quad = heads // quads
    groups = UNIT // GROUP
    lane_head = lax.broadcasted_iota(jnp.int32, (UNIT, CHUNK), 1) // (CHUNK // per_quad)

    @pl.when(unit == 0)
    def _():
        gl_ref[...] = jnp.zeros_like(gl_ref)
        gp_ref[...] = jnp.zeros_like(gp_ref)

    @pl.when(inner == 0)
    def _():
        dk_total[...] = jnp.zeros_like(dk_total)
        dv_total[...] = jnp.zeros_like(dv_total)

    for quad in range(quads):
        wide_q = spread_heads(q_ref[0], lane_head, quad, per_quad)
        qx[quad] = wide_q
        qxt[quad] = wide_q.T
        wide_o = spread_heads(do_ref[0], lane_head, quad, per_quad)
        dox[quad] = wide_o
        doxt[quad] = wide_o.T
        dq_total[quad] = jnp.zeros_like(dq_total[quad])
    delta[...] = jnp.zeros_like(delta)

    def keys_of(chunk):
        return pl.ds(pl.multiple_of((last_unit - 2 * (chunk + 1)) * UNIT, UNIT), CHUNK)

    def add_to(total, chunk, quad, term):
        first = last_unit - 2 * (chunk + 1)
        lanes = slice(quad * CHUNK, (quad + 1) * CHUNK)
        total[first, lanes, :] += term[:, :UNIT]
        total[first + 1, lanes, :] += term[:, UNIT:]

    @pl.loop(0, chunks)
    def _(chunk):
        for quad in range(quads):
            lanes = slice(quad * CHUNK, (quad + 1) * CHUNK)
            hs = slice(quad * per_quad, (quad + 1) * per_quad)
            s = dot_nt(qx[quad], k_ref[0, keys_of(chunk), lanes])
            score[chunk, hs] = s.reshape(per_quad, UNIT, CHUNK).astype(jnp.bfloat16)
            da = dot_nt(dox[quad], v_ref[0, keys_of(chunk), lanes])
            grad_mixed[0, hs] = da.reshape(per_quad, UNIT, CHUNK).astype(jnp.bfloat16)
        for group in range(groups):
            rows = slice(GROUP * group, GROUP * (group + 1))
            l = dot_nn(mixl_ref[...], group_rows(score, chunk, group, heads)).reshape(heads, GROUP, CHUNK)
            lse = lse_ref[0, :, rows, :]
            l = l - jnp.concatenate([lse, lse], axis=-1)
            p = jnp.exp(jnp.where(allowed_keys(chunk, group, blocks)[None], l, masked))
            p_low = p.astype(jnp.bfloat16)
            prob[chunk, :, rows, :] = p_low
            p_low = p_low.reshape(heads * GROUP, CHUNK)
            da = group_rows(grad_mixed, 0, group, heads)
            dp = dot_nn(mixpt_ref[...], da).reshape(heads, GROUP, CHUNK)
            grad_prob[chunk, :, rows, :] = dp
            term = p * dp
            delta[:, rows, :] += term[:, :, :UNIT] + term[:, :, UNIT:]
            mixed[:, rows, :] = dot_nn(mixp_ref[...], p_low).astype(jnp.bfloat16).reshape(heads, GROUP, CHUNK)
            gp_ref[...] += dot_nt(p_low, da)
        for quad in range(quads):
            a = mixed[quad * per_quad : (quad + 1) * per_quad].reshape(per_quad * UNIT, CHUNK)
            add_to(dv_total, chunk, quad, dot_nn(doxt[quad], a))

    for head in range(heads):
        delta[head] = jnp.broadcast_to(jnp.sum(delta[head], axis=-1, keepdims=True), (UNIT, UNIT))

    @pl.loop(0, chunks)
    def _(chunk):
        for group in range(groups):
            rows = slice(GROUP * group, GROUP * (group + 1))
            d = delta[:, rows, :]
            dp = grad_prob[chunk, :, rows, :] - jnp.concatenate([d, d], axis=-1)
            dl = (prob[chunk, :, rows, :].astype(jnp.float32) * dp).astype(jnp.bfloat16).reshape(heads * GROUP, CHUNK)
            ds = dot_nn(mixlt_ref[...], dl)
            mixed[:, rows, :] = ds.astype(jnp.bfloat16).reshape(heads, GROUP, CHUNK)
            gl_ref[...] += dot_nt(group_rows(score, chunk, group, heads), dl)
        for quad in range(quads):
            ds = mixed[quad * per_quad : (quad + 1) * per_quad].reshape(per_quad * UNIT, CHUNK)
            dq_total[quad] += dot_nn(ds, k_ref[0, keys_of(chunk), quad * CHUNK : (quad + 1) * CHUNK])
            add_to(dk_total, chunk, quad, dot_nn(qxt[quad], ds))

    for quad in range(quads):
        dq = own_lanes(dq_total[quad], lane_head, per_quad) * 0.125
        dq_ref[0, :, quad * CHUNK : (quad + 1) * CHUNK] = dq.astype(jnp.bfloat16)

    @pl.when(inner == units_per_row - 1)
    def _():
        for key_unit in range(key_units):
            keys = slice(key_unit * UNIT, (key_unit + 1) * UNIT)
            dk_ref[0, keys, :] = dk_total[key_unit].T.astype(dk_ref.dtype)
            dv_ref[0, keys, :] = dv_total[key_unit].T.astype(dv_ref.dtype)


def attention_bwd(blocks, q, k, v, grad_out, lse, mixl, mixlt, mixp, mixpt, heads):
    units, _, width = q.shape
    per_row = units // k.shape[0]
    key_units = k.shape[1] // UNIT
    quads = width // CHUNK
    per_quad = heads // quads
    wide = heads * GROUP
    whole = pl.BlockSpec((wide, wide), lambda u, _: (0, 0))
    kv_spec = pl.BlockSpec((1,) + k.shape[1:], lambda u, _: (u // per_row, 0, 0))
    unit_spec = pl.BlockSpec((1, UNIT, width), lambda u, _: (u, 0, 0))
    spread = (quads, per_quad * UNIT, CHUNK)
    return pl.pallas_call(
        partial(bwd_kernel, heads, per_row),
        grid_spec=pltpu.PrefetchScalarGridSpec(
            num_scalar_prefetch=1,
            grid=(units,),
            in_specs=[
                unit_spec,
                kv_spec,
                kv_spec,
                unit_spec,
                pl.BlockSpec((1, heads, UNIT, UNIT), lambda u, _: (u, 0, 0, 0)),
                whole,
                whole,
                whole,
                whole,
            ],
            out_specs=[unit_spec, kv_spec, kv_spec, whole, whole],
            scratch_shapes=[
                pltpu.VMEM(spread, jnp.bfloat16),
                pltpu.VMEM((quads, CHUNK, per_quad * UNIT), jnp.bfloat16),
                pltpu.VMEM(spread, jnp.bfloat16),
                pltpu.VMEM((quads, CHUNK, per_quad * UNIT), jnp.bfloat16),
                pltpu.VMEM((MAX_CHUNKS, heads, UNIT, CHUNK), jnp.bfloat16),
                pltpu.VMEM((MAX_CHUNKS, heads, UNIT, CHUNK), jnp.bfloat16),
                pltpu.VMEM((MAX_CHUNKS, heads, UNIT, CHUNK), jnp.float32),
                pltpu.VMEM((1, heads, UNIT, CHUNK), jnp.bfloat16),
                pltpu.VMEM((heads, UNIT, CHUNK), jnp.bfloat16),
                pltpu.VMEM((heads, UNIT, UNIT), jnp.float32),
                pltpu.VMEM(spread, jnp.float32),
                pltpu.VMEM((key_units, width, UNIT), jnp.float32),
                pltpu.VMEM((key_units, width, UNIT), jnp.float32),
            ],
        ),
        out_shape=[
            jax.ShapeDtypeStruct((units, UNIT, width), jnp.bfloat16),
            jax.ShapeDtypeStruct(k.shape, jnp.bfloat16),
            jax.ShapeDtypeStruct(v.shape, jnp.bfloat16),
            jax.ShapeDtypeStruct((wide, wide), jnp.float32),
            jax.ShapeDtypeStruct((wide, wide), jnp.float32),
        ],
        compiler_params=pltpu.CompilerParams(vmem_limit_bytes=56 * 1024 * 1024),
        name="attention_bwd",
    )(blocks, q, k, v, grad_out, lse, mixl, mixlt, mixp, mixpt)


def spread_mix(mix):
    heads = mix.shape[0]
    eye = jnp.eye(GROUP, dtype=mix.dtype)
    return (mix[:, None, :, None] * eye[None, :, None, :]).reshape(heads * GROUP, heads * GROUP)


def fold_mix(wide, heads):
    grid = wide.reshape(heads, GROUP, heads, GROUP)
    return jnp.sum(jnp.where(jnp.eye(GROUP, dtype=bool)[None, :, None, :], grid, 0.0), axis=(1, 3))


def from_behind(value, steps):
    count = lax.axis_size("dev")
    first, last = (max(0, -steps), min(count, count - steps))
    return lax.ppermute(value, "dev", [(source, source + steps) for source in range(first, last)])


def seq_starts(lengths_row, query_rows):
    seq_ends = jnp.cumsum(lengths_row)
    starts = seq_ends - lengths_row
    return jnp.max(jnp.where(starts[None, :] <= query_rows[:, None], starts[None, :], 0), axis=1)


def normalize(values, gain_vec):
    inv_rms = lax.rsqrt(jnp.mean(values * values, axis=-1, keepdims=True) + norm_eps)
    normed = values * inv_rms
    return (normed, inv_rms, (normed * gain_vec.astype(jnp.float32)).astype(jnp.bfloat16))


def norm_back(grad_hidden, normed, inv_rms, gain_vec):
    grad_gain = jnp.sum(grad_hidden * normed, axis=0)
    grad_normed = grad_hidden * gain_vec.astype(jnp.float32)
    inner_mean = jnp.mean(grad_normed * normed, axis=-1, keepdims=True)
    return (inv_rms * (grad_normed - normed * inner_mean), grad_gain)


def matmul(left, right):
    return jnp.dot(left, right, preferred_element_type=jnp.float32)


def matmul_left_t(left, right):
    return lax.dot_general(left, right, (((0,), (0,)), ((), ())), preferred_element_type=jnp.float32)


def matmul_right_t(left, right):
    return lax.dot_general(left, right, (((1,), (1,)), ((), ())), preferred_element_type=jnp.float32)


def exchange(value):
    return lax.all_to_all(value, "dev", split_axis=0, concat_axis=0, tiled=True)


def plan_lookup(tok_ids, own_rows, stride, room):
    count = lax.axis_size("dev")
    owner = tok_ids // own_rows
    place = jnp.arange(tok_ids.shape[0], dtype=jnp.int32)
    same = tok_ids[:, None] == tok_ids[None, :]
    repeated = jnp.any(same & (place[None, :] < place[:, None]), axis=1)
    before = (owner[:, None] == owner[None, :]) & (tok_ids[None, :] < tok_ids[:, None]) & ~repeated[None, :]
    rank = jnp.sum(before, axis=1, dtype=jnp.int32)
    slot = jnp.where(rank < room, owner * stride + rank, -1)
    chosen = slot[None, :] == jnp.arange(count * stride, dtype=jnp.int32)[:, None]
    wanted = jnp.max(jnp.where(chosen, (tok_ids % own_rows)[None, :], -1), axis=1).reshape(count, stride)
    full = jnp.any(rank >= room).astype(jnp.int32)
    flags = jnp.broadcast_to(full, (count, stride))
    asked = exchange(jnp.concatenate([wanted, flags], axis=1))
    overflow = jnp.max(asked[:, stride:]) > 0
    pick = (asked[:, :stride].reshape(-1, 1) == jnp.arange(own_rows, dtype=jnp.int32)[None, :]).astype(jnp.bfloat16)
    return (chosen.astype(jnp.bfloat16), pick, overflow)


def lookup(embedding, tok_ids, extra_row, chosen, pick, overflow, stride):
    count = lax.axis_size("dev")
    rows = matmul(pick, embedding).astype(jnp.bfloat16).reshape(count, stride, -1)
    is_extra = (jnp.arange(stride, dtype=jnp.int32) == stride - 1)[None, :, None]
    rows = jnp.where(is_extra, extra_row[None, None, :], rows)
    got = exchange(rows.reshape(count * stride, -1))
    extra = got.reshape(count, stride, -1)[:, stride - 1]
    fast = matmul_left_t(chosen, got).astype(jnp.bfloat16)

    def whole_table(fast_rows):
        table = lax.all_gather(embedding, "dev", axis=0, tiled=True)
        return jnp.take(table, tok_ids, axis=0)

    return (lax.cond(overflow, whole_table, lambda fast_rows: fast_rows, fast), extra)


def table_back(grad_rows, tok_ids, extra_rows, chosen, pick, overflow, stride, own_rows):
    count = lax.axis_size("dev")
    summed = matmul(chosen, grad_rows.astype(jnp.bfloat16)).astype(jnp.bfloat16).reshape(count, stride, -1)
    place = jnp.arange(stride, dtype=jnp.int32)[None, :, None]
    high, low = extra_rows
    summed = jnp.where(place == stride - 2, high[:, None, :], summed)
    summed = jnp.where(place == stride - 1, low[:, None, :], summed)
    got = exchange(summed.reshape(count * stride, -1))
    extra = got.reshape(count, stride, -1)[:, stride - 2 :].astype(jnp.float32)
    fast = matmul_left_t(pick, got)

    def whole_table(fast_rows):
        running = jnp.zeros((own_rows * count, grad_rows.shape[1]), jnp.float32)
        running = running.at[tok_ids].add(grad_rows)
        return lax.psum_scatter(running, "dev", scatter_dimension=0, tiled=True)

    return (lax.cond(overflow, whole_table, lambda fast_rows: fast_rows, fast), jnp.sum(extra, axis=(0, 1)))


def gather_parts(pieces):
    count = lax.axis_size("dev")
    sizes = [piece.shape[0] for piece in pieces]
    whole = lax.all_gather(jnp.concatenate(pieces, axis=0), "dev", axis=0, tiled=True)
    whole = whole.reshape(count, sum(sizes), -1)
    parts, start = ([], 0)
    for size in sizes:
        parts.append(whole[:, start : start + size].reshape(count * size, -1))
        start += size
    return parts


def stack_parts(parts):
    count = lax.axis_size("dev")
    shaped = [part.astype(jnp.bfloat16).reshape(count, part.shape[0] // count, -1) for part in parts]
    return jnp.concatenate(shaped, axis=1)


def scatter_sum(parts):
    count = lax.axis_size("dev")
    sizes = [part.shape[0] // count for part in parts]
    stacked = stack_parts(parts)
    summed = lax.psum_scatter(stacked.reshape(count * sum(sizes), -1), "dev", scatter_dimension=0, tiled=True)
    return split_rows(summed, sizes)


def split_rows(summed, sizes):
    pieces, start = ([], 0)
    for size in sizes:
        pieces.append(summed[start : start + size].astype(jnp.float32))
        start += size
    return pieces


def halving_sum(parts):
    count = lax.axis_size("dev")
    steps = count.bit_length() - 1
    me = lax.axis_index("dev")
    sizes = [part.shape[0] // count for part in parts]
    stacked = stack_parts(parts)
    width = stacked.shape[-1]
    bits = stacked.reshape((2,) * steps + (sum(sizes), width))
    held = bits.transpose(tuple(reversed(range(steps))) + (steps, steps + 1)).reshape(count, sum(sizes), width)
    for step in range(steps):
        half = held.shape[0] // 2
        mine = (me >> step) & 1
        keep = lax.dynamic_slice_in_dim(held, mine * half, half, 0)
        give = lax.dynamic_slice_in_dim(held, (1 - mine) * half, half, 0)
        came = lax.ppermute(give, "dev", [(source, source ^ (1 << step)) for source in range(count)])
        total = keep.astype(jnp.float32) + came.astype(jnp.float32)
        held = total if step == steps - 1 else total.astype(jnp.bfloat16)
    return split_rows(held.reshape(sum(sizes), width), sizes)


def split_low(values):
    high = lax.reduce_precision(values, 8, 7)
    return (high.astype(jnp.bfloat16), (values - high).astype(jnp.bfloat16))


def shards(
    token_ids,
    lengths,
    embedding,
    norm1_gain,
    w_query,
    w_key,
    w_value,
    w_out,
    mix_logits,
    mix_weights,
    norm2_gain,
    w_up,
    w_down,
    cotangent,
):
    count = lax.axis_size("dev")
    me = lax.axis_index("dev")
    micros, row_count = token_ids.shape
    own_rows, width = embedding.shape
    heads = mix_logits.shape[0]
    part = norm1_gain.shape[0]
    per_row = row_count // UNIT
    tokens = micros * row_count
    tok_ids = token_ids.reshape(-1)
    stride = max(16, 1024 // count)
    room = stride - 2

    up_cols = w_up.shape[1] // width
    w_q, w_k, w_v = gather_parts([w_query, w_key, w_value])
    up_pieces = [w_up[:, col * width : (col + 1) * width] for col in range(up_cols)]
    late = gather_parts([w_out] + up_pieces + [w_down])
    w_o, w_d = (late[0], late[-1])
    w_u = jnp.concatenate(late[1:-1], axis=1)

    unit_rows = me * row_count + UNIT * jnp.arange(per_row, dtype=jnp.int32)
    begins = jnp.stack([seq_starts(lengths[micro], unit_rows) for micro in range(micros)])
    blocks = ((unit_rows[None, :] - begins) // UNIT + 1).reshape(-1).astype(jnp.int32)

    mixl, mixlt = (spread_mix(mix_logits.T), spread_mix(mix_logits))
    mixp, mixpt = (spread_mix(mix_weights.T), spread_mix(mix_weights))

    chosen, pick, overflow = plan_lookup(tok_ids, own_rows, stride, room)
    gains_row = jnp.concatenate([norm1_gain, norm2_gain, jnp.zeros((width - 2 * part,), jnp.bfloat16)])
    picked, gains = lookup(embedding, tok_ids, gains_row, chosen, pick, overflow, stride)
    gain_one = gains[:, :part].reshape(-1)
    gain_two = gains[:, part : 2 * part].reshape(-1)
    inputs = picked.astype(jnp.float32)

    normed_one, inv_one, hidden_one = normalize(inputs, gain_one)
    own_hidden = hidden_one.reshape(micros, row_count, width)
    behind = [from_behind(own_hidden, steps) for steps in (1, 2, 3)]
    behind.append(from_behind(own_hidden[:, row_count - UNIT :], 4))
    all_hidden = jnp.concatenate(behind[::-1] + [own_hidden], axis=1)
    key_rows = all_hidden.shape[1]
    flat_hidden = all_hidden.reshape(micros * key_rows, width)
    query = (matmul(hidden_one, w_q).astype(jnp.bfloat16) * jnp.bfloat16(0.125)).reshape(-1, UNIT, width)
    key = matmul(flat_hidden, w_k).astype(jnp.bfloat16).reshape(micros, key_rows, width)
    value = matmul(flat_hidden, w_v).astype(jnp.bfloat16).reshape(micros, key_rows, width)
    attended, lse = attention_fwd(blocks, query, key, value, mixl, mixp, heads)
    attended = attended.reshape(tokens, width)

    middle = inputs + matmul(attended, w_o)
    normed_two, inv_two, hidden_two = normalize(middle, gain_two)
    up_proj = matmul(hidden_two, w_u)
    activated, gelu_pull = jax.vjp(jax.nn.gelu, up_proj)
    activated = activated.astype(jnp.bfloat16)
    output = (middle + matmul(activated, w_d)).astype(jnp.bfloat16)

    grad_rows = cotangent.reshape(tokens, width)
    grad_act = matmul_right_t(grad_rows, w_d)
    grad_upb = gelu_pull(grad_act)[0].astype(jnp.bfloat16)
    grad_down = matmul_left_t(activated, grad_rows)
    grad_up = matmul_left_t(hidden_two, grad_upb)
    grad_hidden_two = matmul_right_t(grad_upb, w_u)
    grad_mid_norm, grad_gain_two = norm_back(grad_hidden_two, normed_two, inv_two, gain_two)
    grad_middle = grad_rows.astype(jnp.float32) + grad_mid_norm
    grad_branch = grad_middle.astype(jnp.bfloat16)
    grad_wout = matmul_left_t(attended, grad_branch)
    grad_att = matmul_right_t(grad_branch, w_o).astype(jnp.bfloat16).reshape(-1, UNIT, width)
    up_terms = [grad_up[:, col * width : (col + 1) * width] for col in range(up_cols)]
    late_sums = scatter_sum([grad_wout] + up_terms + [grad_down])

    grad_query, grad_key, grad_value, wide_logit, wide_prob = attention_bwd(
        blocks, query, key, value, grad_att, lse, mixl, mixlt, mixp, mixpt, heads
    )
    grad_query = grad_query.reshape(tokens, width)
    grad_key = grad_key.reshape(micros * key_rows, width)
    grad_value = grad_value.reshape(micros * key_rows, width)
    grad_flat = (matmul_right_t(grad_key, w_k) + matmul_right_t(grad_value, w_v)).reshape(micros, key_rows, width)
    returned = []
    start = 0
    for steps, size in ((4, UNIT), (3, row_count), (2, row_count), (1, row_count)):
        term = grad_flat[:, start : start + size].astype(jnp.bfloat16)
        returned.append((size, from_behind(term, -steps)))
        start += size
    grad_wq = matmul_left_t(hidden_one, grad_query)
    grad_wk = matmul_left_t(flat_hidden, grad_key)
    grad_wv = matmul_left_t(flat_hidden, grad_value)
    early_sums = halving_sum([grad_wq, grad_wk, grad_wv])
    grad_own = grad_flat[:, start:]
    for size, term in returned:
        term = term.astype(jnp.float32)
        if size < row_count:
            term = jnp.pad(term, ((0, 0), (row_count - size, 0), (0, 0)))
        grad_own = grad_own + term
    grad_hidden_one = grad_own.reshape(tokens, width) + matmul_right_t(grad_query, w_q)
    grad_in_norm, grad_gain_one = norm_back(grad_hidden_one, normed_one, inv_one, gain_one)
    grad_inputs = grad_middle + grad_in_norm

    mix_terms = jnp.concatenate([fold_mix(wide_logit, heads).reshape(-1), fold_mix(wide_prob, heads).reshape(-1)])
    mix_size = mix_terms.shape[0]
    small = jnp.concatenate(
        [
            grad_gain_one.reshape(count, part),
            grad_gain_two.reshape(count, part),
            jnp.broadcast_to(mix_terms[None, :], (count, mix_size)),
            jnp.zeros((count, width - 2 * part - mix_size), jnp.float32),
        ],
        axis=1,
    )
    table_grad, small_sum = table_back(grad_inputs, tok_ids, split_low(small), chosen, pick, overflow, stride, own_rows)
    mixes = small_sum[2 * part : 2 * part + mix_size].reshape(2, heads, heads)
    return (
        output.reshape(micros, row_count, width),
        grad_inputs.reshape(micros, row_count, width),
        table_grad,
        small_sum[:part],
        early_sums[0],
        early_sums[1],
        early_sums[2],
        late_sums[0],
        mixes[0],
        mixes[1],
        small_sum[part : 2 * part],
        jnp.concatenate(late_sums[1:-1], axis=1),
        late_sums[-1],
    )


def solution(mesh):
    in_specs = (
        P(None, "dev"),
        P(),
        P("dev", None),
        P("dev"),
        P("dev", None),
        P("dev", None),
        P("dev", None),
        P("dev", None),
        P(),
        P(),
        P("dev"),
        P("dev", None),
        P("dev", None),
        P(None, "dev", None),
    )
    out_specs = (
        P(None, "dev", None),
        P(None, "dev", None),
        P("dev", None),
        P("dev"),
        P("dev", None),
        P("dev", None),
        P("dev", None),
        P("dev", None),
        P(),
        P(),
        P("dev"),
        P("dev", None),
        P("dev", None),
    )
    return jax.shard_map(shards, mesh=mesh, in_specs=in_specs, out_specs=out_specs, check_vma=False)
```

```python
from functools import partial

import jax
import jax.numpy as jnp
from jax import lax
from jax.experimental import pallas as pl
from jax.experimental.pallas import tpu as pltpu
from jax.sharding import PartitionSpec as P

norm_eps = 1e-06

masked = -1e30
UNIT = 128
CHUNK = 256
GROUP = 16
MAX_CHUNKS = 4


def dot_nn(left, right):
    return lax.dot_general(left, right, (((1,), (0,)), ((), ())), preferred_element_type=jnp.float32)


def dot_nt(left, right):
    return lax.dot_general(left, right, (((1,), (1,)), ((), ())), preferred_element_type=jnp.float32)


def spread_heads(rows, lane_head, quad, heads_per_quad):
    part = rows[:, quad * CHUNK : (quad + 1) * CHUNK]
    zero = jnp.zeros_like(part)
    return jnp.concatenate([jnp.where(lane_head == head, part, zero) for head in range(heads_per_quad)], axis=0)


def own_lanes(wide, lane_head, heads_per_quad):
    total = jnp.where(lane_head == 0, wide[:UNIT], 0.0)
    for head in range(1, heads_per_quad):
        total = total + jnp.where(lane_head == head, wide[head * UNIT : (head + 1) * UNIT], 0.0)
    return total


def group_rows(ref, chunk, group, heads):
    rows = ref[chunk, :, GROUP * group : GROUP * (group + 1), :]
    return rows.reshape(heads * GROUP, rows.shape[-1])


def allowed_keys(chunk, group, blocks):
    key = lax.broadcasted_iota(jnp.int32, (GROUP, CHUNK), 1) - (UNIT + CHUNK * chunk)
    row = lax.broadcasted_iota(jnp.int32, (GROUP, CHUNK), 0) + GROUP * group
    return (key <= row) & (key >= (1 - blocks) * UNIT)


def fwd_kernel(heads, units_per_row, blocks_ref, q_ref, k_ref, v_ref, mixl_ref, mixp_ref, att_ref, lse_ref, qx, score, logit, mixed, total, top, row_sum):
    unit = pl.program_id(0)
    blocks = blocks_ref[unit]
    chunks = (blocks + 1) // 2
    last_key = k_ref.shape[1] - units_per_row * UNIT + UNIT * (unit % units_per_row + 1)
    quads = q_ref.shape[2] // CHUNK
    per_quad = heads // quads
    groups = UNIT // GROUP
    lane_head = lax.broadcasted_iota(jnp.int32, (UNIT, CHUNK), 1) // (CHUNK // per_quad)
    for quad in range(quads):
        qx[quad] = spread_heads(q_ref[0], lane_head, quad, per_quad)
        total[quad] = jnp.zeros_like(total[quad])
    top[...] = jnp.full_like(top, masked)
    row_sum[...] = jnp.zeros_like(row_sum)

    def keys_of(chunk):
        return pl.ds(pl.multiple_of(last_key - CHUNK * (chunk + 1), UNIT), CHUNK)

    @pl.loop(0, chunks)
    def _(chunk):
        for quad in range(quads):
            s = dot_nt(qx[quad], k_ref[0, keys_of(chunk), quad * CHUNK : (quad + 1) * CHUNK])
            score[0, quad * per_quad : (quad + 1) * per_quad] = s.reshape(per_quad, UNIT, CHUNK).astype(jnp.bfloat16)
        for group in range(groups):
            rows = slice(GROUP * group, GROUP * (group + 1))
            l = dot_nn(mixl_ref[...], group_rows(score, 0, group, heads)).reshape(heads, GROUP, CHUNK)
            l = jnp.where(allowed_keys(chunk, group, blocks)[None], l, masked)
            logit[chunk, :, rows, :] = l
            top[:, rows, :] = jnp.maximum(top[:, rows, :], jnp.maximum(l[:, :, :UNIT], l[:, :, UNIT:]))

    for head in range(heads):
        top[head] = jnp.broadcast_to(jnp.max(top[head], axis=-1, keepdims=True), (UNIT, UNIT))

    @pl.loop(0, chunks)
    def _(chunk):
        for head in range(heads):
            row_top = top[head]
            left = jnp.exp(logit[chunk, head, :, :UNIT] - row_top)
            right = jnp.exp(logit[chunk, head, :, UNIT:] - row_top)
            logit[chunk, head, :, :UNIT] = left
            logit[chunk, head, :, UNIT:] = right
            row_sum[head] += left + right

    for head in range(heads):
        norm = jnp.broadcast_to(jnp.sum(row_sum[head], axis=-1, keepdims=True), (UNIT, UNIT))
        lse_ref[0, head] = top[head] + jnp.log(norm)
        row_sum[head] = 1.0 / norm

    @pl.loop(0, chunks)
    def _(chunk):
        for group in range(groups):
            rows = slice(GROUP * group, GROUP * (group + 1))
            scale = row_sum[:, rows, :]
            p = logit[chunk, :, rows, :]
            p = jnp.concatenate([p[:, :, :UNIT] * scale, p[:, :, UNIT:] * scale], axis=-1)
            p = p.astype(jnp.bfloat16).reshape(heads * GROUP, CHUNK)
            a = dot_nn(mixp_ref[...], p)
            mixed[:, rows, :] = a.astype(jnp.bfloat16).reshape(heads, GROUP, CHUNK)
        for quad in range(quads):
            a = mixed[quad * per_quad : (quad + 1) * per_quad].reshape(per_quad * UNIT, CHUNK)
            total[quad] += dot_nn(a, v_ref[0, keys_of(chunk), quad * CHUNK : (quad + 1) * CHUNK])

    for quad in range(quads):
        att_ref[0, :, quad * CHUNK : (quad + 1) * CHUNK] = own_lanes(total[quad], lane_head, per_quad).astype(jnp.bfloat16)


def attention_fwd(blocks, q, k, v, mixl, mixp, heads):
    units, _, width = q.shape
    per_row = units // k.shape[0]
    quads = width // CHUNK
    per_quad = heads // quads
    wide = heads * GROUP
    whole = pl.BlockSpec((wide, wide), lambda u, _: (0, 0))
    kv_spec = pl.BlockSpec((1,) + k.shape[1:], lambda u, _: (u // per_row, 0, 0))
    return pl.pallas_call(
        partial(fwd_kernel, heads, per_row),
        grid_spec=pltpu.PrefetchScalarGridSpec(
            num_scalar_prefetch=1,
            grid=(units,),
            in_specs=[
                pl.BlockSpec((1, UNIT, width), lambda u, _: (u, 0, 0)),
                kv_spec,
                kv_spec,
                whole,
                whole,
            ],
            out_specs=[
                pl.BlockSpec((1, UNIT, width), lambda u, _: (u, 0, 0)),
                pl.BlockSpec((1, heads, UNIT, UNIT), lambda u, _: (u, 0, 0, 0)),
            ],
            scratch_shapes=[
                pltpu.VMEM((quads, per_quad * UNIT, CHUNK), jnp.bfloat16),
                pltpu.VMEM((1, heads, UNIT, CHUNK), jnp.bfloat16),
                pltpu.VMEM((MAX_CHUNKS, heads, UNIT, CHUNK), jnp.float32),
                pltpu.VMEM((heads, UNIT, CHUNK), jnp.bfloat16),
                pltpu.VMEM((quads, per_quad * UNIT, CHUNK), jnp.float32),
                pltpu.VMEM((heads, UNIT, UNIT), jnp.float32),
                pltpu.VMEM((heads, UNIT, UNIT), jnp.float32),
            ],
        ),
        out_shape=[
            jax.ShapeDtypeStruct((units, UNIT, width), jnp.bfloat16),
            jax.ShapeDtypeStruct((units, heads, UNIT, UNIT), jnp.float32),
        ],
        compiler_params=pltpu.CompilerParams(vmem_limit_bytes=48 * 1024 * 1024),
        cost_estimate=pl.CostEstimate(flops=20_000_000_000, bytes_accessed=16_000_000, transcendentals=0),
        name="attention_fwd",
    )(blocks, q, k, v, mixl, mixp)


def bwd_kernel(heads, units_per_row, blocks_ref, q_ref, k_ref, v_ref, do_ref, lse_ref, mixl_ref, mixlt_ref, mixp_ref, mixpt_ref,
               dq_ref, dk_ref, dv_ref, gl_ref, gp_ref,
               qx, qxt, dox, doxt, score, prob, grad_prob, grad_mixed, mixed, delta, dq_total, dk_total, dv_total):
    unit = pl.program_id(0)
    blocks = blocks_ref[unit]
    chunks = (blocks + 1) // 2
    key_units = k_ref.shape[1] // UNIT
    inner = unit % units_per_row
    last_unit = key_units - units_per_row + inner + 1
    quads = q_ref.shape[2] // CHUNK
    per_quad = heads // quads
    groups = UNIT // GROUP
    lane_head = lax.broadcasted_iota(jnp.int32, (UNIT, CHUNK), 1) // (CHUNK // per_quad)

    @pl.when(unit == 0)
    def _():
        gl_ref[...] = jnp.zeros_like(gl_ref)
        gp_ref[...] = jnp.zeros_like(gp_ref)

    @pl.when(inner == 0)
    def _():
        dk_total[...] = jnp.zeros_like(dk_total)
        dv_total[...] = jnp.zeros_like(dv_total)

    for quad in range(quads):
        wide_q = spread_heads(q_ref[0], lane_head, quad, per_quad)
        qx[quad] = wide_q
        qxt[quad] = wide_q.T
        wide_o = spread_heads(do_ref[0], lane_head, quad, per_quad)
        dox[quad] = wide_o
        doxt[quad] = wide_o.T
        dq_total[quad] = jnp.zeros_like(dq_total[quad])
    delta[...] = jnp.zeros_like(delta)

    def keys_of(chunk):
        return pl.ds(pl.multiple_of((last_unit - 2 * (chunk + 1)) * UNIT, UNIT), CHUNK)

    def add_to(total, chunk, quad, term):
        first = last_unit - 2 * (chunk + 1)
        lanes = slice(quad * CHUNK, (quad + 1) * CHUNK)
        total[first, lanes, :] += term[:, :UNIT]
        total[first + 1, lanes, :] += term[:, UNIT:]

    @pl.loop(0, chunks)
    def _(chunk):
        for quad in range(quads):
            lanes = slice(quad * CHUNK, (quad + 1) * CHUNK)
            hs = slice(quad * per_quad, (quad + 1) * per_quad)
            s = dot_nt(qx[quad], k_ref[0, keys_of(chunk), lanes])
            score[chunk, hs] = s.reshape(per_quad, UNIT, CHUNK).astype(jnp.bfloat16)
            da = dot_nt(dox[quad], v_ref[0, keys_of(chunk), lanes])
            grad_mixed[0, hs] = da.reshape(per_quad, UNIT, CHUNK).astype(jnp.bfloat16)
        for group in range(groups):
            rows = slice(GROUP * group, GROUP * (group + 1))
            l = dot_nn(mixl_ref[...], group_rows(score, chunk, group, heads)).reshape(heads, GROUP, CHUNK)
            lse = lse_ref[0, :, rows, :]
            l = l - jnp.concatenate([lse, lse], axis=-1)
            p = jnp.exp(jnp.where(allowed_keys(chunk, group, blocks)[None], l, masked))
            p_low = p.astype(jnp.bfloat16)
            prob[chunk, :, rows, :] = p_low
            p_low = p_low.reshape(heads * GROUP, CHUNK)
            da = group_rows(grad_mixed, 0, group, heads)
            dp = dot_nn(mixpt_ref[...], da).reshape(heads, GROUP, CHUNK)
            grad_prob[chunk, :, rows, :] = dp
            term = p * dp
            delta[:, rows, :] += term[:, :, :UNIT] + term[:, :, UNIT:]
            mixed[:, rows, :] = dot_nn(mixp_ref[...], p_low).astype(jnp.bfloat16).reshape(heads, GROUP, CHUNK)
            gp_ref[...] += dot_nt(p_low, da)
        for quad in range(quads):
            a = mixed[quad * per_quad : (quad + 1) * per_quad].reshape(per_quad * UNIT, CHUNK)
            add_to(dv_total, chunk, quad, dot_nn(doxt[quad], a))

    for head in range(heads):
        delta[head] = jnp.broadcast_to(jnp.sum(delta[head], axis=-1, keepdims=True), (UNIT, UNIT))

    @pl.loop(0, chunks)
    def _(chunk):
        for group in range(groups):
            rows = slice(GROUP * group, GROUP * (group + 1))
            d = delta[:, rows, :]
            dp = grad_prob[chunk, :, rows, :] - jnp.concatenate([d, d], axis=-1)
            dl = (prob[chunk, :, rows, :].astype(jnp.float32) * dp).astype(jnp.bfloat16).reshape(heads * GROUP, CHUNK)
            ds = dot_nn(mixlt_ref[...], dl)
            mixed[:, rows, :] = ds.astype(jnp.bfloat16).reshape(heads, GROUP, CHUNK)
            gl_ref[...] += dot_nt(group_rows(score, chunk, group, heads), dl)
        for quad in range(quads):
            ds = mixed[quad * per_quad : (quad + 1) * per_quad].reshape(per_quad * UNIT, CHUNK)
            dq_total[quad] += dot_nn(ds, k_ref[0, keys_of(chunk), quad * CHUNK : (quad + 1) * CHUNK])
            add_to(dk_total, chunk, quad, dot_nn(qxt[quad], ds))

    for quad in range(quads):
        dq = own_lanes(dq_total[quad], lane_head, per_quad) * 0.125
        dq_ref[0, :, quad * CHUNK : (quad + 1) * CHUNK] = dq.astype(jnp.bfloat16)

    @pl.when(inner == units_per_row - 1)
    def _():
        for key_unit in range(key_units):
            keys = slice(key_unit * UNIT, (key_unit + 1) * UNIT)
            dk_ref[0, keys, :] = dk_total[key_unit].T.astype(dk_ref.dtype)
            dv_ref[0, keys, :] = dv_total[key_unit].T.astype(dv_ref.dtype)


def attention_bwd(blocks, q, k, v, grad_out, lse, mixl, mixlt, mixp, mixpt, heads):
    units, _, width = q.shape
    per_row = units // k.shape[0]
    key_units = k.shape[1] // UNIT
    quads = width // CHUNK
    per_quad = heads // quads
    wide = heads * GROUP
    whole = pl.BlockSpec((wide, wide), lambda u, _: (0, 0))
    kv_spec = pl.BlockSpec((1,) + k.shape[1:], lambda u, _: (u // per_row, 0, 0))
    unit_spec = pl.BlockSpec((1, UNIT, width), lambda u, _: (u, 0, 0))
    spread = (quads, per_quad * UNIT, CHUNK)
    return pl.pallas_call(
        partial(bwd_kernel, heads, per_row),
        grid_spec=pltpu.PrefetchScalarGridSpec(
            num_scalar_prefetch=1,
            grid=(units,),
            in_specs=[
                unit_spec,
                kv_spec,
                kv_spec,
                unit_spec,
                pl.BlockSpec((1, heads, UNIT, UNIT), lambda u, _: (u, 0, 0, 0)),
                whole,
                whole,
                whole,
                whole,
            ],
            out_specs=[unit_spec, kv_spec, kv_spec, whole, whole],
            scratch_shapes=[
                pltpu.VMEM(spread, jnp.bfloat16),
                pltpu.VMEM((quads, CHUNK, per_quad * UNIT), jnp.bfloat16),
                pltpu.VMEM(spread, jnp.bfloat16),
                pltpu.VMEM((quads, CHUNK, per_quad * UNIT), jnp.bfloat16),
                pltpu.VMEM((MAX_CHUNKS, heads, UNIT, CHUNK), jnp.bfloat16),
                pltpu.VMEM((MAX_CHUNKS, heads, UNIT, CHUNK), jnp.bfloat16),
                pltpu.VMEM((MAX_CHUNKS, heads, UNIT, CHUNK), jnp.float32),
                pltpu.VMEM((1, heads, UNIT, CHUNK), jnp.bfloat16),
                pltpu.VMEM((heads, UNIT, CHUNK), jnp.bfloat16),
                pltpu.VMEM((heads, UNIT, UNIT), jnp.float32),
                pltpu.VMEM(spread, jnp.float32),
                pltpu.VMEM((key_units, width, UNIT), jnp.float32),
                pltpu.VMEM((key_units, width, UNIT), jnp.float32),
            ],
        ),
        out_shape=[
            jax.ShapeDtypeStruct((units, UNIT, width), jnp.bfloat16),
            jax.ShapeDtypeStruct(k.shape, jnp.bfloat16),
            jax.ShapeDtypeStruct(v.shape, jnp.bfloat16),
            jax.ShapeDtypeStruct((wide, wide), jnp.float32),
            jax.ShapeDtypeStruct((wide, wide), jnp.float32),
        ],
        compiler_params=pltpu.CompilerParams(vmem_limit_bytes=56 * 1024 * 1024),
        cost_estimate=pl.CostEstimate(flops=60_000_000_000, bytes_accessed=24_000_000, transcendentals=0),
        name="attention_bwd",
    )(blocks, q, k, v, grad_out, lse, mixl, mixlt, mixp, mixpt)


def spread_mix(mix):
    heads = mix.shape[0]
    eye = jnp.eye(GROUP, dtype=mix.dtype)
    return (mix[:, None, :, None] * eye[None, :, None, :]).reshape(heads * GROUP, heads * GROUP)


def fold_mix(wide, heads):
    grid = wide.reshape(heads, GROUP, heads, GROUP)
    return jnp.sum(jnp.where(jnp.eye(GROUP, dtype=bool)[None, :, None, :], grid, 0.0), axis=(1, 3))


def from_behind(value, steps):
    count = lax.axis_size("dev")
    first, last = (max(0, -steps), min(count, count - steps))
    return lax.ppermute(value, "dev", [(source, source + steps) for source in range(first, last)])


def seq_starts(lengths_row, query_rows):
    seq_ends = jnp.cumsum(lengths_row)
    starts = seq_ends - lengths_row
    return jnp.max(jnp.where(starts[None, :] <= query_rows[:, None], starts[None, :], 0), axis=1)


def normalize(values, gain_vec):
    inv_rms = lax.rsqrt(jnp.mean(values * values, axis=-1, keepdims=True) + norm_eps)
    normed = values * inv_rms
    return (normed, inv_rms, (normed * gain_vec.astype(jnp.float32)).astype(jnp.bfloat16))


def norm_back(grad_hidden, normed, inv_rms, gain_vec):
    grad_gain = jnp.sum(grad_hidden * normed, axis=0)
    grad_normed = grad_hidden * gain_vec.astype(jnp.float32)
    inner_mean = jnp.mean(grad_normed * normed, axis=-1, keepdims=True)
    return (inv_rms * (grad_normed - normed * inner_mean), grad_gain)


def matmul(left, right):
    return jnp.dot(left, right, preferred_element_type=jnp.float32)


def matmul_left_t(left, right):
    return lax.dot_general(left, right, (((0,), (0,)), ((), ())), preferred_element_type=jnp.float32)


def matmul_right_t(left, right):
    return lax.dot_general(left, right, (((1,), (1,)), ((), ())), preferred_element_type=jnp.float32)


def exchange(value):
    return lax.all_to_all(value, "dev", split_axis=0, concat_axis=0, tiled=True)


def split_ids(tok_ids, own_rows):
    owner = tok_ids // own_rows
    place = jnp.arange(tok_ids.shape[0], dtype=jnp.int32)
    same = tok_ids[:, None] == tok_ids[None, :]
    repeated = jnp.any(same & (place[None, :] < place[:, None]), axis=1)
    before = (owner[:, None] == owner[None, :]) & (tok_ids[None, :] < tok_ids[:, None]) & ~repeated[None, :]
    return (owner, tok_ids % own_rows, jnp.sum(before, axis=1, dtype=jnp.int32))


def plan_round(ids, index, own_rows, stride, room):
    count = lax.axis_size("dev")
    owner, local, rank = ids
    here = rank - index * room
    slot = jnp.where((here >= 0) & (here < room), owner * stride + here, -1)
    chosen = slot[None, :] == jnp.arange(count * stride, dtype=jnp.int32)[:, None]
    wanted = jnp.max(jnp.where(chosen, local[None, :], -1), axis=1).reshape(count, stride)
    rounds = jnp.broadcast_to(jnp.max(rank) // room + 1, (count, stride))
    asked = exchange(jnp.concatenate([wanted, rounds], axis=1))
    pick = asked[:, :stride].reshape(-1, 1) == jnp.arange(own_rows, dtype=jnp.int32)[None, :]
    return (chosen.astype(jnp.bfloat16), pick.astype(jnp.bfloat16), jnp.max(asked[:, stride:]))


def answer(embedding, chosen, pick, stride, extra_row):
    count = lax.axis_size("dev")
    rows = matmul(pick, embedding).astype(jnp.bfloat16).reshape(count, stride, -1)
    if extra_row is not None:
        is_extra = (jnp.arange(stride, dtype=jnp.int32) == stride - 1)[None, :, None]
        rows = jnp.where(is_extra, extra_row[None, None, :], rows)
    got = exchange(rows.reshape(count * stride, -1))
    return (matmul_left_t(chosen, got).astype(jnp.bfloat16), got.reshape(count, stride, -1)[:, stride - 1])


def lookup(embedding, tok_ids, extra_row, stride, room):
    own_rows = embedding.shape[0]
    ids = split_ids(tok_ids, own_rows)
    chosen, pick, rounds = plan_round(ids, 0, own_rows, stride, room)
    first, extra = answer(embedding, chosen, pick, stride, extra_row)

    def more(carry):
        index, rows = carry
        again, its_pick, _ = plan_round(ids, index, own_rows, stride, room)
        return (index + 1, rows + answer(embedding, again, its_pick, stride, None)[0])

    _, rows = lax.while_loop(lambda carry: carry[0] < rounds, more, (jnp.int32(1), first))
    return (rows, extra, ids, chosen, pick, rounds)


def send_grads(grad_low, chosen, pick, stride, extra_rows):
    count = lax.axis_size("dev")
    summed = matmul(chosen, grad_low).astype(jnp.bfloat16).reshape(count, stride, -1)
    if extra_rows is not None:
        place = jnp.arange(stride, dtype=jnp.int32)[None, :, None]
        high, low = extra_rows
        summed = jnp.where(place == stride - 2, high[:, None, :], summed)
        summed = jnp.where(place == stride - 1, low[:, None, :], summed)
    got = exchange(summed.reshape(count * stride, -1))
    return (matmul_left_t(pick, got), got.reshape(count, stride, -1)[:, stride - 2 :])


def table_back(grad_rows, extra_rows, plan, own_rows, stride, room):
    ids, chosen, pick, rounds = plan
    grad_low = grad_rows.astype(jnp.bfloat16)
    first, extra = send_grads(grad_low, chosen, pick, stride, extra_rows)

    def more(carry):
        index, total = carry
        again, its_pick, _ = plan_round(ids, index, own_rows, stride, room)
        return (index + 1, total + send_grads(grad_low, again, its_pick, stride, None)[0])

    _, total = lax.while_loop(lambda carry: carry[0] < rounds, more, (jnp.int32(1), first))
    return (total, jnp.sum(extra.astype(jnp.float32), axis=(0, 1)))


def gather_parts(pieces):
    count = lax.axis_size("dev")
    sizes = [piece.shape[0] for piece in pieces]
    whole = lax.all_gather(jnp.concatenate(pieces, axis=0), "dev", axis=0, tiled=True)
    whole = whole.reshape(count, sum(sizes), -1)
    parts, start = ([], 0)
    for size in sizes:
        parts.append(whole[:, start : start + size].reshape(count * size, -1))
        start += size
    return parts


def stack_parts(parts):
    count = lax.axis_size("dev")
    shaped = [part.astype(jnp.bfloat16).reshape(count, part.shape[0] // count, -1) for part in parts]
    return jnp.concatenate(shaped, axis=1)


def scatter_sum(stacked):
    count = lax.axis_size("dev")
    return lax.psum_scatter(stacked.reshape(count * stacked.shape[1], -1), "dev", scatter_dimension=0, tiled=True)


def split_rows(summed, sizes):
    pieces, start = ([], 0)
    for size in sizes:
        pieces.append(summed[start : start + size].astype(jnp.float32))
        start += size
    return pieces


def halving_sum(parts):
    count = lax.axis_size("dev")
    steps = count.bit_length() - 1
    me = lax.axis_index("dev")
    sizes = [part.shape[0] // count for part in parts]
    stacked = stack_parts(parts)
    width = stacked.shape[-1]
    bits = stacked.reshape((2,) * steps + (sum(sizes), width))
    held = bits.transpose(tuple(reversed(range(steps))) + (steps, steps + 1)).reshape(count, sum(sizes), width)
    for step in range(steps):
        half = held.shape[0] // 2
        mine = (me >> step) & 1
        keep = lax.dynamic_slice_in_dim(held, mine * half, half, 0)
        give = lax.dynamic_slice_in_dim(held, (1 - mine) * half, half, 0)
        came = lax.ppermute(give, "dev", [(source, source ^ (1 << step)) for source in range(count)])
        total = keep.astype(jnp.float32) + came.astype(jnp.float32)
        held = total if step == steps - 1 else total.astype(jnp.bfloat16)
    return split_rows(held.reshape(sum(sizes), width), sizes)


def split_low(values):
    high = lax.reduce_precision(values, 8, 7)
    return (high.astype(jnp.bfloat16), (values - high).astype(jnp.bfloat16))


def shards(
    token_ids,
    lengths,
    embedding,
    norm1_gain,
    w_query,
    w_key,
    w_value,
    w_out,
    mix_logits,
    mix_weights,
    norm2_gain,
    w_up,
    w_down,
    cotangent,
):
    count = lax.axis_size("dev")
    me = lax.axis_index("dev")
    micros, row_count = token_ids.shape
    own_rows, width = embedding.shape
    heads = mix_logits.shape[0]
    part = norm1_gain.shape[0]
    per_row = row_count // UNIT
    tokens = micros * row_count
    tok_ids = token_ids.reshape(-1)
    stride = max(16, 1024 // count)
    room = stride - 2

    up_cols = w_up.shape[1] // width
    w_q, w_k, w_v = gather_parts([w_query, w_key, w_value])
    up_pieces = [w_up[:, col * width : (col + 1) * width] for col in range(up_cols)]
    late = gather_parts([w_out] + up_pieces + [w_down])
    w_o, w_d = (late[0], late[-1])
    w_u = jnp.concatenate(late[1:-1], axis=1)

    unit_rows = me * row_count + UNIT * jnp.arange(per_row, dtype=jnp.int32)
    begins = jnp.stack([seq_starts(lengths[micro], unit_rows) for micro in range(micros)])
    blocks = ((unit_rows[None, :] - begins) // UNIT + 1).reshape(-1).astype(jnp.int32)

    mixl, mixlt = (spread_mix(mix_logits.T), spread_mix(mix_logits))
    mixp, mixpt = (spread_mix(mix_weights.T), spread_mix(mix_weights))

    gains_row = jnp.concatenate([norm1_gain, norm2_gain, jnp.zeros((width - 2 * part,), jnp.bfloat16)])
    picked, gains, *plan = lookup(embedding, tok_ids, gains_row, stride, room)
    gain_one = gains[:, :part].reshape(-1)
    gain_two = gains[:, part : 2 * part].reshape(-1)
    inputs = picked.astype(jnp.float32)

    normed_one, inv_one, hidden_one = normalize(inputs, gain_one)
    own_hidden = hidden_one.reshape(micros, row_count, width)
    behind = [from_behind(own_hidden, steps) for steps in (1, 2, 3)]
    behind.append(from_behind(own_hidden[:, row_count - UNIT :], 4))
    all_hidden = jnp.concatenate(behind[::-1] + [own_hidden], axis=1)
    key_rows = all_hidden.shape[1]
    flat_hidden = all_hidden.reshape(micros * key_rows, width)
    query = (matmul(hidden_one, w_q).astype(jnp.bfloat16) * jnp.bfloat16(0.125)).reshape(-1, UNIT, width)
    key = matmul(flat_hidden, w_k).astype(jnp.bfloat16).reshape(micros, key_rows, width)
    value = matmul(flat_hidden, w_v).astype(jnp.bfloat16).reshape(micros, key_rows, width)
    attended, lse = attention_fwd(blocks, query, key, value, mixl, mixp, heads)
    attended = attended.reshape(tokens, width)

    middle = inputs + matmul(attended, w_o)
    normed_two, inv_two, hidden_two = normalize(middle, gain_two)
    up_proj = matmul(hidden_two, w_u)
    activated, gelu_pull = jax.vjp(jax.nn.gelu, up_proj)
    activated = activated.astype(jnp.bfloat16)
    output = (middle + matmul(activated, w_d)).astype(jnp.bfloat16)

    grad_rows = cotangent.reshape(tokens, width)
    grad_act = matmul_right_t(grad_rows, w_d)
    grad_upb = gelu_pull(grad_act)[0].astype(jnp.bfloat16)
    grad_down = matmul_left_t(activated, grad_rows)
    grad_up = matmul_left_t(hidden_two, grad_upb)
    grad_hidden_two = matmul_right_t(grad_upb, w_u)
    grad_mid_norm, grad_gain_two = norm_back(grad_hidden_two, normed_two, inv_two, gain_two)
    grad_middle = grad_rows.astype(jnp.float32) + grad_mid_norm
    grad_branch = grad_middle.astype(jnp.bfloat16)
    grad_wout = matmul_left_t(attended, grad_branch)
    grad_att = matmul_right_t(grad_branch, w_o).astype(jnp.bfloat16).reshape(-1, UNIT, width)
    up_terms = [grad_up[:, col * width : (col + 1) * width] for col in range(up_cols)]
    late_terms = [grad_wout] + up_terms + [grad_down]
    late_stack, grad_att = lax.optimization_barrier((stack_parts(late_terms), grad_att))
    late_sums = split_rows(scatter_sum(late_stack), [term.shape[0] // count for term in late_terms])

    grad_query, grad_key, grad_value, wide_logit, wide_prob = attention_bwd(
        blocks, query, key, value, grad_att, lse, mixl, mixlt, mixp, mixpt, heads
    )
    grad_query = grad_query.reshape(tokens, width)
    grad_key = grad_key.reshape(micros * key_rows, width)
    grad_value = grad_value.reshape(micros * key_rows, width)
    grad_flat = (matmul_right_t(grad_key, w_k) + matmul_right_t(grad_value, w_v)).reshape(micros, key_rows, width)
    returned = []
    start = 0
    for steps, size in ((4, UNIT), (3, row_count), (2, row_count), (1, row_count)):
        term = grad_flat[:, start : start + size].astype(jnp.bfloat16)
        returned.append((size, from_behind(term, -steps)))
        start += size
    grad_wq = matmul_left_t(hidden_one, grad_query)
    grad_wk = matmul_left_t(flat_hidden, grad_key)
    grad_wv = matmul_left_t(flat_hidden, grad_value)
    early_sums = halving_sum([grad_wq, grad_wk, grad_wv])
    grad_own = grad_flat[:, start:]
    for size, term in returned:
        term = term.astype(jnp.float32)
        if size < row_count:
            term = jnp.pad(term, ((0, 0), (row_count - size, 0), (0, 0)))
        grad_own = grad_own + term
    grad_hidden_one = grad_own.reshape(tokens, width) + matmul_right_t(grad_query, w_q)
    grad_in_norm, grad_gain_one = norm_back(grad_hidden_one, normed_one, inv_one, gain_one)
    grad_inputs = grad_middle + grad_in_norm

    mix_terms = jnp.concatenate([fold_mix(wide_logit, heads).reshape(-1), fold_mix(wide_prob, heads).reshape(-1)])
    mix_size = mix_terms.shape[0]
    small = jnp.concatenate(
        [
            grad_gain_one.reshape(count, part),
            grad_gain_two.reshape(count, part),
            jnp.broadcast_to(mix_terms[None, :], (count, mix_size)),
            jnp.zeros((count, width - 2 * part - mix_size), jnp.float32),
        ],
        axis=1,
    )
    grad_inputs, late_sums = lax.optimization_barrier((grad_inputs, late_sums))
    table_grad, small_sum = table_back(grad_inputs, split_low(small), plan, own_rows, stride, room)
    mixes = small_sum[2 * part : 2 * part + mix_size].reshape(2, heads, heads)
    return (
        output.reshape(micros, row_count, width),
        grad_inputs.reshape(micros, row_count, width),
        table_grad,
        small_sum[:part],
        early_sums[0],
        early_sums[1],
        early_sums[2],
        late_sums[0],
        mixes[0],
        mixes[1],
        small_sum[part : 2 * part],
        jnp.concatenate(late_sums[1:-1], axis=1),
        late_sums[-1],
    )


def solution(mesh):
    in_specs = (
        P(None, "dev"),
        P(),
        P("dev", None),
        P("dev"),
        P("dev", None),
        P("dev", None),
        P("dev", None),
        P("dev", None),
        P(),
        P(),
        P("dev"),
        P("dev", None),
        P("dev", None),
        P(None, "dev", None),
    )
    out_specs = (
        P(None, "dev", None),
        P(None, "dev", None),
        P("dev", None),
        P("dev"),
        P("dev", None),
        P("dev", None),
        P("dev", None),
        P("dev", None),
        P(),
        P(),
        P("dev"),
        P("dev", None),
        P("dev", None),
    )
    return jax.shard_map(shards, mesh=mesh, in_specs=in_specs, out_specs=out_specs, check_vma=False)
```

```python
from functools import partial

import jax
import jax.numpy as jnp
from jax import lax
from jax.experimental import pallas as pl
from jax.experimental.pallas import tpu as pltpu
from jax.sharding import PartitionSpec as P

norm_eps = 1e-06

masked = -1e30
UNIT = 128
CHUNK = 256
GROUP = 16
MAX_CHUNKS = 4


def dot_nn(left, right):
    return lax.dot_general(left, right, (((1,), (0,)), ((), ())), preferred_element_type=jnp.float32)


def dot_nt(left, right):
    return lax.dot_general(left, right, (((1,), (1,)), ((), ())), preferred_element_type=jnp.float32)


def spread_heads(rows, lane_head, quad, heads_per_quad):
    part = rows[:, quad * CHUNK : (quad + 1) * CHUNK]
    zero = jnp.zeros_like(part)
    return jnp.concatenate([jnp.where(lane_head == head, part, zero) for head in range(heads_per_quad)], axis=0)


def own_lanes(wide, lane_head, heads_per_quad):
    total = jnp.where(lane_head == 0, wide[:UNIT], 0.0)
    for head in range(1, heads_per_quad):
        total = total + jnp.where(lane_head == head, wide[head * UNIT : (head + 1) * UNIT], 0.0)
    return total


def allowed_keys(chunk, group, blocks):
    key = lax.broadcasted_iota(jnp.int32, (GROUP, CHUNK), 1) - (UNIT + CHUNK * chunk)
    row = lax.broadcasted_iota(jnp.int32, (GROUP, CHUNK), 0) + GROUP * group
    return (key <= row) & (key >= (1 - blocks) * UNIT)


def twice(rows):
    return jnp.concatenate([rows, rows], axis=-1)


def fwd_kernel(heads, blocks_ref, q_ref, k_ref, v_ref, mix_ref, att_ref, lse_ref, qx, score, logit, mixed, total):
    inner = pl.program_id(1)
    blocks = blocks_ref[pl.program_id(0) * pl.num_programs(1) + inner]
    chunks = (blocks + 1) // 2
    last_unit = k_ref.shape[0] - pl.num_programs(1) + inner + 1
    quads = q_ref.shape[3] // CHUNK
    per_quad = heads // quads
    groups = UNIT // GROUP
    wide = heads * GROUP
    lane_head = lax.broadcasted_iota(jnp.int32, (UNIT, CHUNK), 1) // (CHUNK // per_quad)
    for quad in range(quads):
        qx[quad] = spread_heads(q_ref[0, 0], lane_head, quad, per_quad)
    total[...] = jnp.zeros_like(total)

    def keys(ref, chunk, quad):
        units = pl.ds(last_unit - 2 * (chunk + 1), 2)
        return ref[units, 0, :, quad * CHUNK : (quad + 1) * CHUNK].reshape(CHUNK, CHUNK)

    @pl.loop(0, chunks)
    def _(chunk):
        for quad in range(quads):
            s = dot_nt(qx[quad], keys(k_ref, chunk, quad))
            score[quad * per_quad : (quad + 1) * per_quad] = s.reshape(per_quad, UNIT, CHUNK).astype(jnp.bfloat16)
        for group in range(groups):
            s = score[:, GROUP * group : GROUP * (group + 1), :].reshape(wide, CHUNK)
            l = dot_nn(mix_ref[0], s).reshape(heads, GROUP, CHUNK)
            l = jnp.where(allowed_keys(chunk, group, blocks)[None], l, masked)
            logit[chunk, group] = l.reshape(wide, CHUNK)

    for group in range(groups):
        def more_top(chunk, top):
            return jnp.maximum(top, jnp.maximum(logit[chunk, group, :, :UNIT], logit[chunk, group, :, UNIT:]))

        top = lax.fori_loop(0, chunks, more_top, jnp.full((wide, UNIT), masked, jnp.float32))
        top = jnp.broadcast_to(jnp.max(top, axis=-1, keepdims=True), (wide, UNIT))

        def more_sum(chunk, running):
            left = jnp.exp(logit[chunk, group, :, :UNIT] - top)
            return running + left + jnp.exp(logit[chunk, group, :, UNIT:] - top)

        norm = lax.fori_loop(0, chunks, more_sum, jnp.zeros((wide, UNIT), jnp.float32))
        norm = jnp.broadcast_to(jnp.sum(norm, axis=-1, keepdims=True), (wide, UNIT))
        lse_ref[0, 0, group] = top + jnp.log(norm)

    @pl.loop(0, chunks)
    def _(chunk):
        for group in range(groups):
            p = jnp.exp(logit[chunk, group] - twice(lse_ref[0, 0, group])).astype(jnp.bfloat16)
            a = dot_nn(mix_ref[2], p).astype(jnp.bfloat16)
            mixed[:, GROUP * group : GROUP * (group + 1), :] = a.reshape(heads, GROUP, CHUNK)
        for quad in range(quads):
            a = mixed[quad * per_quad : (quad + 1) * per_quad].reshape(per_quad * UNIT, CHUNK)
            o = own_lanes(dot_nn(a, keys(v_ref, chunk, quad)), lane_head, per_quad)
            total[:, quad * CHUNK : (quad + 1) * CHUNK] += o

    att_ref[0, 0] = total[...].astype(jnp.bfloat16)


def attention_specs(q, k, heads):
    per_row, micros, _, width = q.shape
    wide = heads * GROUP
    groups = UNIT // GROUP
    return (
        pl.BlockSpec((1, 1, UNIT, width), lambda m, u, _: (u, m, 0, 0)),
        pl.BlockSpec((k.shape[0], 1, UNIT, width), lambda m, u, _: (0, m, 0, 0)),
        pl.BlockSpec((1, 1, groups, wide, UNIT), lambda m, u, _: (u, m, 0, 0, 0)),
        pl.BlockSpec((4, wide, wide), lambda m, u, _: (0, 0, 0)),
    )


def attention_fwd(blocks, q, k, v, mixes, heads):
    per_row, micros, _, width = q.shape
    wide = heads * GROUP
    groups = UNIT // GROUP
    quads = width // CHUNK
    unit_spec, kv_spec, lse_spec, mix_spec = attention_specs(q, k, heads)
    return pl.pallas_call(
        partial(fwd_kernel, heads),
        grid_spec=pltpu.PrefetchScalarGridSpec(
            num_scalar_prefetch=1,
            grid=(micros, per_row),
            in_specs=[unit_spec, kv_spec, kv_spec, mix_spec],
            out_specs=[unit_spec, lse_spec],
            scratch_shapes=[
                pltpu.VMEM((quads, heads // quads * UNIT, CHUNK), jnp.bfloat16),
                pltpu.VMEM((heads, UNIT, CHUNK), jnp.bfloat16),
                pltpu.VMEM((MAX_CHUNKS, groups, wide, CHUNK), jnp.float32),
                pltpu.VMEM((heads, UNIT, CHUNK), jnp.bfloat16),
                pltpu.VMEM((UNIT, width), jnp.float32),
            ],
        ),
        out_shape=[
            jax.ShapeDtypeStruct(q.shape, jnp.bfloat16),
            jax.ShapeDtypeStruct((per_row, micros, groups, wide, UNIT), jnp.float32),
        ],
        compiler_params=pltpu.CompilerParams(vmem_limit_bytes=48 * 1024 * 1024),
        cost_estimate=pl.CostEstimate(flops=20_000_000_000, bytes_accessed=16_000_000, transcendentals=0),
        name="attention_fwd",
    )(blocks, q, k, v, mixes)


def bwd_kernel(heads, blocks_ref, q_ref, k_ref, v_ref, do_ref, lse_ref, mix_ref,
               dq_ref, dk_ref, dv_ref, gl_ref, gp_ref,
               qx, qxt, dox, doxt, score, prob, grad_prob, grad_mixed, grad_logit, mixed, delta, dq_total, dk_total, dv_total):
    micro, inner, per_row = (pl.program_id(0), pl.program_id(1), pl.num_programs(1))
    blocks = blocks_ref[micro * per_row + inner]
    chunks = (blocks + 1) // 2
    key_units = k_ref.shape[0]
    last_unit = key_units - per_row + inner + 1
    quads = q_ref.shape[3] // CHUNK
    per_quad = heads // quads
    groups = UNIT // GROUP
    wide = heads * GROUP
    lane_head = lax.broadcasted_iota(jnp.int32, (UNIT, CHUNK), 1) // (CHUNK // per_quad)
    row_head = lax.broadcasted_iota(jnp.int32, (CHUNK, UNIT), 0) // (CHUNK // per_quad)
    lowest = key_units
    for other in range(key_units - 7):
        its_chunks = (blocks_ref[micro * per_row + other] + 1) // 2
        lowest = jnp.minimum(lowest, key_units - per_row + other + 1 - 2 * its_chunks)

    @pl.when((micro == 0) & (inner == 0))
    def _():
        gl_ref[...] = jnp.zeros_like(gl_ref)
        gp_ref[...] = jnp.zeros_like(gp_ref)

    @pl.when(inner == 0)
    def _():
        @pl.loop(lowest, key_units)
        def _(key_unit):
            dk_total[key_unit] = jnp.zeros_like(dk_total[key_unit])
            dv_total[key_unit] = jnp.zeros_like(dv_total[key_unit])

    def spread_turned(rows, quad):
        turned = rows[:, quad * CHUNK : (quad + 1) * CHUNK].T
        zero = jnp.zeros_like(turned)
        return jnp.concatenate([jnp.where(row_head == head, turned, zero) for head in range(per_quad)], axis=1)

    for quad in range(quads):
        qx[quad] = spread_heads(q_ref[0, 0], lane_head, quad, per_quad)
        qxt[quad] = spread_turned(q_ref[0, 0], quad)
        dox[quad] = spread_heads(do_ref[0, 0], lane_head, quad, per_quad)
        doxt[quad] = spread_turned(do_ref[0, 0], quad)
    dq_total[...] = jnp.zeros_like(dq_total)
    delta[...] = jnp.zeros_like(delta)

    def keys(ref, chunk, quad):
        units = pl.ds(last_unit - 2 * (chunk + 1), 2)
        return ref[units, 0, :, quad * CHUNK : (quad + 1) * CHUNK].reshape(CHUNK, CHUNK)

    def add_to(total, chunk, quad, term):
        first = last_unit - 2 * (chunk + 1)
        lanes = slice(quad * CHUNK, (quad + 1) * CHUNK)
        total[first, lanes, :] += term[:, :UNIT]
        total[first + 1, lanes, :] += term[:, UNIT:]

    def put_groups(ref, quad, term):
        low = term.astype(jnp.bfloat16)
        for head in range(per_quad):
            rows = slice((quad * per_quad + head) * GROUP, (quad * per_quad + head + 1) * GROUP)
            for group in range(groups):
                start = head * UNIT + group * GROUP
                ref[rows, group * CHUNK : (group + 1) * CHUNK] = low[start : start + GROUP]

    @pl.loop(0, chunks)
    def _(chunk):
        for quad in range(quads):
            put_groups(score.at[chunk], quad, dot_nt(qx[quad], keys(k_ref, chunk, quad)))
            put_groups(grad_mixed, quad, dot_nt(dox[quad], keys(v_ref, chunk, quad)))
        for group in range(groups):
            cols = slice(group * CHUNK, (group + 1) * CHUNK)
            l = dot_nn(mix_ref[0], score[chunk, :, cols]) - twice(lse_ref[0, 0, group])
            allowed = allowed_keys(chunk, group, blocks)[None]
            p = jnp.exp(jnp.where(allowed, l.reshape(heads, GROUP, CHUNK), masked)).reshape(wide, CHUNK)
            p_low = p.astype(jnp.bfloat16)
            prob[chunk, :, cols] = p_low
            dp = dot_nn(mix_ref[3], grad_mixed[:, cols])
            grad_prob[chunk, :, cols] = dp.astype(grad_prob.dtype)
            term = p * dp
            delta[group] += term[:, :UNIT] + term[:, UNIT:]
            a = dot_nn(mix_ref[2], p_low).astype(jnp.bfloat16)
            mixed[:, GROUP * group : GROUP * (group + 1), :] = a.reshape(heads, GROUP, CHUNK)
        gp_ref[...] += dot_nt(prob[chunk], grad_mixed[...])
        for quad in range(quads):
            a = mixed[quad * per_quad : (quad + 1) * per_quad].reshape(per_quad * UNIT, CHUNK)
            add_to(dv_total, chunk, quad, dot_nn(doxt[quad], a))

    for group in range(groups):
        delta[group] = jnp.broadcast_to(jnp.sum(delta[group], axis=-1, keepdims=True), (wide, UNIT))

    @pl.loop(0, chunks)
    def _(chunk):
        for group in range(groups):
            cols = slice(group * CHUNK, (group + 1) * CHUNK)
            dp = grad_prob[chunk, :, cols].astype(jnp.float32) - twice(delta[group])
            dl = (prob[chunk, :, cols].astype(jnp.float32) * dp).astype(jnp.bfloat16)
            grad_logit[:, cols] = dl
            ds = dot_nn(mix_ref[1], dl).astype(jnp.bfloat16)
            mixed[:, GROUP * group : GROUP * (group + 1), :] = ds.reshape(heads, GROUP, CHUNK)
        gl_ref[...] += dot_nt(score[chunk], grad_logit[...])
        for quad in range(quads):
            ds = mixed[quad * per_quad : (quad + 1) * per_quad].reshape(per_quad * UNIT, CHUNK)
            dq = own_lanes(dot_nn(ds, keys(k_ref, chunk, quad)), lane_head, per_quad)
            dq_total[:, quad * CHUNK : (quad + 1) * CHUNK] += dq
            add_to(dk_total, chunk, quad, dot_nn(qxt[quad], ds))

    dq_ref[0, 0] = (dq_total[...] * 0.125).astype(jnp.bfloat16)

    @pl.when(inner == per_row - 1)
    def _():
        @pl.loop(0, lowest)
        def _(key_unit):
            dk_ref[key_unit, 0] = jnp.zeros_like(dk_ref[key_unit, 0])
            dv_ref[key_unit, 0] = jnp.zeros_like(dv_ref[key_unit, 0])

        @pl.loop(lowest, key_units)
        def _(key_unit):
            dk_ref[key_unit, 0] = dk_total[key_unit].astype(jnp.bfloat16).T
            dv_ref[key_unit, 0] = dv_total[key_unit].astype(jnp.bfloat16).T


def attention_bwd(blocks, q, k, v, grad_out, lse, mixes, heads):
    per_row, micros, _, width = q.shape
    key_units = k.shape[0]
    wide = heads * GROUP
    groups = UNIT // GROUP
    quads = width // CHUNK
    spread = (quads, heads // quads * UNIT, CHUNK)
    turned = (quads, CHUNK, heads // quads * UNIT)
    unit_spec, kv_spec, lse_spec, mix_spec = attention_specs(q, k, heads)
    sum_spec = pl.BlockSpec((wide, wide), lambda m, u, _: (0, 0))
    return pl.pallas_call(
        partial(bwd_kernel, heads),
        grid_spec=pltpu.PrefetchScalarGridSpec(
            num_scalar_prefetch=1,
            grid=(micros, per_row),
            in_specs=[unit_spec, kv_spec, kv_spec, unit_spec, lse_spec, mix_spec],
            out_specs=[unit_spec, kv_spec, kv_spec, sum_spec, sum_spec],
            scratch_shapes=[
                pltpu.VMEM(spread, jnp.bfloat16),
                pltpu.VMEM(turned, jnp.bfloat16),
                pltpu.VMEM(spread, jnp.bfloat16),
                pltpu.VMEM(turned, jnp.bfloat16),
                pltpu.VMEM((MAX_CHUNKS, wide, groups * CHUNK), jnp.bfloat16),
                pltpu.VMEM((MAX_CHUNKS, wide, groups * CHUNK), jnp.bfloat16),
                pltpu.VMEM((MAX_CHUNKS, wide, groups * CHUNK), jnp.bfloat16),
                pltpu.VMEM((wide, groups * CHUNK), jnp.bfloat16),
                pltpu.VMEM((wide, groups * CHUNK), jnp.bfloat16),
                pltpu.VMEM((heads, UNIT, CHUNK), jnp.bfloat16),
                pltpu.VMEM((groups, wide, UNIT), jnp.float32),
                pltpu.VMEM((UNIT, width), jnp.float32),
                pltpu.VMEM((key_units, width, UNIT), jnp.float32),
                pltpu.VMEM((key_units, width, UNIT), jnp.float32),
            ],
        ),
        out_shape=[
            jax.ShapeDtypeStruct(q.shape, jnp.bfloat16),
            jax.ShapeDtypeStruct(k.shape, jnp.bfloat16),
            jax.ShapeDtypeStruct(v.shape, jnp.bfloat16),
            jax.ShapeDtypeStruct((wide, wide), jnp.float32),
            jax.ShapeDtypeStruct((wide, wide), jnp.float32),
        ],
        compiler_params=pltpu.CompilerParams(vmem_limit_bytes=56 * 1024 * 1024),
        cost_estimate=pl.CostEstimate(flops=60_000_000_000, bytes_accessed=24_000_000, transcendentals=0),
        name="attention_bwd",
    )(blocks, q, k, v, grad_out, lse, mixes)


def spread_mixes(mix_logits, mix_weights):
    heads = mix_logits.shape[0]
    wide = heads * GROUP
    place = jnp.arange(wide, dtype=jnp.int32)
    pick = (place[:, None] // GROUP == jnp.arange(heads, dtype=jnp.int32)[None, :]).astype(mix_logits.dtype)
    same_row = (place[:, None] % GROUP == place[None, :] % GROUP)[None]
    tables = jnp.stack([mix_logits.T, mix_logits, mix_weights.T, mix_weights]).reshape(4 * heads, heads)
    across = jnp.dot(tables, pick.T, preferred_element_type=jnp.float32).astype(mix_logits.dtype)
    down = jnp.einsum("wh,bhx->bwx", pick, across.reshape(4, heads, wide), preferred_element_type=jnp.float32)
    return jnp.where(same_row, down, 0.0).astype(mix_logits.dtype)


def fold_mix(wide, heads):
    grid = wide.reshape(heads, GROUP, heads, GROUP)
    return jnp.sum(jnp.where(jnp.eye(GROUP, dtype=bool)[None, :, None, :], grid, 0.0), axis=(1, 3))


def from_behind(value, steps):
    count = lax.axis_size("dev")
    first, last = (max(0, -steps), min(count, count - steps))
    return lax.ppermute(value, "dev", [(source, source + steps) for source in range(first, last)])


def seq_starts(lengths_row, query_rows):
    seq_ends = jnp.cumsum(lengths_row)
    starts = seq_ends - lengths_row
    return jnp.max(jnp.where(starts[None, :] <= query_rows[:, None], starts[None, :], 0), axis=1)


def normalize(values, gain_vec):
    inv_rms = lax.rsqrt(jnp.mean(values * values, axis=-1, keepdims=True) + norm_eps)
    normed = values * inv_rms
    return (normed, inv_rms, (normed * gain_vec.astype(jnp.float32)).astype(jnp.bfloat16))


def norm_back(grad_hidden, normed, inv_rms, gain_vec):
    grad_gain = jnp.sum(grad_hidden * normed, axis=0)
    grad_normed = grad_hidden * gain_vec.astype(jnp.float32)
    inner_mean = jnp.mean(grad_normed * normed, axis=-1, keepdims=True)
    return (inv_rms * (grad_normed - normed * inner_mean), grad_gain)


def matmul(left, right):
    return jnp.dot(left, right, preferred_element_type=jnp.float32)


def matmul_left_t(left, right):
    return lax.dot_general(left, right, (((0,), (0,)), ((), ())), preferred_element_type=jnp.float32)


def matmul_right_t(left, right):
    return lax.dot_general(left, right, (((1,), (1,)), ((), ())), preferred_element_type=jnp.float32)


def exchange(value):
    return lax.all_to_all(value, "dev", split_axis=0, concat_axis=0, tiled=True)


def split_ids(tok_ids, own_rows):
    owner = tok_ids // own_rows
    place = jnp.arange(tok_ids.shape[0], dtype=jnp.int32)
    same = tok_ids[:, None] == tok_ids[None, :]
    repeated = jnp.any(same & (place[None, :] < place[:, None]), axis=1)
    before = (owner[:, None] == owner[None, :]) & (tok_ids[None, :] < tok_ids[:, None]) & ~repeated[None, :]
    return (owner, tok_ids % own_rows, jnp.sum(before, axis=1, dtype=jnp.int32))


def plan_round(ids, index, own_rows, stride, room):
    count = lax.axis_size("dev")
    owner, local, rank = ids
    here = rank - index * room
    slot = jnp.where((here >= 0) & (here < room), owner * stride + here, -1)
    chosen = slot[None, :] == jnp.arange(count * stride, dtype=jnp.int32)[:, None]
    wanted = jnp.max(jnp.where(chosen, local[None, :], -1), axis=1).reshape(count, stride)
    rounds = jnp.broadcast_to(jnp.max(rank) // room + 1, (count, stride))
    asked = exchange(jnp.concatenate([wanted, rounds], axis=1))
    pick = asked[:, :stride].reshape(-1, 1) == jnp.arange(own_rows, dtype=jnp.int32)[None, :]
    return (chosen.astype(jnp.bfloat16), pick.astype(jnp.bfloat16), jnp.max(asked[:, stride:]))


def answer(embedding, chosen, pick, stride, extra_row):
    count = lax.axis_size("dev")
    rows = matmul(pick, embedding).astype(jnp.bfloat16).reshape(count, stride, -1)
    if extra_row is not None:
        is_extra = (jnp.arange(stride, dtype=jnp.int32) == stride - 1)[None, :, None]
        rows = jnp.where(is_extra, extra_row[None, None, :], rows)
    got = exchange(rows.reshape(count * stride, -1))
    return (matmul_left_t(chosen, got).astype(jnp.bfloat16), got.reshape(count, stride, -1)[:, stride - 1])


def lookup(embedding, tok_ids, extra_row, stride, room):
    own_rows = embedding.shape[0]
    ids = split_ids(tok_ids, own_rows)
    chosen, pick, rounds = plan_round(ids, 0, own_rows, stride, room)
    first, extra = answer(embedding, chosen, pick, stride, extra_row)

    def more(carry):
        index, rows = carry
        again, its_pick, _ = plan_round(ids, index, own_rows, stride, room)
        return (index + 1, rows + answer(embedding, again, its_pick, stride, None)[0])

    _, rows = lax.while_loop(lambda carry: carry[0] < rounds, more, (jnp.int32(1), first))
    return (rows, extra, ids, chosen, pick, rounds)


def send_grads(grad_low, chosen, pick, stride, extra_rows):
    count = lax.axis_size("dev")
    summed = matmul(chosen, grad_low).astype(jnp.bfloat16).reshape(count, stride, -1)
    if extra_rows is not None:
        place = jnp.arange(stride, dtype=jnp.int32)[None, :, None]
        high, low = extra_rows
        summed = jnp.where(place == stride - 2, high[:, None, :], summed)
        summed = jnp.where(place == stride - 1, low[:, None, :], summed)
    got = exchange(summed.reshape(count * stride, -1))
    return (matmul_left_t(pick, got), got.reshape(count, stride, -1)[:, stride - 2 :])


def table_back(grad_rows, extra_rows, plan, own_rows, stride, room):
    ids, chosen, pick, rounds = plan
    grad_low = grad_rows.astype(jnp.bfloat16)
    first, extra = send_grads(grad_low, chosen, pick, stride, extra_rows)

    def more(carry):
        index, total = carry
        again, its_pick, _ = plan_round(ids, index, own_rows, stride, room)
        return (index + 1, total + send_grads(grad_low, again, its_pick, stride, None)[0])

    _, total = lax.while_loop(lambda carry: carry[0] < rounds, more, (jnp.int32(1), first))
    return (total, jnp.sum(extra.astype(jnp.float32), axis=(0, 1)))


def gather_parts(pieces):
    count = lax.axis_size("dev")
    sizes = [piece.shape[0] for piece in pieces]
    whole = lax.all_gather(jnp.concatenate(pieces, axis=0), "dev", axis=0, tiled=True)
    whole = whole.reshape(count, sum(sizes), -1)
    parts, start = ([], 0)
    for size in sizes:
        parts.append(whole[:, start : start + size].reshape(count * size, -1))
        start += size
    return parts


def stack_parts(parts):
    count = lax.axis_size("dev")
    shaped = [part.astype(jnp.bfloat16).reshape(count, part.shape[0] // count, -1) for part in parts]
    return jnp.concatenate(shaped, axis=1)


def scatter_sum(stacked):
    count = lax.axis_size("dev")
    return lax.psum_scatter(stacked.reshape(count * stacked.shape[1], -1), "dev", scatter_dimension=0, tiled=True)


def split_rows(summed, sizes):
    pieces, start = ([], 0)
    for size in sizes:
        pieces.append(summed[start : start + size].astype(jnp.float32))
        start += size
    return pieces


def halving_sum(parts):
    count = lax.axis_size("dev")
    steps = count.bit_length() - 1
    me = lax.axis_index("dev")
    sizes = [part.shape[0] // count for part in parts]
    stacked = stack_parts(parts)
    width = stacked.shape[-1]
    bits = stacked.reshape((2,) * steps + (sum(sizes), width))
    held = bits.transpose(tuple(reversed(range(steps))) + (steps, steps + 1)).reshape(count, sum(sizes), width)
    for step in range(steps):
        half = held.shape[0] // 2
        mine = (me >> step) & 1
        keep = lax.dynamic_slice_in_dim(held, mine * half, half, 0)
        give = lax.dynamic_slice_in_dim(held, (1 - mine) * half, half, 0)
        came = lax.ppermute(give, "dev", [(source, source ^ (1 << step)) for source in range(count)])
        total = keep.astype(jnp.float32) + came.astype(jnp.float32)
        held = total if step == steps - 1 else total.astype(jnp.bfloat16)
    return split_rows(held.reshape(sum(sizes), width), sizes)


def split_low(values):
    high = lax.reduce_precision(values, 8, 7)
    return (high.astype(jnp.bfloat16), (values - high).astype(jnp.bfloat16))


def by_unit(array):
    cut = array.reshape((array.shape[0], array.shape[1] // UNIT, UNIT) + array.shape[2:])
    return cut.swapaxes(0, 1)


def by_row(array, micros):
    cut = array.reshape(-1, micros, UNIT, array.shape[-1])
    return cut.swapaxes(0, 1).reshape(micros, -1, array.shape[-1])


def shards(
    token_ids,
    lengths,
    embedding,
    norm1_gain,
    w_query,
    w_key,
    w_value,
    w_out,
    mix_logits,
    mix_weights,
    norm2_gain,
    w_up,
    w_down,
    cotangent,
):
    count = lax.axis_size("dev")
    me = lax.axis_index("dev")
    micros, row_count = token_ids.shape
    own_rows, width = embedding.shape
    heads = mix_logits.shape[0]
    part = norm1_gain.shape[0]
    per_row = row_count // UNIT
    tokens = micros * row_count
    tok_ids = by_unit(token_ids).reshape(-1)
    stride = max(16, 1024 // count)
    room = stride - 2

    up_cols = w_up.shape[1] // width
    w_q, w_k, w_v = gather_parts([w_query, w_key, w_value])
    up_pieces = [w_up[:, col * width : (col + 1) * width] for col in range(up_cols)]
    late = gather_parts([w_out] + up_pieces + [w_down])
    w_o, w_d = (late[0], late[-1])
    w_u = jnp.concatenate(late[1:-1], axis=1)

    unit_rows = me * row_count + UNIT * jnp.arange(per_row, dtype=jnp.int32)
    begins = jnp.stack([seq_starts(lengths[micro], unit_rows) for micro in range(micros)])
    blocks = ((unit_rows[None, :] - begins) // UNIT + 1).reshape(-1).astype(jnp.int32)

    mixes = spread_mixes(mix_logits, mix_weights)

    gains_row = jnp.concatenate([norm1_gain, norm2_gain, jnp.zeros((width - 2 * part,), jnp.bfloat16)])
    picked, gains, *plan = lookup(embedding, tok_ids, gains_row, stride, room)
    gain_one = gains[:, :part].reshape(-1)
    gain_two = gains[:, part : 2 * part].reshape(-1)
    inputs = picked.astype(jnp.float32)

    normed_one, inv_one, hidden_one = normalize(inputs, gain_one)
    own_hidden = hidden_one.reshape(per_row, micros, UNIT, width)
    behind = [from_behind(own_hidden, steps) for steps in (1, 2, 3)]
    behind.append(from_behind(own_hidden[per_row - 1 :], 4))
    all_hidden = jnp.concatenate(behind[::-1] + [own_hidden], axis=0)
    flat_hidden = all_hidden.reshape(-1, width)
    query = (matmul(hidden_one, w_q).astype(jnp.bfloat16) * jnp.bfloat16(0.125)).reshape(own_hidden.shape)
    key = matmul(flat_hidden, w_k).astype(jnp.bfloat16).reshape(all_hidden.shape)
    value = matmul(flat_hidden, w_v).astype(jnp.bfloat16).reshape(all_hidden.shape)
    attended, lse = attention_fwd(blocks, query, key, value, mixes, heads)
    attended = attended.reshape(tokens, width)

    middle = inputs + matmul(attended, w_o)
    normed_two, inv_two, hidden_two = normalize(middle, gain_two)
    up_proj = matmul(hidden_two, w_u)
    activated, gelu_pull = jax.vjp(jax.nn.gelu, up_proj)
    activated = activated.astype(jnp.bfloat16)
    output = (middle + matmul(activated, w_d)).astype(jnp.bfloat16)

    grad_rows = by_unit(cotangent).reshape(tokens, width)
    grad_act = matmul_right_t(grad_rows, w_d)
    grad_upb = gelu_pull(grad_act)[0].astype(jnp.bfloat16)
    grad_down = matmul_left_t(activated, grad_rows)
    grad_up = matmul_left_t(hidden_two, grad_upb)
    grad_hidden_two = matmul_right_t(grad_upb, w_u)
    grad_mid_norm, grad_gain_two = norm_back(grad_hidden_two, normed_two, inv_two, gain_two)
    grad_middle = grad_rows.astype(jnp.float32) + grad_mid_norm
    grad_branch = grad_middle.astype(jnp.bfloat16)
    grad_wout = matmul_left_t(attended, grad_branch)
    grad_att = matmul_right_t(grad_branch, w_o).astype(jnp.bfloat16).reshape(own_hidden.shape)
    up_terms = [grad_up[:, col * width : (col + 1) * width] for col in range(up_cols)]
    late_terms = [grad_wout] + up_terms + [grad_down]
    late_stack, grad_att = lax.optimization_barrier((stack_parts(late_terms), grad_att))
    late_sums = split_rows(scatter_sum(late_stack), [term.shape[0] // count for term in late_terms])

    grad_query, grad_key, grad_value, wide_logit, wide_prob = attention_bwd(
        blocks, query, key, value, grad_att, lse, mixes, heads
    )
    grad_query = grad_query.reshape(tokens, width)
    grad_key = grad_key.reshape(-1, width)
    grad_value = grad_value.reshape(-1, width)
    grad_flat = (matmul_right_t(grad_key, w_k) + matmul_right_t(grad_value, w_v)).reshape(all_hidden.shape)
    returned = []
    start = 0
    for steps, size in ((4, 1), (3, per_row), (2, per_row), (1, per_row)):
        term = grad_flat[start : start + size].astype(jnp.bfloat16)
        returned.append((size, from_behind(term, -steps)))
        start += size
    grad_wq = matmul_left_t(hidden_one, grad_query)
    grad_wk = matmul_left_t(flat_hidden, grad_key)
    grad_wv = matmul_left_t(flat_hidden, grad_value)
    early_sums = halving_sum([grad_wq, grad_wk, grad_wv])
    grad_own = grad_flat[start:]
    for size, term in returned:
        term = term.astype(jnp.float32)
        if size < per_row:
            term = jnp.pad(term, ((per_row - size, 0), (0, 0), (0, 0), (0, 0)))
        grad_own = grad_own + term
    grad_hidden_one = grad_own.reshape(tokens, width) + matmul_right_t(grad_query, w_q)
    grad_in_norm, grad_gain_one = norm_back(grad_hidden_one, normed_one, inv_one, gain_one)
    grad_inputs = grad_middle + grad_in_norm

    mix_terms = jnp.concatenate([fold_mix(wide_logit, heads).reshape(-1), fold_mix(wide_prob, heads).reshape(-1)])
    mix_size = mix_terms.shape[0]
    small = jnp.concatenate(
        [
            grad_gain_one.reshape(count, part),
            grad_gain_two.reshape(count, part),
            jnp.broadcast_to(mix_terms[None, :], (count, mix_size)),
            jnp.zeros((count, width - 2 * part - mix_size), jnp.float32),
        ],
        axis=1,
    )
    grad_inputs, late_sums = lax.optimization_barrier((grad_inputs, late_sums))
    table_grad, small_sum = table_back(grad_inputs, split_low(small), plan, own_rows, stride, room)
    mixes = small_sum[2 * part : 2 * part + mix_size].reshape(2, heads, heads)
    return (
        by_row(output, micros),
        by_row(grad_inputs, micros),
        table_grad,
        small_sum[:part],
        early_sums[0],
        early_sums[1],
        early_sums[2],
        late_sums[0],
        mixes[0],
        mixes[1],
        small_sum[part : 2 * part],
        jnp.concatenate(late_sums[1:-1], axis=1),
        late_sums[-1],
    )


def solution(mesh):
    in_specs = (
        P(None, "dev"),
        P(),
        P("dev", None),
        P("dev"),
        P("dev", None),
        P("dev", None),
        P("dev", None),
        P("dev", None),
        P(),
        P(),
        P("dev"),
        P("dev", None),
        P("dev", None),
        P(None, "dev", None),
    )
    out_specs = (
        P(None, "dev", None),
        P(None, "dev", None),
        P("dev", None),
        P("dev"),
        P("dev", None),
        P("dev", None),
        P("dev", None),
        P("dev", None),
        P(),
        P(),
        P("dev"),
        P("dev", None),
        P("dev", None),
    )
    return jax.shard_map(shards, mesh=mesh, in_specs=in_specs, out_specs=out_specs, check_vma=False)
```

```python
from functools import partial

import jax
import jax.numpy as jnp
from jax import lax
from jax.experimental import pallas as pl
from jax.experimental.pallas import tpu as pltpu
from jax.sharding import Mesh
from jax.sharding import PartitionSpec as P

norm_eps = 1e-06
AXES = ("outer", "inner")

masked = -1e30
UNIT = 128
CHUNK = 256
GROUP = 16
MAX_CHUNKS = 4


def dot_nn(left, right):
    return lax.dot_general(left, right, (((1,), (0,)), ((), ())), preferred_element_type=jnp.float32)


def dot_nt(left, right):
    return lax.dot_general(left, right, (((1,), (1,)), ((), ())), preferred_element_type=jnp.float32)


def spread_heads(rows, lane_head, quad, heads_per_quad):
    part = rows[:, quad * CHUNK : (quad + 1) * CHUNK]
    zero = jnp.zeros_like(part)
    return jnp.concatenate([jnp.where(lane_head == head, part, zero) for head in range(heads_per_quad)], axis=0)


def own_lanes(wide, lane_head, heads_per_quad):
    total = jnp.where(lane_head == 0, wide[:UNIT], 0.0)
    for head in range(1, heads_per_quad):
        total = total + jnp.where(lane_head == head, wide[head * UNIT : (head + 1) * UNIT], 0.0)
    return total


def allowed_keys(chunk, group, blocks):
    key = lax.broadcasted_iota(jnp.int32, (GROUP, CHUNK), 1) - (UNIT + CHUNK * chunk)
    row = lax.broadcasted_iota(jnp.int32, (GROUP, CHUNK), 0) + GROUP * group
    return (key <= row) & (key >= (1 - blocks) * UNIT)


def twice(rows):
    return jnp.concatenate([rows, rows], axis=-1)


def fwd_kernel(heads, blocks_ref, q_ref, k_ref, v_ref, mix_ref, att_ref, lse_ref, qx, score, logit, mixed, total):
    inner = pl.program_id(1)
    blocks = blocks_ref[pl.program_id(0) * pl.num_programs(1) + inner]
    chunks = (blocks + 1) // 2
    last_unit = k_ref.shape[0] - pl.num_programs(1) + inner + 1
    quads = q_ref.shape[3] // CHUNK
    per_quad = heads // quads
    groups = UNIT // GROUP
    wide = heads * GROUP
    lane_head = lax.broadcasted_iota(jnp.int32, (UNIT, CHUNK), 1) // (CHUNK // per_quad)
    for quad in range(quads):
        qx[quad] = spread_heads(q_ref[0, 0], lane_head, quad, per_quad)
    total[...] = jnp.zeros_like(total)

    def keys(ref, chunk, quad):
        units = pl.ds(last_unit - 2 * (chunk + 1), 2)
        return ref[units, 0, :, quad * CHUNK : (quad + 1) * CHUNK].reshape(CHUNK, CHUNK)

    @pl.loop(0, chunks)
    def _(chunk):
        for quad in range(quads):
            s = dot_nt(qx[quad], keys(k_ref, chunk, quad))
            score[quad * per_quad : (quad + 1) * per_quad] = s.reshape(per_quad, UNIT, CHUNK).astype(jnp.bfloat16)
        for group in range(groups):
            s = score[:, GROUP * group : GROUP * (group + 1), :].reshape(wide, CHUNK)
            l = dot_nn(mix_ref[0], s).reshape(heads, GROUP, CHUNK)
            l = jnp.where(allowed_keys(chunk, group, blocks)[None], l, masked)
            logit[chunk, group] = l.reshape(wide, CHUNK)

    for group in range(groups):
        def more_top(chunk, top):
            return jnp.maximum(top, jnp.maximum(logit[chunk, group, :, :UNIT], logit[chunk, group, :, UNIT:]))

        top = lax.fori_loop(0, chunks, more_top, jnp.full((wide, UNIT), masked, jnp.float32))
        top = jnp.broadcast_to(jnp.max(top, axis=-1, keepdims=True), (wide, UNIT))

        def more_sum(chunk, running):
            left = jnp.exp(logit[chunk, group, :, :UNIT] - top)
            return running + left + jnp.exp(logit[chunk, group, :, UNIT:] - top)

        norm = lax.fori_loop(0, chunks, more_sum, jnp.zeros((wide, UNIT), jnp.float32))
        norm = jnp.broadcast_to(jnp.sum(norm, axis=-1, keepdims=True), (wide, UNIT))
        lse_ref[0, 0, group] = top + jnp.log(norm)

    @pl.loop(0, chunks)
    def _(chunk):
        for group in range(groups):
            p = jnp.exp(logit[chunk, group] - twice(lse_ref[0, 0, group])).astype(jnp.bfloat16)
            a = dot_nn(mix_ref[2], p).astype(jnp.bfloat16)
            mixed[:, GROUP * group : GROUP * (group + 1), :] = a.reshape(heads, GROUP, CHUNK)
        for quad in range(quads):
            a = mixed[quad * per_quad : (quad + 1) * per_quad].reshape(per_quad * UNIT, CHUNK)
            o = own_lanes(dot_nn(a, keys(v_ref, chunk, quad)), lane_head, per_quad)
            total[:, quad * CHUNK : (quad + 1) * CHUNK] += o

    att_ref[0, 0] = total[...].astype(jnp.bfloat16)


def attention_specs(q, k, heads):
    per_row, micros, _, width = q.shape
    wide = heads * GROUP
    groups = UNIT // GROUP
    return (
        pl.BlockSpec((1, 1, UNIT, width), lambda m, u, _: (u, m, 0, 0)),
        pl.BlockSpec((k.shape[0], 1, UNIT, width), lambda m, u, _: (0, m, 0, 0)),
        pl.BlockSpec((1, 1, groups, wide, UNIT), lambda m, u, _: (u, m, 0, 0, 0)),
        pl.BlockSpec((4, wide, wide), lambda m, u, _: (0, 0, 0)),
    )


def attention_fwd(blocks, q, k, v, mixes, heads):
    per_row, micros, _, width = q.shape
    wide = heads * GROUP
    groups = UNIT // GROUP
    quads = width // CHUNK
    unit_spec, kv_spec, lse_spec, mix_spec = attention_specs(q, k, heads)
    return pl.pallas_call(
        partial(fwd_kernel, heads),
        grid_spec=pltpu.PrefetchScalarGridSpec(
            num_scalar_prefetch=1,
            grid=(micros, per_row),
            in_specs=[unit_spec, kv_spec, kv_spec, mix_spec],
            out_specs=[unit_spec, lse_spec],
            scratch_shapes=[
                pltpu.VMEM((quads, heads // quads * UNIT, CHUNK), jnp.bfloat16),
                pltpu.VMEM((heads, UNIT, CHUNK), jnp.bfloat16),
                pltpu.VMEM((MAX_CHUNKS, groups, wide, CHUNK), jnp.float32),
                pltpu.VMEM((heads, UNIT, CHUNK), jnp.bfloat16),
                pltpu.VMEM((UNIT, width), jnp.float32),
            ],
        ),
        out_shape=[
            jax.ShapeDtypeStruct(q.shape, jnp.bfloat16),
            jax.ShapeDtypeStruct((per_row, micros, groups, wide, UNIT), jnp.float32),
        ],
        compiler_params=pltpu.CompilerParams(vmem_limit_bytes=48 * 1024 * 1024),
        cost_estimate=pl.CostEstimate(flops=20_000_000_000, bytes_accessed=16_000_000, transcendentals=0),
        name="attention_fwd",
    )(blocks, q, k, v, mixes)


def bwd_kernel(heads, blocks_ref, q_ref, k_ref, v_ref, do_ref, lse_ref, mix_ref,
               dq_ref, dk_ref, dv_ref, gl_ref, gp_ref,
               qx, qxt, dox, doxt, score, prob, grad_prob, grad_mixed, grad_logit, mixed, delta, dq_total, dk_total, dv_total):
    micro, inner, per_row = (pl.program_id(0), pl.program_id(1), pl.num_programs(1))
    blocks = blocks_ref[micro * per_row + inner]
    chunks = (blocks + 1) // 2
    key_units = k_ref.shape[0]
    last_unit = key_units - per_row + inner + 1
    quads = q_ref.shape[3] // CHUNK
    per_quad = heads // quads
    groups = UNIT // GROUP
    wide = heads * GROUP
    lane_head = lax.broadcasted_iota(jnp.int32, (UNIT, CHUNK), 1) // (CHUNK // per_quad)
    row_head = lax.broadcasted_iota(jnp.int32, (CHUNK, UNIT), 0) // (CHUNK // per_quad)
    lowest = key_units
    for other in range(key_units - 7):
        its_chunks = (blocks_ref[micro * per_row + other] + 1) // 2
        lowest = jnp.minimum(lowest, key_units - per_row + other + 1 - 2 * its_chunks)

    @pl.when((micro == 0) & (inner == 0))
    def _():
        gl_ref[...] = jnp.zeros_like(gl_ref)
        gp_ref[...] = jnp.zeros_like(gp_ref)

    @pl.when(inner == 0)
    def _():
        @pl.loop(lowest, key_units)
        def _(key_unit):
            dk_total[key_unit] = jnp.zeros_like(dk_total[key_unit])
            dv_total[key_unit] = jnp.zeros_like(dv_total[key_unit])

    def spread_turned(rows, quad):
        turned = rows[:, quad * CHUNK : (quad + 1) * CHUNK].T
        zero = jnp.zeros_like(turned)
        return jnp.concatenate([jnp.where(row_head == head, turned, zero) for head in range(per_quad)], axis=1)

    for quad in range(quads):
        qx[quad] = spread_heads(q_ref[0, 0], lane_head, quad, per_quad)
        qxt[quad] = spread_turned(q_ref[0, 0], quad)
        dox[quad] = spread_heads(do_ref[0, 0], lane_head, quad, per_quad)
        doxt[quad] = spread_turned(do_ref[0, 0], quad)
    dq_total[...] = jnp.zeros_like(dq_total)
    delta[...] = jnp.zeros_like(delta)

    def keys(ref, chunk, quad):
        units = pl.ds(last_unit - 2 * (chunk + 1), 2)
        return ref[units, 0, :, quad * CHUNK : (quad + 1) * CHUNK].reshape(CHUNK, CHUNK)

    def add_to(total, chunk, quad, term):
        first = last_unit - 2 * (chunk + 1)
        lanes = slice(quad * CHUNK, (quad + 1) * CHUNK)
        total[first, lanes, :] += term[:, :UNIT]
        total[first + 1, lanes, :] += term[:, UNIT:]

    def put_groups(ref, quad, term):
        low = term.astype(jnp.bfloat16)
        for head in range(per_quad):
            rows = slice((quad * per_quad + head) * GROUP, (quad * per_quad + head + 1) * GROUP)
            for group in range(groups):
                start = head * UNIT + group * GROUP
                ref[rows, group * CHUNK : (group + 1) * CHUNK] = low[start : start + GROUP]

    @pl.loop(0, chunks)
    def _(chunk):
        for quad in range(quads):
            put_groups(score.at[chunk], quad, dot_nt(qx[quad], keys(k_ref, chunk, quad)))
            put_groups(grad_mixed, quad, dot_nt(dox[quad], keys(v_ref, chunk, quad)))
        for group in range(groups):
            cols = slice(group * CHUNK, (group + 1) * CHUNK)
            l = dot_nn(mix_ref[0], score[chunk, :, cols]) - twice(lse_ref[0, 0, group])
            allowed = allowed_keys(chunk, group, blocks)[None]
            p = jnp.exp(jnp.where(allowed, l.reshape(heads, GROUP, CHUNK), masked)).reshape(wide, CHUNK)
            p_low = p.astype(jnp.bfloat16)
            prob[chunk, :, cols] = p_low
            dp = dot_nn(mix_ref[3], grad_mixed[:, cols])
            grad_prob[chunk, :, cols] = dp.astype(grad_prob.dtype)
            term = p * dp
            delta[group] += term[:, :UNIT] + term[:, UNIT:]
            a = dot_nn(mix_ref[2], p_low).astype(jnp.bfloat16)
            mixed[:, GROUP * group : GROUP * (group + 1), :] = a.reshape(heads, GROUP, CHUNK)
        gp_ref[...] += dot_nt(prob[chunk], grad_mixed[...])
        for quad in range(quads):
            a = mixed[quad * per_quad : (quad + 1) * per_quad].reshape(per_quad * UNIT, CHUNK)
            add_to(dv_total, chunk, quad, dot_nn(doxt[quad], a))

    for group in range(groups):
        delta[group] = jnp.broadcast_to(jnp.sum(delta[group], axis=-1, keepdims=True), (wide, UNIT))

    @pl.loop(0, chunks)
    def _(chunk):
        for group in range(groups):
            cols = slice(group * CHUNK, (group + 1) * CHUNK)
            dp = grad_prob[chunk, :, cols].astype(jnp.float32) - twice(delta[group])
            dl = (prob[chunk, :, cols].astype(jnp.float32) * dp).astype(jnp.bfloat16)
            grad_logit[:, cols] = dl
            ds = dot_nn(mix_ref[1], dl).astype(jnp.bfloat16)
            mixed[:, GROUP * group : GROUP * (group + 1), :] = ds.reshape(heads, GROUP, CHUNK)
        gl_ref[...] += dot_nt(score[chunk], grad_logit[...])
        for quad in range(quads):
            ds = mixed[quad * per_quad : (quad + 1) * per_quad].reshape(per_quad * UNIT, CHUNK)
            dq = own_lanes(dot_nn(ds, keys(k_ref, chunk, quad)), lane_head, per_quad)
            dq_total[:, quad * CHUNK : (quad + 1) * CHUNK] += dq
            add_to(dk_total, chunk, quad, dot_nn(qxt[quad], ds))

    dq_ref[0, 0] = (dq_total[...] * 0.125).astype(jnp.bfloat16)

    @pl.when(inner == per_row - 1)
    def _():
        @pl.loop(0, lowest)
        def _(key_unit):
            dk_ref[key_unit, 0] = jnp.zeros_like(dk_ref[key_unit, 0])
            dv_ref[key_unit, 0] = jnp.zeros_like(dv_ref[key_unit, 0])

        @pl.loop(lowest, key_units)
        def _(key_unit):
            dk_ref[key_unit, 0] = dk_total[key_unit].astype(jnp.bfloat16).T
            dv_ref[key_unit, 0] = dv_total[key_unit].astype(jnp.bfloat16).T


def attention_bwd(blocks, q, k, v, grad_out, lse, mixes, heads):
    per_row, micros, _, width = q.shape
    key_units = k.shape[0]
    wide = heads * GROUP
    groups = UNIT // GROUP
    quads = width // CHUNK
    spread = (quads, heads // quads * UNIT, CHUNK)
    turned = (quads, CHUNK, heads // quads * UNIT)
    unit_spec, kv_spec, lse_spec, mix_spec = attention_specs(q, k, heads)
    sum_spec = pl.BlockSpec((wide, wide), lambda m, u, _: (0, 0))
    return pl.pallas_call(
        partial(bwd_kernel, heads),
        grid_spec=pltpu.PrefetchScalarGridSpec(
            num_scalar_prefetch=1,
            grid=(micros, per_row),
            in_specs=[unit_spec, kv_spec, kv_spec, unit_spec, lse_spec, mix_spec],
            out_specs=[unit_spec, kv_spec, kv_spec, sum_spec, sum_spec],
            scratch_shapes=[
                pltpu.VMEM(spread, jnp.bfloat16),
                pltpu.VMEM(turned, jnp.bfloat16),
                pltpu.VMEM(spread, jnp.bfloat16),
                pltpu.VMEM(turned, jnp.bfloat16),
                pltpu.VMEM((MAX_CHUNKS, wide, groups * CHUNK), jnp.bfloat16),
                pltpu.VMEM((MAX_CHUNKS, wide, groups * CHUNK), jnp.bfloat16),
                pltpu.VMEM((MAX_CHUNKS, wide, groups * CHUNK), jnp.bfloat16),
                pltpu.VMEM((wide, groups * CHUNK), jnp.bfloat16),
                pltpu.VMEM((wide, groups * CHUNK), jnp.bfloat16),
                pltpu.VMEM((heads, UNIT, CHUNK), jnp.bfloat16),
                pltpu.VMEM((groups, wide, UNIT), jnp.float32),
                pltpu.VMEM((UNIT, width), jnp.float32),
                pltpu.VMEM((key_units, width, UNIT), jnp.float32),
                pltpu.VMEM((key_units, width, UNIT), jnp.float32),
            ],
        ),
        out_shape=[
            jax.ShapeDtypeStruct(q.shape, jnp.bfloat16),
            jax.ShapeDtypeStruct(k.shape, jnp.bfloat16),
            jax.ShapeDtypeStruct(v.shape, jnp.bfloat16),
            jax.ShapeDtypeStruct((wide, wide), jnp.float32),
            jax.ShapeDtypeStruct((wide, wide), jnp.float32),
        ],
        compiler_params=pltpu.CompilerParams(vmem_limit_bytes=56 * 1024 * 1024),
        cost_estimate=pl.CostEstimate(flops=60_000_000_000, bytes_accessed=24_000_000, transcendentals=0),
        name="attention_bwd",
    )(blocks, q, k, v, grad_out, lse, mixes)


def spread_mixes(mix_logits, mix_weights):
    heads = mix_logits.shape[0]
    wide = heads * GROUP
    place = jnp.arange(wide, dtype=jnp.int32)
    pick = (place[:, None] // GROUP == jnp.arange(heads, dtype=jnp.int32)[None, :]).astype(mix_logits.dtype)
    same_row = (place[:, None] % GROUP == place[None, :] % GROUP)[None]
    tables = jnp.stack([mix_logits.T, mix_logits, mix_weights.T, mix_weights]).reshape(4 * heads, heads)
    across = jnp.dot(tables, pick.T, preferred_element_type=jnp.float32).astype(mix_logits.dtype)
    down = jnp.einsum("wh,bhx->bwx", pick, across.reshape(4, heads, wide), preferred_element_type=jnp.float32)
    return jnp.where(same_row, down, 0.0).astype(mix_logits.dtype)


def fold_mix(wide, heads):
    grid = wide.reshape(heads, GROUP, heads, GROUP)
    return jnp.sum(jnp.where(jnp.eye(GROUP, dtype=bool)[None, :, None, :], grid, 0.0), axis=(1, 3))


def from_behind(value, steps):
    count = lax.axis_size(AXES)
    first, last = (max(0, -steps), min(count, count - steps))
    return lax.ppermute(value, AXES, [(source, source + steps) for source in range(first, last)])


def seq_starts(lengths_row, query_rows):
    seq_ends = jnp.cumsum(lengths_row)
    starts = seq_ends - lengths_row
    return jnp.max(jnp.where(starts[None, :] <= query_rows[:, None], starts[None, :], 0), axis=1)


def normalize(values, gain_vec):
    inv_rms = lax.rsqrt(jnp.mean(values * values, axis=-1, keepdims=True) + norm_eps)
    normed = values * inv_rms
    return (normed, inv_rms, (normed * gain_vec.astype(jnp.float32)).astype(jnp.bfloat16))


def norm_back(grad_hidden, normed, inv_rms, gain_vec):
    grad_gain = jnp.sum(grad_hidden * normed, axis=0)
    grad_normed = grad_hidden * gain_vec.astype(jnp.float32)
    inner_mean = jnp.mean(grad_normed * normed, axis=-1, keepdims=True)
    return (inv_rms * (grad_normed - normed * inner_mean), grad_gain)


def matmul(left, right):
    return jnp.dot(left, right, preferred_element_type=jnp.float32)


def matmul_left_t(left, right):
    return lax.dot_general(left, right, (((0,), (0,)), ((), ())), preferred_element_type=jnp.float32)


def matmul_right_t(left, right):
    return lax.dot_general(left, right, (((1,), (1,)), ((), ())), preferred_element_type=jnp.float32)


def exchange(value):
    return lax.all_to_all(value, AXES, split_axis=0, concat_axis=0, tiled=True)


def split_ids(tok_ids, own_rows):
    owner = tok_ids // own_rows
    place = jnp.arange(tok_ids.shape[0], dtype=jnp.int32)
    same = tok_ids[:, None] == tok_ids[None, :]
    repeated = jnp.any(same & (place[None, :] < place[:, None]), axis=1)
    before = (owner[:, None] == owner[None, :]) & (tok_ids[None, :] < tok_ids[:, None]) & ~repeated[None, :]
    return (owner, tok_ids % own_rows, jnp.sum(before, axis=1, dtype=jnp.int32))


def plan_round(ids, index, own_rows, stride, room):
    count = lax.axis_size(AXES)
    owner, local, rank = ids
    here = rank - index * room
    slot = jnp.where((here >= 0) & (here < room), owner * stride + here, -1)
    chosen = slot[None, :] == jnp.arange(count * stride, dtype=jnp.int32)[:, None]
    wanted = jnp.max(jnp.where(chosen, local[None, :], -1), axis=1).reshape(count, stride)
    rounds = jnp.broadcast_to(jnp.max(rank) // room + 1, (count, stride))
    asked = exchange(jnp.concatenate([wanted, rounds], axis=1))
    pick = asked[:, :stride].reshape(-1, 1) == jnp.arange(own_rows, dtype=jnp.int32)[None, :]
    return (chosen.astype(jnp.bfloat16), pick.astype(jnp.bfloat16), jnp.max(asked[:, stride:]))


def answer(embedding, chosen, pick, stride, extra_row):
    count = lax.axis_size(AXES)
    rows = matmul(pick, embedding).astype(jnp.bfloat16).reshape(count, stride, -1)
    if extra_row is not None:
        is_extra = (jnp.arange(stride, dtype=jnp.int32) == stride - 1)[None, :, None]
        rows = jnp.where(is_extra, extra_row[None, None, :], rows)
    got = exchange(rows.reshape(count * stride, -1))
    return (matmul_left_t(chosen, got).astype(jnp.bfloat16), got.reshape(count, stride, -1)[:, stride - 1])


def lookup(embedding, tok_ids, extra_row, stride, room):
    own_rows = embedding.shape[0]
    ids = split_ids(tok_ids, own_rows)
    chosen, pick, rounds = plan_round(ids, 0, own_rows, stride, room)
    first, extra = answer(embedding, chosen, pick, stride, extra_row)

    def more(carry):
        index, rows = carry
        again, its_pick, _ = plan_round(ids, index, own_rows, stride, room)
        return (index + 1, rows + answer(embedding, again, its_pick, stride, None)[0])

    _, rows = lax.while_loop(lambda carry: carry[0] < rounds, more, (jnp.int32(1), first))
    return (rows, extra, ids, chosen, pick, rounds)


def send_grads(grad_low, chosen, pick, stride, extra_rows):
    count = lax.axis_size(AXES)
    summed = matmul(chosen, grad_low).astype(jnp.bfloat16).reshape(count, stride, -1)
    if extra_rows is not None:
        place = jnp.arange(stride, dtype=jnp.int32)[None, :, None]
        high, low = extra_rows
        summed = jnp.where(place == stride - 2, high[:, None, :], summed)
        summed = jnp.where(place == stride - 1, low[:, None, :], summed)
    got = exchange(summed.reshape(count * stride, -1))
    return (matmul_left_t(pick, got), got.reshape(count, stride, -1)[:, stride - 2 :])


def table_back(grad_rows, extra_rows, plan, own_rows, stride, room, beside):
    ids, chosen, pick, rounds = plan
    grad_low = grad_rows.astype(jnp.bfloat16)
    first, extra = send_grads(grad_low, chosen, pick, stride, extra_rows)
    first, beside = lax.optimization_barrier((first, beside))

    def more(carry):
        index, total = carry
        again, its_pick, _ = plan_round(ids, index, own_rows, stride, room)
        return (index + 1, total + send_grads(grad_low, again, its_pick, stride, None)[0])

    _, total = lax.while_loop(lambda carry: carry[0] < rounds, more, (jnp.int32(1), first))
    return (total, jnp.sum(extra.astype(jnp.float32), axis=(0, 1)), beside)


def gather_parts(pieces):
    count = lax.axis_size(AXES)
    sizes = [piece.shape[0] for piece in pieces]
    some = lax.all_gather(jnp.concatenate(pieces, axis=0), "outer", axis=0)
    whole = lax.all_gather(some, "inner", axis=0)
    parts, start = ([], 0)
    for size in sizes:
        parts.append(whole[:, :, start : start + size].swapaxes(0, 1).reshape(count * size, -1))
        start += size
    return parts


def stack_parts(parts):
    outer, inner = (lax.axis_size("outer"), lax.axis_size("inner"))
    shaped = []
    for part in parts:
        rows = part.shape[0] // (outer * inner)
        shaped.append(part.astype(jnp.bfloat16).reshape(outer, inner, rows, -1).swapaxes(0, 1))
    return jnp.concatenate(shaped, axis=2)


def sum_inner(stacked):
    return lax.psum_scatter(stacked, "inner", scatter_dimension=0, tiled=False)


def sum_outer(some):
    return lax.psum_scatter(some, "outer", scatter_dimension=0, tiled=False)


def split_rows(summed, sizes):
    pieces, start = ([], 0)
    for size in sizes:
        pieces.append(summed[start : start + size].astype(jnp.float32))
        start += size
    return pieces


def split_low(values):
    high = lax.reduce_precision(values, 8, 7)
    return (high.astype(jnp.bfloat16), (values - high).astype(jnp.bfloat16))


def by_unit(array):
    cut = array.reshape((array.shape[0], array.shape[1] // UNIT, UNIT) + array.shape[2:])
    return cut.swapaxes(0, 1)


def by_row(array, micros):
    cut = array.reshape(-1, micros, UNIT, array.shape[-1])
    return cut.swapaxes(0, 1).reshape(micros, -1, array.shape[-1])


def shards(
    token_ids,
    lengths,
    embedding,
    norm1_gain,
    w_query,
    w_key,
    w_value,
    w_out,
    mix_logits,
    mix_weights,
    norm2_gain,
    w_up,
    w_down,
    cotangent,
):
    count = lax.axis_size(AXES)
    me = lax.axis_index(AXES)
    micros, row_count = token_ids.shape
    own_rows, width = embedding.shape
    heads = mix_logits.shape[0]
    part = norm1_gain.shape[0]
    per_row = row_count // UNIT
    tokens = micros * row_count
    tok_ids = by_unit(token_ids).reshape(-1)
    stride = max(16, 1024 // count)
    room = stride - 2

    up_cols = w_up.shape[1] // width
    w_q, w_k, w_v = gather_parts([w_query, w_key, w_value])
    up_pieces = [w_up[:, col * width : (col + 1) * width] for col in range(up_cols)]
    late = gather_parts([w_out] + up_pieces + [w_down])
    w_o, w_d = (late[0], late[-1])
    w_u = jnp.concatenate(late[1:-1], axis=1)

    unit_rows = me * row_count + UNIT * jnp.arange(per_row, dtype=jnp.int32)
    begins = jnp.stack([seq_starts(lengths[micro], unit_rows) for micro in range(micros)])
    blocks = ((unit_rows[None, :] - begins) // UNIT + 1).reshape(-1).astype(jnp.int32)

    mixes = spread_mixes(mix_logits, mix_weights)

    gains_row = jnp.concatenate([norm1_gain, norm2_gain, jnp.zeros((width - 2 * part,), jnp.bfloat16)])
    picked, gains, *plan = lookup(embedding, tok_ids, gains_row, stride, room)
    gain_one = gains[:, :part].reshape(-1)
    gain_two = gains[:, part : 2 * part].reshape(-1)
    inputs = picked.astype(jnp.float32)

    normed_one, inv_one, hidden_one = normalize(inputs, gain_one)
    own_hidden = hidden_one.reshape(per_row, micros, UNIT, width)
    behind = [from_behind(own_hidden, steps) for steps in (1, 2, 3)]
    behind.append(from_behind(own_hidden[per_row - 1 :], 4))
    all_hidden = jnp.concatenate(behind[::-1] + [own_hidden], axis=0)
    flat_hidden = all_hidden.reshape(-1, width)
    query = (matmul(hidden_one, w_q).astype(jnp.bfloat16) * jnp.bfloat16(0.125)).reshape(own_hidden.shape)
    key = matmul(flat_hidden, w_k).astype(jnp.bfloat16).reshape(all_hidden.shape)
    value = matmul(flat_hidden, w_v).astype(jnp.bfloat16).reshape(all_hidden.shape)
    attended, lse = attention_fwd(blocks, query, key, value, mixes, heads)
    attended = attended.reshape(tokens, width)

    middle = inputs + matmul(attended, w_o)
    normed_two, inv_two, hidden_two = normalize(middle, gain_two)
    up_proj = matmul(hidden_two, w_u)
    activated, gelu_pull = jax.vjp(jax.nn.gelu, up_proj)
    activated = activated.astype(jnp.bfloat16)
    output = (middle + matmul(activated, w_d)).astype(jnp.bfloat16)

    grad_rows = by_unit(cotangent).reshape(tokens, width)
    grad_act = matmul_right_t(grad_rows, w_d)
    grad_upb = gelu_pull(grad_act)[0].astype(jnp.bfloat16)
    grad_down = matmul_left_t(activated, grad_rows)
    grad_up = matmul_left_t(hidden_two, grad_upb)
    grad_hidden_two = matmul_right_t(grad_upb, w_u)
    grad_mid_norm, grad_gain_two = norm_back(grad_hidden_two, normed_two, inv_two, gain_two)
    grad_middle = grad_rows.astype(jnp.float32) + grad_mid_norm
    grad_branch = grad_middle.astype(jnp.bfloat16)
    grad_wout = matmul_left_t(attended, grad_branch)
    grad_att = matmul_right_t(grad_branch, w_o).astype(jnp.bfloat16).reshape(own_hidden.shape)
    up_terms = [grad_up[:, col * width : (col + 1) * width] for col in range(up_cols)]
    late_terms = [grad_wout] + up_terms + [grad_down]
    late_stack, grad_att = lax.optimization_barrier((stack_parts(late_terms), grad_att))
    late_some = sum_inner(late_stack)

    grad_query, grad_key, grad_value, wide_logit, wide_prob = attention_bwd(
        blocks, query, key, value, grad_att, lse, mixes, heads
    )
    grad_query = grad_query.reshape(tokens, width)
    grad_key = grad_key.reshape(-1, width)
    grad_value = grad_value.reshape(-1, width)
    grad_flat = (matmul_right_t(grad_key, w_k) + matmul_right_t(grad_value, w_v)).reshape(all_hidden.shape)
    returned = []
    start = 0
    for steps, size in ((4, 1), (3, per_row), (2, per_row), (1, per_row)):
        term = grad_flat[start : start + size].astype(jnp.bfloat16)
        returned.append(from_behind(term, -steps))
        start += size
    grad_wq = matmul_left_t(hidden_one, grad_query)
    grad_wk = matmul_left_t(flat_hidden, grad_key)
    grad_wv = matmul_left_t(flat_hidden, grad_value)
    early_terms = [grad_wq, grad_wk, grad_wv]
    early_some = sum_inner(stack_parts(early_terms))
    late_some, returned = lax.optimization_barrier((late_some, returned))
    late_sums = split_rows(sum_outer(late_some), [term.shape[0] // count for term in late_terms])
    grad_own = grad_flat[start:]
    for term in returned:
        term = term.astype(jnp.float32)
        if term.shape[0] < per_row:
            term = jnp.pad(term, ((per_row - term.shape[0], 0), (0, 0), (0, 0), (0, 0)))
        grad_own = grad_own + term
    grad_hidden_one = grad_own.reshape(tokens, width) + matmul_right_t(grad_query, w_q)
    grad_in_norm, grad_gain_one = norm_back(grad_hidden_one, normed_one, inv_one, gain_one)
    grad_inputs = grad_middle + grad_in_norm

    mix_terms = jnp.concatenate([fold_mix(wide_logit, heads).reshape(-1), fold_mix(wide_prob, heads).reshape(-1)])
    mix_size = mix_terms.shape[0]
    small = jnp.concatenate(
        [
            grad_gain_one.reshape(count, part),
            grad_gain_two.reshape(count, part),
            jnp.broadcast_to(mix_terms[None, :], (count, mix_size)),
            jnp.zeros((count, width - 2 * part - mix_size), jnp.float32),
        ],
        axis=1,
    )
    table_grad, small_sum, early_some = table_back(
        grad_inputs, split_low(small), plan, own_rows, stride, room, early_some
    )
    early_sums = split_rows(sum_outer(early_some), [term.shape[0] // count for term in early_terms])
    mixes = small_sum[2 * part : 2 * part + mix_size].reshape(2, heads, heads)
    return (
        by_row(output, micros),
        by_row(grad_inputs, micros),
        table_grad,
        small_sum[:part],
        early_sums[0],
        early_sums[1],
        early_sums[2],
        late_sums[0],
        mixes[0],
        mixes[1],
        small_sum[part : 2 * part],
        jnp.concatenate(late_sums[1:-1], axis=1),
        late_sums[-1],
    )


def solution(mesh):
    count = mesh.devices.size
    outer = 1 << ((count.bit_length() - 1) // 2)
    mesh = Mesh(mesh.devices.reshape(outer, count // outer), AXES)
    in_specs = (
        P(None, AXES),
        P(),
        P(AXES, None),
        P(AXES),
        P(AXES, None),
        P(AXES, None),
        P(AXES, None),
        P(AXES, None),
        P(),
        P(),
        P(AXES),
        P(AXES, None),
        P(AXES, None),
        P(None, AXES, None),
    )
    out_specs = (
        P(None, AXES, None),
        P(None, AXES, None),
        P(AXES, None),
        P(AXES),
        P(AXES, None),
        P(AXES, None),
        P(AXES, None),
        P(AXES, None),
        P(),
        P(),
        P(AXES),
        P(AXES, None),
        P(AXES, None),
    )
    return jax.shard_map(shards, mesh=mesh, in_specs=in_specs, out_specs=out_specs, check_vma=False)
```

```python
from functools import partial

import jax
import jax.numpy as jnp
from jax import lax
from jax.experimental import pallas as pl
from jax.experimental.pallas import tpu as pltpu
from jax.sharding import PartitionSpec as P

norm_eps = 1e-06

masked = -1e30
UNIT = 128
CHUNK = 256
GROUP = 16
MAX_CHUNKS = 4


def dot_nn(left, right):
    return lax.dot_general(left, right, (((1,), (0,)), ((), ())), preferred_element_type=jnp.float32)


def dot_nt(left, right):
    return lax.dot_general(left, right, (((1,), (1,)), ((), ())), preferred_element_type=jnp.float32)


def spread_heads(rows, lane_head, quad, heads_per_quad):
    part = rows[:, quad * CHUNK : (quad + 1) * CHUNK]
    zero = jnp.zeros_like(part)
    return jnp.concatenate([jnp.where(lane_head == head, part, zero) for head in range(heads_per_quad)], axis=0)


def own_lanes(wide, lane_head, heads_per_quad):
    total = jnp.where(lane_head == 0, wide[:UNIT], 0.0)
    for head in range(1, heads_per_quad):
        total = total + jnp.where(lane_head == head, wide[head * UNIT : (head + 1) * UNIT], 0.0)
    return total


def allowed_keys(chunk, group, blocks):
    key = lax.broadcasted_iota(jnp.int32, (GROUP, CHUNK), 1) - (UNIT + CHUNK * chunk)
    row = lax.broadcasted_iota(jnp.int32, (GROUP, CHUNK), 0) + GROUP * group
    return (key <= row) & (key >= (1 - blocks) * UNIT)


def twice(rows):
    return jnp.concatenate([rows, rows], axis=-1)


def put_groups(ref, quad, per_quad, term):
    low = term.astype(jnp.bfloat16)
    for head in range(per_quad):
        rows = slice((quad * per_quad + head) * GROUP, (quad * per_quad + head + 1) * GROUP)
        for group in range(UNIT // GROUP):
            start = head * UNIT + group * GROUP
            ref[rows, group * CHUNK : (group + 1) * CHUNK] = low[start : start + GROUP]


def fwd_kernel(heads, blocks_ref, q_ref, k_ref, v_ref, mix_ref, att_ref, score_out, prob_out, mixed_out,
               qx, score, prob, mixed, logit, top, norm, total, sems):
    micro, inner, per_row = (pl.program_id(0), pl.program_id(1), pl.num_programs(1))
    blocks = blocks_ref[micro * per_row + inner]
    chunks = (blocks + 1) // 2
    last_unit = k_ref.shape[0] - per_row + inner + 1
    quads = q_ref.shape[3] // CHUNK
    per_quad = heads // quads
    groups = UNIT // GROUP
    wide = heads * GROUP
    lane_head = lax.broadcasted_iota(jnp.int32, (UNIT, CHUNK), 1) // (CHUNK // per_quad)
    for quad in range(quads):
        qx[quad] = spread_heads(q_ref[0, 0], lane_head, quad, per_quad)
    total[...] = jnp.zeros_like(total)
    top[...] = jnp.full_like(top, masked)
    norm[...] = jnp.zeros_like(norm)

    def keys(ref, chunk, quad):
        units = pl.ds(last_unit - 2 * (chunk + 1), 2)
        return ref[units, 0, :, quad * CHUNK : (quad + 1) * CHUNK].reshape(CHUNK, CHUNK)

    def keep(chunk, kind):
        source, target = ((score, score_out), (prob, prob_out), (mixed, mixed_out))[kind]
        return pltpu.make_async_copy(source.at[chunk], target.at[inner, micro, chunk], sems.at[kind, chunk])

    @pl.loop(0, chunks)
    def _(chunk):
        for quad in range(quads):
            put_groups(score.at[chunk], quad, per_quad, dot_nt(qx[quad], keys(k_ref, chunk, quad)))
        keep(chunk, 0).start()
        for group in range(groups):
            l = dot_nn(mix_ref[0], score[chunk, :, group * CHUNK : (group + 1) * CHUNK])
            l = jnp.where(allowed_keys(chunk, group, blocks)[None], l.reshape(heads, GROUP, CHUNK), masked)
            l = l.reshape(wide, CHUNK)
            logit[chunk, group] = l
            old = top[group]
            new = jnp.maximum(old, jnp.maximum(l[:, :UNIT], l[:, UNIT:]))
            terms = jnp.exp(l[:, :UNIT] - new) + jnp.exp(l[:, UNIT:] - new)
            norm[group] = norm[group] * jnp.exp(old - new) + terms
            top[group] = new

    for group in range(groups):
        lanes = top[group]
        high = jnp.broadcast_to(jnp.max(lanes, axis=-1, keepdims=True), lanes.shape)
        whole = jnp.sum(norm[group] * jnp.exp(lanes - high), axis=-1, keepdims=True)
        top[group] = high + jnp.log(jnp.broadcast_to(whole, lanes.shape))

    @pl.loop(0, chunks)
    def _(chunk):
        for group in range(groups):
            p = jnp.exp(logit[chunk, group] - twice(top[group])).astype(jnp.bfloat16)
            prob[chunk, :, group * CHUNK : (group + 1) * CHUNK] = p
            a = dot_nn(mix_ref[2], p).astype(jnp.bfloat16)
            mixed[chunk, :, GROUP * group : GROUP * (group + 1), :] = a.reshape(heads, GROUP, CHUNK)
        keep(chunk, 1).start()
        keep(chunk, 2).start()
        for quad in range(quads):
            a = mixed[chunk, quad * per_quad : (quad + 1) * per_quad].reshape(per_quad * UNIT, CHUNK)
            o = own_lanes(dot_nn(a, keys(v_ref, chunk, quad)), lane_head, per_quad)
            total[:, quad * CHUNK : (quad + 1) * CHUNK] += o

    att_ref[0, 0] = total[...].astype(jnp.bfloat16)

    @pl.loop(0, chunks)
    def _(chunk):
        for kind in range(3):
            keep(chunk, kind).wait()


def attention_specs(q, k, heads):
    per_row, micros, _, width = q.shape
    wide = heads * GROUP
    return (
        pl.BlockSpec((1, 1, UNIT, width), lambda m, u, _: (u, m, 0, 0)),
        pl.BlockSpec((k.shape[0], 1, UNIT, width), lambda m, u, _: (0, m, 0, 0)),
        pl.BlockSpec((4, wide, wide), lambda m, u, _: (0, 0, 0)),
    )


def kept_shapes(heads):
    wide = heads * GROUP
    flat = (MAX_CHUNKS, wide, UNIT // GROUP * CHUNK)
    return (flat, flat, (MAX_CHUNKS, heads, UNIT, CHUNK))


def attention_fwd(blocks, q, k, v, mixes, heads):
    per_row, micros, _, width = q.shape
    wide = heads * GROUP
    groups = UNIT // GROUP
    quads = width // CHUNK
    unit_spec, kv_spec, mix_spec = attention_specs(q, k, heads)
    kept = kept_shapes(heads)
    anywhere = pl.BlockSpec(memory_space=pl.ANY)
    return pl.pallas_call(
        partial(fwd_kernel, heads),
        grid_spec=pltpu.PrefetchScalarGridSpec(
            num_scalar_prefetch=1,
            grid=(micros, per_row),
            in_specs=[unit_spec, kv_spec, kv_spec, mix_spec],
            out_specs=[unit_spec, anywhere, anywhere, anywhere],
            scratch_shapes=[pltpu.VMEM((quads, heads // quads * UNIT, CHUNK), jnp.bfloat16)]
            + [pltpu.VMEM(shape, jnp.bfloat16) for shape in kept]
            + [
                pltpu.VMEM((MAX_CHUNKS, groups, wide, CHUNK), jnp.float32),
                pltpu.VMEM((groups, wide, UNIT), jnp.float32),
                pltpu.VMEM((groups, wide, UNIT), jnp.float32),
                pltpu.VMEM((UNIT, width), jnp.float32),
                pltpu.SemaphoreType.DMA((3, MAX_CHUNKS)),
            ],
        ),
        out_shape=[jax.ShapeDtypeStruct(q.shape, jnp.bfloat16)]
        + [jax.ShapeDtypeStruct((per_row, micros) + shape, jnp.bfloat16) for shape in kept],
        compiler_params=pltpu.CompilerParams(vmem_limit_bytes=50 * 1024 * 1024),
        cost_estimate=pl.CostEstimate(flops=20_000_000_000, bytes_accessed=30_000_000, transcendentals=0),
        name="attention_fwd",
    )(blocks, q, k, v, mixes)


def bwd_kernel(heads, blocks_ref, q_ref, k_ref, v_ref, do_ref, mix_ref, score_in, prob_in, mixed_in,
               dq_ref, dk_ref, dv_ref, gl_ref, gp_ref,
               qxt, dox, doxt, score, prob, mixed, grad_prob, grad_mixed, grad_logit, grad_score,
               delta, dq_total, dk_total, dv_total, sems):
    micro, inner, per_row = (pl.program_id(0), pl.program_id(1), pl.num_programs(1))
    step = micro * per_row + inner
    slot = step % 2
    blocks = blocks_ref[step]
    chunks = (blocks + 1) // 2
    key_units = k_ref.shape[0]
    last_unit = key_units - per_row + inner + 1
    quads = q_ref.shape[3] // CHUNK
    per_quad = heads // quads
    groups = UNIT // GROUP
    wide = heads * GROUP
    lane_head = lax.broadcasted_iota(jnp.int32, (UNIT, CHUNK), 1) // (CHUNK // per_quad)
    row_head = lax.broadcasted_iota(jnp.int32, (CHUNK, UNIT), 0) // (CHUNK // per_quad)
    lowest = key_units
    for other in range(key_units - 7):
        its_chunks = (blocks_ref[micro * per_row + other] + 1) // 2
        lowest = jnp.minimum(lowest, key_units - per_row + other + 1 - 2 * its_chunks)

    def fetch(at, chunk, kind):
        source, target = ((score_in, score), (prob_in, prob), (mixed_in, mixed))[kind]
        place = source.at[at % per_row, at // per_row, chunk]
        return pltpu.make_async_copy(place, target.at[at % 2, chunk], sems.at[kind, at % 2, chunk])

    def fetch_all(at):
        @pl.loop(0, (blocks_ref[at] + 1) // 2)
        def _(chunk):
            for kind in (1, 2, 0):
                fetch(at, chunk, kind).start()

    @pl.when(step == 0)
    def _():
        fetch_all(0)
        gl_ref[...] = jnp.zeros_like(gl_ref)
        gp_ref[...] = jnp.zeros_like(gp_ref)

    @pl.when(step + 1 < pl.num_programs(0) * per_row)
    def _():
        fetch_all(step + 1)

    @pl.when(inner == 0)
    def _():
        @pl.loop(lowest, key_units)
        def _(key_unit):
            dk_total[key_unit] = jnp.zeros_like(dk_total[key_unit])
            dv_total[key_unit] = jnp.zeros_like(dv_total[key_unit])

    def spread_turned(rows, quad):
        turned = rows[:, quad * CHUNK : (quad + 1) * CHUNK].T
        zero = jnp.zeros_like(turned)
        return jnp.concatenate([jnp.where(row_head == head, turned, zero) for head in range(per_quad)], axis=1)

    for quad in range(quads):
        qxt[quad] = spread_turned(q_ref[0, 0], quad)
        dox[quad] = spread_heads(do_ref[0, 0], lane_head, quad, per_quad)
        doxt[quad] = spread_turned(do_ref[0, 0], quad)
    dq_total[...] = jnp.zeros_like(dq_total)
    delta[...] = jnp.zeros_like(delta)

    def keys(ref, chunk, quad):
        units = pl.ds(last_unit - 2 * (chunk + 1), 2)
        return ref[units, 0, :, quad * CHUNK : (quad + 1) * CHUNK].reshape(CHUNK, CHUNK)

    def add_to(total, chunk, quad, term):
        first = last_unit - 2 * (chunk + 1)
        lanes = slice(quad * CHUNK, (quad + 1) * CHUNK)
        total[first, lanes, :] += term[:, :UNIT]
        total[first + 1, lanes, :] += term[:, UNIT:]

    @pl.loop(0, chunks)
    def _(chunk):
        for quad in range(quads):
            put_groups(grad_mixed, quad, per_quad, dot_nt(dox[quad], keys(v_ref, chunk, quad)))
        fetch(step, chunk, 1).wait()
        for group in range(groups):
            cols = slice(group * CHUNK, (group + 1) * CHUNK)
            dp = dot_nn(mix_ref[3], grad_mixed[:, cols])
            grad_prob[chunk, :, cols] = dp.astype(grad_prob.dtype)
            term = prob[slot, chunk, :, cols].astype(jnp.float32) * dp
            delta[group] += term[:, :UNIT] + term[:, UNIT:]
        gp_ref[...] += dot_nt(prob[slot, chunk], grad_mixed[...])
        fetch(step, chunk, 2).wait()
        for quad in range(quads):
            a = mixed[slot, chunk, quad * per_quad : (quad + 1) * per_quad].reshape(per_quad * UNIT, CHUNK)
            add_to(dv_total, chunk, quad, dot_nn(doxt[quad], a))

    for group in range(groups):
        delta[group] = jnp.broadcast_to(jnp.sum(delta[group], axis=-1, keepdims=True), (wide, UNIT))

    @pl.loop(0, chunks)
    def _(chunk):
        for group in range(groups):
            cols = slice(group * CHUNK, (group + 1) * CHUNK)
            dp = grad_prob[chunk, :, cols].astype(jnp.float32) - twice(delta[group])
            dl = (prob[slot, chunk, :, cols].astype(jnp.float32) * dp).astype(jnp.bfloat16)
            grad_logit[:, cols] = dl
            ds = dot_nn(mix_ref[1], dl).astype(jnp.bfloat16)
            grad_score[:, GROUP * group : GROUP * (group + 1), :] = ds.reshape(heads, GROUP, CHUNK)
        fetch(step, chunk, 0).wait()
        gl_ref[...] += dot_nt(score[slot, chunk], grad_logit[...])
        for quad in range(quads):
            ds = grad_score[quad * per_quad : (quad + 1) * per_quad].reshape(per_quad * UNIT, CHUNK)
            dq = own_lanes(dot_nn(ds, keys(k_ref, chunk, quad)), lane_head, per_quad)
            dq_total[:, quad * CHUNK : (quad + 1) * CHUNK] += dq
            add_to(dk_total, chunk, quad, dot_nn(qxt[quad], ds))

    dq_ref[0, 0] = (dq_total[...] * 0.125).astype(jnp.bfloat16)

    @pl.when(inner == per_row - 1)
    def _():
        @pl.loop(0, lowest)
        def _(key_unit):
            dk_ref[key_unit, 0] = jnp.zeros_like(dk_ref[key_unit, 0])
            dv_ref[key_unit, 0] = jnp.zeros_like(dv_ref[key_unit, 0])

        @pl.loop(lowest, key_units)
        def _(key_unit):
            dk_ref[key_unit, 0] = dk_total[key_unit].astype(jnp.bfloat16).T
            dv_ref[key_unit, 0] = dv_total[key_unit].astype(jnp.bfloat16).T


def attention_bwd(blocks, q, k, v, grad_out, kept, mixes, heads):
    per_row, micros, _, width = q.shape
    key_units = k.shape[0]
    wide = heads * GROUP
    groups = UNIT // GROUP
    quads = width // CHUNK
    turned = (quads, CHUNK, heads // quads * UNIT)
    unit_spec, kv_spec, mix_spec = attention_specs(q, k, heads)
    sum_spec = pl.BlockSpec((wide, wide), lambda m, u, _: (0, 0))
    anywhere = pl.BlockSpec(memory_space=pl.ANY)
    return pl.pallas_call(
        partial(bwd_kernel, heads),
        grid_spec=pltpu.PrefetchScalarGridSpec(
            num_scalar_prefetch=1,
            grid=(micros, per_row),
            in_specs=[unit_spec, kv_spec, kv_spec, unit_spec, mix_spec] + [anywhere] * 3,
            out_specs=[unit_spec, kv_spec, kv_spec, sum_spec, sum_spec],
            scratch_shapes=[
                pltpu.VMEM(turned, jnp.bfloat16),
                pltpu.VMEM((quads, heads // quads * UNIT, CHUNK), jnp.bfloat16),
                pltpu.VMEM(turned, jnp.bfloat16),
            ]
            + [pltpu.VMEM((2,) + shape, jnp.bfloat16) for shape in kept_shapes(heads)]
            + [
                pltpu.VMEM((MAX_CHUNKS, wide, groups * CHUNK), jnp.bfloat16),
                pltpu.VMEM((wide, groups * CHUNK), jnp.bfloat16),
                pltpu.VMEM((wide, groups * CHUNK), jnp.bfloat16),
                pltpu.VMEM((heads, UNIT, CHUNK), jnp.bfloat16),
                pltpu.VMEM((groups, wide, UNIT), jnp.float32),
                pltpu.VMEM((UNIT, width), jnp.float32),
                pltpu.VMEM((key_units, width, UNIT), jnp.float32),
                pltpu.VMEM((key_units, width, UNIT), jnp.float32),
                pltpu.SemaphoreType.DMA((3, 2, MAX_CHUNKS)),
            ],
        ),
        out_shape=[
            jax.ShapeDtypeStruct(q.shape, jnp.bfloat16),
            jax.ShapeDtypeStruct(k.shape, jnp.bfloat16),
            jax.ShapeDtypeStruct(v.shape, jnp.bfloat16),
            jax.ShapeDtypeStruct((wide, wide), jnp.float32),
            jax.ShapeDtypeStruct((wide, wide), jnp.float32),
        ],
        compiler_params=pltpu.CompilerParams(vmem_limit_bytes=58 * 1024 * 1024),
        cost_estimate=pl.CostEstimate(flops=45_000_000_000, bytes_accessed=40_000_000, transcendentals=0),
        name="attention_bwd",
    )(blocks, q, k, v, grad_out, mixes, *kept)


def piece_bases(key_units, per_row):
    sizes = [1] + [per_row] * ((key_units - 1) // per_row)
    return [(sum(sizes[:at]), size) for at, size in enumerate(sizes)]


def project_kernel(low_ref, *refs):
    pieces, (w_q, w_k, w_v, q_ref, k_ref, v_ref) = (refs[:-6], refs[-6:])
    key_units, width = (k_ref.shape[0], k_ref.shape[3])
    per_row = q_ref.shape[0]
    low = low_ref[pl.program_id(0)]

    for piece, (base, size) in zip(pieces, piece_bases(key_units, per_row)):
        @pl.when(base + size > low)
        def _():
            rows = piece[:, 0].reshape(size * UNIT, width)
            k_ref[base : base + size, 0] = dot_nn(rows, w_k[...]).astype(jnp.bfloat16).reshape(size, UNIT, width)
            v_ref[base : base + size, 0] = dot_nn(rows, w_v[...]).astype(jnp.bfloat16).reshape(size, UNIT, width)

    rows = pieces[-1][:, 0].reshape(per_row * UNIT, width)
    query = dot_nn(rows, w_q[...]).astype(jnp.bfloat16) * jnp.bfloat16(0.125)
    q_ref[:, 0] = query.reshape(per_row, UNIT, width)


def project(low, pieces, weights):
    micros, width = pieces[0].shape[1], pieces[0].shape[3]
    key_units = sum(piece.shape[0] for piece in pieces)
    per_row = pieces[-1].shape[0]

    def spec(units):
        return pl.BlockSpec((units, 1, UNIT, width), lambda m, _: (0, m, 0, 0))

    weight_spec = pl.BlockSpec((width, width), lambda m, _: (0, 0))
    shapes = [(units, micros, UNIT, width) for units in (per_row, key_units, key_units)]
    return pl.pallas_call(
        project_kernel,
        grid_spec=pltpu.PrefetchScalarGridSpec(
            num_scalar_prefetch=1,
            grid=(micros,),
            in_specs=[spec(piece.shape[0]) for piece in pieces] + [weight_spec] * 3,
            out_specs=[spec(shape[0]) for shape in shapes],
        ),
        out_shape=[jax.ShapeDtypeStruct(shape, jnp.bfloat16) for shape in shapes],
        compiler_params=pltpu.CompilerParams(vmem_limit_bytes=44 * 1024 * 1024),
        cost_estimate=pl.CostEstimate(flops=6_000_000_000, bytes_accessed=15_000_000, transcendentals=0),
        name="project",
    )(low, *pieces, *weights)


def project_back_kernel(low_ref, dq_ref, dk_ref, dv_ref, w_q, w_k, w_v, *outs):
    key_units, width = (dk_ref.shape[0], dk_ref.shape[3])
    per_row = dq_ref.shape[0]
    low = low_ref[pl.program_id(0)]
    bases = piece_bases(key_units, per_row)

    def from_keys(base, size):
        rows = slice(base, base + size)
        key_term = dot_nt(dk_ref[rows, 0].reshape(size * UNIT, width), w_k[...])
        return key_term + dot_nt(dv_ref[rows, 0].reshape(size * UNIT, width), w_v[...])

    for out, (base, size) in zip(outs[:-1], bases[:-1]):
        @pl.when(base + size > low)
        def _():
            out[:, 0] = from_keys(base, size).astype(jnp.bfloat16).reshape(size, UNIT, width)

        @pl.when(base + size <= low)
        def _():
            out[...] = jnp.zeros_like(out)

    own = from_keys(*bases[-1]) + dot_nt(dq_ref[:, 0].reshape(per_row * UNIT, width), w_q[...])
    outs[-1][:, 0] = own.reshape(per_row, UNIT, width)


def project_back(low, grad_query, grad_key, grad_value, weights):
    per_row, micros, _, width = grad_query.shape
    key_units = grad_key.shape[0]

    def spec(units):
        return pl.BlockSpec((units, 1, UNIT, width), lambda m, _: (0, m, 0, 0))

    weight_spec = pl.BlockSpec((width, width), lambda m, _: (0, 0))
    sizes = [size for _, size in piece_bases(key_units, per_row)]
    shapes = [(size, micros, UNIT, width) for size in sizes]
    kinds = [jnp.bfloat16] * (len(sizes) - 1) + [jnp.float32]
    return pl.pallas_call(
        project_back_kernel,
        grid_spec=pltpu.PrefetchScalarGridSpec(
            num_scalar_prefetch=1,
            grid=(micros,),
            in_specs=[spec(per_row), spec(key_units), spec(key_units)] + [weight_spec] * 3,
            out_specs=[spec(size) for size in sizes],
        ),
        out_shape=[jax.ShapeDtypeStruct(shape, kind) for shape, kind in zip(shapes, kinds)],
        compiler_params=pltpu.CompilerParams(vmem_limit_bytes=44 * 1024 * 1024),
        cost_estimate=pl.CostEstimate(flops=6_000_000_000, bytes_accessed=15_000_000, transcendentals=0),
        name="project_back",
    )(low, grad_query, grad_key, grad_value, *weights)


def spread_mixes(mix_logits, mix_weights):
    heads = mix_logits.shape[0]
    wide = heads * GROUP
    place = jnp.arange(wide, dtype=jnp.int32)
    pick = (place[:, None] // GROUP == jnp.arange(heads, dtype=jnp.int32)[None, :]).astype(mix_logits.dtype)
    same_row = (place[:, None] % GROUP == place[None, :] % GROUP)[None]
    tables = jnp.stack([mix_logits.T, mix_logits, mix_weights.T, mix_weights]).reshape(4 * heads, heads)
    across = jnp.dot(tables, pick.T, preferred_element_type=jnp.float32).astype(mix_logits.dtype)
    down = jnp.einsum("wh,bhx->bwx", pick, across.reshape(4, heads, wide), preferred_element_type=jnp.float32)
    return jnp.where(same_row, down, 0.0).astype(mix_logits.dtype)


def fold_mix(wide, heads):
    place = jnp.arange(heads * GROUP, dtype=jnp.int32)
    pick = (place[:, None] // GROUP == jnp.arange(heads, dtype=jnp.int32)[None, :]).astype(jnp.float32)
    same_row = place[:, None] % GROUP == place[None, :] % GROUP
    down = jnp.dot(pick.T, jnp.where(same_row, wide, 0.0), precision=lax.Precision.HIGHEST)
    return jnp.dot(down, pick, precision=lax.Precision.HIGHEST)


def from_behind(value, steps):
    count = lax.axis_size("dev")
    first, last = (max(0, -steps), min(count, count - steps))
    return lax.ppermute(value, "dev", [(source, source + steps) for source in range(first, last)])


def seq_starts(lengths_row, query_rows):
    seq_ends = jnp.cumsum(lengths_row)
    starts = seq_ends - lengths_row
    return jnp.max(jnp.where(starts[None, :] <= query_rows[:, None], starts[None, :], 0), axis=1)


def normalize(values, gain_vec):
    inv_rms = lax.rsqrt(jnp.mean(values * values, axis=-1, keepdims=True) + norm_eps)
    normed = values * inv_rms
    return (normed, inv_rms, (normed * gain_vec.astype(jnp.float32)).astype(jnp.bfloat16))


def norm_back(grad_hidden, normed, inv_rms, gain_vec):
    grad_gain = jnp.sum(grad_hidden * normed, axis=0)
    grad_normed = grad_hidden * gain_vec.astype(jnp.float32)
    inner_mean = jnp.mean(grad_normed * normed, axis=-1, keepdims=True)
    return (inv_rms * (grad_normed - normed * inner_mean), grad_gain)


def matmul(left, right):
    return jnp.dot(left, right, preferred_element_type=jnp.float32)


def matmul_left_t(left, right):
    return lax.dot_general(left, right, (((0,), (0,)), ((), ())), preferred_element_type=jnp.float32)


def matmul_right_t(left, right):
    return lax.dot_general(left, right, (((1,), (1,)), ((), ())), preferred_element_type=jnp.float32)


def exchange(value):
    return lax.all_to_all(value, "dev", split_axis=0, concat_axis=0, tiled=True)


def split_ids(tok_ids, own_rows):
    owner = tok_ids // own_rows
    place = jnp.arange(tok_ids.shape[0], dtype=jnp.int32)
    same = tok_ids[:, None] == tok_ids[None, :]
    repeated = jnp.any(same & (place[None, :] < place[:, None]), axis=1)
    before = (owner[:, None] == owner[None, :]) & (tok_ids[None, :] < tok_ids[:, None]) & ~repeated[None, :]
    return (owner, tok_ids % own_rows, jnp.sum(before, axis=1, dtype=jnp.int32))


def ask_round(ids, index, own_rows, stride, room):
    count = lax.axis_size("dev")
    owner, local, rank = ids
    here = rank - index * room
    slot = jnp.where((here >= 0) & (here < room), owner * stride + here, -1)
    chosen = slot[None, :] == jnp.arange(count * stride, dtype=jnp.int32)[:, None]
    wanted = jnp.max(jnp.where(chosen, local[None, :], -1), axis=1).reshape(count, stride)
    rounds = jnp.broadcast_to(jnp.max(rank) // room + 1, (count, stride))
    return (jnp.concatenate([wanted, rounds], axis=1), chosen.astype(jnp.bfloat16))


def hear_round(message, own_rows, stride):
    asked = exchange(message)
    pick = asked[:, :stride].reshape(-1, 1) == jnp.arange(own_rows, dtype=jnp.int32)[None, :]
    return (pick.astype(jnp.bfloat16), jnp.max(asked[:, stride:]))


def plan_round(ids, index, own_rows, stride, room):
    message, chosen = ask_round(ids, index, own_rows, stride, room)
    pick, _ = hear_round(message, own_rows, stride)
    return (chosen, pick)


def answer(embedding, chosen, pick, stride, extra_row):
    count = lax.axis_size("dev")
    rows = matmul(pick, embedding).astype(jnp.bfloat16).reshape(count, stride, -1)
    if extra_row is not None:
        is_extra = (jnp.arange(stride, dtype=jnp.int32) == stride - 1)[None, :, None]
        rows = jnp.where(is_extra, extra_row[None, None, :], rows)
    got = exchange(rows.reshape(count * stride, -1))
    return (matmul_left_t(chosen, got).astype(jnp.bfloat16), got.reshape(count, stride, -1)[:, stride - 1])


def lookup(embedding, ids, message, chosen, extra_row, stride, room):
    own_rows = embedding.shape[0]
    pick, rounds = hear_round(message, own_rows, stride)
    first, extra = answer(embedding, chosen, pick, stride, extra_row)

    def more(carry):
        index, rows = carry
        again, its_pick = plan_round(ids, index, own_rows, stride, room)
        return (index + 1, rows + answer(embedding, again, its_pick, stride, None)[0])

    _, rows = lax.while_loop(lambda carry: carry[0] < rounds, more, (jnp.int32(1), first))
    return (rows, extra, ids, chosen, pick, rounds)


def send_grads(grad_low, chosen, pick, stride, extra_rows):
    count = lax.axis_size("dev")
    summed = matmul(chosen, grad_low).astype(jnp.bfloat16).reshape(count, stride, -1)
    if extra_rows is not None:
        place = jnp.arange(stride, dtype=jnp.int32)[None, :, None]
        high, low = extra_rows
        summed = jnp.where(place == stride - 2, high[:, None, :], summed)
        summed = jnp.where(place == stride - 1, low[:, None, :], summed)
    got = exchange(summed.reshape(count * stride, -1))
    return (matmul_left_t(pick, got), got.reshape(count, stride, -1)[:, stride - 2 :])


def table_back(grad_rows, extra_rows, plan, own_rows, stride, room):
    ids, chosen, pick, rounds = plan
    grad_low = grad_rows.astype(jnp.bfloat16)
    first, extra = send_grads(grad_low, chosen, pick, stride, extra_rows)

    def more(carry):
        index, total = carry
        again, its_pick = plan_round(ids, index, own_rows, stride, room)
        return (index + 1, total + send_grads(grad_low, again, its_pick, stride, None)[0])

    _, total = lax.while_loop(lambda carry: carry[0] < rounds, more, (jnp.int32(1), first))
    return (total, jnp.sum(extra.astype(jnp.float32), axis=(0, 1)))


def gather_parts(pieces):
    count = lax.axis_size("dev")
    sizes = [piece.shape[0] for piece in pieces]
    whole = lax.all_gather(jnp.concatenate(pieces, axis=0), "dev", axis=0)
    parts, start = ([], 0)
    for size in sizes:
        parts.append(whole[:, start : start + size].reshape(count * size, -1))
        start += size
    return parts


def stack_parts(parts):
    count = lax.axis_size("dev")
    shaped = [part.astype(jnp.bfloat16).reshape(count, part.shape[0] // count, -1) for part in parts]
    return jnp.concatenate(shaped, axis=1)


def split_rows(summed, sizes):
    pieces, start = ([], 0)
    for size in sizes:
        pieces.append(summed[start : start + size].astype(jnp.float32))
        start += size
    return pieces


def swap_halves(held, bit, last):
    count = lax.axis_size("dev")
    mine = (lax.axis_index("dev") >> bit) & 1
    keep = lax.dynamic_index_in_dim(held, mine, 0, keepdims=False)
    give = lax.dynamic_index_in_dim(held, 1 - mine, 0, keepdims=False)
    came = lax.ppermute(give, "dev", [(source, source ^ (1 << bit)) for source in range(count)])
    total = keep.astype(jnp.float32) + came.astype(jnp.float32)
    return total if last else total.astype(jnp.bfloat16)


def cube_sum(stacked):
    count, rows, width = stacked.shape
    bits = count.bit_length() - 1
    middle = list(range(1, bits - 1))
    grid = stacked.reshape((2,) * bits + (rows, width))
    held = swap_halves(jnp.moveaxis(grid, bits - 1, 0), 0, False)
    lanes = width // 3
    thirds = []
    for turn in range(3):
        order = middle[turn:] + middle[:turn] + [bits - 1]
        axes = [bits - 1 - bit for bit in order]
        third = held[..., turn * lanes : (turn + 1) * lanes].transpose(axes + [bits - 1, bits])
        thirds.append((third, order))
    for stage in range(len(middle)):
        thirds = [(swap_halves(third, order[stage], False), order) for third, order in thirds]
    return swap_halves(jnp.concatenate([third for third, _ in thirds], axis=-1), bits - 1, True)


def split_low(values):
    high = lax.reduce_precision(values, 8, 7)
    return (high.astype(jnp.bfloat16), (values - high).astype(jnp.bfloat16))


def low_units(blocks):
    per_row = blocks.shape[1]
    place = 8 + jnp.arange(per_row, dtype=jnp.int32)[None, :]
    return jnp.min(place - 2 * ((blocks + 1) // 2), axis=1).astype(jnp.int32)


def by_unit(array):
    cut = array.reshape((array.shape[0], array.shape[1] // UNIT, UNIT) + array.shape[2:])
    return cut.swapaxes(0, 1)


def by_row(array, micros):
    cut = array.reshape(-1, micros, UNIT, array.shape[-1])
    return cut.swapaxes(0, 1).reshape(micros, -1, array.shape[-1])


def shards(
    token_ids,
    lengths,
    embedding,
    norm1_gain,
    w_query,
    w_key,
    w_value,
    w_out,
    mix_logits,
    mix_weights,
    norm2_gain,
    w_up,
    w_down,
    cotangent,
):
    count = lax.axis_size("dev")
    me = lax.axis_index("dev")
    micros, row_count = token_ids.shape
    own_rows, width = embedding.shape
    heads = mix_logits.shape[0]
    part = norm1_gain.shape[0]
    per_row = row_count // UNIT
    tokens = micros * row_count
    tok_ids = by_unit(token_ids).reshape(-1)
    stride = max(16, 1024 // count)
    room = stride - 2

    unit_rows = me * row_count + UNIT * jnp.arange(per_row, dtype=jnp.int32)
    begins = jnp.stack([seq_starts(lengths[micro], unit_rows) for micro in range(micros)])
    blocks = ((unit_rows[None, :] - begins) // UNIT + 1).reshape(-1).astype(jnp.int32)

    lows = low_units(blocks.reshape(micros, per_row))
    mixes = spread_mixes(mix_logits, mix_weights)

    up_cols = w_up.shape[1] // width
    up_pieces = [w_up[:, col * width : (col + 1) * width] for col in range(up_cols)]
    weight_pieces = [w_query, w_key, w_value, w_out] + up_pieces + [w_down]
    ids = split_ids(tok_ids, own_rows)
    message, chosen = ask_round(ids, 0, own_rows, stride, room)
    message, weight_pieces = lax.optimization_barrier((message, weight_pieces))
    gathered = gather_parts(weight_pieces)
    w_q, w_k, w_v, w_o = gathered[:4]
    w_u, w_d = (jnp.concatenate(gathered[4:-1], axis=1), gathered[-1])
    gains_row = jnp.concatenate([norm1_gain, norm2_gain, jnp.zeros((width - 2 * part,), jnp.bfloat16)])
    picked, gains, *plan = lookup(embedding, ids, message, chosen, gains_row, stride, room)
    gain_one = gains[:, :part].reshape(-1)
    gain_two = gains[:, part : 2 * part].reshape(-1)
    inputs = picked.astype(jnp.float32)

    normed_one, inv_one, hidden_one = normalize(inputs, gain_one)
    own_hidden = hidden_one.reshape(per_row, micros, UNIT, width)
    pieces = [from_behind(own_hidden[per_row - 1 :], 4)]
    pieces += [from_behind(own_hidden, steps) for steps in (3, 2, 1)] + [own_hidden]
    query, key, value = project(lows, pieces, (w_q, w_k, w_v))
    attended, *kept = attention_fwd(blocks, query, key, value, mixes, heads)
    attended = attended.reshape(tokens, width)

    middle = inputs + matmul(attended, w_o)
    normed_two, inv_two, hidden_two = normalize(middle, gain_two)
    up_proj = matmul(hidden_two, w_u)
    activated, gelu_pull = jax.vjp(jax.nn.gelu, up_proj)
    activated = activated.astype(jnp.bfloat16)
    output = (middle + matmul(activated, w_d)).astype(jnp.bfloat16)

    grad_rows = by_unit(cotangent).reshape(tokens, width)
    grad_act = matmul_right_t(grad_rows, w_d)
    grad_upb = gelu_pull(grad_act)[0].astype(jnp.bfloat16)
    grad_down = matmul_left_t(activated, grad_rows)
    grad_up = matmul_left_t(hidden_two, grad_upb)
    grad_hidden_two = matmul_right_t(grad_upb, w_u)
    grad_mid_norm, grad_gain_two = norm_back(grad_hidden_two, normed_two, inv_two, gain_two)
    grad_middle = grad_rows.astype(jnp.float32) + grad_mid_norm
    grad_branch = grad_middle.astype(jnp.bfloat16)
    grad_wout = matmul_left_t(attended, grad_branch)
    grad_att = matmul_right_t(grad_branch, w_o).astype(jnp.bfloat16).reshape(own_hidden.shape)
    up_terms = [grad_up[:, col * width : (col + 1) * width] for col in range(up_cols)]
    late_terms = [grad_wout] + up_terms + [grad_down]
    late_stack, grad_att = lax.optimization_barrier((stack_parts(late_terms), grad_att))
    late_sums = lax.psum_scatter(
        late_stack.reshape(count * late_stack.shape[1], width), "dev", scatter_dimension=0, tiled=True
    )

    grad_query, grad_key, grad_value, wide_logit, wide_prob = attention_bwd(
        blocks, query, key, value, grad_att, kept, mixes, heads
    )
    *terms, grad_own = project_back(lows, grad_query, grad_key, grad_value, (w_q, w_k, w_v))
    returned = [from_behind(term, -steps) for term, steps in zip(terms, (4, 3, 2, 1))]
    grad_own, grad_query, grad_key, grad_value, pieces, hidden_one = lax.optimization_barrier(
        (grad_own, grad_query, grad_key, grad_value, pieces, hidden_one)
    )
    grad_query = grad_query.reshape(tokens, width)
    grad_key = grad_key.reshape(-1, width)
    grad_value = grad_value.reshape(-1, width)
    flat_hidden = jnp.concatenate(pieces, axis=0).reshape(-1, width)
    grad_wq = matmul_left_t(hidden_one, grad_query)
    grad_wk = matmul_left_t(flat_hidden, grad_key)
    grad_wv = matmul_left_t(flat_hidden, grad_value)
    early_terms = [grad_wq, grad_wk, grad_wv]
    early_sums = cube_sum(stack_parts(early_terms))
    early_sums = split_rows(early_sums, [term.shape[0] // count for term in early_terms])
    late_sums = split_rows(late_sums, [term.shape[0] // count for term in late_terms])
    for term in returned:
        term = term.astype(jnp.float32)
        if term.shape[0] < per_row:
            term = jnp.pad(term, ((per_row - term.shape[0], 0), (0, 0), (0, 0), (0, 0)))
        grad_own = grad_own + term
    grad_hidden_one = grad_own.reshape(tokens, width)
    grad_in_norm, grad_gain_one = norm_back(grad_hidden_one, normed_one, inv_one, gain_one)
    grad_inputs = grad_middle + grad_in_norm

    mix_terms = jnp.concatenate([fold_mix(wide_logit, heads).reshape(-1), fold_mix(wide_prob, heads).reshape(-1)])
    mix_size = mix_terms.shape[0]
    small = jnp.concatenate(
        [
            grad_gain_one.reshape(count, part),
            grad_gain_two.reshape(count, part),
            jnp.broadcast_to(mix_terms[None, :], (count, mix_size)),
            jnp.zeros((count, width - 2 * part - mix_size), jnp.float32),
        ],
        axis=1,
    )
    grad_inputs, late_sums = lax.optimization_barrier((grad_inputs, late_sums))
    table_grad, small_sum = table_back(grad_inputs, split_low(small), plan, own_rows, stride, room)
    mixes = small_sum[2 * part : 2 * part + mix_size].reshape(2, heads, heads)
    return (
        by_row(output, micros),
        by_row(grad_inputs, micros),
        table_grad,
        small_sum[:part],
        early_sums[0],
        early_sums[1],
        early_sums[2],
        late_sums[0],
        mixes[0],
        mixes[1],
        small_sum[part : 2 * part],
        jnp.concatenate(late_sums[1:-1], axis=1),
        late_sums[-1],
    )


def solution(mesh):
    in_specs = (
        P(None, "dev"),
        P(),
        P("dev", None),
        P("dev"),
        P("dev", None),
        P("dev", None),
        P("dev", None),
        P("dev", None),
        P(),
        P(),
        P("dev"),
        P("dev", None),
        P("dev", None),
        P(None, "dev", None),
    )
    out_specs = (
        P(None, "dev", None),
        P(None, "dev", None),
        P("dev", None),
        P("dev"),
        P("dev", None),
        P("dev", None),
        P("dev", None),
        P("dev", None),
        P(),
        P(),
        P("dev"),
        P("dev", None),
        P("dev", None),
    )
    return jax.shard_map(shards, mesh=mesh, in_specs=in_specs, out_specs=out_specs, check_vma=False)
```

```python
from functools import partial

import jax
import jax.numpy as jnp
from jax import lax
from jax.experimental import pallas as pl
from jax.experimental.pallas import tpu as pltpu
from jax.sharding import PartitionSpec as P

norm_eps = 1e-06

masked = -1e30
UNIT = 128
CHUNK = 256
GROUP = 16
MAX_CHUNKS = 4


def dot_nn(left, right):
    return lax.dot_general(left, right, (((1,), (0,)), ((), ())), preferred_element_type=jnp.float32)


def dot_nt(left, right):
    return lax.dot_general(left, right, (((1,), (1,)), ((), ())), preferred_element_type=jnp.float32)


def spread_heads(rows, lane_head, quad, heads_per_quad):
    part = rows[:, quad * CHUNK : (quad + 1) * CHUNK]
    zero = jnp.zeros_like(part)
    return jnp.concatenate([jnp.where(lane_head == head, part, zero) for head in range(heads_per_quad)], axis=0)


def own_lanes(wide, lane_head, heads_per_quad):
    total = jnp.where(lane_head == 0, wide[:UNIT], 0.0)
    for head in range(1, heads_per_quad):
        total = total + jnp.where(lane_head == head, wide[head * UNIT : (head + 1) * UNIT], 0.0)
    return total


def allowed_keys(chunk, group, blocks):
    key = lax.broadcasted_iota(jnp.int32, (GROUP, CHUNK), 1) - (UNIT + CHUNK * chunk)
    row = lax.broadcasted_iota(jnp.int32, (GROUP, CHUNK), 0) + GROUP * group
    return (key <= row) & (key >= (1 - blocks) * UNIT)


def twice(rows):
    return jnp.concatenate([rows, rows], axis=-1)


def put_groups(ref, quad, per_quad, term):
    low = term.astype(jnp.bfloat16)
    for head in range(per_quad):
        rows = slice((quad * per_quad + head) * GROUP, (quad * per_quad + head + 1) * GROUP)
        for group in range(UNIT // GROUP):
            start = head * UNIT + group * GROUP
            ref[rows, group * CHUNK : (group + 1) * CHUNK] = low[start : start + GROUP]


def fwd_kernel(heads, blocks_ref, q_ref, k_ref, v_ref, mix_ref, att_ref, score_out, prob_out, mixed_out,
               qx, score, prob, mixed, logit, top, norm, total, sems):
    micro, inner, per_row = (pl.program_id(0), pl.program_id(1), pl.num_programs(1))
    blocks = blocks_ref[micro * per_row + inner]
    chunks = (blocks + 1) // 2
    last_unit = k_ref.shape[0] - per_row + inner + 1
    quads = q_ref.shape[3] // CHUNK
    per_quad = heads // quads
    groups = UNIT // GROUP
    wide = heads * GROUP
    lane_head = lax.broadcasted_iota(jnp.int32, (UNIT, CHUNK), 1) // (CHUNK // per_quad)
    for quad in range(quads):
        qx[quad] = spread_heads(q_ref[0, 0], lane_head, quad, per_quad)
    total[...] = jnp.zeros_like(total)
    top[...] = jnp.full_like(top, masked)
    norm[...] = jnp.zeros_like(norm)

    def keys(ref, chunk, quad):
        units = pl.ds(last_unit - 2 * (chunk + 1), 2)
        return ref[units, 0, :, quad * CHUNK : (quad + 1) * CHUNK].reshape(CHUNK, CHUNK)

    def keep(chunk, kind):
        source, target = ((score, score_out), (prob, prob_out), (mixed, mixed_out))[kind]
        return pltpu.make_async_copy(source.at[chunk], target.at[inner, micro, chunk], sems.at[kind, chunk])

    @pl.loop(0, chunks)
    def _(chunk):
        for quad in range(quads):
            put_groups(score.at[chunk], quad, per_quad, dot_nt(qx[quad], keys(k_ref, chunk, quad)))
        keep(chunk, 0).start()
        for group in range(groups):
            l = dot_nn(mix_ref[0], score[chunk, :, group * CHUNK : (group + 1) * CHUNK])
            l = jnp.where(allowed_keys(chunk, group, blocks)[None], l.reshape(heads, GROUP, CHUNK), masked)
            l = l.reshape(wide, CHUNK)
            logit[chunk, group] = l
            old = top[group]
            new = jnp.maximum(old, jnp.maximum(l[:, :UNIT], l[:, UNIT:]))
            terms = jnp.exp(l[:, :UNIT] - new) + jnp.exp(l[:, UNIT:] - new)
            norm[group] = norm[group] * jnp.exp(old - new) + terms
            top[group] = new

    for group in range(groups):
        lanes = top[group]
        high = jnp.broadcast_to(jnp.max(lanes, axis=-1, keepdims=True), lanes.shape)
        whole = jnp.sum(norm[group] * jnp.exp(lanes - high), axis=-1, keepdims=True)
        top[group] = high + jnp.log(jnp.broadcast_to(whole, lanes.shape))

    @pl.loop(0, chunks)
    def _(chunk):
        for group in range(groups):
            p = jnp.exp(logit[chunk, group] - twice(top[group])).astype(jnp.bfloat16)
            prob[chunk, :, group * CHUNK : (group + 1) * CHUNK] = p
            a = dot_nn(mix_ref[2], p).astype(jnp.bfloat16)
            mixed[chunk, :, GROUP * group : GROUP * (group + 1), :] = a.reshape(heads, GROUP, CHUNK)
        keep(chunk, 1).start()
        keep(chunk, 2).start()
        for quad in range(quads):
            a = mixed[chunk, quad * per_quad : (quad + 1) * per_quad].reshape(per_quad * UNIT, CHUNK)
            o = own_lanes(dot_nn(a, keys(v_ref, chunk, quad)), lane_head, per_quad)
            total[:, quad * CHUNK : (quad + 1) * CHUNK] += o

    att_ref[0, 0] = total[...].astype(jnp.bfloat16)

    @pl.loop(0, chunks)
    def _(chunk):
        for kind in range(3):
            keep(chunk, kind).wait()


def attention_specs(q, k, heads):
    per_row, micros, _, width = q.shape
    wide = heads * GROUP
    return (
        pl.BlockSpec((1, 1, UNIT, width), lambda m, u, _: (u, m, 0, 0)),
        pl.BlockSpec((k.shape[0], 1, UNIT, width), lambda m, u, _: (0, m, 0, 0)),
        pl.BlockSpec((4, wide, wide), lambda m, u, _: (0, 0, 0)),
    )


def kept_shapes(heads):
    wide = heads * GROUP
    flat = (MAX_CHUNKS, wide, UNIT // GROUP * CHUNK)
    return (flat, flat, (MAX_CHUNKS, heads, UNIT, CHUNK))


def attention_fwd(blocks, q, k, v, mixes, heads):
    per_row, micros, _, width = q.shape
    wide = heads * GROUP
    groups = UNIT // GROUP
    quads = width // CHUNK
    unit_spec, kv_spec, mix_spec = attention_specs(q, k, heads)
    kept = kept_shapes(heads)
    anywhere = pl.BlockSpec(memory_space=pl.ANY)
    return pl.pallas_call(
        partial(fwd_kernel, heads),
        grid_spec=pltpu.PrefetchScalarGridSpec(
            num_scalar_prefetch=1,
            grid=(micros, per_row),
            in_specs=[unit_spec, kv_spec, kv_spec, mix_spec],
            out_specs=[unit_spec, anywhere, anywhere, anywhere],
            scratch_shapes=[pltpu.VMEM((quads, heads // quads * UNIT, CHUNK), jnp.bfloat16)]
            + [pltpu.VMEM(shape, jnp.bfloat16) for shape in kept]
            + [
                pltpu.VMEM((MAX_CHUNKS, groups, wide, CHUNK), jnp.float32),
                pltpu.VMEM((groups, wide, UNIT), jnp.float32),
                pltpu.VMEM((groups, wide, UNIT), jnp.float32),
                pltpu.VMEM((UNIT, width), jnp.float32),
                pltpu.SemaphoreType.DMA((3, MAX_CHUNKS)),
            ],
        ),
        out_shape=[jax.ShapeDtypeStruct(q.shape, jnp.bfloat16)]
        + [jax.ShapeDtypeStruct((per_row, micros) + shape, jnp.bfloat16) for shape in kept],
        compiler_params=pltpu.CompilerParams(vmem_limit_bytes=50 * 1024 * 1024),
        cost_estimate=pl.CostEstimate(flops=20_000_000_000, bytes_accessed=30_000_000, transcendentals=0),
        name="attention_fwd",
    )(blocks, q, k, v, mixes)


def bwd_kernel(heads, blocks_ref, q_ref, k_ref, v_ref, do_ref, mix_ref, score_in, prob_in, mixed_in,
               dq_ref, dk_ref, dv_ref, gl_ref, gp_ref,
               qxt, dox, doxt, score, prob, mixed, grad_prob, grad_mixed, grad_logit, grad_score,
               delta, dq_total, dk_total, dv_total, sems):
    micro, inner, per_row = (pl.program_id(0), pl.program_id(1), pl.num_programs(1))
    step = micro * per_row + inner
    slot = step % 2
    blocks = blocks_ref[step]
    chunks = (blocks + 1) // 2
    key_units = k_ref.shape[0]
    last_unit = key_units - per_row + inner + 1
    quads = q_ref.shape[3] // CHUNK
    per_quad = heads // quads
    groups = UNIT // GROUP
    wide = heads * GROUP
    lane_head = lax.broadcasted_iota(jnp.int32, (UNIT, CHUNK), 1) // (CHUNK // per_quad)
    row_head = lax.broadcasted_iota(jnp.int32, (CHUNK, UNIT), 0) // (CHUNK // per_quad)
    lowest = key_units
    for other in range(key_units - 7):
        its_chunks = (blocks_ref[micro * per_row + other] + 1) // 2
        lowest = jnp.minimum(lowest, key_units - per_row + other + 1 - 2 * its_chunks)

    def fetch(at, chunk, kind):
        source, target = ((score_in, score), (prob_in, prob), (mixed_in, mixed))[kind]
        place = source.at[at % per_row, at // per_row, chunk]
        return pltpu.make_async_copy(place, target.at[at % 2, chunk], sems.at[kind, at % 2, chunk])

    def fetch_all(at):
        @pl.loop(0, (blocks_ref[at] + 1) // 2)
        def _(chunk):
            for kind in (1, 2, 0):
                fetch(at, chunk, kind).start()

    @pl.when(step == 0)
    def _():
        fetch_all(0)
        gl_ref[...] = jnp.zeros_like(gl_ref)
        gp_ref[...] = jnp.zeros_like(gp_ref)

    @pl.when(step + 1 < pl.num_programs(0) * per_row)
    def _():
        fetch_all(step + 1)

    @pl.when(inner == 0)
    def _():
        @pl.loop(lowest, key_units)
        def _(key_unit):
            dk_total[key_unit] = jnp.zeros_like(dk_total[key_unit])
            dv_total[key_unit] = jnp.zeros_like(dv_total[key_unit])

    def spread_turned(rows, quad):
        turned = rows[:, quad * CHUNK : (quad + 1) * CHUNK].T
        zero = jnp.zeros_like(turned)
        return jnp.concatenate([jnp.where(row_head == head, turned, zero) for head in range(per_quad)], axis=1)

    for quad in range(quads):
        qxt[quad] = spread_turned(q_ref[0, 0], quad)
        dox[quad] = spread_heads(do_ref[0, 0], lane_head, quad, per_quad)
        doxt[quad] = spread_turned(do_ref[0, 0], quad)
    dq_total[...] = jnp.zeros_like(dq_total)
    delta[...] = jnp.zeros_like(delta)

    def keys(ref, chunk, quad):
        units = pl.ds(last_unit - 2 * (chunk + 1), 2)
        return ref[units, 0, :, quad * CHUNK : (quad + 1) * CHUNK].reshape(CHUNK, CHUNK)

    def add_to(total, chunk, quad, term):
        first = last_unit - 2 * (chunk + 1)
        lanes = slice(quad * CHUNK, (quad + 1) * CHUNK)
        total[first, lanes, :] += term[:, :UNIT]
        total[first + 1, lanes, :] += term[:, UNIT:]

    @pl.loop(0, chunks)
    def _(chunk):
        for quad in range(quads):
            put_groups(grad_mixed, quad, per_quad, dot_nt(dox[quad], keys(v_ref, chunk, quad)))
        fetch(step, chunk, 1).wait()
        for group in range(groups):
            cols = slice(group * CHUNK, (group + 1) * CHUNK)
            dp = dot_nn(mix_ref[3], grad_mixed[:, cols])
            grad_prob[chunk, :, cols] = dp.astype(grad_prob.dtype)
            term = prob[slot, chunk, :, cols].astype(jnp.float32) * dp
            delta[group] += term[:, :UNIT] + term[:, UNIT:]
        gp_ref[...] += dot_nt(prob[slot, chunk], grad_mixed[...])
        fetch(step, chunk, 2).wait()
        for quad in range(quads):
            a = mixed[slot, chunk, quad * per_quad : (quad + 1) * per_quad].reshape(per_quad * UNIT, CHUNK)
            add_to(dv_total, chunk, quad, dot_nn(doxt[quad], a))

    for group in range(groups):
        delta[group] = jnp.broadcast_to(jnp.sum(delta[group], axis=-1, keepdims=True), (wide, UNIT))

    @pl.loop(0, chunks)
    def _(chunk):
        for group in range(groups):
            cols = slice(group * CHUNK, (group + 1) * CHUNK)
            dp = grad_prob[chunk, :, cols].astype(jnp.float32) - twice(delta[group])
            dl = (prob[slot, chunk, :, cols].astype(jnp.float32) * dp).astype(jnp.bfloat16)
            grad_logit[:, cols] = dl
            ds = dot_nn(mix_ref[1], dl).astype(jnp.bfloat16)
            grad_score[:, GROUP * group : GROUP * (group + 1), :] = ds.reshape(heads, GROUP, CHUNK)
        fetch(step, chunk, 0).wait()
        gl_ref[...] += dot_nt(score[slot, chunk], grad_logit[...])
        for quad in range(quads):
            ds = grad_score[quad * per_quad : (quad + 1) * per_quad].reshape(per_quad * UNIT, CHUNK)
            dq = own_lanes(dot_nn(ds, keys(k_ref, chunk, quad)), lane_head, per_quad)
            dq_total[:, quad * CHUNK : (quad + 1) * CHUNK] += dq
            add_to(dk_total, chunk, quad, dot_nn(qxt[quad], ds))

    dq_ref[0, 0] = (dq_total[...] * 0.125).astype(jnp.bfloat16)

    @pl.when(inner == per_row - 1)
    def _():
        @pl.loop(0, lowest)
        def _(key_unit):
            dk_ref[key_unit, 0] = jnp.zeros_like(dk_ref[key_unit, 0])
            dv_ref[key_unit, 0] = jnp.zeros_like(dv_ref[key_unit, 0])

        @pl.loop(lowest, key_units)
        def _(key_unit):
            dk_ref[key_unit, 0] = dk_total[key_unit].astype(jnp.bfloat16).T
            dv_ref[key_unit, 0] = dv_total[key_unit].astype(jnp.bfloat16).T


def attention_bwd(blocks, q, k, v, grad_out, kept, mixes, heads):
    per_row, micros, _, width = q.shape
    key_units = k.shape[0]
    wide = heads * GROUP
    groups = UNIT // GROUP
    quads = width // CHUNK
    turned = (quads, CHUNK, heads // quads * UNIT)
    unit_spec, kv_spec, mix_spec = attention_specs(q, k, heads)
    sum_spec = pl.BlockSpec((wide, wide), lambda m, u, _: (0, 0))
    anywhere = pl.BlockSpec(memory_space=pl.ANY)
    return pl.pallas_call(
        partial(bwd_kernel, heads),
        grid_spec=pltpu.PrefetchScalarGridSpec(
            num_scalar_prefetch=1,
            grid=(micros, per_row),
            in_specs=[unit_spec, kv_spec, kv_spec, unit_spec, mix_spec] + [anywhere] * 3,
            out_specs=[unit_spec, kv_spec, kv_spec, sum_spec, sum_spec],
            scratch_shapes=[
                pltpu.VMEM(turned, jnp.bfloat16),
                pltpu.VMEM((quads, heads // quads * UNIT, CHUNK), jnp.bfloat16),
                pltpu.VMEM(turned, jnp.bfloat16),
            ]
            + [pltpu.VMEM((2,) + shape, jnp.bfloat16) for shape in kept_shapes(heads)]
            + [
                pltpu.VMEM((MAX_CHUNKS, wide, groups * CHUNK), jnp.bfloat16),
                pltpu.VMEM((wide, groups * CHUNK), jnp.bfloat16),
                pltpu.VMEM((wide, groups * CHUNK), jnp.bfloat16),
                pltpu.VMEM((heads, UNIT, CHUNK), jnp.bfloat16),
                pltpu.VMEM((groups, wide, UNIT), jnp.float32),
                pltpu.VMEM((UNIT, width), jnp.float32),
                pltpu.VMEM((key_units, width, UNIT), jnp.float32),
                pltpu.VMEM((key_units, width, UNIT), jnp.float32),
                pltpu.SemaphoreType.DMA((3, 2, MAX_CHUNKS)),
            ],
        ),
        out_shape=[
            jax.ShapeDtypeStruct(q.shape, jnp.bfloat16),
            jax.ShapeDtypeStruct(k.shape, jnp.bfloat16),
            jax.ShapeDtypeStruct(v.shape, jnp.bfloat16),
            jax.ShapeDtypeStruct((wide, wide), jnp.float32),
            jax.ShapeDtypeStruct((wide, wide), jnp.float32),
        ],
        compiler_params=pltpu.CompilerParams(vmem_limit_bytes=58 * 1024 * 1024),
        cost_estimate=pl.CostEstimate(flops=45_000_000_000, bytes_accessed=40_000_000, transcendentals=0),
        name="attention_bwd",
    )(blocks, q, k, v, grad_out, mixes, *kept)


def piece_bases(key_units, per_row):
    sizes = [1] + [per_row] * ((key_units - 1) // per_row)
    return [(sum(sizes[:at]), size) for at, size in enumerate(sizes)]


def project_kernel(low_ref, *refs):
    pieces, (w_q, w_k, w_v, q_ref, k_ref, v_ref) = (refs[:-6], refs[-6:])
    key_units, width = (k_ref.shape[0], k_ref.shape[3])
    per_row = q_ref.shape[0]
    low = low_ref[pl.program_id(0)]

    for piece, (base, size) in zip(pieces, piece_bases(key_units, per_row)):
        @pl.when(base + size > low)
        def _():
            rows = piece[:, 0].reshape(size * UNIT, width)
            k_ref[base : base + size, 0] = dot_nn(rows, w_k[...]).astype(jnp.bfloat16).reshape(size, UNIT, width)
            v_ref[base : base + size, 0] = dot_nn(rows, w_v[...]).astype(jnp.bfloat16).reshape(size, UNIT, width)

    rows = pieces[-1][:, 0].reshape(per_row * UNIT, width)
    query = dot_nn(rows, w_q[...]).astype(jnp.bfloat16) * jnp.bfloat16(0.125)
    q_ref[:, 0] = query.reshape(per_row, UNIT, width)


def project(low, pieces, weights):
    micros, width = pieces[0].shape[1], pieces[0].shape[3]
    key_units = sum(piece.shape[0] for piece in pieces)
    per_row = pieces[-1].shape[0]

    def spec(units):
        return pl.BlockSpec((units, 1, UNIT, width), lambda m, _: (0, m, 0, 0))

    weight_spec = pl.BlockSpec((width, width), lambda m, _: (0, 0))
    shapes = [(units, micros, UNIT, width) for units in (per_row, key_units, key_units)]
    return pl.pallas_call(
        project_kernel,
        grid_spec=pltpu.PrefetchScalarGridSpec(
            num_scalar_prefetch=1,
            grid=(micros,),
            in_specs=[spec(piece.shape[0]) for piece in pieces] + [weight_spec] * 3,
            out_specs=[spec(shape[0]) for shape in shapes],
        ),
        out_shape=[jax.ShapeDtypeStruct(shape, jnp.bfloat16) for shape in shapes],
        compiler_params=pltpu.CompilerParams(vmem_limit_bytes=44 * 1024 * 1024),
        cost_estimate=pl.CostEstimate(flops=6_000_000_000, bytes_accessed=15_000_000, transcendentals=0),
        name="project",
    )(low, *pieces, *weights)


def project_back_kernel(low_ref, dq_ref, dk_ref, dv_ref, w_q, w_k, w_v, *outs):
    key_units, width = (dk_ref.shape[0], dk_ref.shape[3])
    per_row = dq_ref.shape[0]
    low = low_ref[pl.program_id(0)]
    bases = piece_bases(key_units, per_row)

    def from_keys(base, size):
        rows = slice(base, base + size)
        key_term = dot_nt(dk_ref[rows, 0].reshape(size * UNIT, width), w_k[...])
        return key_term + dot_nt(dv_ref[rows, 0].reshape(size * UNIT, width), w_v[...])

    for out, (base, size) in zip(outs[:-1], bases[:-1]):
        @pl.when(base + size > low)
        def _():
            out[:, 0] = from_keys(base, size).astype(jnp.bfloat16).reshape(size, UNIT, width)

        @pl.when(base + size <= low)
        def _():
            out[...] = jnp.zeros_like(out)

    own = from_keys(*bases[-1]) + dot_nt(dq_ref[:, 0].reshape(per_row * UNIT, width), w_q[...])
    outs[-1][:, 0] = own.reshape(per_row, UNIT, width)


def project_back(low, grad_query, grad_key, grad_value, weights):
    per_row, micros, _, width = grad_query.shape
    key_units = grad_key.shape[0]

    def spec(units):
        return pl.BlockSpec((units, 1, UNIT, width), lambda m, _: (0, m, 0, 0))

    weight_spec = pl.BlockSpec((width, width), lambda m, _: (0, 0))
    sizes = [size for _, size in piece_bases(key_units, per_row)]
    shapes = [(size, micros, UNIT, width) for size in sizes]
    kinds = [jnp.bfloat16] * (len(sizes) - 1) + [jnp.float32]
    return pl.pallas_call(
        project_back_kernel,
        grid_spec=pltpu.PrefetchScalarGridSpec(
            num_scalar_prefetch=1,
            grid=(micros,),
            in_specs=[spec(per_row), spec(key_units), spec(key_units)] + [weight_spec] * 3,
            out_specs=[spec(size) for size in sizes],
        ),
        out_shape=[jax.ShapeDtypeStruct(shape, kind) for shape, kind in zip(shapes, kinds)],
        compiler_params=pltpu.CompilerParams(vmem_limit_bytes=44 * 1024 * 1024),
        cost_estimate=pl.CostEstimate(flops=6_000_000_000, bytes_accessed=15_000_000, transcendentals=0),
        name="project_back",
    )(low, grad_query, grad_key, grad_value, *weights)


def spread_mixes(mix_logits, mix_weights):
    heads = mix_logits.shape[0]
    wide = heads * GROUP
    place = jnp.arange(wide, dtype=jnp.int32)
    pick = (place[:, None] // GROUP == jnp.arange(heads, dtype=jnp.int32)[None, :]).astype(mix_logits.dtype)
    same_row = (place[:, None] % GROUP == place[None, :] % GROUP)[None]
    tables = jnp.stack([mix_logits.T, mix_logits, mix_weights.T, mix_weights]).reshape(4 * heads, heads)
    across = jnp.dot(tables, pick.T, preferred_element_type=jnp.float32).astype(mix_logits.dtype)
    down = jnp.einsum("wh,bhx->bwx", pick, across.reshape(4, heads, wide), preferred_element_type=jnp.float32)
    return jnp.where(same_row, down, 0.0).astype(mix_logits.dtype)


def fold_mix(wide, heads):
    place = jnp.arange(heads * GROUP, dtype=jnp.int32)
    pick = (place[:, None] // GROUP == jnp.arange(heads, dtype=jnp.int32)[None, :]).astype(jnp.float32)
    same_row = place[:, None] % GROUP == place[None, :] % GROUP
    down = jnp.dot(pick.T, jnp.where(same_row, wide, 0.0), precision=lax.Precision.HIGHEST)
    return jnp.dot(down, pick, precision=lax.Precision.HIGHEST)


def from_behind(value, steps):
    count = lax.axis_size("dev")
    first, last = (max(0, -steps), min(count, count - steps))
    return lax.ppermute(value, "dev", [(source, source + steps) for source in range(first, last)])


def with_sibling(value):
    count = lax.axis_size("dev")
    return lax.ppermute(value, "dev", [(source, source ^ 1) for source in range(count)])


def earlier_rows(own):
    size = own.shape[0]
    first_core = lax.axis_index("dev") % 2 == 0
    two, four = (from_behind(own, 2), from_behind(own, 4))
    give = jnp.concatenate([jnp.where(first_core, own, two), jnp.where(first_core, two, four)], axis=0)
    came = with_sibling(give)
    return [four[size - 1 :], came[size:], two, came[:size], own]


def return_rows(four, two, came, grad_own):
    size = two.shape[0]
    first_core = lax.axis_index("dev") % 2 == 0
    came = came.astype(jnp.float32)
    one, three = (came[:size], came[size:])
    give_two = two.astype(jnp.float32) + jnp.where(first_core, three, one)
    padded = jnp.pad(four.astype(jnp.float32), ((size - four.shape[0], 0), (0, 0), (0, 0), (0, 0)))
    give_four = padded + jnp.where(first_core, 0.0, three)
    back_two = from_behind(give_two.astype(jnp.bfloat16), -2).astype(jnp.float32)
    back_four = from_behind(give_four.astype(jnp.bfloat16), -4).astype(jnp.float32)
    return grad_own + jnp.where(first_core, one, 0.0) + back_two + back_four


def seq_starts(lengths_row, query_rows):
    seq_ends = jnp.cumsum(lengths_row)
    starts = seq_ends - lengths_row
    return jnp.max(jnp.where(starts[None, :] <= query_rows[:, None], starts[None, :], 0), axis=1)


def normalize(values, gain_vec):
    inv_rms = lax.rsqrt(jnp.mean(values * values, axis=-1, keepdims=True) + norm_eps)
    normed = values * inv_rms
    return (normed, inv_rms, (normed * gain_vec.astype(jnp.float32)).astype(jnp.bfloat16))


def norm_back(grad_hidden, normed, inv_rms, gain_vec):
    grad_gain = jnp.sum(grad_hidden * normed, axis=0)
    grad_normed = grad_hidden * gain_vec.astype(jnp.float32)
    inner_mean = jnp.mean(grad_normed * normed, axis=-1, keepdims=True)
    return (inv_rms * (grad_normed - normed * inner_mean), grad_gain)


def matmul(left, right):
    return jnp.dot(left, right, preferred_element_type=jnp.float32)


def matmul_left_t(left, right):
    return lax.dot_general(left, right, (((0,), (0,)), ((), ())), preferred_element_type=jnp.float32)


def matmul_right_t(left, right):
    return lax.dot_general(left, right, (((1,), (1,)), ((), ())), preferred_element_type=jnp.float32)


def exchange(value):
    return lax.all_to_all(value, "dev", split_axis=0, concat_axis=0, tiled=True)


def split_ids(tok_ids, own_rows):
    owner = tok_ids // own_rows
    place = jnp.arange(tok_ids.shape[0], dtype=jnp.int32)
    same = tok_ids[:, None] == tok_ids[None, :]
    repeated = jnp.any(same & (place[None, :] < place[:, None]), axis=1)
    before = (owner[:, None] == owner[None, :]) & (tok_ids[None, :] < tok_ids[:, None]) & ~repeated[None, :]
    return (owner, tok_ids % own_rows, jnp.sum(before, axis=1, dtype=jnp.int32))


def ask_round(ids, index, own_rows, stride, room):
    count = lax.axis_size("dev")
    owner, local, rank = ids
    here = rank - index * room
    slot = jnp.where((here >= 0) & (here < room), owner * stride + here, -1)
    chosen = slot[None, :] == jnp.arange(count * stride, dtype=jnp.int32)[:, None]
    wanted = jnp.max(jnp.where(chosen, local[None, :], -1), axis=1).reshape(count, stride)
    rounds = jnp.broadcast_to(jnp.max(rank) // room + 1, (count, stride))
    return (jnp.concatenate([wanted, rounds], axis=1), chosen.astype(jnp.bfloat16))


def hear_round(message, own_rows, stride):
    asked = exchange(message)
    pick = asked[:, :stride].reshape(-1, 1) == jnp.arange(own_rows, dtype=jnp.int32)[None, :]
    return (pick.astype(jnp.bfloat16), jnp.max(asked[:, stride:]))


def plan_round(ids, index, own_rows, stride, room):
    message, chosen = ask_round(ids, index, own_rows, stride, room)
    pick, _ = hear_round(message, own_rows, stride)
    return (chosen, pick)


def answer(embedding, chosen, pick, stride, extra_row):
    count = lax.axis_size("dev")
    rows = matmul(pick, embedding).astype(jnp.bfloat16).reshape(count, stride, -1)
    if extra_row is not None:
        is_extra = (jnp.arange(stride, dtype=jnp.int32) == stride - 1)[None, :, None]
        rows = jnp.where(is_extra, extra_row[None, None, :], rows)
    got = exchange(rows.reshape(count * stride, -1))
    return (matmul_left_t(chosen, got).astype(jnp.bfloat16), got.reshape(count, stride, -1)[:, stride - 1])


def lookup(embedding, ids, message, chosen, extra_row, stride, room):
    own_rows = embedding.shape[0]
    pick, rounds = hear_round(message, own_rows, stride)
    first, extra = answer(embedding, chosen, pick, stride, extra_row)

    def more(carry):
        index, rows = carry
        again, its_pick = plan_round(ids, index, own_rows, stride, room)
        return (index + 1, rows + answer(embedding, again, its_pick, stride, None)[0])

    _, rows = lax.while_loop(lambda carry: carry[0] < rounds, more, (jnp.int32(1), first))
    return (rows, extra, ids, chosen, pick, rounds)


def send_grads(grad_low, chosen, pick, stride, extra_rows):
    count = lax.axis_size("dev")
    summed = matmul(chosen, grad_low).astype(jnp.bfloat16).reshape(count, stride, -1)
    if extra_rows is not None:
        place = jnp.arange(stride, dtype=jnp.int32)[None, :, None]
        high, low = extra_rows
        summed = jnp.where(place == stride - 2, high[:, None, :], summed)
        summed = jnp.where(place == stride - 1, low[:, None, :], summed)
    got = exchange(summed.reshape(count * stride, -1))
    return (matmul_left_t(pick, got), got.reshape(count, stride, -1)[:, stride - 2 :])


def table_back(grad_rows, extra_rows, plan, own_rows, stride, room):
    ids, chosen, pick, rounds = plan
    grad_low = grad_rows.astype(jnp.bfloat16)
    first, extra = send_grads(grad_low, chosen, pick, stride, extra_rows)

    def more(carry):
        index, total = carry
        again, its_pick = plan_round(ids, index, own_rows, stride, room)
        return (index + 1, total + send_grads(grad_low, again, its_pick, stride, None)[0])

    _, total = lax.while_loop(lambda carry: carry[0] < rounds, more, (jnp.int32(1), first))
    return (total, jnp.sum(extra.astype(jnp.float32), axis=(0, 1)))


def gather_parts(pieces):
    count = lax.axis_size("dev")
    sizes = [piece.shape[0] for piece in pieces]
    whole = lax.all_gather(jnp.concatenate(pieces, axis=0), "dev", axis=0)
    parts, start = ([], 0)
    for size in sizes:
        parts.append(whole[:, start : start + size].reshape(count * size, -1))
        start += size
    return parts


def stack_parts(parts):
    count = lax.axis_size("dev")
    shaped = [part.astype(jnp.bfloat16).reshape(count, part.shape[0] // count, -1) for part in parts]
    return jnp.concatenate(shaped, axis=1)


def split_rows(summed, sizes):
    pieces, start = ([], 0)
    for size in sizes:
        pieces.append(summed[start : start + size].astype(jnp.float32))
        start += size
    return pieces


def swap_halves(held, bit, last):
    count = lax.axis_size("dev")
    mine = (lax.axis_index("dev") >> bit) & 1
    keep = lax.dynamic_index_in_dim(held, mine, 0, keepdims=False)
    give = lax.dynamic_index_in_dim(held, 1 - mine, 0, keepdims=False)
    came = lax.ppermute(give, "dev", [(source, source ^ (1 << bit)) for source in range(count)])
    total = keep.astype(jnp.float32) + came.astype(jnp.float32)
    return total if last else total.astype(jnp.bfloat16)


def cube_begin(stacked):
    count, rows, width = stacked.shape
    bits = count.bit_length() - 1
    middle = list(range(1, bits - 1))
    grid = stacked.reshape((2,) * bits + (rows, width))
    held = swap_halves(jnp.moveaxis(grid, bits - 1, 0), 0, False)
    lanes = width // 3
    thirds = []
    for turn in range(3):
        order = middle[turn:] + middle[:turn] + [bits - 1]
        axes = [bits - 1 - bit for bit in order]
        third = held[..., turn * lanes : (turn + 1) * lanes].transpose(axes + [bits - 1, bits])
        thirds.append(swap_halves(third, order[0], False))
    return thirds


def cube_end(thirds):
    bits = lax.axis_size("dev").bit_length() - 1
    middle = list(range(1, bits - 1))
    for stage in range(1, len(middle)):
        thirds = [swap_halves(third, middle[(turn + stage) % len(middle)], False) for turn, third in enumerate(thirds)]
    return swap_halves(jnp.concatenate(thirds, axis=-1), bits - 1, True)


def split_low(values):
    high = lax.reduce_precision(values, 8, 7)
    return (high.astype(jnp.bfloat16), (values - high).astype(jnp.bfloat16))


def low_units(blocks):
    per_row = blocks.shape[1]
    place = 8 + jnp.arange(per_row, dtype=jnp.int32)[None, :]
    return jnp.min(place - 2 * ((blocks + 1) // 2), axis=1).astype(jnp.int32)


def by_unit(array):
    cut = array.reshape((array.shape[0], array.shape[1] // UNIT, UNIT) + array.shape[2:])
    return cut.swapaxes(0, 1)


def by_row(array, micros):
    cut = array.reshape(-1, micros, UNIT, array.shape[-1])
    return cut.swapaxes(0, 1).reshape(micros, -1, array.shape[-1])


def shards(
    token_ids,
    lengths,
    embedding,
    norm1_gain,
    w_query,
    w_key,
    w_value,
    w_out,
    mix_logits,
    mix_weights,
    norm2_gain,
    w_up,
    w_down,
    cotangent,
):
    count = lax.axis_size("dev")
    me = lax.axis_index("dev")
    micros, row_count = token_ids.shape
    own_rows, width = embedding.shape
    heads = mix_logits.shape[0]
    part = norm1_gain.shape[0]
    per_row = row_count // UNIT
    tokens = micros * row_count
    tok_ids = by_unit(token_ids).reshape(-1)
    stride = max(16, 1024 // count)
    room = stride - 2

    unit_rows = me * row_count + UNIT * jnp.arange(per_row, dtype=jnp.int32)
    begins = jnp.stack([seq_starts(lengths[micro], unit_rows) for micro in range(micros)])
    blocks = ((unit_rows[None, :] - begins) // UNIT + 1).reshape(-1).astype(jnp.int32)

    lows = low_units(blocks.reshape(micros, per_row))
    mixes = spread_mixes(mix_logits, mix_weights)

    up_cols = w_up.shape[1] // width
    up_pieces = [w_up[:, col * width : (col + 1) * width] for col in range(up_cols)]
    weight_pieces = [w_query, w_key, w_value, w_out] + up_pieces + [w_down]
    ids = split_ids(tok_ids, own_rows)
    message, chosen = ask_round(ids, 0, own_rows, stride, room)
    message, weight_pieces = lax.optimization_barrier((message, weight_pieces))
    gathered = gather_parts(weight_pieces)
    w_q, w_k, w_v, w_o = gathered[:4]
    w_u, w_d = (jnp.concatenate(gathered[4:-1], axis=1), gathered[-1])
    gains_row = jnp.concatenate([norm1_gain, norm2_gain, jnp.zeros((width - 2 * part,), jnp.bfloat16)])
    picked, gains, *plan = lookup(embedding, ids, message, chosen, gains_row, stride, room)
    gain_one = gains[:, :part].reshape(-1)
    gain_two = gains[:, part : 2 * part].reshape(-1)
    inputs = picked.astype(jnp.float32)

    normed_one, inv_one, hidden_one = normalize(inputs, gain_one)
    own_hidden = hidden_one.reshape(per_row, micros, UNIT, width)
    pieces = earlier_rows(own_hidden)
    query, key, value = project(lows, pieces, (w_q, w_k, w_v))
    attended, *kept = attention_fwd(blocks, query, key, value, mixes, heads)
    attended = attended.reshape(tokens, width)

    middle = inputs + matmul(attended, w_o)
    normed_two, inv_two, hidden_two = normalize(middle, gain_two)
    up_proj = matmul(hidden_two, w_u)
    activated, gelu_pull = jax.vjp(jax.nn.gelu, up_proj)
    activated = activated.astype(jnp.bfloat16)
    output = (middle + matmul(activated, w_d)).astype(jnp.bfloat16)

    grad_rows = by_unit(cotangent).reshape(tokens, width)
    grad_act = matmul_right_t(grad_rows, w_d)
    grad_upb = gelu_pull(grad_act)[0].astype(jnp.bfloat16)
    grad_down = matmul_left_t(activated, grad_rows)
    grad_up = matmul_left_t(hidden_two, grad_upb)
    grad_hidden_two = matmul_right_t(grad_upb, w_u)
    grad_mid_norm, grad_gain_two = norm_back(grad_hidden_two, normed_two, inv_two, gain_two)
    grad_middle = grad_rows.astype(jnp.float32) + grad_mid_norm
    grad_branch = grad_middle.astype(jnp.bfloat16)
    grad_wout = matmul_left_t(attended, grad_branch)
    grad_att = matmul_right_t(grad_branch, w_o).astype(jnp.bfloat16).reshape(own_hidden.shape)
    up_terms = [grad_up[:, col * width : (col + 1) * width] for col in range(up_cols)]
    late_terms = [grad_wout] + up_terms + [grad_down]
    late_stack, grad_att = lax.optimization_barrier((stack_parts(late_terms), grad_att))
    late_sums = lax.psum_scatter(
        late_stack.reshape(count * late_stack.shape[1], width), "dev", scatter_dimension=0, tiled=True
    )

    def tail(pieces, hidden_one, query, key, value, grad_att, kept):
        grad_query, grad_key, grad_value, wide_logit, wide_prob = attention_bwd(
            blocks, query, key, value, grad_att, kept, mixes, heads
        )
        *terms, grad_own = project_back(lows, grad_query, grad_key, grad_value, (w_q, w_k, w_v))
        came = with_sibling(jnp.concatenate([terms[3], terms[1]], axis=0))
        came, grad_query, grad_key, grad_value, pieces, hidden_one = lax.optimization_barrier(
            (came, grad_query, grad_key, grad_value, pieces, hidden_one)
        )
        grad_own = return_rows(terms[0], terms[2], came, grad_own)
        grad_query = grad_query.reshape(tokens, width)
        grad_key = grad_key.reshape(-1, width)
        grad_value = grad_value.reshape(-1, width)
        flat_hidden = jnp.concatenate(pieces, axis=0).reshape(-1, width)
        grad_wq = matmul_left_t(hidden_one, grad_query)
        grad_wk = matmul_left_t(flat_hidden, grad_key)
        grad_wv = matmul_left_t(flat_hidden, grad_value)
        early_terms = [grad_wq, grad_wk, grad_wv]
        thirds = cube_begin(stack_parts(early_terms))
        grad_hidden_one = grad_own.reshape(tokens, width)
        grad_in_norm, grad_gain_one = norm_back(grad_hidden_one, normed_one, inv_one, gain_one)
        grad_inputs = grad_middle + grad_in_norm

        mix_terms = jnp.concatenate([fold_mix(wide_logit, heads).reshape(-1), fold_mix(wide_prob, heads).reshape(-1)])
        mix_size = mix_terms.shape[0]
        small = jnp.concatenate(
            [
                grad_gain_one.reshape(count, part),
                grad_gain_two.reshape(count, part),
                jnp.broadcast_to(mix_terms[None, :], (count, mix_size)),
                jnp.zeros((count, width - 2 * part - mix_size), jnp.float32),
            ],
            axis=1,
        )
        grad_inputs, thirds = lax.optimization_barrier((grad_inputs, thirds))
        table_grad, small_sum = table_back(grad_inputs, split_low(small), plan, own_rows, stride, room)
        early_sums = cube_end(thirds)
        return (grad_inputs, table_grad, small_sum, early_sums)

    def no_tail(*operands):
        wide_zeros = jnp.zeros((tokens, width), jnp.float32)
        table_zeros = jnp.zeros((own_rows, width), jnp.float32)
        early_zeros = jnp.zeros((3 * w_query.shape[0], width), jnp.float32)
        return (wide_zeros, table_zeros, jnp.zeros((width,), jnp.float32), early_zeros)

    grad_inputs, table_grad, small_sum, early_sums = lax.cond(
        plan[-1] > 0, tail, no_tail, pieces, hidden_one, query, key, value, grad_att, kept
    )
    early_sums = split_rows(early_sums, [w_query.shape[0]] * 3)
    late_sums = split_rows(late_sums, [term.shape[0] // count for term in late_terms])
    mix_size = 2 * heads * heads
    mixes = small_sum[2 * part : 2 * part + mix_size].reshape(2, heads, heads)
    return (
        by_row(output, micros),
        by_row(grad_inputs, micros),
        table_grad,
        small_sum[:part],
        early_sums[0],
        early_sums[1],
        early_sums[2],
        late_sums[0],
        mixes[0],
        mixes[1],
        small_sum[part : 2 * part],
        jnp.concatenate(late_sums[1:-1], axis=1),
        late_sums[-1],
    )


def solution(mesh):
    in_specs = (
        P(None, "dev"),
        P(),
        P("dev", None),
        P("dev"),
        P("dev", None),
        P("dev", None),
        P("dev", None),
        P("dev", None),
        P(),
        P(),
        P("dev"),
        P("dev", None),
        P("dev", None),
        P(None, "dev", None),
    )
    out_specs = (
        P(None, "dev", None),
        P(None, "dev", None),
        P("dev", None),
        P("dev"),
        P("dev", None),
        P("dev", None),
        P("dev", None),
        P("dev", None),
        P(),
        P(),
        P("dev"),
        P("dev", None),
        P("dev", None),
    )
    return jax.shard_map(shards, mesh=mesh, in_specs=in_specs, out_specs=out_specs, check_vma=False)
```

```python
from functools import partial

import jax
import jax.numpy as jnp
from jax import lax
from jax.experimental import pallas as pl
from jax.experimental.pallas import tpu as pltpu
from jax.sharding import PartitionSpec as P

norm_eps = 1e-06

masked = -1e30
UNIT = 128
CHUNK = 256
GROUP = 16
MAX_CHUNKS = 4


def dot_nn(left, right):
    return lax.dot_general(left, right, (((1,), (0,)), ((), ())), preferred_element_type=jnp.float32)


def dot_nt(left, right):
    return lax.dot_general(left, right, (((1,), (1,)), ((), ())), preferred_element_type=jnp.float32)


def spread_heads(rows, lane_head, quad, heads_per_quad):
    part = rows[:, quad * CHUNK : (quad + 1) * CHUNK]
    zero = jnp.zeros_like(part)
    return jnp.concatenate([jnp.where(lane_head == head, part, zero) for head in range(heads_per_quad)], axis=0)


def own_lanes(wide, lane_head, heads_per_quad):
    total = jnp.where(lane_head == 0, wide[:UNIT], 0.0)
    for head in range(1, heads_per_quad):
        total = total + jnp.where(lane_head == head, wide[head * UNIT : (head + 1) * UNIT], 0.0)
    return total


def allowed_keys(chunk, group, blocks):
    key = lax.broadcasted_iota(jnp.int32, (GROUP, CHUNK), 1) - (UNIT + CHUNK * chunk)
    row = lax.broadcasted_iota(jnp.int32, (GROUP, CHUNK), 0) + GROUP * group
    return (key <= row) & (key >= (1 - blocks) * UNIT)


def twice(rows):
    return jnp.concatenate([rows, rows], axis=-1)


def put_groups(ref, quad, per_quad, term):
    low = term.astype(jnp.bfloat16)
    for head in range(per_quad):
        rows = slice((quad * per_quad + head) * GROUP, (quad * per_quad + head + 1) * GROUP)
        for group in range(UNIT // GROUP):
            start = head * UNIT + group * GROUP
            ref[rows, group * CHUNK : (group + 1) * CHUNK] = low[start : start + GROUP]


def fwd_kernel(heads, blocks_ref, q_ref, k_ref, v_ref, mix_ref, att_ref, score_out, prob_out, mixed_out,
               qx, score, prob, mixed, logit, top, norm, total, sems):
    micro, inner, per_row = (pl.program_id(0), pl.program_id(1), pl.num_programs(1))
    blocks = blocks_ref[micro * per_row + inner]
    chunks = (blocks + 1) // 2
    last_unit = k_ref.shape[0] - per_row + inner + 1
    quads = q_ref.shape[3] // CHUNK
    per_quad = heads // quads
    groups = UNIT // GROUP
    wide = heads * GROUP
    lane_head = lax.broadcasted_iota(jnp.int32, (UNIT, CHUNK), 1) // (CHUNK // per_quad)
    for quad in range(quads):
        qx[quad] = spread_heads(q_ref[0, 0], lane_head, quad, per_quad)
    total[...] = jnp.zeros_like(total)
    top[...] = jnp.full_like(top, masked)
    norm[...] = jnp.zeros_like(norm)

    def keys(ref, chunk, quad):
        units = pl.ds(last_unit - 2 * (chunk + 1), 2)
        return ref[units, 0, :, quad * CHUNK : (quad + 1) * CHUNK].reshape(CHUNK, CHUNK)

    def keep(chunk, kind):
        source, target = ((score, score_out), (prob, prob_out), (mixed, mixed_out))[kind]
        return pltpu.make_async_copy(source.at[chunk], target.at[inner, micro, chunk], sems.at[kind, chunk])

    @pl.loop(0, chunks)
    def _(chunk):
        for quad in range(quads):
            put_groups(score.at[chunk], quad, per_quad, dot_nt(qx[quad], keys(k_ref, chunk, quad)))
        keep(chunk, 0).start()
        for group in range(groups):
            l = dot_nn(mix_ref[0], score[chunk, :, group * CHUNK : (group + 1) * CHUNK])
            l = jnp.where(allowed_keys(chunk, group, blocks)[None], l.reshape(heads, GROUP, CHUNK), masked)
            l = l.reshape(wide, CHUNK)
            logit[chunk, group] = l
            old = top[group]
            new = jnp.maximum(old, jnp.maximum(l[:, :UNIT], l[:, UNIT:]))
            terms = jnp.exp(l[:, :UNIT] - new) + jnp.exp(l[:, UNIT:] - new)
            norm[group] = norm[group] * jnp.exp(old - new) + terms
            top[group] = new

    for group in range(groups):
        lanes = top[group]
        high = jnp.broadcast_to(jnp.max(lanes, axis=-1, keepdims=True), lanes.shape)
        whole = jnp.sum(norm[group] * jnp.exp(lanes - high), axis=-1, keepdims=True)
        top[group] = high + jnp.log(jnp.broadcast_to(whole, lanes.shape))

    @pl.loop(0, chunks)
    def _(chunk):
        for group in range(groups):
            p = jnp.exp(logit[chunk, group] - twice(top[group])).astype(jnp.bfloat16)
            prob[chunk, :, group * CHUNK : (group + 1) * CHUNK] = p
            a = dot_nn(mix_ref[2], p).astype(jnp.bfloat16)
            mixed[chunk, :, GROUP * group : GROUP * (group + 1), :] = a.reshape(heads, GROUP, CHUNK)
        keep(chunk, 1).start()
        keep(chunk, 2).start()
        for quad in range(quads):
            a = mixed[chunk, quad * per_quad : (quad + 1) * per_quad].reshape(per_quad * UNIT, CHUNK)
            o = own_lanes(dot_nn(a, keys(v_ref, chunk, quad)), lane_head, per_quad)
            total[:, quad * CHUNK : (quad + 1) * CHUNK] += o

    att_ref[0, 0] = total[...].astype(jnp.bfloat16)

    @pl.loop(0, chunks)
    def _(chunk):
        for kind in range(3):
            keep(chunk, kind).wait()


def attention_specs(q, k, heads):
    per_row, micros, _, width = q.shape
    wide = heads * GROUP
    return (
        pl.BlockSpec((1, 1, UNIT, width), lambda m, u, _: (u, m, 0, 0)),
        pl.BlockSpec((k.shape[0], 1, UNIT, width), lambda m, u, _: (0, m, 0, 0)),
        pl.BlockSpec((4, wide, wide), lambda m, u, _: (0, 0, 0)),
    )


def kept_shapes(heads):
    wide = heads * GROUP
    flat = (MAX_CHUNKS, wide, UNIT // GROUP * CHUNK)
    return (flat, flat, (MAX_CHUNKS, heads, UNIT, CHUNK))


def attention_fwd(blocks, q, k, v, mixes, heads):
    per_row, micros, _, width = q.shape
    wide = heads * GROUP
    groups = UNIT // GROUP
    quads = width // CHUNK
    unit_spec, kv_spec, mix_spec = attention_specs(q, k, heads)
    kept = kept_shapes(heads)
    anywhere = pl.BlockSpec(memory_space=pl.ANY)
    return pl.pallas_call(
        partial(fwd_kernel, heads),
        grid_spec=pltpu.PrefetchScalarGridSpec(
            num_scalar_prefetch=1,
            grid=(micros, per_row),
            in_specs=[unit_spec, kv_spec, kv_spec, mix_spec],
            out_specs=[unit_spec, anywhere, anywhere, anywhere],
            scratch_shapes=[pltpu.VMEM((quads, heads // quads * UNIT, CHUNK), jnp.bfloat16)]
            + [pltpu.VMEM(shape, jnp.bfloat16) for shape in kept]
            + [
                pltpu.VMEM((MAX_CHUNKS, groups, wide, CHUNK), jnp.float32),
                pltpu.VMEM((groups, wide, UNIT), jnp.float32),
                pltpu.VMEM((groups, wide, UNIT), jnp.float32),
                pltpu.VMEM((UNIT, width), jnp.float32),
                pltpu.SemaphoreType.DMA((3, MAX_CHUNKS)),
            ],
        ),
        out_shape=[jax.ShapeDtypeStruct(q.shape, jnp.bfloat16)]
        + [jax.ShapeDtypeStruct((per_row, micros) + shape, jnp.bfloat16) for shape in kept],
        compiler_params=pltpu.CompilerParams(vmem_limit_bytes=50 * 1024 * 1024),
        cost_estimate=pl.CostEstimate(flops=20_000_000_000, bytes_accessed=30_000_000, transcendentals=0),
        name="attention_fwd",
    )(blocks, q, k, v, mixes)


def bwd_kernel(heads, blocks_ref, q_ref, k_ref, v_ref, do_ref, mix_ref, score_in, prob_in, mixed_in,
               dq_ref, dk_ref, dv_ref, gl_ref, gp_ref,
               qxt, dox, doxt, score, prob, mixed, grad_prob, grad_mixed, grad_logit, grad_score,
               delta, dq_total, dk_total, dv_total, sems):
    micro, inner, per_row = (pl.program_id(0), pl.program_id(1), pl.num_programs(1))
    step = micro * per_row + inner
    slot = step % 2
    blocks = blocks_ref[step]
    chunks = (blocks + 1) // 2
    key_units = k_ref.shape[0]
    last_unit = key_units - per_row + inner + 1
    quads = q_ref.shape[3] // CHUNK
    per_quad = heads // quads
    groups = UNIT // GROUP
    wide = heads * GROUP
    lane_head = lax.broadcasted_iota(jnp.int32, (UNIT, CHUNK), 1) // (CHUNK // per_quad)
    row_head = lax.broadcasted_iota(jnp.int32, (CHUNK, UNIT), 0) // (CHUNK // per_quad)
    lowest = key_units
    for other in range(key_units - 7):
        its_chunks = (blocks_ref[micro * per_row + other] + 1) // 2
        lowest = jnp.minimum(lowest, key_units - per_row + other + 1 - 2 * its_chunks)

    def fetch(at, chunk, kind):
        source, target = ((score_in, score), (prob_in, prob), (mixed_in, mixed))[kind]
        place = source.at[at % per_row, at // per_row, chunk]
        return pltpu.make_async_copy(place, target.at[at % 2, chunk], sems.at[kind, at % 2, chunk])

    def fetch_all(at):
        @pl.loop(0, (blocks_ref[at] + 1) // 2)
        def _(chunk):
            for kind in (1, 2, 0):
                fetch(at, chunk, kind).start()

    @pl.when(step == 0)
    def _():
        fetch_all(0)
        gl_ref[...] = jnp.zeros_like(gl_ref)
        gp_ref[...] = jnp.zeros_like(gp_ref)

    @pl.when(step + 1 < pl.num_programs(0) * per_row)
    def _():
        fetch_all(step + 1)

    @pl.when(inner == 0)
    def _():
        @pl.loop(lowest, key_units)
        def _(key_unit):
            dk_total[key_unit] = jnp.zeros_like(dk_total[key_unit])
            dv_total[key_unit] = jnp.zeros_like(dv_total[key_unit])

    def spread_turned(rows, quad):
        turned = rows[:, quad * CHUNK : (quad + 1) * CHUNK].T
        zero = jnp.zeros_like(turned)
        return jnp.concatenate([jnp.where(row_head == head, turned, zero) for head in range(per_quad)], axis=1)

    for quad in range(quads):
        qxt[quad] = spread_turned(q_ref[0, 0], quad)
        dox[quad] = spread_heads(do_ref[0, 0], lane_head, quad, per_quad)
        doxt[quad] = spread_turned(do_ref[0, 0], quad)
    dq_total[...] = jnp.zeros_like(dq_total)
    delta[...] = jnp.zeros_like(delta)

    def keys(ref, chunk, quad):
        units = pl.ds(last_unit - 2 * (chunk + 1), 2)
        return ref[units, 0, :, quad * CHUNK : (quad + 1) * CHUNK].reshape(CHUNK, CHUNK)

    def add_to(total, chunk, quad, term):
        first = last_unit - 2 * (chunk + 1)
        lanes = slice(quad * CHUNK, (quad + 1) * CHUNK)
        total[first, lanes, :] += term[:, :UNIT]
        total[first + 1, lanes, :] += term[:, UNIT:]

    @pl.loop(0, chunks)
    def _(chunk):
        for quad in range(quads):
            put_groups(grad_mixed, quad, per_quad, dot_nt(dox[quad], keys(v_ref, chunk, quad)))
        fetch(step, chunk, 1).wait()
        for group in range(groups):
            cols = slice(group * CHUNK, (group + 1) * CHUNK)
            dp = dot_nn(mix_ref[3], grad_mixed[:, cols])
            grad_prob[chunk, :, cols] = dp.astype(grad_prob.dtype)
            term = prob[slot, chunk, :, cols].astype(jnp.float32) * dp
            delta[group] += term[:, :UNIT] + term[:, UNIT:]
        gp_ref[...] += dot_nt(prob[slot, chunk], grad_mixed[...])
        fetch(step, chunk, 2).wait()
        for quad in range(quads):
            a = mixed[slot, chunk, quad * per_quad : (quad + 1) * per_quad].reshape(per_quad * UNIT, CHUNK)
            add_to(dv_total, chunk, quad, dot_nn(doxt[quad], a))

    for group in range(groups):
        delta[group] = jnp.broadcast_to(jnp.sum(delta[group], axis=-1, keepdims=True), (wide, UNIT))

    @pl.loop(0, chunks)
    def _(chunk):
        for group in range(groups):
            cols = slice(group * CHUNK, (group + 1) * CHUNK)
            dp = grad_prob[chunk, :, cols].astype(jnp.float32) - twice(delta[group])
            dl = (prob[slot, chunk, :, cols].astype(jnp.float32) * dp).astype(jnp.bfloat16)
            grad_logit[:, cols] = dl
            ds = dot_nn(mix_ref[1], dl).astype(jnp.bfloat16)
            grad_score[:, GROUP * group : GROUP * (group + 1), :] = ds.reshape(heads, GROUP, CHUNK)
        fetch(step, chunk, 0).wait()
        gl_ref[...] += dot_nt(score[slot, chunk], grad_logit[...])
        for quad in range(quads):
            ds = grad_score[quad * per_quad : (quad + 1) * per_quad].reshape(per_quad * UNIT, CHUNK)
            dq = own_lanes(dot_nn(ds, keys(k_ref, chunk, quad)), lane_head, per_quad)
            dq_total[:, quad * CHUNK : (quad + 1) * CHUNK] += dq
            add_to(dk_total, chunk, quad, dot_nn(qxt[quad], ds))

    dq_ref[0, 0] = (dq_total[...] * 0.125).astype(jnp.bfloat16)

    @pl.when(inner == per_row - 1)
    def _():
        @pl.loop(0, lowest)
        def _(key_unit):
            dk_ref[key_unit, 0] = jnp.zeros_like(dk_ref[key_unit, 0])
            dv_ref[key_unit, 0] = jnp.zeros_like(dv_ref[key_unit, 0])

        @pl.loop(lowest, key_units)
        def _(key_unit):
            dk_ref[key_unit, 0] = dk_total[key_unit].astype(jnp.bfloat16).T
            dv_ref[key_unit, 0] = dv_total[key_unit].astype(jnp.bfloat16).T


def attention_bwd(blocks, q, k, v, grad_out, kept, mixes, heads):
    per_row, micros, _, width = q.shape
    key_units = k.shape[0]
    wide = heads * GROUP
    groups = UNIT // GROUP
    quads = width // CHUNK
    turned = (quads, CHUNK, heads // quads * UNIT)
    unit_spec, kv_spec, mix_spec = attention_specs(q, k, heads)
    sum_spec = pl.BlockSpec((wide, wide), lambda m, u, _: (0, 0))
    anywhere = pl.BlockSpec(memory_space=pl.ANY)
    return pl.pallas_call(
        partial(bwd_kernel, heads),
        grid_spec=pltpu.PrefetchScalarGridSpec(
            num_scalar_prefetch=1,
            grid=(micros, per_row),
            in_specs=[unit_spec, kv_spec, kv_spec, unit_spec, mix_spec] + [anywhere] * 3,
            out_specs=[unit_spec, kv_spec, kv_spec, sum_spec, sum_spec],
            scratch_shapes=[
                pltpu.VMEM(turned, jnp.bfloat16),
                pltpu.VMEM((quads, heads // quads * UNIT, CHUNK), jnp.bfloat16),
                pltpu.VMEM(turned, jnp.bfloat16),
            ]
            + [pltpu.VMEM((2,) + shape, jnp.bfloat16) for shape in kept_shapes(heads)]
            + [
                pltpu.VMEM((MAX_CHUNKS, wide, groups * CHUNK), jnp.bfloat16),
                pltpu.VMEM((wide, groups * CHUNK), jnp.bfloat16),
                pltpu.VMEM((wide, groups * CHUNK), jnp.bfloat16),
                pltpu.VMEM((heads, UNIT, CHUNK), jnp.bfloat16),
                pltpu.VMEM((groups, wide, UNIT), jnp.float32),
                pltpu.VMEM((UNIT, width), jnp.float32),
                pltpu.VMEM((key_units, width, UNIT), jnp.float32),
                pltpu.VMEM((key_units, width, UNIT), jnp.float32),
                pltpu.SemaphoreType.DMA((3, 2, MAX_CHUNKS)),
            ],
        ),
        out_shape=[
            jax.ShapeDtypeStruct(q.shape, jnp.bfloat16),
            jax.ShapeDtypeStruct(k.shape, jnp.bfloat16),
            jax.ShapeDtypeStruct(v.shape, jnp.bfloat16),
            jax.ShapeDtypeStruct((wide, wide), jnp.float32),
            jax.ShapeDtypeStruct((wide, wide), jnp.float32),
        ],
        compiler_params=pltpu.CompilerParams(vmem_limit_bytes=58 * 1024 * 1024),
        cost_estimate=pl.CostEstimate(flops=45_000_000_000, bytes_accessed=40_000_000, transcendentals=0),
        name="attention_bwd",
    )(blocks, q, k, v, grad_out, mixes, *kept)


def piece_bases(key_units, per_row):
    sizes = [1] + [per_row] * ((key_units - 1) // per_row)
    return [(sum(sizes[:at]), size) for at, size in enumerate(sizes)]


def project_kernel(low_ref, *refs):
    pieces, (w_q, w_k, w_v, q_ref, k_ref, v_ref) = (refs[:-6], refs[-6:])
    key_units, width = (k_ref.shape[0], k_ref.shape[3])
    per_row = q_ref.shape[0]
    low = low_ref[pl.program_id(0)]

    for piece, (base, size) in zip(pieces, piece_bases(key_units, per_row)):
        @pl.when(base + size > low)
        def _():
            rows = piece[:, 0].reshape(size * UNIT, width)
            k_ref[base : base + size, 0] = dot_nn(rows, w_k[...]).astype(jnp.bfloat16).reshape(size, UNIT, width)
            v_ref[base : base + size, 0] = dot_nn(rows, w_v[...]).astype(jnp.bfloat16).reshape(size, UNIT, width)

    rows = pieces[-1][:, 0].reshape(per_row * UNIT, width)
    query = dot_nn(rows, w_q[...]).astype(jnp.bfloat16) * jnp.bfloat16(0.125)
    q_ref[:, 0] = query.reshape(per_row, UNIT, width)


def project(low, pieces, weights):
    micros, width = pieces[0].shape[1], pieces[0].shape[3]
    key_units = sum(piece.shape[0] for piece in pieces)
    per_row = pieces[-1].shape[0]

    def spec(units):
        return pl.BlockSpec((units, 1, UNIT, width), lambda m, _: (0, m, 0, 0))

    weight_spec = pl.BlockSpec((width, width), lambda m, _: (0, 0))
    shapes = [(units, micros, UNIT, width) for units in (per_row, key_units, key_units)]
    return pl.pallas_call(
        project_kernel,
        grid_spec=pltpu.PrefetchScalarGridSpec(
            num_scalar_prefetch=1,
            grid=(micros,),
            in_specs=[spec(piece.shape[0]) for piece in pieces] + [weight_spec] * 3,
            out_specs=[spec(shape[0]) for shape in shapes],
        ),
        out_shape=[jax.ShapeDtypeStruct(shape, jnp.bfloat16) for shape in shapes],
        compiler_params=pltpu.CompilerParams(vmem_limit_bytes=44 * 1024 * 1024),
        cost_estimate=pl.CostEstimate(flops=6_000_000_000, bytes_accessed=15_000_000, transcendentals=0),
        name="project",
    )(low, *pieces, *weights)


def project_back_kernel(low_ref, dq_ref, dk_ref, dv_ref, w_q, w_k, w_v, *outs):
    key_units, width = (dk_ref.shape[0], dk_ref.shape[3])
    per_row = dq_ref.shape[0]
    low = low_ref[pl.program_id(0)]
    bases = piece_bases(key_units, per_row)

    def from_keys(base, size):
        rows = slice(base, base + size)
        key_term = dot_nt(dk_ref[rows, 0].reshape(size * UNIT, width), w_k[...])
        return key_term + dot_nt(dv_ref[rows, 0].reshape(size * UNIT, width), w_v[...])

    for out, (base, size) in zip(outs[:-1], bases[:-1]):
        @pl.when(base + size > low)
        def _():
            out[:, 0] = from_keys(base, size).astype(jnp.bfloat16).reshape(size, UNIT, width)

        @pl.when(base + size <= low)
        def _():
            out[...] = jnp.zeros_like(out)

    own = from_keys(*bases[-1]) + dot_nt(dq_ref[:, 0].reshape(per_row * UNIT, width), w_q[...])
    outs[-1][:, 0] = own.reshape(per_row, UNIT, width)


def project_back(low, grad_query, grad_key, grad_value, weights):
    per_row, micros, _, width = grad_query.shape
    key_units = grad_key.shape[0]

    def spec(units):
        return pl.BlockSpec((units, 1, UNIT, width), lambda m, _: (0, m, 0, 0))

    weight_spec = pl.BlockSpec((width, width), lambda m, _: (0, 0))
    sizes = [size for _, size in piece_bases(key_units, per_row)]
    shapes = [(size, micros, UNIT, width) for size in sizes]
    kinds = [jnp.bfloat16] * (len(sizes) - 1) + [jnp.float32]
    return pl.pallas_call(
        project_back_kernel,
        grid_spec=pltpu.PrefetchScalarGridSpec(
            num_scalar_prefetch=1,
            grid=(micros,),
            in_specs=[spec(per_row), spec(key_units), spec(key_units)] + [weight_spec] * 3,
            out_specs=[spec(size) for size in sizes],
        ),
        out_shape=[jax.ShapeDtypeStruct(shape, kind) for shape, kind in zip(shapes, kinds)],
        compiler_params=pltpu.CompilerParams(vmem_limit_bytes=44 * 1024 * 1024),
        cost_estimate=pl.CostEstimate(flops=6_000_000_000, bytes_accessed=15_000_000, transcendentals=0),
        name="project_back",
    )(low, grad_query, grad_key, grad_value, *weights)


def spread_mixes(mix_logits, mix_weights):
    heads = mix_logits.shape[0]
    wide = heads * GROUP
    place = jnp.arange(wide, dtype=jnp.int32)
    pick = (place[:, None] // GROUP == jnp.arange(heads, dtype=jnp.int32)[None, :]).astype(mix_logits.dtype)
    same_row = (place[:, None] % GROUP == place[None, :] % GROUP)[None]
    tables = jnp.stack([mix_logits.T, mix_logits, mix_weights.T, mix_weights]).reshape(4 * heads, heads)
    across = jnp.dot(tables, pick.T, preferred_element_type=jnp.float32).astype(mix_logits.dtype)
    down = jnp.einsum("wh,bhx->bwx", pick, across.reshape(4, heads, wide), preferred_element_type=jnp.float32)
    return jnp.where(same_row, down, 0.0).astype(mix_logits.dtype)


def fold_mix(wide, heads):
    place = jnp.arange(heads * GROUP, dtype=jnp.int32)
    pick = (place[:, None] // GROUP == jnp.arange(heads, dtype=jnp.int32)[None, :]).astype(jnp.float32)
    same_row = place[:, None] % GROUP == place[None, :] % GROUP
    down = jnp.dot(pick.T, jnp.where(same_row, wide, 0.0), precision=lax.Precision.HIGHEST)
    return jnp.dot(down, pick, precision=lax.Precision.HIGHEST)


def from_behind(value, steps):
    count = lax.axis_size("dev")
    first, last = (max(0, -steps), min(count, count - steps))
    return lax.ppermute(value, "dev", [(source, source + steps) for source in range(first, last)])


def with_sibling(value):
    count = lax.axis_size("dev")
    return lax.ppermute(value, "dev", [(source, source ^ 1) for source in range(count)])


def earlier_rows(own):
    size = own.shape[0]
    first_core = lax.axis_index("dev") % 2 == 0
    two, four = (from_behind(own, 2), from_behind(own, 4))
    give = jnp.concatenate([jnp.where(first_core, own, two), jnp.where(first_core, two, four)], axis=0)
    came = with_sibling(give)
    return [four[size - 1 :], came[size:], two, came[:size], own]


def return_rows(four, two, came, grad_own):
    size = two.shape[0]
    first_core = lax.axis_index("dev") % 2 == 0
    came = came.astype(jnp.float32)
    one, three = (came[:size], came[size:])
    give_two = two.astype(jnp.float32) + jnp.where(first_core, three, one)
    padded = jnp.pad(four.astype(jnp.float32), ((size - four.shape[0], 0), (0, 0), (0, 0), (0, 0)))
    give_four = padded + jnp.where(first_core, 0.0, three)
    back_two = from_behind(give_two.astype(jnp.bfloat16), -2).astype(jnp.float32)
    back_four = from_behind(give_four.astype(jnp.bfloat16), -4).astype(jnp.float32)
    return grad_own + jnp.where(first_core, one, 0.0) + back_two + back_four


def seq_starts(lengths_row, query_rows):
    seq_ends = jnp.cumsum(lengths_row)
    starts = seq_ends - lengths_row
    return jnp.max(jnp.where(starts[None, :] <= query_rows[:, None], starts[None, :], 0), axis=1)


def normalize(values, gain_vec):
    inv_rms = lax.rsqrt(jnp.mean(values * values, axis=-1, keepdims=True) + norm_eps)
    normed = values * inv_rms
    return (normed, inv_rms, (normed * gain_vec.astype(jnp.float32)).astype(jnp.bfloat16))


def norm_back(grad_hidden, normed, inv_rms, gain_vec):
    grad_gain = jnp.sum(grad_hidden * normed, axis=0)
    grad_normed = grad_hidden * gain_vec.astype(jnp.float32)
    inner_mean = jnp.mean(grad_normed * normed, axis=-1, keepdims=True)
    return (inv_rms * (grad_normed - normed * inner_mean), grad_gain)


def matmul(left, right):
    return jnp.dot(left, right, preferred_element_type=jnp.float32)


def matmul_left_t(left, right):
    return lax.dot_general(left, right, (((0,), (0,)), ((), ())), preferred_element_type=jnp.float32)


def matmul_right_t(left, right):
    return lax.dot_general(left, right, (((1,), (1,)), ((), ())), preferred_element_type=jnp.float32)


def exchange(value):
    return lax.all_to_all(value, "dev", split_axis=0, concat_axis=0, tiled=True)


def split_ids(tok_ids, own_rows):
    owner = tok_ids // own_rows
    place = jnp.arange(tok_ids.shape[0], dtype=jnp.int32)
    same = tok_ids[:, None] == tok_ids[None, :]
    repeated = jnp.any(same & (place[None, :] < place[:, None]), axis=1)
    before = (owner[:, None] == owner[None, :]) & (tok_ids[None, :] < tok_ids[:, None]) & ~repeated[None, :]
    return (owner, tok_ids % own_rows, jnp.sum(before, axis=1, dtype=jnp.int32))


def ask_round(ids, index, own_rows, stride, room):
    count = lax.axis_size("dev")
    owner, local, rank = ids
    here = rank - index * room
    slot = jnp.where((here >= 0) & (here < room), owner * stride + here, -1)
    chosen = slot[None, :] == jnp.arange(count * stride, dtype=jnp.int32)[:, None]
    wanted = jnp.max(jnp.where(chosen, local[None, :], -1), axis=1).reshape(count, stride)
    rounds = jnp.broadcast_to(jnp.max(rank) // room + 1, (count, stride))
    return (jnp.concatenate([wanted, rounds], axis=1), chosen.astype(jnp.bfloat16))


def hear_round(message, own_rows, stride):
    asked = exchange(message)
    pick = asked[:, :stride].reshape(-1, 1) == jnp.arange(own_rows, dtype=jnp.int32)[None, :]
    return (pick.astype(jnp.bfloat16), jnp.max(asked[:, stride:]))


def plan_round(ids, index, own_rows, stride, room):
    message, chosen = ask_round(ids, index, own_rows, stride, room)
    pick, _ = hear_round(message, own_rows, stride)
    return (chosen, pick)


def answer(embedding, chosen, pick, stride, extra_row):
    count = lax.axis_size("dev")
    rows = matmul(pick, embedding).astype(jnp.bfloat16).reshape(count, stride, -1)
    if extra_row is not None:
        is_extra = (jnp.arange(stride, dtype=jnp.int32) == stride - 1)[None, :, None]
        rows = jnp.where(is_extra, extra_row[None, None, :], rows)
    got = exchange(rows.reshape(count * stride, -1))
    return (matmul_left_t(chosen, got).astype(jnp.bfloat16), got.reshape(count, stride, -1)[:, stride - 1])


def lookup(embedding, ids, message, chosen, extra_row, stride, room):
    own_rows = embedding.shape[0]
    pick, rounds = hear_round(message, own_rows, stride)
    first, extra = answer(embedding, chosen, pick, stride, extra_row)

    def more(carry):
        index, rows = carry
        again, its_pick = plan_round(ids, index, own_rows, stride, room)
        return (index + 1, rows + answer(embedding, again, its_pick, stride, None)[0])

    _, rows = lax.while_loop(lambda carry: carry[0] < rounds, more, (jnp.int32(1), first))
    return (rows, extra, ids, chosen, pick, rounds)


def send_grads(grad_low, chosen, pick, stride, extra_rows):
    count = lax.axis_size("dev")
    summed = matmul(chosen, grad_low).astype(jnp.bfloat16).reshape(count, stride, -1)
    if extra_rows is not None:
        place = jnp.arange(stride, dtype=jnp.int32)[None, :, None]
        high, low = extra_rows
        summed = jnp.where(place == stride - 2, high[:, None, :], summed)
        summed = jnp.where(place == stride - 1, low[:, None, :], summed)
    got = exchange(summed.reshape(count * stride, -1))
    return (matmul_left_t(pick, got), got.reshape(count, stride, -1)[:, stride - 2 :])


def table_back(grad_rows, extra_rows, plan, own_rows, stride, room):
    ids, chosen, pick, rounds = plan
    grad_low = grad_rows.astype(jnp.bfloat16)
    first, extra = send_grads(grad_low, chosen, pick, stride, extra_rows)

    def more(carry):
        index, total = carry
        again, its_pick = plan_round(ids, index, own_rows, stride, room)
        return (index + 1, total + send_grads(grad_low, again, its_pick, stride, None)[0])

    _, total = lax.while_loop(lambda carry: carry[0] < rounds, more, (jnp.int32(1), first))
    return (total, jnp.sum(extra.astype(jnp.float32), axis=(0, 1)))


def gather_parts(pieces):
    count = lax.axis_size("dev")
    sizes = [piece.shape[0] for piece in pieces]
    whole = lax.all_gather(jnp.concatenate(pieces, axis=0), "dev", axis=0)
    parts, start = ([], 0)
    for size in sizes:
        parts.append(whole[:, start : start + size].reshape(count * size, -1))
        start += size
    return parts


def split_rows(summed, sizes):
    pieces, start = ([], 0)
    for size in sizes:
        pieces.append(summed[start : start + size])
        start += size
    return pieces


def swap_halves(held, bit, last=False):
    count = lax.axis_size("dev")
    mine = (lax.axis_index("dev") >> bit) & 1
    keep = lax.dynamic_index_in_dim(held, mine, 0, keepdims=False)
    give = lax.dynamic_index_in_dim(held, 1 - mine, 0, keepdims=False)
    came = lax.ppermute(give, "dev", [(source, source ^ (1 << bit)) for source in range(count)])
    total = keep.astype(jnp.float32) + came.astype(jnp.float32)
    return total if last else total.astype(jnp.bfloat16)


def middle_bits():
    return list(range(1, lax.axis_size("dev").bit_length() - 2))


def sum_cores(term):
    count = lax.axis_size("dev")
    rows = term.shape[0] // count
    grid = term.astype(jnp.bfloat16).reshape(count // 2, 2, rows, term.shape[1])
    return swap_halves(grid.swapaxes(0, 1), 0)


def cut_thirds(held):
    _, rows, width = held.shape
    middle = middle_bits()
    bits = len(middle) + 1
    grid = held.reshape((2,) * bits + (rows, width))
    thirds = []
    for turn in range(3):
        shift = turn % len(middle)
        order = middle[shift:] + middle[:shift] + [bits]
        axes = [bits - bit for bit in order]
        part = grid[..., turn * (width // 3) : (turn + 1) * (width // 3)]
        thirds.append(part.transpose(axes + [bits, bits + 1]))
    return thirds


def sum_stage(thirds, stage):
    middle = middle_bits()
    return [swap_halves(third, middle[(turn + stage) % len(middle)]) for turn, third in enumerate(thirds)]


def sum_stages(thirds, first):
    for stage in range(first, len(middle_bits())):
        thirds = sum_stage(thirds, stage)
    return thirds


def sum_last(groups):
    whole = [jnp.concatenate(thirds, axis=-1) for thirds in groups]
    return swap_halves(jnp.concatenate(whole, axis=1), len(middle_bits()) + 1, True)


def split_low(values):
    high = lax.reduce_precision(values, 8, 7)
    return (high.astype(jnp.bfloat16), (values - high).astype(jnp.bfloat16))


def low_units(blocks):
    per_row = blocks.shape[1]
    place = 8 + jnp.arange(per_row, dtype=jnp.int32)[None, :]
    return jnp.min(place - 2 * ((blocks + 1) // 2), axis=1).astype(jnp.int32)


def by_unit(array):
    cut = array.reshape((array.shape[0], array.shape[1] // UNIT, UNIT) + array.shape[2:])
    return cut.swapaxes(0, 1)


def by_row(array, micros):
    cut = array.reshape(-1, micros, UNIT, array.shape[-1])
    return cut.swapaxes(0, 1).reshape(micros, -1, array.shape[-1])


def shards(
    token_ids,
    lengths,
    embedding,
    norm1_gain,
    w_query,
    w_key,
    w_value,
    w_out,
    mix_logits,
    mix_weights,
    norm2_gain,
    w_up,
    w_down,
    cotangent,
):
    count = lax.axis_size("dev")
    me = lax.axis_index("dev")
    micros, row_count = token_ids.shape
    own_rows, width = embedding.shape
    heads = mix_logits.shape[0]
    part = norm1_gain.shape[0]
    per_row = row_count // UNIT
    tokens = micros * row_count
    tok_ids = by_unit(token_ids).reshape(-1)
    stride = max(16, 1024 // count)
    room = stride - 2

    unit_rows = me * row_count + UNIT * jnp.arange(per_row, dtype=jnp.int32)
    begins = jnp.stack([seq_starts(lengths[micro], unit_rows) for micro in range(micros)])
    blocks = ((unit_rows[None, :] - begins) // UNIT + 1).reshape(-1).astype(jnp.int32)

    lows = low_units(blocks.reshape(micros, per_row))
    mixes = spread_mixes(mix_logits, mix_weights)

    up_cols = w_up.shape[1] // width
    up_pieces = [w_up[:, col * width : (col + 1) * width] for col in range(up_cols)]
    w_q, w_k, w_v = gather_parts([w_query, w_key, w_value])
    weight_pieces = [w_out] + up_pieces + [w_down]
    ids = split_ids(tok_ids, own_rows)
    message, chosen = ask_round(ids, 0, own_rows, stride, room)
    message, weight_pieces = lax.optimization_barrier((message, weight_pieces))
    gathered = gather_parts(weight_pieces)
    w_o, w_d = (gathered[0], gathered[-1])
    w_u = jnp.concatenate(gathered[1:-1], axis=1)
    gains_row = jnp.concatenate([norm1_gain, norm2_gain, jnp.zeros((width - 2 * part,), jnp.bfloat16)])
    picked, gains, *plan = lookup(embedding, ids, message, chosen, gains_row, stride, room)
    gain_one = gains[:, :part].reshape(-1)
    gain_two = gains[:, part : 2 * part].reshape(-1)
    inputs = picked.astype(jnp.float32)

    normed_one, inv_one, hidden_one = normalize(inputs, gain_one)
    own_hidden = hidden_one.reshape(per_row, micros, UNIT, width)
    pieces = earlier_rows(own_hidden)
    query, key, value = project(lows, pieces, (w_q, w_k, w_v))
    attended, *kept = attention_fwd(blocks, query, key, value, mixes, heads)
    attended = attended.reshape(tokens, width)

    middle = inputs + matmul(attended, w_o)
    normed_two, inv_two, hidden_two = normalize(middle, gain_two)
    up_proj = matmul(hidden_two, w_u)
    activated, gelu_pull = jax.vjp(jax.nn.gelu, up_proj)
    activated = activated.astype(jnp.bfloat16)
    output = (middle + matmul(activated, w_d)).astype(jnp.bfloat16)

    grad_rows = by_unit(cotangent).reshape(tokens, width)
    grad_act = matmul_right_t(grad_rows, w_d)
    grad_upb = gelu_pull(grad_act)[0].astype(jnp.bfloat16)
    grad_down = matmul_left_t(activated, grad_rows).astype(jnp.bfloat16)
    grad_down, grad_upb = lax.optimization_barrier((grad_down, grad_upb))
    down_sum = sum_cores(grad_down)
    grad_up = matmul_left_t(hidden_two, grad_upb).astype(jnp.bfloat16)
    grad_up, grad_upb = lax.optimization_barrier((grad_up, grad_upb))
    up_sum = sum_cores(grad_up)
    grad_hidden_two = matmul_right_t(grad_upb, w_u)
    grad_mid_norm, grad_gain_two = norm_back(grad_hidden_two, normed_two, inv_two, gain_two)
    grad_middle = grad_rows.astype(jnp.float32) + grad_mid_norm
    grad_branch = grad_middle.astype(jnp.bfloat16)
    grad_wout = matmul_left_t(attended, grad_branch)
    grad_att = matmul_right_t(grad_branch, w_o).astype(jnp.bfloat16).reshape(own_hidden.shape)
    up_sum = up_sum.reshape(count // 2, -1, up_cols, width).swapaxes(1, 2).reshape(count // 2, -1, width)
    late = cut_thirds(jnp.concatenate([down_sum, up_sum], axis=1))
    late, grad_att = lax.optimization_barrier((late, grad_att))
    late = sum_stage(late, 0)

    grad_query, grad_key, grad_value, wide_logit, wide_prob = attention_bwd(
        blocks, query, key, value, grad_att, kept, mixes, heads
    )
    late, grad_query, grad_key, grad_value = lax.optimization_barrier((late, grad_query, grad_key, grad_value))
    *terms, grad_own = project_back(lows, grad_query, grad_key, grad_value, (w_q, w_k, w_v))
    came = with_sibling(jnp.concatenate([terms[3], terms[1]], axis=0))
    came, grad_query, grad_key, grad_value, pieces, hidden_one = lax.optimization_barrier(
        (came, grad_query, grad_key, grad_value, pieces, hidden_one)
    )
    grad_own = return_rows(terms[0], terms[2], came, grad_own)
    grad_query = grad_query.reshape(tokens, width)
    grad_key = grad_key.reshape(-1, width)
    grad_value = grad_value.reshape(-1, width)
    flat_hidden = jnp.concatenate(pieces, axis=0).reshape(-1, width)
    grad_wq = matmul_left_t(hidden_one, grad_query)
    grad_wk = matmul_left_t(flat_hidden, grad_key)
    grad_wv = matmul_left_t(flat_hidden, grad_value)
    early_terms = [grad_wq, grad_wk, grad_wv, grad_wout]
    shaped = [term.astype(jnp.bfloat16).reshape(count, -1, width) for term in early_terms]
    early = sum_cores(jnp.concatenate(shaped, axis=1).reshape(-1, width))
    early = cut_thirds(early)
    late = sum_stage(late, 1)
    grad_hidden_one = grad_own.reshape(tokens, width)
    grad_in_norm, grad_gain_one = norm_back(grad_hidden_one, normed_one, inv_one, gain_one)
    grad_inputs = grad_middle + grad_in_norm

    mix_terms = jnp.concatenate([fold_mix(wide_logit, heads).reshape(-1), fold_mix(wide_prob, heads).reshape(-1)])
    mix_size = mix_terms.shape[0]
    small = jnp.concatenate(
        [
            grad_gain_one.reshape(count, part),
            grad_gain_two.reshape(count, part),
            jnp.broadcast_to(mix_terms[None, :], (count, mix_size)),
            jnp.zeros((count, width - 2 * part - mix_size), jnp.float32),
        ],
        axis=1,
    )
    grad_inputs, early, late = lax.optimization_barrier((grad_inputs, early, late))
    table_grad, small_sum = table_back(grad_inputs, split_low(small), plan, own_rows, stride, room)
    summed = sum_last([sum_stages(early, 0), sum_stages(late, 2)])
    row_sizes = [part] * 4 + [w_down.shape[0]] + [part] * up_cols
    weight_sums = split_rows(summed, row_sizes)
    mixes = small_sum[2 * part : 2 * part + mix_size].reshape(2, heads, heads)
    return (
        by_row(output, micros),
        by_row(grad_inputs, micros),
        table_grad,
        small_sum[:part],
        *weight_sums[:4],
        mixes[0],
        mixes[1],
        small_sum[part : 2 * part],
        jnp.concatenate(weight_sums[5:], axis=1),
        weight_sums[4],
    )


def solution(mesh):
    in_specs = (
        P(None, "dev"),
        P(),
        P("dev", None),
        P("dev"),
        P("dev", None),
        P("dev", None),
        P("dev", None),
        P("dev", None),
        P(),
        P(),
        P("dev"),
        P("dev", None),
        P("dev", None),
        P(None, "dev", None),
    )
    out_specs = (
        P(None, "dev", None),
        P(None, "dev", None),
        P("dev", None),
        P("dev"),
        P("dev", None),
        P("dev", None),
        P("dev", None),
        P("dev", None),
        P(),
        P(),
        P("dev"),
        P("dev", None),
        P("dev", None),
    )
    return jax.shard_map(shards, mesh=mesh, in_specs=in_specs, out_specs=out_specs, check_vma=False)
```

```python
from functools import partial

import jax
import jax.numpy as jnp
from jax import lax
from jax.experimental import pallas as pl
from jax.experimental.pallas import tpu as pltpu
from jax.sharding import PartitionSpec as P

norm_eps = 1e-06
gelu_scale = 0.7978845608028654
gelu_cube = 0.044715
FF_STEP = 256

masked = -1e30
UNIT = 128
CHUNK = 256
GROUP = 16
MAX_CHUNKS = 4


def dot_nn(left, right):
    return lax.dot_general(left, right, (((1,), (0,)), ((), ())), preferred_element_type=jnp.float32)


def dot_nt(left, right):
    return lax.dot_general(left, right, (((1,), (1,)), ((), ())), preferred_element_type=jnp.float32)


def spread_heads(rows, lane_head, quad, heads_per_quad):
    part = rows[:, quad * CHUNK : (quad + 1) * CHUNK]
    zero = jnp.zeros_like(part)
    return jnp.concatenate([jnp.where(lane_head == head, part, zero) for head in range(heads_per_quad)], axis=0)


def own_lanes(wide, lane_head, heads_per_quad):
    total = jnp.where(lane_head == 0, wide[:UNIT], 0.0)
    for head in range(1, heads_per_quad):
        total = total + jnp.where(lane_head == head, wide[head * UNIT : (head + 1) * UNIT], 0.0)
    return total


def allowed_keys(chunk, group, blocks):
    key = lax.broadcasted_iota(jnp.int32, (GROUP, CHUNK), 1) - (UNIT + CHUNK * chunk)
    row = lax.broadcasted_iota(jnp.int32, (GROUP, CHUNK), 0) + GROUP * group
    return (key <= row) & (key >= (1 - blocks) * UNIT)


def twice(rows):
    return jnp.concatenate([rows, rows], axis=-1)


def put_groups(ref, quad, per_quad, term):
    low = term.astype(jnp.bfloat16)
    for head in range(per_quad):
        rows = slice((quad * per_quad + head) * GROUP, (quad * per_quad + head + 1) * GROUP)
        for group in range(UNIT // GROUP):
            start = head * UNIT + group * GROUP
            ref[rows, group * CHUNK : (group + 1) * CHUNK] = low[start : start + GROUP]


def fwd_kernel(heads, blocks_ref, q_ref, k_ref, v_ref, mix_ref, att_ref, score_out, prob_out, mixed_out,
               qx, score, prob, mixed, logit, top, norm, total, sems):
    micro, inner, per_row = (pl.program_id(0), pl.program_id(1), pl.num_programs(1))
    blocks = blocks_ref[micro * per_row + inner]
    chunks = (blocks + 1) // 2
    last_unit = k_ref.shape[0] - per_row + inner + 1
    quads = q_ref.shape[3] // CHUNK
    per_quad = heads // quads
    groups = UNIT // GROUP
    wide = heads * GROUP
    lane_head = lax.broadcasted_iota(jnp.int32, (UNIT, CHUNK), 1) // (CHUNK // per_quad)
    for quad in range(quads):
        qx[quad] = spread_heads(q_ref[0, 0], lane_head, quad, per_quad)
    total[...] = jnp.zeros_like(total)
    top[...] = jnp.full_like(top, masked)
    norm[...] = jnp.zeros_like(norm)

    def keys(ref, chunk, quad):
        units = pl.ds(last_unit - 2 * (chunk + 1), 2)
        return ref[units, 0, :, quad * CHUNK : (quad + 1) * CHUNK].reshape(CHUNK, CHUNK)

    def keep(chunk, kind):
        source, target = ((score, score_out), (prob, prob_out), (mixed, mixed_out))[kind]
        return pltpu.make_async_copy(source.at[chunk], target.at[inner, micro, chunk], sems.at[kind, chunk])

    @pl.loop(0, chunks)
    def _(chunk):
        for quad in range(quads):
            put_groups(score.at[chunk], quad, per_quad, dot_nt(qx[quad], keys(k_ref, chunk, quad)))
        keep(chunk, 0).start()
        for group in range(groups):
            l = dot_nn(mix_ref[0], score[chunk, :, group * CHUNK : (group + 1) * CHUNK])
            l = jnp.where(allowed_keys(chunk, group, blocks)[None], l.reshape(heads, GROUP, CHUNK), masked)
            l = l.reshape(wide, CHUNK)
            logit[chunk, group] = l
            old = top[group]
            new = jnp.maximum(old, jnp.maximum(l[:, :UNIT], l[:, UNIT:]))
            terms = jnp.exp(l[:, :UNIT] - new) + jnp.exp(l[:, UNIT:] - new)
            norm[group] = norm[group] * jnp.exp(old - new) + terms
            top[group] = new

    for group in range(groups):
        lanes = top[group]
        high = jnp.broadcast_to(jnp.max(lanes, axis=-1, keepdims=True), lanes.shape)
        whole = jnp.sum(norm[group] * jnp.exp(lanes - high), axis=-1, keepdims=True)
        top[group] = high + jnp.log(jnp.broadcast_to(whole, lanes.shape))

    @pl.loop(0, chunks)
    def _(chunk):
        for group in range(groups):
            p = jnp.exp(logit[chunk, group] - twice(top[group])).astype(jnp.bfloat16)
            prob[chunk, :, group * CHUNK : (group + 1) * CHUNK] = p
            a = dot_nn(mix_ref[2], p).astype(jnp.bfloat16)
            mixed[chunk, :, GROUP * group : GROUP * (group + 1), :] = a.reshape(heads, GROUP, CHUNK)
        keep(chunk, 1).start()
        keep(chunk, 2).start()
        for quad in range(quads):
            a = mixed[chunk, quad * per_quad : (quad + 1) * per_quad].reshape(per_quad * UNIT, CHUNK)
            o = own_lanes(dot_nn(a, keys(v_ref, chunk, quad)), lane_head, per_quad)
            total[:, quad * CHUNK : (quad + 1) * CHUNK] += o

    att_ref[0, 0] = total[...].astype(jnp.bfloat16)

    @pl.loop(0, chunks)
    def _(chunk):
        for kind in range(3):
            keep(chunk, kind).wait()


def attention_specs(q, k, heads):
    per_row, micros, _, width = q.shape
    wide = heads * GROUP
    return (
        pl.BlockSpec((1, 1, UNIT, width), lambda m, u, _: (u, m, 0, 0)),
        pl.BlockSpec((k.shape[0], 1, UNIT, width), lambda m, u, _: (0, m, 0, 0)),
        pl.BlockSpec((4, wide, wide), lambda m, u, _: (0, 0, 0)),
    )


def kept_shapes(heads):
    wide = heads * GROUP
    flat = (MAX_CHUNKS, wide, UNIT // GROUP * CHUNK)
    return (flat, flat, (MAX_CHUNKS, heads, UNIT, CHUNK))


def attention_fwd(blocks, q, k, v, mixes, heads):
    per_row, micros, _, width = q.shape
    wide = heads * GROUP
    groups = UNIT // GROUP
    quads = width // CHUNK
    unit_spec, kv_spec, mix_spec = attention_specs(q, k, heads)
    kept = kept_shapes(heads)
    anywhere = pl.BlockSpec(memory_space=pl.ANY)
    return pl.pallas_call(
        partial(fwd_kernel, heads),
        grid_spec=pltpu.PrefetchScalarGridSpec(
            num_scalar_prefetch=1,
            grid=(micros, per_row),
            in_specs=[unit_spec, kv_spec, kv_spec, mix_spec],
            out_specs=[unit_spec, anywhere, anywhere, anywhere],
            scratch_shapes=[pltpu.VMEM((quads, heads // quads * UNIT, CHUNK), jnp.bfloat16)]
            + [pltpu.VMEM(shape, jnp.bfloat16) for shape in kept]
            + [
                pltpu.VMEM((MAX_CHUNKS, groups, wide, CHUNK), jnp.float32),
                pltpu.VMEM((groups, wide, UNIT), jnp.float32),
                pltpu.VMEM((groups, wide, UNIT), jnp.float32),
                pltpu.VMEM((UNIT, width), jnp.float32),
                pltpu.SemaphoreType.DMA((3, MAX_CHUNKS)),
            ],
        ),
        out_shape=[jax.ShapeDtypeStruct(q.shape, jnp.bfloat16)]
        + [jax.ShapeDtypeStruct((per_row, micros) + shape, jnp.bfloat16) for shape in kept],
        compiler_params=pltpu.CompilerParams(vmem_limit_bytes=50 * 1024 * 1024),
        cost_estimate=pl.CostEstimate(flops=20_000_000_000, bytes_accessed=30_000_000, transcendentals=0),
        name="attention_fwd",
    )(blocks, q, k, v, mixes)


def bwd_kernel(heads, blocks_ref, q_ref, k_ref, v_ref, do_ref, mix_ref, score_in, prob_in, mixed_in,
               dq_ref, dk_ref, dv_ref, gl_ref, gp_ref,
               qxt, dox, doxt, score, prob, mixed, grad_prob, grad_mixed, grad_logit, grad_score,
               delta, dq_total, dk_total, dv_total, sems):
    micro, inner, per_row = (pl.program_id(0), pl.program_id(1), pl.num_programs(1))
    step = micro * per_row + inner
    slot = step % 2
    blocks = blocks_ref[step]
    chunks = (blocks + 1) // 2
    key_units = k_ref.shape[0]
    last_unit = key_units - per_row + inner + 1
    quads = q_ref.shape[3] // CHUNK
    per_quad = heads // quads
    groups = UNIT // GROUP
    wide = heads * GROUP
    lane_head = lax.broadcasted_iota(jnp.int32, (UNIT, CHUNK), 1) // (CHUNK // per_quad)
    row_head = lax.broadcasted_iota(jnp.int32, (CHUNK, UNIT), 0) // (CHUNK // per_quad)
    lowest = key_units
    for other in range(key_units - 7):
        its_chunks = (blocks_ref[micro * per_row + other] + 1) // 2
        lowest = jnp.minimum(lowest, key_units - per_row + other + 1 - 2 * its_chunks)

    def fetch(at, chunk, kind):
        source, target = ((score_in, score), (prob_in, prob), (mixed_in, mixed))[kind]
        place = source.at[at % per_row, at // per_row, chunk]
        return pltpu.make_async_copy(place, target.at[at % 2, chunk], sems.at[kind, at % 2, chunk])

    def fetch_all(at):
        @pl.loop(0, (blocks_ref[at] + 1) // 2)
        def _(chunk):
            for kind in (1, 2, 0):
                fetch(at, chunk, kind).start()

    @pl.when(step == 0)
    def _():
        fetch_all(0)
        gl_ref[...] = jnp.zeros_like(gl_ref)
        gp_ref[...] = jnp.zeros_like(gp_ref)

    @pl.when(step + 1 < pl.num_programs(0) * per_row)
    def _():
        fetch_all(step + 1)

    @pl.when(inner == 0)
    def _():
        @pl.loop(lowest, key_units)
        def _(key_unit):
            dk_total[key_unit] = jnp.zeros_like(dk_total[key_unit])
            dv_total[key_unit] = jnp.zeros_like(dv_total[key_unit])

    def spread_turned(rows, quad):
        turned = rows[:, quad * CHUNK : (quad + 1) * CHUNK].T
        zero = jnp.zeros_like(turned)
        return jnp.concatenate([jnp.where(row_head == head, turned, zero) for head in range(per_quad)], axis=1)

    for quad in range(quads):
        qxt[quad] = spread_turned(q_ref[0, 0], quad)
        dox[quad] = spread_heads(do_ref[0, 0], lane_head, quad, per_quad)
        doxt[quad] = spread_turned(do_ref[0, 0], quad)
    dq_total[...] = jnp.zeros_like(dq_total)
    delta[...] = jnp.zeros_like(delta)

    def keys(ref, chunk, quad):
        units = pl.ds(last_unit - 2 * (chunk + 1), 2)
        return ref[units, 0, :, quad * CHUNK : (quad + 1) * CHUNK].reshape(CHUNK, CHUNK)

    def add_to(total, chunk, quad, term):
        first = last_unit - 2 * (chunk + 1)
        lanes = slice(quad * CHUNK, (quad + 1) * CHUNK)
        total[first, lanes, :] += term[:, :UNIT]
        total[first + 1, lanes, :] += term[:, UNIT:]

    @pl.loop(0, chunks)
    def _(chunk):
        for quad in range(quads):
            put_groups(grad_mixed, quad, per_quad, dot_nt(dox[quad], keys(v_ref, chunk, quad)))
        fetch(step, chunk, 1).wait()
        for group in range(groups):
            cols = slice(group * CHUNK, (group + 1) * CHUNK)
            dp = dot_nn(mix_ref[3], grad_mixed[:, cols])
            grad_prob[chunk, :, cols] = dp.astype(grad_prob.dtype)
            term = prob[slot, chunk, :, cols].astype(jnp.float32) * dp
            delta[group] += term[:, :UNIT] + term[:, UNIT:]
        gp_ref[...] += dot_nt(prob[slot, chunk], grad_mixed[...])
        fetch(step, chunk, 2).wait()
        for quad in range(quads):
            a = mixed[slot, chunk, quad * per_quad : (quad + 1) * per_quad].reshape(per_quad * UNIT, CHUNK)
            add_to(dv_total, chunk, quad, dot_nn(doxt[quad], a))

    for group in range(groups):
        delta[group] = jnp.broadcast_to(jnp.sum(delta[group], axis=-1, keepdims=True), (wide, UNIT))

    @pl.loop(0, chunks)
    def _(chunk):
        for group in range(groups):
            cols = slice(group * CHUNK, (group + 1) * CHUNK)
            dp = grad_prob[chunk, :, cols].astype(jnp.float32) - twice(delta[group])
            dl = (prob[slot, chunk, :, cols].astype(jnp.float32) * dp).astype(jnp.bfloat16)
            grad_logit[:, cols] = dl
            ds = dot_nn(mix_ref[1], dl).astype(jnp.bfloat16)
            grad_score[:, GROUP * group : GROUP * (group + 1), :] = ds.reshape(heads, GROUP, CHUNK)
        fetch(step, chunk, 0).wait()
        gl_ref[...] += dot_nt(score[slot, chunk], grad_logit[...])
        for quad in range(quads):
            ds = grad_score[quad * per_quad : (quad + 1) * per_quad].reshape(per_quad * UNIT, CHUNK)
            dq = own_lanes(dot_nn(ds, keys(k_ref, chunk, quad)), lane_head, per_quad)
            dq_total[:, quad * CHUNK : (quad + 1) * CHUNK] += dq
            add_to(dk_total, chunk, quad, dot_nn(qxt[quad], ds))

    dq_ref[0, 0] = (dq_total[...] * 0.125).astype(jnp.bfloat16)

    @pl.when(inner == per_row - 1)
    def _():
        @pl.loop(0, lowest)
        def _(key_unit):
            dk_ref[key_unit, 0] = jnp.zeros_like(dk_ref[key_unit, 0])
            dv_ref[key_unit, 0] = jnp.zeros_like(dv_ref[key_unit, 0])

        @pl.loop(lowest, key_units)
        def _(key_unit):
            dk_ref[key_unit, 0] = dk_total[key_unit].astype(jnp.bfloat16).T
            dv_ref[key_unit, 0] = dv_total[key_unit].astype(jnp.bfloat16).T


def attention_bwd(blocks, q, k, v, grad_out, kept, mixes, heads):
    per_row, micros, _, width = q.shape
    key_units = k.shape[0]
    wide = heads * GROUP
    groups = UNIT // GROUP
    quads = width // CHUNK
    turned = (quads, CHUNK, heads // quads * UNIT)
    unit_spec, kv_spec, mix_spec = attention_specs(q, k, heads)
    sum_spec = pl.BlockSpec((wide, wide), lambda m, u, _: (0, 0))
    anywhere = pl.BlockSpec(memory_space=pl.ANY)
    return pl.pallas_call(
        partial(bwd_kernel, heads),
        grid_spec=pltpu.PrefetchScalarGridSpec(
            num_scalar_prefetch=1,
            grid=(micros, per_row),
            in_specs=[unit_spec, kv_spec, kv_spec, unit_spec, mix_spec] + [anywhere] * 3,
            out_specs=[unit_spec, kv_spec, kv_spec, sum_spec, sum_spec],
            scratch_shapes=[
                pltpu.VMEM(turned, jnp.bfloat16),
                pltpu.VMEM((quads, heads // quads * UNIT, CHUNK), jnp.bfloat16),
                pltpu.VMEM(turned, jnp.bfloat16),
            ]
            + [pltpu.VMEM((2,) + shape, jnp.bfloat16) for shape in kept_shapes(heads)]
            + [
                pltpu.VMEM((MAX_CHUNKS, wide, groups * CHUNK), jnp.bfloat16),
                pltpu.VMEM((wide, groups * CHUNK), jnp.bfloat16),
                pltpu.VMEM((wide, groups * CHUNK), jnp.bfloat16),
                pltpu.VMEM((heads, UNIT, CHUNK), jnp.bfloat16),
                pltpu.VMEM((groups, wide, UNIT), jnp.float32),
                pltpu.VMEM((UNIT, width), jnp.float32),
                pltpu.VMEM((key_units, width, UNIT), jnp.float32),
                pltpu.VMEM((key_units, width, UNIT), jnp.float32),
                pltpu.SemaphoreType.DMA((3, 2, MAX_CHUNKS)),
            ],
        ),
        out_shape=[
            jax.ShapeDtypeStruct(q.shape, jnp.bfloat16),
            jax.ShapeDtypeStruct(k.shape, jnp.bfloat16),
            jax.ShapeDtypeStruct(v.shape, jnp.bfloat16),
            jax.ShapeDtypeStruct((wide, wide), jnp.float32),
            jax.ShapeDtypeStruct((wide, wide), jnp.float32),
        ],
        compiler_params=pltpu.CompilerParams(vmem_limit_bytes=58 * 1024 * 1024),
        cost_estimate=pl.CostEstimate(flops=45_000_000_000, bytes_accessed=40_000_000, transcendentals=0),
        name="attention_bwd",
    )(blocks, q, k, v, grad_out, mixes, *kept)


def piece_bases(key_units, per_row):
    sizes = [1] + [per_row] * ((key_units - 1) // per_row)
    return [(sum(sizes[:at]), size) for at, size in enumerate(sizes)]


def project_kernel(low_ref, *refs):
    pieces, (w_q, w_k, w_v, q_ref, k_ref, v_ref) = (refs[:-6], refs[-6:])
    key_units, width = (k_ref.shape[0], k_ref.shape[3])
    per_row = q_ref.shape[0]
    low = low_ref[pl.program_id(0)]

    for piece, (base, size) in zip(pieces, piece_bases(key_units, per_row)):
        @pl.when(base + size > low)
        def _():
            rows = piece[:, 0].reshape(size * UNIT, width)
            k_ref[base : base + size, 0] = dot_nn(rows, w_k[...]).astype(jnp.bfloat16).reshape(size, UNIT, width)
            v_ref[base : base + size, 0] = dot_nn(rows, w_v[...]).astype(jnp.bfloat16).reshape(size, UNIT, width)

    rows = pieces[-1][:, 0].reshape(per_row * UNIT, width)
    query = dot_nn(rows, w_q[...]).astype(jnp.bfloat16) * jnp.bfloat16(0.125)
    q_ref[:, 0] = query.reshape(per_row, UNIT, width)


def project(low, pieces, weights):
    micros, width = pieces[0].shape[1], pieces[0].shape[3]
    key_units = sum(piece.shape[0] for piece in pieces)
    per_row = pieces[-1].shape[0]

    def spec(units):
        return pl.BlockSpec((units, 1, UNIT, width), lambda m, _: (0, m, 0, 0))

    weight_spec = pl.BlockSpec((width, width), lambda m, _: (0, 0))
    shapes = [(units, micros, UNIT, width) for units in (per_row, key_units, key_units)]
    return pl.pallas_call(
        project_kernel,
        grid_spec=pltpu.PrefetchScalarGridSpec(
            num_scalar_prefetch=1,
            grid=(micros,),
            in_specs=[spec(piece.shape[0]) for piece in pieces] + [weight_spec] * 3,
            out_specs=[spec(shape[0]) for shape in shapes],
        ),
        out_shape=[jax.ShapeDtypeStruct(shape, jnp.bfloat16) for shape in shapes],
        compiler_params=pltpu.CompilerParams(vmem_limit_bytes=44 * 1024 * 1024),
        cost_estimate=pl.CostEstimate(flops=6_000_000_000, bytes_accessed=15_000_000, transcendentals=0),
        name="project",
    )(low, *pieces, *weights)


def project_back_kernel(low_ref, dq_ref, dk_ref, dv_ref, w_q, w_k, w_v, *outs):
    key_units, width = (dk_ref.shape[0], dk_ref.shape[3])
    per_row = dq_ref.shape[0]
    low = low_ref[pl.program_id(0)]
    bases = piece_bases(key_units, per_row)

    def from_keys(base, size):
        rows = slice(base, base + size)
        key_term = dot_nt(dk_ref[rows, 0].reshape(size * UNIT, width), w_k[...])
        return key_term + dot_nt(dv_ref[rows, 0].reshape(size * UNIT, width), w_v[...])

    for out, (base, size) in zip(outs[:-1], bases[:-1]):
        @pl.when(base + size > low)
        def _():
            out[:, 0] = from_keys(base, size).astype(jnp.bfloat16).reshape(size, UNIT, width)

        @pl.when(base + size <= low)
        def _():
            out[...] = jnp.zeros_like(out)

    own = from_keys(*bases[-1]) + dot_nt(dq_ref[:, 0].reshape(per_row * UNIT, width), w_q[...])
    outs[-1][:, 0] = own.reshape(per_row, UNIT, width)


def project_back(low, grad_query, grad_key, grad_value, weights):
    per_row, micros, _, width = grad_query.shape
    key_units = grad_key.shape[0]

    def spec(units):
        return pl.BlockSpec((units, 1, UNIT, width), lambda m, _: (0, m, 0, 0))

    weight_spec = pl.BlockSpec((width, width), lambda m, _: (0, 0))
    sizes = [size for _, size in piece_bases(key_units, per_row)]
    shapes = [(size, micros, UNIT, width) for size in sizes]
    kinds = [jnp.bfloat16] * (len(sizes) - 1) + [jnp.float32]
    return pl.pallas_call(
        project_back_kernel,
        grid_spec=pltpu.PrefetchScalarGridSpec(
            num_scalar_prefetch=1,
            grid=(micros,),
            in_specs=[spec(per_row), spec(key_units), spec(key_units)] + [weight_spec] * 3,
            out_specs=[spec(size) for size in sizes],
        ),
        out_shape=[jax.ShapeDtypeStruct(shape, kind) for shape, kind in zip(shapes, kinds)],
        compiler_params=pltpu.CompilerParams(vmem_limit_bytes=44 * 1024 * 1024),
        cost_estimate=pl.CostEstimate(flops=6_000_000_000, bytes_accessed=15_000_000, transcendentals=0),
        name="project_back",
    )(low, grad_query, grad_key, grad_value, *weights)


def feed_kernel(x_ref, att_ref, w_o_ref, gain_ref, up_ref, down_ref, cot_ref,
                mid_ref, out_ref, grad_hidden_ref, grad_up_ref, grad_down_ref,
                hidden, turned, out_total, back_total):
    step = pl.program_id(0)

    @pl.when(step == 0)
    def _():
        middle = x_ref[...].astype(jnp.float32) + dot_nn(att_ref[...], w_o_ref[...])
        mid_ref[...] = middle
        inv_rms = lax.rsqrt(jnp.mean(middle * middle, axis=-1, keepdims=True) + norm_eps)
        rows = (middle * inv_rms * gain_ref[...]).astype(jnp.bfloat16)
        hidden[...] = rows
        turned[...] = rows.T
        out_total[...] = jnp.zeros_like(out_total)
        back_total[...] = jnp.zeros_like(back_total)

    for start in range(0, up_ref.shape[2], FF_STEP):
        cols = slice(start, start + FF_STEP)
        up = dot_nn(hidden[...], up_ref[0, :, cols])
        square = up * up
        bent = jnp.tanh(gelu_scale * up * (1.0 + gelu_cube * square))
        half = 0.5 + 0.5 * bent
        slope = half + 0.5 * up * (1.0 - bent * bent) * (gelu_scale * (1.0 + 3.0 * gelu_cube * square))
        active = (up * half).astype(jnp.bfloat16)
        grad_up = (dot_nt(cot_ref[...], down_ref[cols, :]) * slope).astype(jnp.bfloat16)
        out_total[...] += dot_nn(active, down_ref[cols, :])
        back_total[...] += dot_nt(grad_up, up_ref[0, :, cols])
        grad_down_ref[cols, :] = dot_nn(active.T, cot_ref[...]).astype(jnp.bfloat16)
        grad_up_ref[0, :, cols] = dot_nn(turned[...], grad_up).astype(jnp.bfloat16)

    @pl.when(step == pl.num_programs(0) - 1)
    def _():
        out_ref[...] = (mid_ref[...] + out_total[...]).astype(jnp.bfloat16)
        grad_hidden_ref[...] = back_total[...]


def feed_forward(rows, attended, w_o, gain, w_up, w_down, cot):
    tokens, width = rows.shape
    pieces = w_up.shape[0]
    whole = pl.BlockSpec((tokens, width), lambda i: (0, 0))
    up_spec = pl.BlockSpec((1, width, width), lambda i: (i, 0, 0))
    down_spec = pl.BlockSpec((width, width), lambda i: (i, 0))
    f32, bf16 = (jnp.float32, jnp.bfloat16)
    return pl.pallas_call(
        feed_kernel,
        grid=(pieces,),
        in_specs=[
            whole,
            whole,
            pl.BlockSpec((width, width), lambda i: (0, 0)),
            pl.BlockSpec((1, width), lambda i: (0, 0)),
            up_spec,
            down_spec,
            whole,
        ],
        out_specs=[whole, whole, whole, up_spec, down_spec],
        out_shape=[
            jax.ShapeDtypeStruct((tokens, width), f32),
            jax.ShapeDtypeStruct((tokens, width), bf16),
            jax.ShapeDtypeStruct((tokens, width), f32),
            jax.ShapeDtypeStruct(w_up.shape, bf16),
            jax.ShapeDtypeStruct(w_down.shape, bf16),
        ],
        scratch_shapes=[
            pltpu.VMEM((tokens, width), bf16),
            pltpu.VMEM((width, tokens), bf16),
            pltpu.VMEM((tokens, width), f32),
            pltpu.VMEM((tokens, width), f32),
        ],
        compiler_params=pltpu.CompilerParams(vmem_limit_bytes=48 * 1024 * 1024),
        cost_estimate=pl.CostEstimate(flops=16_000_000_000, bytes_accessed=30_000_000, transcendentals=0),
        name="feed_forward",
    )(rows, attended, w_o, gain, w_up, w_down, cot)


def spread_mixes(mix_logits, mix_weights):
    heads = mix_logits.shape[0]
    wide = heads * GROUP
    place = jnp.arange(wide, dtype=jnp.int32)
    pick = (place[:, None] // GROUP == jnp.arange(heads, dtype=jnp.int32)[None, :]).astype(mix_logits.dtype)
    same_row = (place[:, None] % GROUP == place[None, :] % GROUP)[None]
    tables = jnp.stack([mix_logits.T, mix_logits, mix_weights.T, mix_weights]).reshape(4 * heads, heads)
    across = jnp.dot(tables, pick.T, preferred_element_type=jnp.float32).astype(mix_logits.dtype)
    down = jnp.einsum("wh,bhx->bwx", pick, across.reshape(4, heads, wide), preferred_element_type=jnp.float32)
    return jnp.where(same_row, down, 0.0).astype(mix_logits.dtype)


def fold_mix(wide, heads):
    place = jnp.arange(heads * GROUP, dtype=jnp.int32)
    pick = (place[:, None] // GROUP == jnp.arange(heads, dtype=jnp.int32)[None, :]).astype(jnp.float32)
    same_row = place[:, None] % GROUP == place[None, :] % GROUP
    down = jnp.dot(pick.T, jnp.where(same_row, wide, 0.0), precision=lax.Precision.HIGHEST)
    return jnp.dot(down, pick, precision=lax.Precision.HIGHEST)


def from_behind(value, steps):
    count = lax.axis_size("dev")
    first, last = (max(0, -steps), min(count, count - steps))
    return lax.ppermute(value, "dev", [(source, source + steps) for source in range(first, last)])


def with_sibling(value):
    count = lax.axis_size("dev")
    return lax.ppermute(value, "dev", [(source, source ^ 1) for source in range(count)])


def earlier_rows(own):
    size = own.shape[0]
    first_core = lax.axis_index("dev") % 2 == 0
    two, four = (from_behind(own, 2), from_behind(own, 4))
    give = jnp.concatenate([jnp.where(first_core, own, two), jnp.where(first_core, two, four)], axis=0)
    came = with_sibling(give)
    return [four[size - 1 :], came[size:], two, came[:size], own]


def return_rows(four, two, came, grad_own):
    size = two.shape[0]
    first_core = lax.axis_index("dev") % 2 == 0
    came = came.astype(jnp.float32)
    one, three = (came[:size], came[size:])
    give_two = two.astype(jnp.float32) + jnp.where(first_core, three, one)
    padded = jnp.pad(four.astype(jnp.float32), ((size - four.shape[0], 0), (0, 0), (0, 0), (0, 0)))
    give_four = padded + jnp.where(first_core, 0.0, three)
    back_two = from_behind(give_two.astype(jnp.bfloat16), -2).astype(jnp.float32)
    back_four = from_behind(give_four.astype(jnp.bfloat16), -4).astype(jnp.float32)
    return grad_own + jnp.where(first_core, one, 0.0) + back_two + back_four


def seq_starts(lengths_row, query_rows):
    seq_ends = jnp.cumsum(lengths_row)
    starts = seq_ends - lengths_row
    return jnp.max(jnp.where(starts[None, :] <= query_rows[:, None], starts[None, :], 0), axis=1)


def normalize(values, gain_vec):
    inv_rms = lax.rsqrt(jnp.mean(values * values, axis=-1, keepdims=True) + norm_eps)
    normed = values * inv_rms
    return (normed, inv_rms, (normed * gain_vec.astype(jnp.float32)).astype(jnp.bfloat16))


def norm_back(grad_hidden, normed, inv_rms, gain_vec):
    grad_gain = jnp.sum(grad_hidden * normed, axis=0)
    grad_normed = grad_hidden * gain_vec.astype(jnp.float32)
    inner_mean = jnp.mean(grad_normed * normed, axis=-1, keepdims=True)
    return (inv_rms * (grad_normed - normed * inner_mean), grad_gain)


def matmul(left, right):
    return jnp.dot(left, right, preferred_element_type=jnp.float32)


def matmul_left_t(left, right):
    return lax.dot_general(left, right, (((0,), (0,)), ((), ())), preferred_element_type=jnp.float32)


def matmul_right_t(left, right):
    return lax.dot_general(left, right, (((1,), (1,)), ((), ())), preferred_element_type=jnp.float32)


def exchange(value):
    return lax.all_to_all(value, "dev", split_axis=0, concat_axis=0, tiled=True)


def split_ids(tok_ids, own_rows):
    owner = tok_ids // own_rows
    place = jnp.arange(tok_ids.shape[0], dtype=jnp.int32)
    same = tok_ids[:, None] == tok_ids[None, :]
    repeated = jnp.any(same & (place[None, :] < place[:, None]), axis=1)
    before = (owner[:, None] == owner[None, :]) & (tok_ids[None, :] < tok_ids[:, None]) & ~repeated[None, :]
    return (owner, tok_ids % own_rows, jnp.sum(before, axis=1, dtype=jnp.int32))


def ask_round(ids, index, own_rows, stride, room):
    count = lax.axis_size("dev")
    owner, local, rank = ids
    here = rank - index * room
    slot = jnp.where((here >= 0) & (here < room), owner * stride + here, -1)
    chosen = slot[None, :] == jnp.arange(count * stride, dtype=jnp.int32)[:, None]
    wanted = jnp.max(jnp.where(chosen, local[None, :], -1), axis=1).reshape(count, stride)
    rounds = jnp.broadcast_to(jnp.max(rank) // room + 1, (count, stride))
    return (jnp.concatenate([wanted, rounds], axis=1), chosen.astype(jnp.bfloat16))


def hear_round(message, own_rows, stride):
    asked = exchange(message)
    pick = asked[:, :stride].reshape(-1, 1) == jnp.arange(own_rows, dtype=jnp.int32)[None, :]
    return (pick.astype(jnp.bfloat16), jnp.max(asked[:, stride:]))


def plan_round(ids, index, own_rows, stride, room):
    message, chosen = ask_round(ids, index, own_rows, stride, room)
    pick, _ = hear_round(message, own_rows, stride)
    return (chosen, pick)


def answer(embedding, chosen, pick, stride, extra_row):
    count = lax.axis_size("dev")
    rows = matmul(pick, embedding).astype(jnp.bfloat16).reshape(count, stride, -1)
    if extra_row is not None:
        is_extra = (jnp.arange(stride, dtype=jnp.int32) == stride - 1)[None, :, None]
        rows = jnp.where(is_extra, extra_row[None, None, :], rows)
    got = exchange(rows.reshape(count * stride, -1))
    return (matmul_left_t(chosen, got).astype(jnp.bfloat16), got.reshape(count, stride, -1)[:, stride - 1])


def lookup(embedding, ids, message, chosen, extra_row, stride, room):
    own_rows = embedding.shape[0]
    pick, rounds = hear_round(message, own_rows, stride)
    first, extra = answer(embedding, chosen, pick, stride, extra_row)

    def more(carry):
        index, rows = carry
        again, its_pick = plan_round(ids, index, own_rows, stride, room)
        return (index + 1, rows + answer(embedding, again, its_pick, stride, None)[0])

    _, rows = lax.while_loop(lambda carry: carry[0] < rounds, more, (jnp.int32(1), first))
    return (rows, extra, ids, chosen, pick, rounds)


def send_grads(grad_low, chosen, pick, stride, extra_rows):
    count = lax.axis_size("dev")
    summed = matmul(chosen, grad_low).astype(jnp.bfloat16).reshape(count, stride, -1)
    if extra_rows is not None:
        place = jnp.arange(stride, dtype=jnp.int32)[None, :, None]
        high, low = extra_rows
        summed = jnp.where(place == stride - 2, high[:, None, :], summed)
        summed = jnp.where(place == stride - 1, low[:, None, :], summed)
    got = exchange(summed.reshape(count * stride, -1))
    return (matmul_left_t(pick, got), got.reshape(count, stride, -1)[:, stride - 2 :])


def table_back(grad_rows, extra_rows, plan, own_rows, stride, room):
    ids, chosen, pick, rounds = plan
    grad_low = grad_rows.astype(jnp.bfloat16)
    first, extra = send_grads(grad_low, chosen, pick, stride, extra_rows)

    def more(carry):
        index, total = carry
        again, its_pick = plan_round(ids, index, own_rows, stride, room)
        return (index + 1, total + send_grads(grad_low, again, its_pick, stride, None)[0])

    _, total = lax.while_loop(lambda carry: carry[0] < rounds, more, (jnp.int32(1), first))
    return (total, jnp.sum(extra.astype(jnp.float32), axis=(0, 1)))


def gather_parts(pieces):
    count = lax.axis_size("dev")
    sizes = [piece.shape[0] for piece in pieces]
    whole = lax.all_gather(jnp.concatenate(pieces, axis=0), "dev", axis=0)
    parts, start = ([], 0)
    for size in sizes:
        parts.append(whole[:, start : start + size].reshape(count * size, -1))
        start += size
    return parts


def gather_late(pieces, part, up_cols):
    width = pieces[0].shape[1]
    whole = lax.all_gather(jnp.concatenate(pieces, axis=0), "dev", axis=0)
    middle = part * (1 + up_cols)
    up = whole[:, part:middle].reshape(-1, up_cols, part, width).swapaxes(0, 1)
    return (whole[:, :part].reshape(-1, width), up.reshape(up_cols, -1, width), whole[:, middle:].reshape(-1, width))


def split_rows(summed, sizes):
    pieces, start = ([], 0)
    for size in sizes:
        pieces.append(summed[start : start + size])
        start += size
    return pieces


def swap_halves(held, bit, last=False):
    count = lax.axis_size("dev")
    mine = (lax.axis_index("dev") >> bit) & 1
    keep = lax.dynamic_index_in_dim(held, mine, 0, keepdims=False)
    give = lax.dynamic_index_in_dim(held, 1 - mine, 0, keepdims=False)
    came = lax.ppermute(give, "dev", [(source, source ^ (1 << bit)) for source in range(count)])
    total = keep.astype(jnp.float32) + came.astype(jnp.float32)
    return total if last else total.astype(jnp.bfloat16)


def middle_bits():
    return list(range(1, lax.axis_size("dev").bit_length() - 2))


def sum_cores(term):
    count, pieces, rows, width = term.shape
    grid = term.reshape(count // 2, 2, pieces, rows, width)
    return swap_halves(grid.swapaxes(0, 1), 0).reshape(count // 2, pieces * rows, width)


def cut_thirds(held):
    _, rows, width = held.shape
    middle = middle_bits()
    bits = len(middle) + 1
    grid = held.reshape((2,) * bits + (rows, width))
    thirds = []
    for turn in range(3):
        shift = turn % len(middle)
        order = middle[shift:] + middle[:shift] + [bits]
        axes = [bits - bit for bit in order]
        part = grid[..., turn * (width // 3) : (turn + 1) * (width // 3)]
        thirds.append(part.transpose(axes + [bits, bits + 1]))
    return thirds


def sum_stage(thirds, stage):
    middle = middle_bits()
    return [swap_halves(third, middle[(turn + stage) % len(middle)]) for turn, third in enumerate(thirds)]


def sum_stages(thirds, first):
    for stage in range(first, len(middle_bits())):
        thirds = sum_stage(thirds, stage)
    return thirds


def sum_last(groups):
    whole = [jnp.concatenate(thirds, axis=-1) for thirds in groups]
    return swap_halves(jnp.concatenate(whole, axis=1), len(middle_bits()) + 1, True)


def split_low(values):
    high = lax.reduce_precision(values, 8, 7)
    return (high.astype(jnp.bfloat16), (values - high).astype(jnp.bfloat16))


def low_units(blocks):
    per_row = blocks.shape[1]
    place = 8 + jnp.arange(per_row, dtype=jnp.int32)[None, :]
    return jnp.min(place - 2 * ((blocks + 1) // 2), axis=1).astype(jnp.int32)


def by_unit(array):
    cut = array.reshape((array.shape[0], array.shape[1] // UNIT, UNIT) + array.shape[2:])
    return cut.swapaxes(0, 1)


def by_row(array, micros):
    cut = array.reshape(-1, micros, UNIT, array.shape[-1])
    return cut.swapaxes(0, 1).reshape(micros, -1, array.shape[-1])


def shards(
    token_ids,
    lengths,
    embedding,
    norm1_gain,
    w_query,
    w_key,
    w_value,
    w_out,
    mix_logits,
    mix_weights,
    norm2_gain,
    w_up,
    w_down,
    cotangent,
):
    count = lax.axis_size("dev")
    me = lax.axis_index("dev")
    micros, row_count = token_ids.shape
    own_rows, width = embedding.shape
    heads = mix_logits.shape[0]
    part = norm1_gain.shape[0]
    per_row = row_count // UNIT
    tokens = micros * row_count
    tok_ids = by_unit(token_ids).reshape(-1)
    stride = max(16, 1024 // count)
    room = stride - 2

    unit_rows = me * row_count + UNIT * jnp.arange(per_row, dtype=jnp.int32)
    begins = jnp.stack([seq_starts(lengths[micro], unit_rows) for micro in range(micros)])
    blocks = ((unit_rows[None, :] - begins) // UNIT + 1).reshape(-1).astype(jnp.int32)

    lows = low_units(blocks.reshape(micros, per_row))
    mixes = spread_mixes(mix_logits, mix_weights)

    up_cols = w_up.shape[1] // width
    up_pieces = [w_up[:, col * width : (col + 1) * width] for col in range(up_cols)]
    w_q, w_k, w_v = gather_parts([w_query, w_key, w_value])
    weight_pieces = [w_out] + up_pieces + [w_down]
    ids = split_ids(tok_ids, own_rows)
    message, chosen = ask_round(ids, 0, own_rows, stride, room)
    message, weight_pieces = lax.optimization_barrier((message, weight_pieces))
    w_o, w_u, w_d = gather_late(weight_pieces, part, up_cols)
    gains_row = jnp.concatenate([norm1_gain, norm2_gain, jnp.zeros((width - 2 * part,), jnp.bfloat16)])
    picked, gains, *plan = lookup(embedding, ids, message, chosen, gains_row, stride, room)
    gain_one = gains[:, :part].reshape(-1)
    gain_two = gains[:, part : 2 * part].reshape(-1)
    inputs = picked.astype(jnp.float32)

    normed_one, inv_one, hidden_one = normalize(inputs, gain_one)
    own_hidden = hidden_one.reshape(per_row, micros, UNIT, width)
    pieces = earlier_rows(own_hidden)
    query, key, value = project(lows, pieces, (w_q, w_k, w_v))
    attended, *kept = attention_fwd(blocks, query, key, value, mixes, heads)
    attended = attended.reshape(tokens, width)

    grad_rows = by_unit(cotangent).reshape(tokens, width)
    gain_row = gain_two.astype(jnp.float32)[None, :]
    middle, output, grad_hidden_two, grad_up, grad_down = feed_forward(
        picked, attended, w_o, gain_row, w_u, w_d, grad_rows
    )
    inv_two = lax.rsqrt(jnp.mean(middle * middle, axis=-1, keepdims=True) + norm_eps)
    normed_two = middle * inv_two
    down_sum = sum_cores(grad_down.reshape(count, 1, -1, width))
    up_sum = sum_cores(grad_up.reshape(up_cols, count, part, width).swapaxes(0, 1))
    grad_mid_norm, grad_gain_two = norm_back(grad_hidden_two, normed_two, inv_two, gain_two)
    grad_middle = grad_rows.astype(jnp.float32) + grad_mid_norm
    grad_branch = grad_middle.astype(jnp.bfloat16)
    grad_wout = matmul_left_t(attended, grad_branch)
    grad_att = matmul_right_t(grad_branch, w_o).astype(jnp.bfloat16).reshape(own_hidden.shape)
    late = cut_thirds(jnp.concatenate([down_sum, up_sum], axis=1))
    late, grad_att = lax.optimization_barrier((late, grad_att))
    late = sum_stage(late, 0)

    grad_query, grad_key, grad_value, wide_logit, wide_prob = attention_bwd(
        blocks, query, key, value, grad_att, kept, mixes, heads
    )
    late, grad_query, grad_key, grad_value = lax.optimization_barrier((late, grad_query, grad_key, grad_value))
    *terms, grad_own = project_back(lows, grad_query, grad_key, grad_value, (w_q, w_k, w_v))
    came = with_sibling(jnp.concatenate([terms[3], terms[1]], axis=0))
    came, grad_query, grad_key, grad_value, pieces, hidden_one = lax.optimization_barrier(
        (came, grad_query, grad_key, grad_value, pieces, hidden_one)
    )
    grad_own = return_rows(terms[0], terms[2], came, grad_own)
    grad_query = grad_query.reshape(tokens, width)
    grad_key = grad_key.reshape(-1, width)
    grad_value = grad_value.reshape(-1, width)
    flat_hidden = jnp.concatenate(pieces, axis=0).reshape(-1, width)
    grad_wq = matmul_left_t(hidden_one, grad_query)
    grad_wk = matmul_left_t(flat_hidden, grad_key)
    grad_wv = matmul_left_t(flat_hidden, grad_value)
    early_terms = [grad_wq, grad_wk, grad_wv, grad_wout]
    shaped = [term.astype(jnp.bfloat16).reshape(count, 1, -1, width) for term in early_terms]
    early = sum_cores(jnp.concatenate(shaped, axis=1))
    early = cut_thirds(early)
    late = sum_stage(late, 1)
    grad_hidden_one = grad_own.reshape(tokens, width)
    grad_in_norm, grad_gain_one = norm_back(grad_hidden_one, normed_one, inv_one, gain_one)
    grad_inputs = grad_middle + grad_in_norm

    mix_terms = jnp.concatenate([fold_mix(wide_logit, heads).reshape(-1), fold_mix(wide_prob, heads).reshape(-1)])
    mix_size = mix_terms.shape[0]
    small = jnp.concatenate(
        [
            grad_gain_one.reshape(count, part),
            grad_gain_two.reshape(count, part),
            jnp.broadcast_to(mix_terms[None, :], (count, mix_size)),
            jnp.zeros((count, width - 2 * part - mix_size), jnp.float32),
        ],
        axis=1,
    )
    grad_inputs, early, late = lax.optimization_barrier((grad_inputs, early, late))
    table_grad, small_sum = table_back(grad_inputs, split_low(small), plan, own_rows, stride, room)
    summed = sum_last([sum_stages(early, 0), sum_stages(late, 2)])
    row_sizes = [part] * 4 + [w_down.shape[0]] + [part] * up_cols
    weight_sums = split_rows(summed, row_sizes)
    mixes = small_sum[2 * part : 2 * part + mix_size].reshape(2, heads, heads)
    return (
        by_row(output, micros),
        by_row(grad_inputs, micros),
        table_grad,
        small_sum[:part],
        *weight_sums[:4],
        mixes[0],
        mixes[1],
        small_sum[part : 2 * part],
        jnp.concatenate(weight_sums[5:], axis=1),
        weight_sums[4],
    )


def solution(mesh):
    in_specs = (
        P(None, "dev"),
        P(),
        P("dev", None),
        P("dev"),
        P("dev", None),
        P("dev", None),
        P("dev", None),
        P("dev", None),
        P(),
        P(),
        P("dev"),
        P("dev", None),
        P("dev", None),
        P(None, "dev", None),
    )
    out_specs = (
        P(None, "dev", None),
        P(None, "dev", None),
        P("dev", None),
        P("dev"),
        P("dev", None),
        P("dev", None),
        P("dev", None),
        P("dev", None),
        P(),
        P(),
        P("dev"),
        P("dev", None),
        P("dev", None),
    )
    return jax.shard_map(shards, mesh=mesh, in_specs=in_specs, out_specs=out_specs, check_vma=False)
```

```python
from functools import partial

import jax
import jax.numpy as jnp
from jax import lax
from jax.experimental import pallas as pl
from jax.experimental.pallas import tpu as pltpu
from jax.sharding import PartitionSpec as P

norm_eps = 1e-06
gelu_scale = 0.7978845608028654
gelu_cube = 0.044715
FF_STEP = 256

masked = -1e30
UNIT = 128
CHUNK = 256
GROUP = 16
MAX_CHUNKS = 4


def dot_nn(left, right):
    return lax.dot_general(left, right, (((1,), (0,)), ((), ())), preferred_element_type=jnp.float32)


def dot_nt(left, right):
    return lax.dot_general(left, right, (((1,), (1,)), ((), ())), preferred_element_type=jnp.float32)


def spread_heads(rows, lane_head, quad, heads_per_quad):
    part = rows[:, quad * CHUNK : (quad + 1) * CHUNK]
    zero = jnp.zeros_like(part)
    return jnp.concatenate([jnp.where(lane_head == head, part, zero) for head in range(heads_per_quad)], axis=0)


def own_lanes(wide, lane_head, heads_per_quad):
    total = jnp.where(lane_head == 0, wide[:UNIT], 0.0)
    for head in range(1, heads_per_quad):
        total = total + jnp.where(lane_head == head, wide[head * UNIT : (head + 1) * UNIT], 0.0)
    return total


def allowed_keys(chunk, group, blocks):
    key = lax.broadcasted_iota(jnp.int32, (GROUP, CHUNK), 1) - (UNIT + CHUNK * chunk)
    row = lax.broadcasted_iota(jnp.int32, (GROUP, CHUNK), 0) + GROUP * group
    return (key <= row) & (key >= (1 - blocks) * UNIT)


def twice(rows):
    return jnp.concatenate([rows, rows], axis=-1)


def put_groups(ref, quad, per_quad, term):
    low = term.astype(jnp.bfloat16)
    for head in range(per_quad):
        rows = slice((quad * per_quad + head) * GROUP, (quad * per_quad + head + 1) * GROUP)
        for group in range(UNIT // GROUP):
            start = head * UNIT + group * GROUP
            ref[rows, group * CHUNK : (group + 1) * CHUNK] = low[start : start + GROUP]


def fwd_kernel(heads, blocks_ref, q_ref, k_ref, v_ref, mix_ref, att_ref, score_out, prob_out, mixed_out,
               qx, score, prob, mixed, logit, top, norm, total, sems):
    micro, inner, per_row = (pl.program_id(0), pl.program_id(1), pl.num_programs(1))
    blocks = blocks_ref[micro * per_row + inner]
    chunks = (blocks + 1) // 2
    last_unit = k_ref.shape[0] - per_row + inner + 1
    quads = q_ref.shape[3] // CHUNK
    per_quad = heads // quads
    groups = UNIT // GROUP
    wide = heads * GROUP
    lane_head = lax.broadcasted_iota(jnp.int32, (UNIT, CHUNK), 1) // (CHUNK // per_quad)
    for quad in range(quads):
        qx[quad] = spread_heads(q_ref[0, 0], lane_head, quad, per_quad)
    total[...] = jnp.zeros_like(total)
    top[...] = jnp.full_like(top, masked)
    norm[...] = jnp.zeros_like(norm)

    def keys(ref, chunk, quad):
        units = pl.ds(last_unit - 2 * (chunk + 1), 2)
        return ref[units, 0, :, quad * CHUNK : (quad + 1) * CHUNK].reshape(CHUNK, CHUNK)

    def keep(chunk, kind):
        source, target = ((score, score_out), (prob, prob_out), (mixed, mixed_out))[kind]
        return pltpu.make_async_copy(source.at[chunk], target.at[inner, micro, chunk], sems.at[kind, chunk])

    @pl.loop(0, chunks)
    def _(chunk):
        for quad in range(quads):
            put_groups(score.at[chunk], quad, per_quad, dot_nt(qx[quad], keys(k_ref, chunk, quad)))
        keep(chunk, 0).start()
        for group in range(groups):
            l = dot_nn(mix_ref[0], score[chunk, :, group * CHUNK : (group + 1) * CHUNK])
            l = jnp.where(allowed_keys(chunk, group, blocks)[None], l.reshape(heads, GROUP, CHUNK), masked)
            l = l.reshape(wide, CHUNK)
            logit[chunk, group] = l
            old = top[group]
            new = jnp.maximum(old, jnp.maximum(l[:, :UNIT], l[:, UNIT:]))
            terms = jnp.exp(l[:, :UNIT] - new) + jnp.exp(l[:, UNIT:] - new)
            norm[group] = norm[group] * jnp.exp(old - new) + terms
            top[group] = new

    for group in range(groups):
        lanes = top[group]
        high = jnp.broadcast_to(jnp.max(lanes, axis=-1, keepdims=True), lanes.shape)
        whole = jnp.sum(norm[group] * jnp.exp(lanes - high), axis=-1, keepdims=True)
        top[group] = high + jnp.log(jnp.broadcast_to(whole, lanes.shape))

    @pl.loop(0, chunks)
    def _(chunk):
        for group in range(groups):
            p = jnp.exp(logit[chunk, group] - twice(top[group])).astype(jnp.bfloat16)
            prob[chunk, :, group * CHUNK : (group + 1) * CHUNK] = p
            a = dot_nn(mix_ref[2], p).astype(jnp.bfloat16)
            mixed[chunk, :, GROUP * group : GROUP * (group + 1), :] = a.reshape(heads, GROUP, CHUNK)
        keep(chunk, 1).start()
        keep(chunk, 2).start()
        for quad in range(quads):
            a = mixed[chunk, quad * per_quad : (quad + 1) * per_quad].reshape(per_quad * UNIT, CHUNK)
            o = own_lanes(dot_nn(a, keys(v_ref, chunk, quad)), lane_head, per_quad)
            total[:, quad * CHUNK : (quad + 1) * CHUNK] += o

    att_ref[0, 0] = total[...].astype(jnp.bfloat16)

    @pl.loop(0, chunks)
    def _(chunk):
        for kind in range(3):
            keep(chunk, kind).wait()


def attention_specs(q, k, heads):
    per_row, micros, _, width = q.shape
    wide = heads * GROUP
    return (
        pl.BlockSpec((1, 1, UNIT, width), lambda m, u, _: (u, m, 0, 0)),
        pl.BlockSpec((k.shape[0], 1, UNIT, width), lambda m, u, _: (0, m, 0, 0)),
        pl.BlockSpec((4, wide, wide), lambda m, u, _: (0, 0, 0)),
    )


def kept_shapes(heads):
    wide = heads * GROUP
    flat = (MAX_CHUNKS, wide, UNIT // GROUP * CHUNK)
    return (flat, flat, (MAX_CHUNKS, heads, UNIT, CHUNK))


def attention_fwd(blocks, q, k, v, mixes, heads):
    per_row, micros, _, width = q.shape
    wide = heads * GROUP
    groups = UNIT // GROUP
    quads = width // CHUNK
    unit_spec, kv_spec, mix_spec = attention_specs(q, k, heads)
    kept = kept_shapes(heads)
    anywhere = pl.BlockSpec(memory_space=pl.ANY)
    return pl.pallas_call(
        partial(fwd_kernel, heads),
        grid_spec=pltpu.PrefetchScalarGridSpec(
            num_scalar_prefetch=1,
            grid=(micros, per_row),
            in_specs=[unit_spec, kv_spec, kv_spec, mix_spec],
            out_specs=[unit_spec, anywhere, anywhere, anywhere],
            scratch_shapes=[pltpu.VMEM((quads, heads // quads * UNIT, CHUNK), jnp.bfloat16)]
            + [pltpu.VMEM(shape, jnp.bfloat16) for shape in kept]
            + [
                pltpu.VMEM((MAX_CHUNKS, groups, wide, CHUNK), jnp.float32),
                pltpu.VMEM((groups, wide, UNIT), jnp.float32),
                pltpu.VMEM((groups, wide, UNIT), jnp.float32),
                pltpu.VMEM((UNIT, width), jnp.float32),
                pltpu.SemaphoreType.DMA((3, MAX_CHUNKS)),
            ],
        ),
        out_shape=[jax.ShapeDtypeStruct(q.shape, jnp.bfloat16)]
        + [jax.ShapeDtypeStruct((per_row, micros) + shape, jnp.bfloat16) for shape in kept],
        compiler_params=pltpu.CompilerParams(vmem_limit_bytes=50 * 1024 * 1024),
        cost_estimate=pl.CostEstimate(flops=20_000_000_000, bytes_accessed=30_000_000, transcendentals=0),
        name="attention_fwd",
    )(blocks, q, k, v, mixes)


def bwd_kernel(heads, blocks_ref, q_ref, k_ref, v_ref, do_ref, mix_ref, score_in, prob_in, mixed_in,
               dq_ref, dk_ref, dv_ref, gl_ref, gp_ref,
               qxt, dox, doxt, score, prob, mixed, grad_prob, grad_mixed, grad_logit, grad_score,
               delta, dq_total, dk_total, dv_total, sems):
    micro, inner, per_row = (pl.program_id(0), pl.program_id(1), pl.num_programs(1))
    step = micro * per_row + inner
    slot = step % 2
    blocks = blocks_ref[step]
    chunks = (blocks + 1) // 2
    key_units = k_ref.shape[0]
    last_unit = key_units - per_row + inner + 1
    quads = q_ref.shape[3] // CHUNK
    per_quad = heads // quads
    groups = UNIT // GROUP
    wide = heads * GROUP
    lane_head = lax.broadcasted_iota(jnp.int32, (UNIT, CHUNK), 1) // (CHUNK // per_quad)
    row_head = lax.broadcasted_iota(jnp.int32, (CHUNK, UNIT), 0) // (CHUNK // per_quad)
    lowest = key_units
    for other in range(key_units - 7):
        its_chunks = (blocks_ref[micro * per_row + other] + 1) // 2
        lowest = jnp.minimum(lowest, key_units - per_row + other + 1 - 2 * its_chunks)

    def fetch(at, chunk, kind):
        source, target = ((score_in, score), (prob_in, prob), (mixed_in, mixed))[kind]
        place = source.at[at % per_row, at // per_row, chunk]
        return pltpu.make_async_copy(place, target.at[at % 2, chunk], sems.at[kind, at % 2, chunk])

    def fetch_all(at):
        @pl.loop(0, (blocks_ref[at] + 1) // 2)
        def _(chunk):
            for kind in (1, 2, 0):
                fetch(at, chunk, kind).start()

    @pl.when(step == 0)
    def _():
        fetch_all(0)
        gl_ref[...] = jnp.zeros_like(gl_ref)
        gp_ref[...] = jnp.zeros_like(gp_ref)

    @pl.when(step + 1 < pl.num_programs(0) * per_row)
    def _():
        fetch_all(step + 1)

    @pl.when(inner == 0)
    def _():
        @pl.loop(lowest, key_units)
        def _(key_unit):
            dk_total[key_unit] = jnp.zeros_like(dk_total[key_unit])
            dv_total[key_unit] = jnp.zeros_like(dv_total[key_unit])

    def spread_turned(rows, quad):
        turned = rows[:, quad * CHUNK : (quad + 1) * CHUNK].T
        zero = jnp.zeros_like(turned)
        return jnp.concatenate([jnp.where(row_head == head, turned, zero) for head in range(per_quad)], axis=1)

    for quad in range(quads):
        qxt[quad] = spread_turned(q_ref[0, 0], quad)
        dox[quad] = spread_heads(do_ref[0, 0], lane_head, quad, per_quad)
        doxt[quad] = spread_turned(do_ref[0, 0], quad)
    dq_total[...] = jnp.zeros_like(dq_total)
    delta[...] = jnp.zeros_like(delta)

    def keys(ref, chunk, quad):
        units = pl.ds(last_unit - 2 * (chunk + 1), 2)
        return ref[units, 0, :, quad * CHUNK : (quad + 1) * CHUNK].reshape(CHUNK, CHUNK)

    def add_to(total, chunk, quad, term):
        first = last_unit - 2 * (chunk + 1)
        lanes = slice(quad * CHUNK, (quad + 1) * CHUNK)
        total[first, lanes, :] += term[:, :UNIT]
        total[first + 1, lanes, :] += term[:, UNIT:]

    @pl.loop(0, chunks)
    def _(chunk):
        for quad in range(quads):
            put_groups(grad_mixed, quad, per_quad, dot_nt(dox[quad], keys(v_ref, chunk, quad)))
        fetch(step, chunk, 1).wait()
        for group in range(groups):
            cols = slice(group * CHUNK, (group + 1) * CHUNK)
            dp = dot_nn(mix_ref[3], grad_mixed[:, cols])
            grad_prob[chunk, :, cols] = dp.astype(grad_prob.dtype)
            term = prob[slot, chunk, :, cols].astype(jnp.float32) * dp
            delta[group] += term[:, :UNIT] + term[:, UNIT:]
        gp_ref[...] += dot_nt(prob[slot, chunk], grad_mixed[...])
        fetch(step, chunk, 2).wait()
        for quad in range(quads):
            a = mixed[slot, chunk, quad * per_quad : (quad + 1) * per_quad].reshape(per_quad * UNIT, CHUNK)
            add_to(dv_total, chunk, quad, dot_nn(doxt[quad], a))

    for group in range(groups):
        delta[group] = jnp.broadcast_to(jnp.sum(delta[group], axis=-1, keepdims=True), (wide, UNIT))

    @pl.loop(0, chunks)
    def _(chunk):
        for group in range(groups):
            cols = slice(group * CHUNK, (group + 1) * CHUNK)
            dp = grad_prob[chunk, :, cols].astype(jnp.float32) - twice(delta[group])
            dl = (prob[slot, chunk, :, cols].astype(jnp.float32) * dp).astype(jnp.bfloat16)
            grad_logit[:, cols] = dl
            ds = dot_nn(mix_ref[1], dl).astype(jnp.bfloat16)
            grad_score[:, GROUP * group : GROUP * (group + 1), :] = ds.reshape(heads, GROUP, CHUNK)
        fetch(step, chunk, 0).wait()
        gl_ref[...] += dot_nt(score[slot, chunk], grad_logit[...])
        for quad in range(quads):
            ds = grad_score[quad * per_quad : (quad + 1) * per_quad].reshape(per_quad * UNIT, CHUNK)
            dq = own_lanes(dot_nn(ds, keys(k_ref, chunk, quad)), lane_head, per_quad)
            dq_total[:, quad * CHUNK : (quad + 1) * CHUNK] += dq
            add_to(dk_total, chunk, quad, dot_nn(qxt[quad], ds))

    dq_ref[0, 0] = (dq_total[...] * 0.125).astype(jnp.bfloat16)

    @pl.when(inner == per_row - 1)
    def _():
        @pl.loop(0, lowest)
        def _(key_unit):
            dk_ref[key_unit, 0] = jnp.zeros_like(dk_ref[key_unit, 0])
            dv_ref[key_unit, 0] = jnp.zeros_like(dv_ref[key_unit, 0])

        @pl.loop(lowest, key_units)
        def _(key_unit):
            dk_ref[key_unit, 0] = dk_total[key_unit].astype(jnp.bfloat16).T
            dv_ref[key_unit, 0] = dv_total[key_unit].astype(jnp.bfloat16).T


def attention_bwd(blocks, q, k, v, grad_out, kept, mixes, heads):
    per_row, micros, _, width = q.shape
    key_units = k.shape[0]
    wide = heads * GROUP
    groups = UNIT // GROUP
    quads = width // CHUNK
    turned = (quads, CHUNK, heads // quads * UNIT)
    unit_spec, kv_spec, mix_spec = attention_specs(q, k, heads)
    sum_spec = pl.BlockSpec((wide, wide), lambda m, u, _: (0, 0))
    anywhere = pl.BlockSpec(memory_space=pl.ANY)
    return pl.pallas_call(
        partial(bwd_kernel, heads),
        grid_spec=pltpu.PrefetchScalarGridSpec(
            num_scalar_prefetch=1,
            grid=(micros, per_row),
            in_specs=[unit_spec, kv_spec, kv_spec, unit_spec, mix_spec] + [anywhere] * 3,
            out_specs=[unit_spec, kv_spec, kv_spec, sum_spec, sum_spec],
            scratch_shapes=[
                pltpu.VMEM(turned, jnp.bfloat16),
                pltpu.VMEM((quads, heads // quads * UNIT, CHUNK), jnp.bfloat16),
                pltpu.VMEM(turned, jnp.bfloat16),
            ]
            + [pltpu.VMEM((2,) + shape, jnp.bfloat16) for shape in kept_shapes(heads)]
            + [
                pltpu.VMEM((MAX_CHUNKS, wide, groups * CHUNK), jnp.bfloat16),
                pltpu.VMEM((wide, groups * CHUNK), jnp.bfloat16),
                pltpu.VMEM((wide, groups * CHUNK), jnp.bfloat16),
                pltpu.VMEM((heads, UNIT, CHUNK), jnp.bfloat16),
                pltpu.VMEM((groups, wide, UNIT), jnp.float32),
                pltpu.VMEM((UNIT, width), jnp.float32),
                pltpu.VMEM((key_units, width, UNIT), jnp.float32),
                pltpu.VMEM((key_units, width, UNIT), jnp.float32),
                pltpu.SemaphoreType.DMA((3, 2, MAX_CHUNKS)),
            ],
        ),
        out_shape=[
            jax.ShapeDtypeStruct(q.shape, jnp.bfloat16),
            jax.ShapeDtypeStruct(k.shape, jnp.bfloat16),
            jax.ShapeDtypeStruct(v.shape, jnp.bfloat16),
            jax.ShapeDtypeStruct((wide, wide), jnp.float32),
            jax.ShapeDtypeStruct((wide, wide), jnp.float32),
        ],
        compiler_params=pltpu.CompilerParams(vmem_limit_bytes=58 * 1024 * 1024),
        cost_estimate=pl.CostEstimate(flops=45_000_000_000, bytes_accessed=40_000_000, transcendentals=0),
        name="attention_bwd",
    )(blocks, q, k, v, grad_out, mixes, *kept)


def piece_bases(key_units, per_row):
    sizes = [1] + [per_row] * ((key_units - 1) // per_row)
    return [(sum(sizes[:at]), size) for at, size in enumerate(sizes)]


def project_kernel(low_ref, *refs):
    pieces, (w_q, w_k, w_v, q_ref, k_ref, v_ref) = (refs[:-6], refs[-6:])
    key_units, width = (k_ref.shape[0], k_ref.shape[3])
    per_row = q_ref.shape[0]
    low = low_ref[pl.program_id(0)]

    for piece, (base, size) in zip(pieces, piece_bases(key_units, per_row)):
        @pl.when(base + size > low)
        def _():
            rows = piece[:, 0].reshape(size * UNIT, width)
            k_ref[base : base + size, 0] = dot_nn(rows, w_k[...]).astype(jnp.bfloat16).reshape(size, UNIT, width)
            v_ref[base : base + size, 0] = dot_nn(rows, w_v[...]).astype(jnp.bfloat16).reshape(size, UNIT, width)

    rows = pieces[-1][:, 0].reshape(per_row * UNIT, width)
    query = dot_nn(rows, w_q[...]).astype(jnp.bfloat16) * jnp.bfloat16(0.125)
    q_ref[:, 0] = query.reshape(per_row, UNIT, width)


def project(low, pieces, weights):
    micros, width = pieces[0].shape[1], pieces[0].shape[3]
    key_units = sum(piece.shape[0] for piece in pieces)
    per_row = pieces[-1].shape[0]

    def spec(units):
        return pl.BlockSpec((units, 1, UNIT, width), lambda m, _: (0, m, 0, 0))

    weight_spec = pl.BlockSpec((width, width), lambda m, _: (0, 0))
    shapes = [(units, micros, UNIT, width) for units in (per_row, key_units, key_units)]
    return pl.pallas_call(
        project_kernel,
        grid_spec=pltpu.PrefetchScalarGridSpec(
            num_scalar_prefetch=1,
            grid=(micros,),
            in_specs=[spec(piece.shape[0]) for piece in pieces] + [weight_spec] * 3,
            out_specs=[spec(shape[0]) for shape in shapes],
        ),
        out_shape=[jax.ShapeDtypeStruct(shape, jnp.bfloat16) for shape in shapes],
        compiler_params=pltpu.CompilerParams(vmem_limit_bytes=44 * 1024 * 1024),
        cost_estimate=pl.CostEstimate(flops=6_000_000_000, bytes_accessed=15_000_000, transcendentals=0),
        name="project",
    )(low, *pieces, *weights)


def project_back_kernel(low_ref, dq_ref, dk_ref, dv_ref, w_q, w_k, w_v, *refs):
    key_units, width = (dk_ref.shape[0], dk_ref.shape[3])
    per_row = dq_ref.shape[0]
    micro = pl.program_id(0)
    low = low_ref[micro]
    bases = piece_bases(key_units, per_row)
    pieces, outs, (grad_ref, total) = (refs[: len(bases)], refs[len(bases) : 2 * len(bases)], refs[-2:])

    @pl.when(micro == 0)
    def _():
        total[...] = jnp.zeros_like(total)

    def keys(ref, base, size):
        return ref[base : base + size, 0].reshape(size * UNIT, width)

    def from_keys(piece, base, size):
        grad_key, grad_value = (keys(dk_ref, base, size), keys(dv_ref, base, size))
        turned = piece[:, 0].reshape(size * UNIT, width).T
        total[1] += dot_nn(turned, grad_key)
        total[2] += dot_nn(turned, grad_value)
        return dot_nt(grad_key, w_k[...]) + dot_nt(grad_value, w_v[...]), turned

    for piece, out, (base, size) in zip(pieces[:-1], outs[:-1], bases[:-1]):
        @pl.when(base + size > low)
        def _():
            term, _ = from_keys(piece, base, size)
            out[:, 0] = term.astype(jnp.bfloat16).reshape(size, UNIT, width)

        @pl.when(base + size <= low)
        def _():
            out[...] = jnp.zeros_like(out)

    term, turned = from_keys(pieces[-1], *bases[-1])
    grad_query = keys(dq_ref, 0, per_row)
    total[0] += dot_nn(turned, grad_query)
    outs[-1][:, 0] = (term + dot_nt(grad_query, w_q[...])).reshape(per_row, UNIT, width)

    @pl.when(micro == pl.num_programs(0) - 1)
    def _():
        grad_ref[...] = total[...].astype(jnp.bfloat16)


def project_back(low, grad_query, grad_key, grad_value, weights, pieces):
    per_row, micros, _, width = grad_query.shape
    key_units = grad_key.shape[0]

    def spec(units):
        return pl.BlockSpec((units, 1, UNIT, width), lambda m, _: (0, m, 0, 0))

    weight_spec = pl.BlockSpec((width, width), lambda m, _: (0, 0))
    sizes = [size for _, size in piece_bases(key_units, per_row)]
    shapes = [(size, micros, UNIT, width) for size in sizes]
    kinds = [jnp.bfloat16] * (len(sizes) - 1) + [jnp.float32]
    return pl.pallas_call(
        project_back_kernel,
        grid_spec=pltpu.PrefetchScalarGridSpec(
            num_scalar_prefetch=1,
            grid=(micros,),
            in_specs=[spec(per_row), spec(key_units), spec(key_units)]
            + [weight_spec] * 3
            + [spec(size) for size in sizes],
            out_specs=[spec(size) for size in sizes] + [pl.BlockSpec((3, width, width), lambda m, _: (0, 0, 0))],
            scratch_shapes=[pltpu.VMEM((3, width, width), jnp.float32)],
        ),
        out_shape=[jax.ShapeDtypeStruct(shape, kind) for shape, kind in zip(shapes, kinds)]
        + [jax.ShapeDtypeStruct((3, width, width), jnp.bfloat16)],
        compiler_params=pltpu.CompilerParams(vmem_limit_bytes=52 * 1024 * 1024),
        cost_estimate=pl.CostEstimate(flops=12_000_000_000, bytes_accessed=20_000_000, transcendentals=0),
        name="project_back",
    )(low, grad_query, grad_key, grad_value, *weights, *pieces)


def feed_kernel(x_ref, att_ref, w_o_ref, gain_ref, up_ref, down_ref, cot_ref,
                mid_ref, out_ref, grad_hidden_ref, grad_up_ref, grad_down_ref,
                hidden, turned, out_total, back_total):
    step = pl.program_id(0)

    @pl.when(step == 0)
    def _():
        middle = x_ref[...].astype(jnp.float32) + dot_nn(att_ref[...], w_o_ref[...])
        mid_ref[...] = middle
        inv_rms = lax.rsqrt(jnp.mean(middle * middle, axis=-1, keepdims=True) + norm_eps)
        rows = (middle * inv_rms * gain_ref[...]).astype(jnp.bfloat16)
        hidden[...] = rows
        turned[...] = rows.T
        out_total[...] = jnp.zeros_like(out_total)
        back_total[...] = jnp.zeros_like(back_total)

    for start in range(0, up_ref.shape[2], FF_STEP):
        cols = slice(start, start + FF_STEP)
        up = dot_nn(hidden[...], up_ref[0, :, cols])
        square = up * up
        bent = jnp.tanh(gelu_scale * up * (1.0 + gelu_cube * square))
        half = 0.5 + 0.5 * bent
        slope = half + 0.5 * up * (1.0 - bent * bent) * (gelu_scale * (1.0 + 3.0 * gelu_cube * square))
        active = (up * half).astype(jnp.bfloat16)
        grad_up = (dot_nt(cot_ref[...], down_ref[cols, :]) * slope).astype(jnp.bfloat16)
        out_total[...] += dot_nn(active, down_ref[cols, :])
        back_total[...] += dot_nt(grad_up, up_ref[0, :, cols])
        grad_down_ref[cols, :] = dot_nn(active.T, cot_ref[...]).astype(jnp.bfloat16)
        grad_up_ref[0, :, cols] = dot_nn(turned[...], grad_up).astype(jnp.bfloat16)

    @pl.when(step == pl.num_programs(0) - 1)
    def _():
        out_ref[...] = (mid_ref[...] + out_total[...]).astype(jnp.bfloat16)
        grad_hidden_ref[...] = back_total[...]


def feed_forward(rows, attended, w_o, gain, w_up, w_down, cot):
    tokens, width = rows.shape
    pieces = w_up.shape[0]
    whole = pl.BlockSpec((tokens, width), lambda i: (0, 0))
    up_spec = pl.BlockSpec((1, width, width), lambda i: (i, 0, 0))
    down_spec = pl.BlockSpec((width, width), lambda i: (i, 0))
    f32, bf16 = (jnp.float32, jnp.bfloat16)
    return pl.pallas_call(
        feed_kernel,
        grid=(pieces,),
        in_specs=[
            whole,
            whole,
            pl.BlockSpec((width, width), lambda i: (0, 0)),
            pl.BlockSpec((1, width), lambda i: (0, 0)),
            up_spec,
            down_spec,
            whole,
        ],
        out_specs=[whole, whole, whole, up_spec, down_spec],
        out_shape=[
            jax.ShapeDtypeStruct((tokens, width), f32),
            jax.ShapeDtypeStruct((tokens, width), bf16),
            jax.ShapeDtypeStruct((tokens, width), f32),
            jax.ShapeDtypeStruct(w_up.shape, bf16),
            jax.ShapeDtypeStruct(w_down.shape, bf16),
        ],
        scratch_shapes=[
            pltpu.VMEM((tokens, width), bf16),
            pltpu.VMEM((width, tokens), bf16),
            pltpu.VMEM((tokens, width), f32),
            pltpu.VMEM((tokens, width), f32),
        ],
        compiler_params=pltpu.CompilerParams(vmem_limit_bytes=48 * 1024 * 1024),
        cost_estimate=pl.CostEstimate(flops=16_000_000_000, bytes_accessed=30_000_000, transcendentals=0),
        name="feed_forward",
    )(rows, attended, w_o, gain, w_up, w_down, cot)


def spread_mixes(mix_logits, mix_weights):
    heads = mix_logits.shape[0]
    wide = heads * GROUP
    place = jnp.arange(wide, dtype=jnp.int32)
    pick = (place[:, None] // GROUP == jnp.arange(heads, dtype=jnp.int32)[None, :]).astype(mix_logits.dtype)
    same_row = (place[:, None] % GROUP == place[None, :] % GROUP)[None]
    tables = jnp.stack([mix_logits.T, mix_logits, mix_weights.T, mix_weights]).reshape(4 * heads, heads)
    across = jnp.dot(tables, pick.T, preferred_element_type=jnp.float32).astype(mix_logits.dtype)
    down = jnp.einsum("wh,bhx->bwx", pick, across.reshape(4, heads, wide), preferred_element_type=jnp.float32)
    return jnp.where(same_row, down, 0.0).astype(mix_logits.dtype)


def fold_mix(wide, heads):
    place = jnp.arange(heads * GROUP, dtype=jnp.int32)
    pick = (place[:, None] // GROUP == jnp.arange(heads, dtype=jnp.int32)[None, :]).astype(jnp.float32)
    same_row = place[:, None] % GROUP == place[None, :] % GROUP
    down = jnp.dot(pick.T, jnp.where(same_row, wide, 0.0), precision=lax.Precision.HIGHEST)
    return jnp.dot(down, pick, precision=lax.Precision.HIGHEST)


def from_behind(value, steps):
    count = lax.axis_size("dev")
    first, last = (max(0, -steps), min(count, count - steps))
    return lax.ppermute(value, "dev", [(source, source + steps) for source in range(first, last)])


def with_sibling(value):
    count = lax.axis_size("dev")
    return lax.ppermute(value, "dev", [(source, source ^ 1) for source in range(count)])


def earlier_rows(own):
    size = own.shape[0]
    first_core = lax.axis_index("dev") % 2 == 0
    two, four = (from_behind(own, 2), from_behind(own, 4))
    give = jnp.concatenate([jnp.where(first_core, own, two), jnp.where(first_core, two, four)], axis=0)
    came = with_sibling(give)
    return [four[size - 1 :], came[size:], two, came[:size], own]


def return_rows(four, two, came, grad_own):
    size = two.shape[0]
    first_core = lax.axis_index("dev") % 2 == 0
    came = came.astype(jnp.float32)
    one, three = (came[:size], came[size:])
    give_two = two.astype(jnp.float32) + jnp.where(first_core, three, one)
    padded = jnp.pad(four.astype(jnp.float32), ((size - four.shape[0], 0), (0, 0), (0, 0), (0, 0)))
    give_four = padded + jnp.where(first_core, 0.0, three)
    back_two = from_behind(give_two.astype(jnp.bfloat16), -2).astype(jnp.float32)
    back_four = from_behind(give_four.astype(jnp.bfloat16), -4).astype(jnp.float32)
    return grad_own + jnp.where(first_core, one, 0.0) + back_two + back_four


def seq_starts(lengths_row, query_rows):
    seq_ends = jnp.cumsum(lengths_row)
    starts = seq_ends - lengths_row
    return jnp.max(jnp.where(starts[None, :] <= query_rows[:, None], starts[None, :], 0), axis=1)


def normalize(values, gain_vec):
    inv_rms = lax.rsqrt(jnp.mean(values * values, axis=-1, keepdims=True) + norm_eps)
    normed = values * inv_rms
    return (normed, inv_rms, (normed * gain_vec.astype(jnp.float32)).astype(jnp.bfloat16))


def norm_back(grad_hidden, normed, inv_rms, gain_vec):
    grad_gain = jnp.sum(grad_hidden * normed, axis=0)
    grad_normed = grad_hidden * gain_vec.astype(jnp.float32)
    inner_mean = jnp.mean(grad_normed * normed, axis=-1, keepdims=True)
    return (inv_rms * (grad_normed - normed * inner_mean), grad_gain)


def matmul(left, right):
    return jnp.dot(left, right, preferred_element_type=jnp.float32)


def matmul_left_t(left, right):
    return lax.dot_general(left, right, (((0,), (0,)), ((), ())), preferred_element_type=jnp.float32)


def matmul_right_t(left, right):
    return lax.dot_general(left, right, (((1,), (1,)), ((), ())), preferred_element_type=jnp.float32)


def exchange(value):
    return lax.all_to_all(value, "dev", split_axis=0, concat_axis=0, tiled=True)


def split_ids(tok_ids, own_rows):
    owner = tok_ids // own_rows
    place = jnp.arange(tok_ids.shape[0], dtype=jnp.int32)
    same = tok_ids[:, None] == tok_ids[None, :]
    repeated = jnp.any(same & (place[None, :] < place[:, None]), axis=1)
    before = (owner[:, None] == owner[None, :]) & (tok_ids[None, :] < tok_ids[:, None]) & ~repeated[None, :]
    return (owner, tok_ids % own_rows, jnp.sum(before, axis=1, dtype=jnp.int32))


def ask_round(ids, index, own_rows, stride, room):
    count = lax.axis_size("dev")
    owner, local, rank = ids
    here = rank - index * room
    slot = jnp.where((here >= 0) & (here < room), owner * stride + here, -1)
    chosen = slot[None, :] == jnp.arange(count * stride, dtype=jnp.int32)[:, None]
    wanted = jnp.max(jnp.where(chosen, local[None, :], -1), axis=1).reshape(count, stride)
    rounds = jnp.broadcast_to(jnp.max(rank) // room + 1, (count, stride))
    return (jnp.concatenate([wanted, rounds], axis=1), chosen.astype(jnp.bfloat16))


def hear_round(message, own_rows, stride):
    asked = exchange(message)
    pick = asked[:, :stride].reshape(-1, 1) == jnp.arange(own_rows, dtype=jnp.int32)[None, :]
    return (pick.astype(jnp.bfloat16), jnp.max(asked[:, stride:]))


def plan_round(ids, index, own_rows, stride, room):
    message, chosen = ask_round(ids, index, own_rows, stride, room)
    pick, _ = hear_round(message, own_rows, stride)
    return (chosen, pick)


def answer(embedding, chosen, pick, stride, extra_row):
    count = lax.axis_size("dev")
    rows = matmul(pick, embedding).astype(jnp.bfloat16).reshape(count, stride, -1)
    if extra_row is not None:
        is_extra = (jnp.arange(stride, dtype=jnp.int32) == stride - 1)[None, :, None]
        rows = jnp.where(is_extra, extra_row[None, None, :], rows)
    got = exchange(rows.reshape(count * stride, -1))
    return (matmul_left_t(chosen, got).astype(jnp.bfloat16), got.reshape(count, stride, -1)[:, stride - 1])


def lookup(embedding, ids, message, chosen, extra_row, stride, room):
    own_rows = embedding.shape[0]
    pick, rounds = hear_round(message, own_rows, stride)
    first, extra = answer(embedding, chosen, pick, stride, extra_row)

    def more(carry):
        index, rows = carry
        again, its_pick = plan_round(ids, index, own_rows, stride, room)
        return (index + 1, rows + answer(embedding, again, its_pick, stride, None)[0])

    _, rows = lax.while_loop(lambda carry: carry[0] < rounds, more, (jnp.int32(1), first))
    return (rows, extra, ids, chosen, pick, rounds)


def send_grads(grad_low, chosen, pick, stride, extra_rows, beside=None):
    count = lax.axis_size("dev")
    summed = matmul(chosen, grad_low).astype(jnp.bfloat16).reshape(count, stride, -1)
    if extra_rows is not None:
        place = jnp.arange(stride, dtype=jnp.int32)[None, :, None]
        high, low = extra_rows
        summed = jnp.where(place == stride - 2, high[:, None, :], summed)
        summed = jnp.where(place == stride - 1, low[:, None, :], summed)
    summed, beside = lax.optimization_barrier((summed.reshape(count * stride, -1), beside))
    got = exchange(summed)
    return (matmul_left_t(pick, got), got.reshape(count, stride, -1)[:, stride - 2 :], beside)


def table_back(grad_rows, extra_rows, plan, own_rows, stride, room, beside):
    ids, chosen, pick, rounds = plan
    grad_low = grad_rows.astype(jnp.bfloat16)
    first, extra, beside = send_grads(grad_low, chosen, pick, stride, extra_rows, beside)

    def more(carry):
        index, total = carry
        again, its_pick = plan_round(ids, index, own_rows, stride, room)
        return (index + 1, total + send_grads(grad_low, again, its_pick, stride, None)[0])

    _, total = lax.while_loop(lambda carry: carry[0] < rounds, more, (jnp.int32(1), first))
    return (total, jnp.sum(extra.astype(jnp.float32), axis=(0, 1)), beside)


def double(held, bit, axis):
    count = lax.axis_size("dev")
    low = ((lax.axis_index("dev") >> bit) & 1) == 0
    came = lax.ppermute(held, "dev", [(source, source ^ (1 << bit)) for source in range(count)])
    return jnp.stack([jnp.where(low, held, came), jnp.where(low, came, held)], axis=axis)


def spread_some(held, first, last):
    bits = lax.axis_size("dev").bit_length() - 1
    for done in range(first, min(last, bits)):
        held = double(held, bits - 1 - done, done)
    return held


def gather_late(pieces, part, up_cols):
    width = pieces[0].shape[1]
    whole = lax.all_gather(jnp.concatenate(pieces, axis=0), "dev", axis=0)
    middle = part * (1 + up_cols)
    up = whole[:, part:middle].reshape(-1, up_cols, part, width).swapaxes(0, 1)
    return (whole[:, :part].reshape(-1, width), up.reshape(up_cols, -1, width), whole[:, middle:].reshape(-1, width))


def split_rows(summed, sizes):
    pieces, start = ([], 0)
    for size in sizes:
        pieces.append(summed[start : start + size])
        start += size
    return pieces


def swap_parts(held, bit):
    count = lax.axis_size("dev")
    mine = (lax.axis_index("dev") >> bit) & 1
    keep = lax.dynamic_index_in_dim(held, mine, 0, keepdims=False)
    give = lax.dynamic_index_in_dim(held, 1 - mine, 0, keepdims=False)
    return (keep, lax.ppermute(give, "dev", [(source, source ^ (1 << bit)) for source in range(count)]))


def join_parts(parts, last=False):
    total = parts[0].astype(jnp.float32) + parts[1].astype(jnp.float32)
    return total if last else total.astype(jnp.bfloat16)


def swap_halves(held, bit, last=False):
    return join_parts(swap_parts(held, bit), last)


def middle_bits():
    return list(range(1, lax.axis_size("dev").bit_length() - 2))


def give_core(grid, axis):
    other = 1 - lax.axis_index("dev") % 2
    return with_sibling(lax.dynamic_index_in_dim(grid, other, axis, keepdims=False))


def first_bits():
    middle = middle_bits()
    return [middle[turn % len(middle)] for turn in range(3)]


def sum_cores(term):
    count, pieces, rows, width = term.shape
    grid = term.reshape(count // 2, 2, pieces, rows, width)
    return swap_halves(grid.swapaxes(0, 1), 0).reshape(count // 2, pieces * rows, width)


def merge_kernel(core_ref, down_ref, down_came_ref, up_ref, up_came_ref, *outs):
    rows, width = down_came_ref.shape[-2:]
    down = down_ref[0, 0].astype(jnp.float32) + down_came_ref[0].astype(jnp.float32)
    up = up_ref[:, 0, 0].astype(jnp.float32) + up_came_ref[:, 0].astype(jnp.float32)
    whole = jnp.concatenate([down, up.reshape(-1, width)], axis=0).astype(jnp.bfloat16)
    for turn, out in enumerate(outs):
        out[0] = whole[:, turn * (width // 3) : (turn + 1) * (width // 3)]


def merge_cores(grad_down, grad_up):
    count = lax.axis_size("dev")
    up_cols, _, width = grad_up.shape
    half = count // 2
    down = grad_down.reshape(half, 2, -1, width)
    up = grad_up.reshape(up_cols, half, 2, -1, width)
    down_came, up_came = (give_core(down, 1), give_core(up, 2))
    down_rows, up_rows = (down.shape[2], up.shape[3])
    rows = down_rows + up_cols * up_rows
    middle = middle_bits()
    bits = len(middle) + 1

    def out_index(turn):
        shift = turn % len(middle)
        order = middle[shift:] + middle[:shift] + [bits]

        def index(dest, _):
            place = 0
            for bit in order:
                place = place * 2 + (dest >> (bit - 1)) % 2
            return (place, 0, 0)

        return index

    third = width // 3
    merged = pl.pallas_call(
        merge_kernel,
        grid_spec=pltpu.PrefetchScalarGridSpec(
            num_scalar_prefetch=1,
            grid=(half,),
            in_specs=[
                pl.BlockSpec((1, 1, down_rows, width), lambda dest, core: (dest, core[0], 0, 0)),
                pl.BlockSpec((1, down_rows, width), lambda dest, core: (dest, 0, 0)),
                pl.BlockSpec((up_cols, 1, 1, up_rows, width), lambda dest, core: (0, dest, core[0], 0, 0)),
                pl.BlockSpec((up_cols, 1, up_rows, width), lambda dest, core: (0, dest, 0, 0)),
            ],
            out_specs=[pl.BlockSpec((1, rows, third), out_index(turn)) for turn in range(3)],
        ),
        out_shape=[jax.ShapeDtypeStruct((half, rows, third), jnp.bfloat16)] * 3,
        cost_estimate=pl.CostEstimate(flops=20_000_000, bytes_accessed=16_000_000, transcendentals=0),
        name="merge_cores",
    )(lax.axis_index("dev").reshape(1) % 2, down, down_came, up, up_came)
    return [out.reshape((2,) * bits + (rows, third)) for out in merged]


def cut_thirds(held):
    _, rows, width = held.shape
    middle = middle_bits()
    bits = len(middle) + 1
    grid = held.reshape((2,) * bits + (rows, width))
    thirds = []
    for turn in range(3):
        shift = turn % len(middle)
        order = middle[shift:] + middle[:shift] + [bits]
        axes = [bits - bit for bit in order]
        part = grid[..., turn * (width // 3) : (turn + 1) * (width // 3)]
        thirds.append(part.transpose(axes + [bits, bits + 1]))
    return thirds


def sum_stage(thirds, stage):
    middle = middle_bits()
    return [swap_halves(third, middle[(turn + stage) % len(middle)]) for turn, third in enumerate(thirds)]


def sum_stages(thirds, first):
    for stage in range(first, len(middle_bits())):
        thirds = sum_stage(thirds, stage)
    return thirds


def sum_last(groups):
    whole = [jnp.concatenate(thirds, axis=-1) for thirds in groups]
    return swap_halves(jnp.concatenate(whole, axis=1), len(middle_bits()) + 1, True)


def split_low(values):
    high = lax.reduce_precision(values, 8, 7)
    return (high.astype(jnp.bfloat16), (values - high).astype(jnp.bfloat16))


def low_units(blocks):
    per_row = blocks.shape[1]
    place = 8 + jnp.arange(per_row, dtype=jnp.int32)[None, :]
    return jnp.min(place - 2 * ((blocks + 1) // 2), axis=1).astype(jnp.int32)


def by_unit(array):
    cut = array.reshape((array.shape[0], array.shape[1] // UNIT, UNIT) + array.shape[2:])
    return cut.swapaxes(0, 1)


def by_row(array, micros):
    cut = array.reshape(-1, micros, UNIT, array.shape[-1])
    return cut.swapaxes(0, 1).reshape(micros, -1, array.shape[-1])


def shards(
    token_ids,
    lengths,
    embedding,
    norm1_gain,
    w_query,
    w_key,
    w_value,
    w_out,
    mix_logits,
    mix_weights,
    norm2_gain,
    w_up,
    w_down,
    cotangent,
):
    count = lax.axis_size("dev")
    me = lax.axis_index("dev")
    micros, row_count = token_ids.shape
    own_rows, width = embedding.shape
    heads = mix_logits.shape[0]
    part = norm1_gain.shape[0]
    per_row = row_count // UNIT
    tokens = micros * row_count
    tok_ids = by_unit(token_ids).reshape(-1)
    stride = max(16, 1024 // count)
    room = stride - 2

    unit_rows = me * row_count + UNIT * jnp.arange(per_row, dtype=jnp.int32)
    begins = jnp.stack([seq_starts(lengths[micro], unit_rows) for micro in range(micros)])
    blocks = ((unit_rows[None, :] - begins) // UNIT + 1).reshape(-1).astype(jnp.int32)

    lows = low_units(blocks.reshape(micros, per_row))
    mixes = spread_mixes(mix_logits, mix_weights)

    up_cols = w_up.shape[1] // width
    up_pieces = [w_up[:, col * width : (col + 1) * width] for col in range(up_cols)]
    first_weights = spread_some(jnp.stack([w_query, w_key, w_value]), 0, 2)
    weight_pieces = [w_out] + up_pieces + [w_down]
    ids = split_ids(tok_ids, own_rows)
    message, chosen = ask_round(ids, 0, own_rows, stride, room)
    message, weight_pieces = lax.optimization_barrier((message, weight_pieces))
    w_o, w_u, w_d = gather_late(weight_pieces, part, up_cols)
    gains_row = jnp.concatenate([norm1_gain, norm2_gain, jnp.zeros((width - 2 * part,), jnp.bfloat16)])
    picked, gains, *plan = lookup(embedding, ids, message, chosen, gains_row, stride, room)
    gain_one = gains[:, :part].reshape(-1)
    gain_two = gains[:, part : 2 * part].reshape(-1)
    first_weights = spread_some(first_weights, 2, 3)
    picked, first_weights = lax.optimization_barrier((picked, first_weights))
    inputs = picked.astype(jnp.float32)

    normed_one, inv_one, hidden_one = normalize(inputs, gain_one)
    own_hidden = hidden_one.reshape(per_row, micros, UNIT, width)
    pieces = earlier_rows(own_hidden)
    first_weights = spread_some(first_weights, 3, 99).reshape(count, 3, part, width)
    w_q, w_k, w_v = (first_weights[:, at].reshape(-1, width) for at in range(3))
    query, key, value = project(lows, pieces, (w_q, w_k, w_v))
    attended, *kept = attention_fwd(blocks, query, key, value, mixes, heads)
    attended = attended.reshape(tokens, width)

    grad_rows = by_unit(cotangent).reshape(tokens, width)
    gain_row = gain_two.astype(jnp.float32)[None, :]
    middle, output, grad_hidden_two, grad_up, grad_down = feed_forward(
        picked, attended, w_o, gain_row, w_u, w_d, grad_rows
    )
    inv_two = lax.rsqrt(jnp.mean(middle * middle, axis=-1, keepdims=True) + norm_eps)
    normed_two = middle * inv_two
    grad_mid_norm, grad_gain_two = norm_back(grad_hidden_two, normed_two, inv_two, gain_two)
    grad_middle = grad_rows.astype(jnp.float32) + grad_mid_norm
    grad_branch = grad_middle.astype(jnp.bfloat16)
    grad_wout = matmul_left_t(attended, grad_branch)
    grad_att = matmul_right_t(grad_branch, w_o).astype(jnp.bfloat16).reshape(own_hidden.shape)
    late = merge_cores(grad_down, grad_up)
    late, grad_att = lax.optimization_barrier((late, grad_att))
    late = [swap_parts(third, bit) for third, bit in zip(late, first_bits())]

    grad_query, grad_key, grad_value, wide_logit, wide_prob = attention_bwd(
        blocks, query, key, value, grad_att, kept, mixes, heads
    )
    late, grad_query, grad_key, grad_value = lax.optimization_barrier((late, grad_query, grad_key, grad_value))
    *terms, grad_own, grad_qkv = project_back(lows, grad_query, grad_key, grad_value, (w_q, w_k, w_v), pieces)
    came = with_sibling(jnp.concatenate([terms[3], terms[1]], axis=0))
    came, grad_qkv = lax.optimization_barrier((came, grad_qkv))
    grad_own = return_rows(terms[0], terms[2], came, grad_own)
    early_terms = jnp.concatenate([grad_qkv, grad_wout.astype(jnp.bfloat16)[None]], axis=0)
    early = sum_cores(early_terms.reshape(4, count, part, width).swapaxes(0, 1))
    early = cut_thirds(early)
    late = sum_stage([join_parts(parts) for parts in late], 1)
    grad_hidden_one = grad_own.reshape(tokens, width)
    grad_in_norm, grad_gain_one = norm_back(grad_hidden_one, normed_one, inv_one, gain_one)
    grad_inputs = grad_middle + grad_in_norm

    mix_terms = jnp.concatenate([fold_mix(wide_logit, heads).reshape(-1), fold_mix(wide_prob, heads).reshape(-1)])
    mix_size = mix_terms.shape[0]
    small = jnp.concatenate(
        [
            grad_gain_one.reshape(count, part),
            grad_gain_two.reshape(count, part),
            jnp.broadcast_to(mix_terms[None, :], (count, mix_size)),
            jnp.zeros((count, width - 2 * part - mix_size), jnp.float32),
        ],
        axis=1,
    )
    table_grad, small_sum, (early, late) = table_back(
        grad_inputs, split_low(small), plan, own_rows, stride, room, (early, late)
    )
    summed = sum_last([sum_stages(early, 0), sum_stages(late, 2)])
    row_sizes = [part] * 4 + [w_down.shape[0]] + [part] * up_cols
    weight_sums = split_rows(summed, row_sizes)
    mixes = small_sum[2 * part : 2 * part + mix_size].reshape(2, heads, heads)
    return (
        by_row(output, micros),
        by_row(grad_inputs, micros),
        table_grad,
        small_sum[:part],
        *weight_sums[:4],
        mixes[0],
        mixes[1],
        small_sum[part : 2 * part],
        jnp.concatenate(weight_sums[5:], axis=1),
        weight_sums[4],
    )


def solution(mesh):
    in_specs = (
        P(None, "dev"),
        P(),
        P("dev", None),
        P("dev"),
        P("dev", None),
        P("dev", None),
        P("dev", None),
        P("dev", None),
        P(),
        P(),
        P("dev"),
        P("dev", None),
        P("dev", None),
        P(None, "dev", None),
    )
    out_specs = (
        P(None, "dev", None),
        P(None, "dev", None),
        P("dev", None),
        P("dev"),
        P("dev", None),
        P("dev", None),
        P("dev", None),
        P("dev", None),
        P(),
        P(),
        P("dev"),
        P("dev", None),
        P("dev", None),
    )
    return jax.shard_map(shards, mesh=mesh, in_specs=in_specs, out_specs=out_specs, check_vma=False)
```

```python
from functools import partial

import jax
import jax.numpy as jnp
from jax import lax
from jax.experimental import pallas as pl
from jax.experimental.pallas import tpu as pltpu
from jax.sharding import PartitionSpec as P

norm_eps = 1e-06
gelu_scale = 0.7978845608028654
gelu_cube = 0.044715
FF_STEP = 256

masked = -1e30
UNIT = 128
CHUNK = 256
GROUP = 16
MAX_CHUNKS = 4


def dot_nn(left, right):
    return lax.dot_general(left, right, (((1,), (0,)), ((), ())), preferred_element_type=jnp.float32)


def dot_nt(left, right):
    return lax.dot_general(left, right, (((1,), (1,)), ((), ())), preferred_element_type=jnp.float32)


def spread_heads(rows, lane_head, quad, heads_per_quad):
    part = rows[:, quad * CHUNK : (quad + 1) * CHUNK]
    zero = jnp.zeros_like(part)
    return jnp.concatenate([jnp.where(lane_head == head, part, zero) for head in range(heads_per_quad)], axis=0)


def own_lanes(wide, lane_head, heads_per_quad):
    total = jnp.where(lane_head == 0, wide[:UNIT], 0.0)
    for head in range(1, heads_per_quad):
        total = total + jnp.where(lane_head == head, wide[head * UNIT : (head + 1) * UNIT], 0.0)
    return total


def allowed_keys(chunk, group, blocks):
    key = lax.broadcasted_iota(jnp.int32, (GROUP, CHUNK), 1) - (UNIT + CHUNK * chunk)
    row = lax.broadcasted_iota(jnp.int32, (GROUP, CHUNK), 0) + GROUP * group
    return (key <= row) & (key >= (1 - blocks) * UNIT)


def twice(rows):
    return jnp.concatenate([rows, rows], axis=-1)


def put_groups(ref, quad, per_quad, term):
    low = term.astype(jnp.bfloat16)
    for head in range(per_quad):
        rows = slice((quad * per_quad + head) * GROUP, (quad * per_quad + head + 1) * GROUP)
        for group in range(UNIT // GROUP):
            start = head * UNIT + group * GROUP
            ref[rows, group * CHUNK : (group + 1) * CHUNK] = low[start : start + GROUP]


def fwd_kernel(heads, blocks_ref, q_ref, k_ref, v_ref, mix_ref, att_ref, score_out, prob_out, mixed_out,
               qx, score, prob, mixed, logit, top, norm, total, sems):
    micro, inner, per_row = (pl.program_id(0), pl.program_id(1), pl.num_programs(1))
    blocks = blocks_ref[micro * per_row + inner]
    chunks = (blocks + 1) // 2
    last_unit = k_ref.shape[0] - per_row + inner + 1
    quads = q_ref.shape[3] // CHUNK
    per_quad = heads // quads
    groups = UNIT // GROUP
    wide = heads * GROUP
    lane_head = lax.broadcasted_iota(jnp.int32, (UNIT, CHUNK), 1) // (CHUNK // per_quad)
    for quad in range(quads):
        qx[quad] = spread_heads(q_ref[0, 0], lane_head, quad, per_quad)
    total[...] = jnp.zeros_like(total)
    top[...] = jnp.full_like(top, masked)
    norm[...] = jnp.zeros_like(norm)

    def keys(ref, chunk, quad):
        units = pl.ds(last_unit - 2 * (chunk + 1), 2)
        return ref[units, 0, :, quad * CHUNK : (quad + 1) * CHUNK].reshape(CHUNK, CHUNK)

    step = micro * per_row + inner

    def keep(at, chunk, kind):
        source, target = ((score, score_out), (prob, prob_out), (mixed, mixed_out))[kind]
        place = target.at[at % per_row, at // per_row, chunk]
        return pltpu.make_async_copy(source.at[chunk], place, sems.at[kind, chunk])

    def finish(at):
        @pl.loop(0, (blocks_ref[at] + 1) // 2)
        def _(chunk):
            for kind in range(3):
                keep(at, chunk, kind).wait()

    @pl.when(step > 0)
    def _():
        finish(step - 1)

    @pl.loop(0, chunks)
    def _(chunk):
        for quad in range(quads):
            put_groups(score.at[chunk], quad, per_quad, dot_nt(qx[quad], keys(k_ref, chunk, quad)))
        keep(step, chunk, 0).start()
        for group in range(groups):
            l = dot_nn(mix_ref[0], score[chunk, :, group * CHUNK : (group + 1) * CHUNK])
            l = jnp.where(allowed_keys(chunk, group, blocks)[None], l.reshape(heads, GROUP, CHUNK), masked)
            l = l.reshape(wide, CHUNK)
            logit[chunk, group] = l
            old = top[group]
            new = jnp.maximum(old, jnp.maximum(l[:, :UNIT], l[:, UNIT:]))
            terms = jnp.exp(l[:, :UNIT] - new) + jnp.exp(l[:, UNIT:] - new)
            norm[group] = norm[group] * jnp.exp(old - new) + terms
            top[group] = new

    for group in range(groups):
        lanes = top[group]
        high = jnp.broadcast_to(jnp.max(lanes, axis=-1, keepdims=True), lanes.shape)
        whole = jnp.sum(norm[group] * jnp.exp(lanes - high), axis=-1, keepdims=True)
        top[group] = high + jnp.log(jnp.broadcast_to(whole, lanes.shape))

    @pl.loop(0, chunks)
    def _(chunk):
        for group in range(groups):
            p = jnp.exp(logit[chunk, group] - twice(top[group])).astype(jnp.bfloat16)
            prob[chunk, :, group * CHUNK : (group + 1) * CHUNK] = p
            a = dot_nn(mix_ref[2], p).astype(jnp.bfloat16)
            mixed[chunk, :, GROUP * group : GROUP * (group + 1), :] = a.reshape(heads, GROUP, CHUNK)
        keep(step, chunk, 1).start()
        keep(step, chunk, 2).start()
        for quad in range(quads):
            a = mixed[chunk, quad * per_quad : (quad + 1) * per_quad].reshape(per_quad * UNIT, CHUNK)
            o = own_lanes(dot_nn(a, keys(v_ref, chunk, quad)), lane_head, per_quad)
            total[:, quad * CHUNK : (quad + 1) * CHUNK] += o

    att_ref[0, 0] = total[...].astype(jnp.bfloat16)

    @pl.when(step == pl.num_programs(0) * per_row - 1)
    def _():
        finish(step)


def attention_specs(q, k, heads):
    per_row, micros, _, width = q.shape
    wide = heads * GROUP
    return (
        pl.BlockSpec((1, 1, UNIT, width), lambda m, u, _: (u, m, 0, 0)),
        pl.BlockSpec((k.shape[0], 1, UNIT, width), lambda m, u, _: (0, m, 0, 0)),
        pl.BlockSpec((4, wide, wide), lambda m, u, _: (0, 0, 0)),
    )


def kept_shapes(heads):
    wide = heads * GROUP
    flat = (MAX_CHUNKS, wide, UNIT // GROUP * CHUNK)
    return (flat, flat, (MAX_CHUNKS, heads, UNIT, CHUNK))


def attention_fwd(blocks, q, k, v, mixes, heads):
    per_row, micros, _, width = q.shape
    wide = heads * GROUP
    groups = UNIT // GROUP
    quads = width // CHUNK
    unit_spec, kv_spec, mix_spec = attention_specs(q, k, heads)
    kept = kept_shapes(heads)
    anywhere = pl.BlockSpec(memory_space=pl.ANY)
    return pl.pallas_call(
        partial(fwd_kernel, heads),
        grid_spec=pltpu.PrefetchScalarGridSpec(
            num_scalar_prefetch=1,
            grid=(micros, per_row),
            in_specs=[unit_spec, kv_spec, kv_spec, mix_spec],
            out_specs=[unit_spec, anywhere, anywhere, anywhere],
            scratch_shapes=[pltpu.VMEM((quads, heads // quads * UNIT, CHUNK), jnp.bfloat16)]
            + [pltpu.VMEM(shape, jnp.bfloat16) for shape in kept]
            + [
                pltpu.VMEM((MAX_CHUNKS, groups, wide, CHUNK), jnp.float32),
                pltpu.VMEM((groups, wide, UNIT), jnp.float32),
                pltpu.VMEM((groups, wide, UNIT), jnp.float32),
                pltpu.VMEM((UNIT, width), jnp.float32),
                pltpu.SemaphoreType.DMA((3, MAX_CHUNKS)),
            ],
        ),
        out_shape=[jax.ShapeDtypeStruct(q.shape, jnp.bfloat16)]
        + [jax.ShapeDtypeStruct((per_row, micros) + shape, jnp.bfloat16) for shape in kept],
        compiler_params=pltpu.CompilerParams(vmem_limit_bytes=50 * 1024 * 1024),
        cost_estimate=pl.CostEstimate(flops=20_000_000_000, bytes_accessed=30_000_000, transcendentals=0),
        name="attention_fwd",
    )(blocks, q, k, v, mixes)


def bwd_kernel(heads, blocks_ref, q_ref, k_ref, v_ref, do_ref, mix_ref, score_in, prob_in, mixed_in,
               dq_ref, dk_ref, dv_ref, gl_ref, gp_ref,
               qxt, dox, doxt, score, prob, mixed, grad_prob, grad_mixed, grad_logit, grad_score,
               delta, dq_total, dk_total, dv_total, sems):
    micro, inner, per_row = (pl.program_id(0), pl.program_id(1), pl.num_programs(1))
    step = micro * per_row + inner
    slot = step % 2
    blocks = blocks_ref[step]
    chunks = (blocks + 1) // 2
    key_units = k_ref.shape[0]
    last_unit = key_units - per_row + inner + 1
    quads = q_ref.shape[3] // CHUNK
    per_quad = heads // quads
    groups = UNIT // GROUP
    wide = heads * GROUP
    lane_head = lax.broadcasted_iota(jnp.int32, (UNIT, CHUNK), 1) // (CHUNK // per_quad)
    row_head = lax.broadcasted_iota(jnp.int32, (CHUNK, UNIT), 0) // (CHUNK // per_quad)
    lowest = key_units
    for other in range(key_units - 7):
        its_chunks = (blocks_ref[micro * per_row + other] + 1) // 2
        lowest = jnp.minimum(lowest, key_units - per_row + other + 1 - 2 * its_chunks)

    def fetch(at, chunk, kind):
        source, target = ((score_in, score), (prob_in, prob), (mixed_in, mixed))[kind]
        place = source.at[at % per_row, at // per_row, chunk]
        return pltpu.make_async_copy(place, target.at[at % 2, chunk], sems.at[kind, at % 2, chunk])

    def fetch_all(at):
        @pl.loop(0, (blocks_ref[at] + 1) // 2)
        def _(chunk):
            for kind in (1, 2, 0):
                fetch(at, chunk, kind).start()

    @pl.when(step == 0)
    def _():
        fetch_all(0)
        gl_ref[...] = jnp.zeros_like(gl_ref)
        gp_ref[...] = jnp.zeros_like(gp_ref)

    @pl.when(step + 1 < pl.num_programs(0) * per_row)
    def _():
        fetch_all(step + 1)

    @pl.when(inner == 0)
    def _():
        @pl.loop(lowest, key_units)
        def _(key_unit):
            dk_total[key_unit] = jnp.zeros_like(dk_total[key_unit])
            dv_total[key_unit] = jnp.zeros_like(dv_total[key_unit])

    def spread_turned(rows, quad):
        turned = rows[:, quad * CHUNK : (quad + 1) * CHUNK].T
        zero = jnp.zeros_like(turned)
        return jnp.concatenate([jnp.where(row_head == head, turned, zero) for head in range(per_quad)], axis=1)

    for quad in range(quads):
        qxt[quad] = spread_turned(q_ref[0, 0], quad)
        dox[quad] = spread_heads(do_ref[0, 0], lane_head, quad, per_quad)
        doxt[quad] = spread_turned(do_ref[0, 0], quad)
    dq_total[...] = jnp.zeros_like(dq_total)
    delta[...] = jnp.zeros_like(delta)

    def keys(ref, chunk, quad):
        units = pl.ds(last_unit - 2 * (chunk + 1), 2)
        return ref[units, 0, :, quad * CHUNK : (quad + 1) * CHUNK].reshape(CHUNK, CHUNK)

    def add_to(total, chunk, quad, term):
        first = last_unit - 2 * (chunk + 1)
        lanes = slice(quad * CHUNK, (quad + 1) * CHUNK)
        total[first, lanes, :] += term[:, :UNIT]
        total[first + 1, lanes, :] += term[:, UNIT:]

    @pl.loop(0, chunks)
    def _(chunk):
        for quad in range(quads):
            put_groups(grad_mixed, quad, per_quad, dot_nt(dox[quad], keys(v_ref, chunk, quad)))
        fetch(step, chunk, 1).wait()
        for group in range(groups):
            cols = slice(group * CHUNK, (group + 1) * CHUNK)
            dp = dot_nn(mix_ref[3], grad_mixed[:, cols])
            grad_prob[chunk, :, cols] = dp.astype(grad_prob.dtype)
            term = prob[slot, chunk, :, cols].astype(jnp.float32) * dp
            delta[group] += term[:, :UNIT] + term[:, UNIT:]
        gp_ref[...] += dot_nt(prob[slot, chunk], grad_mixed[...])
        fetch(step, chunk, 2).wait()
        for quad in range(quads):
            a = mixed[slot, chunk, quad * per_quad : (quad + 1) * per_quad].reshape(per_quad * UNIT, CHUNK)
            add_to(dv_total, chunk, quad, dot_nn(doxt[quad], a))

    for group in range(groups):
        delta[group] = jnp.broadcast_to(jnp.sum(delta[group], axis=-1, keepdims=True), (wide, UNIT))

    @pl.loop(0, chunks)
    def _(chunk):
        for group in range(groups):
            cols = slice(group * CHUNK, (group + 1) * CHUNK)
            dp = grad_prob[chunk, :, cols].astype(jnp.float32) - twice(delta[group])
            dl = (prob[slot, chunk, :, cols].astype(jnp.float32) * dp).astype(jnp.bfloat16)
            grad_logit[:, cols] = dl
            ds = dot_nn(mix_ref[1], dl).astype(jnp.bfloat16)
            grad_score[:, GROUP * group : GROUP * (group + 1), :] = ds.reshape(heads, GROUP, CHUNK)
        fetch(step, chunk, 0).wait()
        gl_ref[...] += dot_nt(score[slot, chunk], grad_logit[...])
        for quad in range(quads):
            ds = grad_score[quad * per_quad : (quad + 1) * per_quad].reshape(per_quad * UNIT, CHUNK)
            dq = own_lanes(dot_nn(ds, keys(k_ref, chunk, quad)), lane_head, per_quad)
            dq_total[:, quad * CHUNK : (quad + 1) * CHUNK] += dq
            add_to(dk_total, chunk, quad, dot_nn(qxt[quad], ds))

    dq_ref[0, 0] = (dq_total[...] * 0.125).astype(jnp.bfloat16)

    @pl.when(inner == per_row - 1)
    def _():
        @pl.loop(0, lowest)
        def _(key_unit):
            dk_ref[key_unit, 0] = jnp.zeros_like(dk_ref[key_unit, 0])
            dv_ref[key_unit, 0] = jnp.zeros_like(dv_ref[key_unit, 0])

        @pl.loop(lowest, key_units)
        def _(key_unit):
            dk_ref[key_unit, 0] = dk_total[key_unit].astype(jnp.bfloat16).T
            dv_ref[key_unit, 0] = dv_total[key_unit].astype(jnp.bfloat16).T


def attention_bwd(blocks, q, k, v, grad_out, kept, mixes, heads):
    per_row, micros, _, width = q.shape
    key_units = k.shape[0]
    wide = heads * GROUP
    groups = UNIT // GROUP
    quads = width // CHUNK
    turned = (quads, CHUNK, heads // quads * UNIT)
    unit_spec, kv_spec, mix_spec = attention_specs(q, k, heads)
    sum_spec = pl.BlockSpec((wide, wide), lambda m, u, _: (0, 0))
    anywhere = pl.BlockSpec(memory_space=pl.ANY)
    return pl.pallas_call(
        partial(bwd_kernel, heads),
        grid_spec=pltpu.PrefetchScalarGridSpec(
            num_scalar_prefetch=1,
            grid=(micros, per_row),
            in_specs=[unit_spec, kv_spec, kv_spec, unit_spec, mix_spec] + [anywhere] * 3,
            out_specs=[unit_spec, kv_spec, kv_spec, sum_spec, sum_spec],
            scratch_shapes=[
                pltpu.VMEM(turned, jnp.bfloat16),
                pltpu.VMEM((quads, heads // quads * UNIT, CHUNK), jnp.bfloat16),
                pltpu.VMEM(turned, jnp.bfloat16),
            ]
            + [pltpu.VMEM((2,) + shape, jnp.bfloat16) for shape in kept_shapes(heads)]
            + [
                pltpu.VMEM((MAX_CHUNKS, wide, groups * CHUNK), jnp.bfloat16),
                pltpu.VMEM((wide, groups * CHUNK), jnp.bfloat16),
                pltpu.VMEM((wide, groups * CHUNK), jnp.bfloat16),
                pltpu.VMEM((heads, UNIT, CHUNK), jnp.bfloat16),
                pltpu.VMEM((groups, wide, UNIT), jnp.float32),
                pltpu.VMEM((UNIT, width), jnp.float32),
                pltpu.VMEM((key_units, width, UNIT), jnp.float32),
                pltpu.VMEM((key_units, width, UNIT), jnp.float32),
                pltpu.SemaphoreType.DMA((3, 2, MAX_CHUNKS)),
            ],
        ),
        out_shape=[
            jax.ShapeDtypeStruct(q.shape, jnp.bfloat16),
            jax.ShapeDtypeStruct(k.shape, jnp.bfloat16),
            jax.ShapeDtypeStruct(v.shape, jnp.bfloat16),
            jax.ShapeDtypeStruct((wide, wide), jnp.float32),
            jax.ShapeDtypeStruct((wide, wide), jnp.float32),
        ],
        compiler_params=pltpu.CompilerParams(vmem_limit_bytes=58 * 1024 * 1024),
        cost_estimate=pl.CostEstimate(flops=45_000_000_000, bytes_accessed=40_000_000, transcendentals=0),
        name="attention_bwd",
    )(blocks, q, k, v, grad_out, mixes, *kept)


def piece_bases(key_units, per_row):
    sizes = [1] + [per_row] * ((key_units - 1) // per_row)
    return [(sum(sizes[:at]), size) for at, size in enumerate(sizes)]


def project_kernel(low_ref, *refs):
    pieces, (w_q, w_k, w_v, q_ref, k_ref, v_ref) = (refs[:-6], refs[-6:])
    key_units, width = (k_ref.shape[0], k_ref.shape[3])
    per_row = q_ref.shape[0]
    low = low_ref[pl.program_id(0)]

    for piece, (base, size) in zip(pieces, piece_bases(key_units, per_row)):
        @pl.when(base + size > low)
        def _():
            rows = piece[:, 0].reshape(size * UNIT, width)
            k_ref[base : base + size, 0] = dot_nn(rows, w_k[...]).astype(jnp.bfloat16).reshape(size, UNIT, width)
            v_ref[base : base + size, 0] = dot_nn(rows, w_v[...]).astype(jnp.bfloat16).reshape(size, UNIT, width)

    rows = pieces[-1][:, 0].reshape(per_row * UNIT, width)
    query = dot_nn(rows, w_q[...]).astype(jnp.bfloat16) * jnp.bfloat16(0.125)
    q_ref[:, 0] = query.reshape(per_row, UNIT, width)


def project(low, pieces, weights):
    micros, width = pieces[0].shape[1], pieces[0].shape[3]
    key_units = sum(piece.shape[0] for piece in pieces)
    per_row = pieces[-1].shape[0]

    def spec(units):
        return pl.BlockSpec((units, 1, UNIT, width), lambda m, _: (0, m, 0, 0))

    weight_spec = pl.BlockSpec((width, width), lambda m, _: (0, 0))
    shapes = [(units, micros, UNIT, width) for units in (per_row, key_units, key_units)]
    return pl.pallas_call(
        project_kernel,
        grid_spec=pltpu.PrefetchScalarGridSpec(
            num_scalar_prefetch=1,
            grid=(micros,),
            in_specs=[spec(piece.shape[0]) for piece in pieces] + [weight_spec] * 3,
            out_specs=[spec(shape[0]) for shape in shapes],
        ),
        out_shape=[jax.ShapeDtypeStruct(shape, jnp.bfloat16) for shape in shapes],
        compiler_params=pltpu.CompilerParams(vmem_limit_bytes=44 * 1024 * 1024),
        cost_estimate=pl.CostEstimate(flops=6_000_000_000, bytes_accessed=15_000_000, transcendentals=0),
        name="project",
    )(low, *pieces, *weights)


def project_back_kernel(low_ref, dq_ref, dk_ref, dv_ref, w_q, w_k, w_v, *refs):
    key_units, width = (dk_ref.shape[0], dk_ref.shape[3])
    per_row = dq_ref.shape[0]
    micro = pl.program_id(0)
    low = low_ref[micro]
    bases = piece_bases(key_units, per_row)
    pieces, outs, (grad_ref, total) = (refs[: len(bases)], refs[len(bases) : 2 * len(bases)], refs[-2:])

    @pl.when(micro == 0)
    def _():
        total[...] = jnp.zeros_like(total)

    def keys(ref, base, size):
        return ref[base : base + size, 0].reshape(size * UNIT, width)

    def from_keys(piece, base, size):
        grad_key, grad_value = (keys(dk_ref, base, size), keys(dv_ref, base, size))
        turned = piece[:, 0].reshape(size * UNIT, width).T
        total[1] += dot_nn(turned, grad_key)
        total[2] += dot_nn(turned, grad_value)
        return dot_nt(grad_key, w_k[...]) + dot_nt(grad_value, w_v[...]), turned

    for piece, out, (base, size) in zip(pieces[:-1], outs[:-1], bases[:-1]):
        @pl.when(base + size > low)
        def _():
            term, _ = from_keys(piece, base, size)
            out[:, 0] = term.astype(jnp.bfloat16).reshape(size, UNIT, width)

        @pl.when(base + size <= low)
        def _():
            out[...] = jnp.zeros_like(out)

    term, turned = from_keys(pieces[-1], *bases[-1])
    grad_query = keys(dq_ref, 0, per_row)
    total[0] += dot_nn(turned, grad_query)
    outs[-1][:, 0] = (term + dot_nt(grad_query, w_q[...])).reshape(per_row, UNIT, width)

    @pl.when(micro == pl.num_programs(0) - 1)
    def _():
        grad_ref[...] = total[...].astype(jnp.bfloat16)


def project_back(low, grad_query, grad_key, grad_value, weights, pieces):
    per_row, micros, _, width = grad_query.shape
    key_units = grad_key.shape[0]

    def spec(units):
        return pl.BlockSpec((units, 1, UNIT, width), lambda m, _: (0, m, 0, 0))

    weight_spec = pl.BlockSpec((width, width), lambda m, _: (0, 0))
    sizes = [size for _, size in piece_bases(key_units, per_row)]
    shapes = [(size, micros, UNIT, width) for size in sizes]
    kinds = [jnp.bfloat16] * (len(sizes) - 1) + [jnp.float32]
    return pl.pallas_call(
        project_back_kernel,
        grid_spec=pltpu.PrefetchScalarGridSpec(
            num_scalar_prefetch=1,
            grid=(micros,),
            in_specs=[spec(per_row), spec(key_units), spec(key_units)]
            + [weight_spec] * 3
            + [spec(size) for size in sizes],
            out_specs=[spec(size) for size in sizes] + [pl.BlockSpec((3, width, width), lambda m, _: (0, 0, 0))],
            scratch_shapes=[pltpu.VMEM((3, width, width), jnp.float32)],
        ),
        out_shape=[jax.ShapeDtypeStruct(shape, kind) for shape, kind in zip(shapes, kinds)]
        + [jax.ShapeDtypeStruct((3, width, width), jnp.bfloat16)],
        compiler_params=pltpu.CompilerParams(vmem_limit_bytes=52 * 1024 * 1024),
        cost_estimate=pl.CostEstimate(flops=12_000_000_000, bytes_accessed=20_000_000, transcendentals=0),
        name="project_back",
    )(low, grad_query, grad_key, grad_value, *weights, *pieces)


def feed_kernel(x_ref, att_ref, w_o_ref, gain_ref, up_ref, down_ref, cot_ref,
                mid_ref, out_ref, grad_hidden_ref, grad_up_ref, grad_down_ref,
                hidden, turned, out_total, back_total):
    step = pl.program_id(0)

    @pl.when(step == 0)
    def _():
        middle = x_ref[...].astype(jnp.float32) + dot_nn(att_ref[...], w_o_ref[...])
        mid_ref[...] = middle
        inv_rms = lax.rsqrt(jnp.mean(middle * middle, axis=-1, keepdims=True) + norm_eps)
        rows = (middle * inv_rms * gain_ref[...]).astype(jnp.bfloat16)
        hidden[...] = rows
        turned[...] = rows.T
        out_total[...] = jnp.zeros_like(out_total)
        back_total[...] = jnp.zeros_like(back_total)

    for start in range(0, up_ref.shape[2], FF_STEP):
        cols = slice(start, start + FF_STEP)
        up = dot_nn(hidden[...], up_ref[0, :, cols])
        square = up * up
        bent = jnp.tanh(gelu_scale * up * (1.0 + gelu_cube * square))
        half = 0.5 + 0.5 * bent
        slope = half + 0.5 * up * (1.0 - bent * bent) * (gelu_scale * (1.0 + 3.0 * gelu_cube * square))
        active = (up * half).astype(jnp.bfloat16)
        grad_up = (dot_nt(cot_ref[...], down_ref[cols, :]) * slope).astype(jnp.bfloat16)
        out_total[...] += dot_nn(active, down_ref[cols, :])
        back_total[...] += dot_nt(grad_up, up_ref[0, :, cols])
        grad_down_ref[cols, :] = dot_nn(active.T, cot_ref[...]).astype(jnp.bfloat16)
        grad_up_ref[0, :, cols] = dot_nn(turned[...], grad_up).astype(jnp.bfloat16)

    @pl.when(step == pl.num_programs(0) - 1)
    def _():
        out_ref[...] = (mid_ref[...] + out_total[...]).astype(jnp.bfloat16)
        grad_hidden_ref[...] = back_total[...]


def feed_forward(rows, attended, w_o, gain, w_up, w_down, cot):
    tokens, width = rows.shape
    pieces = w_up.shape[0]
    whole = pl.BlockSpec((tokens, width), lambda i: (0, 0))
    up_spec = pl.BlockSpec((1, width, width), lambda i: (i, 0, 0))
    down_spec = pl.BlockSpec((width, width), lambda i: (i, 0))
    f32, bf16 = (jnp.float32, jnp.bfloat16)
    return pl.pallas_call(
        feed_kernel,
        grid=(pieces,),
        in_specs=[
            whole,
            whole,
            pl.BlockSpec((width, width), lambda i: (0, 0)),
            pl.BlockSpec((1, width), lambda i: (0, 0)),
            up_spec,
            down_spec,
            whole,
        ],
        out_specs=[whole, whole, whole, up_spec, down_spec],
        out_shape=[
            jax.ShapeDtypeStruct((tokens, width), f32),
            jax.ShapeDtypeStruct((tokens, width), bf16),
            jax.ShapeDtypeStruct((tokens, width), f32),
            jax.ShapeDtypeStruct(w_up.shape, bf16),
            jax.ShapeDtypeStruct(w_down.shape, bf16),
        ],
        scratch_shapes=[
            pltpu.VMEM((tokens, width), bf16),
            pltpu.VMEM((width, tokens), bf16),
            pltpu.VMEM((tokens, width), f32),
            pltpu.VMEM((tokens, width), f32),
        ],
        compiler_params=pltpu.CompilerParams(vmem_limit_bytes=48 * 1024 * 1024),
        cost_estimate=pl.CostEstimate(flops=16_000_000_000, bytes_accessed=30_000_000, transcendentals=0),
        name="feed_forward",
    )(rows, attended, w_o, gain, w_up, w_down, cot)


def spread_mixes(mix_logits, mix_weights):
    heads = mix_logits.shape[0]
    wide = heads * GROUP
    place = jnp.arange(wide, dtype=jnp.int32)
    pick = (place[:, None] // GROUP == jnp.arange(heads, dtype=jnp.int32)[None, :]).astype(mix_logits.dtype)
    same_row = (place[:, None] % GROUP == place[None, :] % GROUP)[None]
    tables = jnp.stack([mix_logits.T, mix_logits, mix_weights.T, mix_weights]).reshape(4 * heads, heads)
    across = jnp.dot(tables, pick.T, preferred_element_type=jnp.float32).astype(mix_logits.dtype)
    down = jnp.einsum("wh,bhx->bwx", pick, across.reshape(4, heads, wide), preferred_element_type=jnp.float32)
    return jnp.where(same_row, down, 0.0).astype(mix_logits.dtype)


def fold_mix(wide, heads):
    place = jnp.arange(heads * GROUP, dtype=jnp.int32)
    pick = (place[:, None] // GROUP == jnp.arange(heads, dtype=jnp.int32)[None, :]).astype(jnp.float32)
    same_row = place[:, None] % GROUP == place[None, :] % GROUP
    down = jnp.dot(pick.T, jnp.where(same_row, wide, 0.0), precision=lax.Precision.HIGHEST)
    return jnp.dot(down, pick, precision=lax.Precision.HIGHEST)


def from_behind(value, steps):
    count = lax.axis_size("dev")
    first, last = (max(0, -steps), min(count, count - steps))
    return lax.ppermute(value, "dev", [(source, source + steps) for source in range(first, last)])


def with_sibling(value):
    count = lax.axis_size("dev")
    return lax.ppermute(value, "dev", [(source, source ^ 1) for source in range(count)])


def earlier_rows(own):
    size = own.shape[0]
    first_core = lax.axis_index("dev") % 2 == 0
    two, four = (from_behind(own, 2), from_behind(own, 4))
    give = jnp.concatenate([jnp.where(first_core, own, two), jnp.where(first_core, two, four)], axis=0)
    came = with_sibling(give)
    return [four[size - 1 :], came[size:], two, came[:size], own]


def return_rows(four, two, came, beside):
    size = two.shape[0]
    first_core = lax.axis_index("dev") % 2 == 0
    came = came.astype(jnp.float32)
    one, three = (came[:size], came[size:])
    give_two = two.astype(jnp.float32) + jnp.where(first_core, three, one)
    padded = jnp.pad(four.astype(jnp.float32), ((size - four.shape[0], 0), (0, 0), (0, 0), (0, 0)))
    give_four = padded + jnp.where(first_core, 0.0, three)
    back_two = from_behind(give_two.astype(jnp.bfloat16), -2)
    back_two, give_four, beside = lax.optimization_barrier((back_two, give_four.astype(jnp.bfloat16), beside))
    back_four = from_behind(give_four, -4)
    return ((jnp.where(first_core, one, 0.0), back_two, back_four), beside)


def seq_starts(lengths_row, query_rows):
    seq_ends = jnp.cumsum(lengths_row)
    starts = seq_ends - lengths_row
    return jnp.max(jnp.where(starts[None, :] <= query_rows[:, None], starts[None, :], 0), axis=1)


def normalize(values, gain_vec):
    inv_rms = lax.rsqrt(jnp.mean(values * values, axis=-1, keepdims=True) + norm_eps)
    normed = values * inv_rms
    return (normed, inv_rms, (normed * gain_vec.astype(jnp.float32)).astype(jnp.bfloat16))


def norm_back(grad_hidden, normed, inv_rms, gain_vec):
    grad_gain = jnp.sum(grad_hidden * normed, axis=0)
    grad_normed = grad_hidden * gain_vec.astype(jnp.float32)
    inner_mean = jnp.mean(grad_normed * normed, axis=-1, keepdims=True)
    return (inv_rms * (grad_normed - normed * inner_mean), grad_gain)


def matmul(left, right):
    return jnp.dot(left, right, preferred_element_type=jnp.float32)


def matmul_left_t(left, right):
    return lax.dot_general(left, right, (((0,), (0,)), ((), ())), preferred_element_type=jnp.float32)


def matmul_right_t(left, right):
    return lax.dot_general(left, right, (((1,), (1,)), ((), ())), preferred_element_type=jnp.float32)


def exchange(value):
    return lax.all_to_all(value, "dev", split_axis=0, concat_axis=0, tiled=True)


def split_ids(tok_ids, own_rows):
    owner = tok_ids // own_rows
    place = jnp.arange(tok_ids.shape[0], dtype=jnp.int32)
    same = tok_ids[:, None] == tok_ids[None, :]
    repeated = jnp.any(same & (place[None, :] < place[:, None]), axis=1)
    before = (owner[:, None] == owner[None, :]) & (tok_ids[None, :] < tok_ids[:, None]) & ~repeated[None, :]
    return (owner, tok_ids % own_rows, jnp.sum(before, axis=1, dtype=jnp.int32))


def ask_round(ids, index, own_rows, stride, room):
    count = lax.axis_size("dev")
    owner, local, rank = ids
    here = rank - index * room
    slot = jnp.where((here >= 0) & (here < room), owner * stride + here, -1)
    chosen = slot[None, :] == jnp.arange(count * stride, dtype=jnp.int32)[:, None]
    wanted = jnp.max(jnp.where(chosen, local[None, :], -1), axis=1).reshape(count, stride)
    rounds = jnp.broadcast_to(jnp.max(rank) // room + 1, (count, stride))
    return (jnp.concatenate([wanted, rounds], axis=1), chosen.astype(jnp.bfloat16))


def hear_round(message, own_rows, stride):
    asked = exchange(message)
    pick = asked[:, :stride].reshape(-1, 1) == jnp.arange(own_rows, dtype=jnp.int32)[None, :]
    return (pick.astype(jnp.bfloat16), jnp.max(asked[:, stride:]))


def plan_round(ids, index, own_rows, stride, room):
    message, chosen = ask_round(ids, index, own_rows, stride, room)
    pick, _ = hear_round(message, own_rows, stride)
    return (chosen, pick)


def answer(embedding, chosen, pick, stride, extra_row):
    count = lax.axis_size("dev")
    rows = matmul(pick, embedding).astype(jnp.bfloat16).reshape(count, stride, -1)
    if extra_row is not None:
        is_extra = (jnp.arange(stride, dtype=jnp.int32) == stride - 1)[None, :, None]
        rows = jnp.where(is_extra, extra_row[None, None, :], rows)
    got = exchange(rows.reshape(count * stride, -1))
    return (matmul_left_t(chosen, got).astype(jnp.bfloat16), got.reshape(count, stride, -1)[:, stride - 1])


def lookup(embedding, ids, message, chosen, extra_row, stride, room):
    own_rows = embedding.shape[0]
    pick, rounds = hear_round(message, own_rows, stride)
    first, extra = answer(embedding, chosen, pick, stride, extra_row)

    def more(carry):
        index, rows = carry
        again, its_pick = plan_round(ids, index, own_rows, stride, room)
        return (index + 1, rows + answer(embedding, again, its_pick, stride, None)[0])

    _, rows = lax.while_loop(lambda carry: carry[0] < rounds, more, (jnp.int32(1), first))
    return (rows, extra, ids, chosen, pick, rounds)


def send_grads(grad_low, chosen, pick, stride, extra_rows, beside=None):
    count = lax.axis_size("dev")
    summed = matmul(chosen, grad_low).astype(jnp.bfloat16).reshape(count, stride, -1)
    if extra_rows is not None:
        place = jnp.arange(stride, dtype=jnp.int32)[None, :, None]
        high, low = extra_rows
        summed = jnp.where(place == stride - 2, high[:, None, :], summed)
        summed = jnp.where(place == stride - 1, low[:, None, :], summed)
    summed, beside = lax.optimization_barrier((summed.reshape(count * stride, -1), beside))
    got = exchange(summed)
    return (matmul_left_t(pick, got), got.reshape(count, stride, -1)[:, stride - 2 :], beside)


def table_back(grad_rows, extra_rows, plan, own_rows, stride, room, beside):
    ids, chosen, pick, rounds = plan
    grad_low = grad_rows.astype(jnp.bfloat16)
    first, extra, beside = send_grads(grad_low, chosen, pick, stride, extra_rows, beside)

    def more(carry):
        index, total = carry
        again, its_pick = plan_round(ids, index, own_rows, stride, room)
        return (index + 1, total + send_grads(grad_low, again, its_pick, stride, None)[0])

    _, total = lax.while_loop(lambda carry: carry[0] < rounds, more, (jnp.int32(1), first))
    return (total, jnp.sum(extra.astype(jnp.float32), axis=(0, 1)), beside)


def double(held, bit, axis):
    count = lax.axis_size("dev")
    low = ((lax.axis_index("dev") >> bit) & 1) == 0
    came = lax.ppermute(held, "dev", [(source, source ^ (1 << bit)) for source in range(count)])
    return jnp.stack([jnp.where(low, held, came), jnp.where(low, came, held)], axis=axis)


def spread_some(held, first, last):
    bits = lax.axis_size("dev").bit_length() - 1
    for done in range(first, min(last, bits)):
        held = double(held, bits - 1 - done, done)
    return held


def gather_late(pieces, part, up_cols):
    width = pieces[0].shape[1]
    whole = lax.all_gather(jnp.concatenate(pieces, axis=0), "dev", axis=0)
    middle = part * (1 + up_cols)
    up = whole[:, part:middle].reshape(-1, up_cols, part, width).swapaxes(0, 1)
    return (whole[:, :part].reshape(-1, width), up.reshape(up_cols, -1, width), whole[:, middle:].reshape(-1, width))


def split_rows(summed, sizes):
    pieces, start = ([], 0)
    for size in sizes:
        pieces.append(summed[start : start + size])
        start += size
    return pieces


def swap_parts(held, bit):
    count = lax.axis_size("dev")
    mine = (lax.axis_index("dev") >> bit) & 1
    keep = lax.dynamic_index_in_dim(held, mine, 0, keepdims=False)
    give = lax.dynamic_index_in_dim(held, 1 - mine, 0, keepdims=False)
    return (keep, lax.ppermute(give, "dev", [(source, source ^ (1 << bit)) for source in range(count)]))


def join_parts(parts, last=False):
    total = parts[0].astype(jnp.float32) + parts[1].astype(jnp.float32)
    return total if last else total.astype(jnp.bfloat16)


def swap_halves(held, bit, last=False):
    return join_parts(swap_parts(held, bit), last)


def middle_bits():
    return list(range(1, lax.axis_size("dev").bit_length() - 2))


def give_core(grid, axis):
    other = 1 - lax.axis_index("dev") % 2
    return with_sibling(lax.dynamic_index_in_dim(grid, other, axis, keepdims=False))


def first_bits():
    middle = middle_bits()
    return [middle[turn % len(middle)] for turn in range(3)]


def sum_cores(term):
    count, pieces, rows, width = term.shape
    grid = term.reshape(count // 2, 2, pieces, rows, width)
    return swap_halves(grid.swapaxes(0, 1), 0).reshape(count // 2, pieces * rows, width)


def merge_kernel(core_ref, down_ref, down_came_ref, up_ref, up_came_ref, *outs):
    rows, width = down_came_ref.shape[-2:]
    down = down_ref[0, 0].astype(jnp.float32) + down_came_ref[0].astype(jnp.float32)
    up = up_ref[:, 0, 0].astype(jnp.float32) + up_came_ref[:, 0].astype(jnp.float32)
    whole = jnp.concatenate([down, up.reshape(-1, width)], axis=0).astype(jnp.bfloat16)
    for turn, out in enumerate(outs):
        out[0] = whole[:, turn * (width // 3) : (turn + 1) * (width // 3)]


def merge_cores(grad_down, grad_up):
    count = lax.axis_size("dev")
    up_cols, _, width = grad_up.shape
    half = count // 2
    down = grad_down.reshape(half, 2, -1, width)
    up = grad_up.reshape(up_cols, half, 2, -1, width)
    down_came, up_came = (give_core(down, 1), give_core(up, 2))
    down_rows, up_rows = (down.shape[2], up.shape[3])
    rows = down_rows + up_cols * up_rows
    middle = middle_bits()
    bits = len(middle) + 1

    def out_index(turn):
        shift = turn % len(middle)
        order = middle[shift:] + middle[:shift] + [bits]

        def index(dest, _):
            place = 0
            for bit in order:
                place = place * 2 + (dest >> (bit - 1)) % 2
            return (place, 0, 0)

        return index

    third = width // 3
    merged = pl.pallas_call(
        merge_kernel,
        grid_spec=pltpu.PrefetchScalarGridSpec(
            num_scalar_prefetch=1,
            grid=(half,),
            in_specs=[
                pl.BlockSpec((1, 1, down_rows, width), lambda dest, core: (dest, core[0], 0, 0)),
                pl.BlockSpec((1, down_rows, width), lambda dest, core: (dest, 0, 0)),
                pl.BlockSpec((up_cols, 1, 1, up_rows, width), lambda dest, core: (0, dest, core[0], 0, 0)),
                pl.BlockSpec((up_cols, 1, up_rows, width), lambda dest, core: (0, dest, 0, 0)),
            ],
            out_specs=[pl.BlockSpec((1, rows, third), out_index(turn)) for turn in range(3)],
        ),
        out_shape=[jax.ShapeDtypeStruct((half, rows, third), jnp.bfloat16)] * 3,
        cost_estimate=pl.CostEstimate(flops=20_000_000, bytes_accessed=16_000_000, transcendentals=0),
        name="merge_cores",
    )(lax.axis_index("dev").reshape(1) % 2, down, down_came, up, up_came)
    return [out.reshape((2,) * bits + (rows, third)) for out in merged]


def cut_thirds(held):
    _, rows, width = held.shape
    middle = middle_bits()
    bits = len(middle) + 1
    grid = held.reshape((2,) * bits + (rows, width))
    thirds = []
    for turn in range(3):
        shift = turn % len(middle)
        order = middle[shift:] + middle[:shift] + [bits]
        axes = [bits - bit for bit in order]
        part = grid[..., turn * (width // 3) : (turn + 1) * (width // 3)]
        thirds.append(part.transpose(axes + [bits, bits + 1]))
    return thirds


def sum_stage(thirds, stage):
    middle = middle_bits()
    return [swap_halves(third, middle[(turn + stage) % len(middle)]) for turn, third in enumerate(thirds)]


def sum_stages(thirds, first):
    for stage in range(first, len(middle_bits())):
        thirds = sum_stage(thirds, stage)
    return thirds


def sum_last(groups):
    whole = [jnp.concatenate(thirds, axis=-1) for thirds in groups]
    return swap_halves(jnp.concatenate(whole, axis=1), len(middle_bits()) + 1, True)


def split_low(values):
    high = lax.reduce_precision(values, 8, 7)
    return (high.astype(jnp.bfloat16), (values - high).astype(jnp.bfloat16))


def low_units(blocks):
    per_row = blocks.shape[1]
    place = 8 + jnp.arange(per_row, dtype=jnp.int32)[None, :]
    return jnp.min(place - 2 * ((blocks + 1) // 2), axis=1).astype(jnp.int32)


def by_unit(array):
    cut = array.reshape((array.shape[0], array.shape[1] // UNIT, UNIT) + array.shape[2:])
    return cut.swapaxes(0, 1)


def by_row(array, micros):
    cut = array.reshape(-1, micros, UNIT, array.shape[-1])
    return cut.swapaxes(0, 1).reshape(micros, -1, array.shape[-1])


def shards(
    token_ids,
    lengths,
    embedding,
    norm1_gain,
    w_query,
    w_key,
    w_value,
    w_out,
    mix_logits,
    mix_weights,
    norm2_gain,
    w_up,
    w_down,
    cotangent,
):
    count = lax.axis_size("dev")
    me = lax.axis_index("dev")
    micros, row_count = token_ids.shape
    own_rows, width = embedding.shape
    heads = mix_logits.shape[0]
    part = norm1_gain.shape[0]
    per_row = row_count // UNIT
    tokens = micros * row_count
    tok_ids = by_unit(token_ids).reshape(-1)
    stride = max(16, 1024 // count)
    room = stride - 2

    unit_rows = me * row_count + UNIT * jnp.arange(per_row, dtype=jnp.int32)
    begins = jnp.stack([seq_starts(lengths[micro], unit_rows) for micro in range(micros)])
    blocks = ((unit_rows[None, :] - begins) // UNIT + 1).reshape(-1).astype(jnp.int32)

    lows = low_units(blocks.reshape(micros, per_row))
    mixes = spread_mixes(mix_logits, mix_weights)

    up_cols = w_up.shape[1] // width
    up_pieces = [w_up[:, col * width : (col + 1) * width] for col in range(up_cols)]
    first_weights = spread_some(jnp.stack([w_query, w_key, w_value]), 0, 2)
    weight_pieces = [w_out] + up_pieces + [w_down]
    ids = split_ids(tok_ids, own_rows)
    message, chosen = ask_round(ids, 0, own_rows, stride, room)
    message, weight_pieces = lax.optimization_barrier((message, weight_pieces))
    w_o, w_u, w_d = gather_late(weight_pieces, part, up_cols)
    gains_row = jnp.concatenate([norm1_gain, norm2_gain, jnp.zeros((width - 2 * part,), jnp.bfloat16)])
    picked, gains, *plan = lookup(embedding, ids, message, chosen, gains_row, stride, room)
    gain_one = gains[:, :part].reshape(-1)
    gain_two = gains[:, part : 2 * part].reshape(-1)
    first_weights = spread_some(first_weights, 2, 3)
    picked, first_weights = lax.optimization_barrier((picked, first_weights))
    inputs = picked.astype(jnp.float32)

    normed_one, inv_one, hidden_one = normalize(inputs, gain_one)
    own_hidden = hidden_one.reshape(per_row, micros, UNIT, width)
    pieces = earlier_rows(own_hidden)
    first_weights = spread_some(first_weights, 3, 99).reshape(count, 3, part, width)
    w_q, w_k, w_v = (first_weights[:, at].reshape(-1, width) for at in range(3))
    query, key, value = project(lows, pieces, (w_q, w_k, w_v))
    attended, *kept = attention_fwd(blocks, query, key, value, mixes, heads)
    attended = attended.reshape(tokens, width)

    grad_rows = by_unit(cotangent).reshape(tokens, width)
    gain_row = gain_two.astype(jnp.float32)[None, :]
    middle, output, grad_hidden_two, grad_up, grad_down = feed_forward(
        picked, attended, w_o, gain_row, w_u, w_d, grad_rows
    )
    inv_two = lax.rsqrt(jnp.mean(middle * middle, axis=-1, keepdims=True) + norm_eps)
    normed_two = middle * inv_two
    grad_mid_norm, grad_gain_two = norm_back(grad_hidden_two, normed_two, inv_two, gain_two)
    grad_middle = grad_rows.astype(jnp.float32) + grad_mid_norm
    grad_branch = grad_middle.astype(jnp.bfloat16)
    grad_wout = matmul_left_t(attended, grad_branch)
    grad_att = matmul_right_t(grad_branch, w_o).astype(jnp.bfloat16).reshape(own_hidden.shape)
    late = merge_cores(grad_down, grad_up)
    late, grad_att = lax.optimization_barrier((late, grad_att))
    late = [swap_parts(third, bit) for third, bit in zip(late, first_bits())]

    grad_query, grad_key, grad_value, wide_logit, wide_prob = attention_bwd(
        blocks, query, key, value, grad_att, kept, mixes, heads
    )
    late, grad_query, grad_key, grad_value = lax.optimization_barrier((late, grad_query, grad_key, grad_value))
    *terms, grad_own, grad_qkv = project_back(lows, grad_query, grad_key, grad_value, (w_q, w_k, w_v), pieces)
    came = with_sibling(jnp.concatenate([terms[3], terms[1]], axis=0))
    backs, (grad_qkv, late) = return_rows(terms[0], terms[2], came, (grad_qkv, late))
    early_terms = jnp.concatenate([grad_qkv, grad_wout.astype(jnp.bfloat16)[None]], axis=0)
    early = cut_thirds(sum_cores(early_terms.reshape(4, count, part, width).swapaxes(0, 1)))
    late = sum_stage([join_parts(parts) for parts in late], 1)
    backs, early, late = lax.optimization_barrier((backs, early, late))
    grad_own = grad_own + backs[0] + backs[1].astype(jnp.float32) + backs[2].astype(jnp.float32)
    early = sum_stage(early, 0)
    late = sum_stages(late, 2)
    grad_hidden_one = grad_own.reshape(tokens, width)
    grad_in_norm, grad_gain_one = norm_back(grad_hidden_one, normed_one, inv_one, gain_one)
    grad_inputs = grad_middle + grad_in_norm

    mix_terms = jnp.concatenate([fold_mix(wide_logit, heads).reshape(-1), fold_mix(wide_prob, heads).reshape(-1)])
    mix_size = mix_terms.shape[0]
    small = jnp.concatenate(
        [
            grad_gain_one.reshape(count, part),
            grad_gain_two.reshape(count, part),
            jnp.broadcast_to(mix_terms[None, :], (count, mix_size)),
            jnp.zeros((count, width - 2 * part - mix_size), jnp.float32),
        ],
        axis=1,
    )
    table_grad, small_sum, (early, late) = table_back(
        grad_inputs, split_low(small), plan, own_rows, stride, room, (early, late)
    )
    summed = sum_last([sum_stages(early, 1), late])
    row_sizes = [part] * 4 + [w_down.shape[0]] + [part] * up_cols
    weight_sums = split_rows(summed, row_sizes)
    mixes = small_sum[2 * part : 2 * part + mix_size].reshape(2, heads, heads)
    return (
        by_row(output, micros),
        by_row(grad_inputs, micros),
        table_grad,
        small_sum[:part],
        *weight_sums[:4],
        mixes[0],
        mixes[1],
        small_sum[part : 2 * part],
        jnp.concatenate(weight_sums[5:], axis=1),
        weight_sums[4],
    )


def solution(mesh):
    in_specs = (
        P(None, "dev"),
        P(),
        P("dev", None),
        P("dev"),
        P("dev", None),
        P("dev", None),
        P("dev", None),
        P("dev", None),
        P(),
        P(),
        P("dev"),
        P("dev", None),
        P("dev", None),
        P(None, "dev", None),
    )
    out_specs = (
        P(None, "dev", None),
        P(None, "dev", None),
        P("dev", None),
        P("dev"),
        P("dev", None),
        P("dev", None),
        P("dev", None),
        P("dev", None),
        P(),
        P(),
        P("dev"),
        P("dev", None),
        P("dev", None),
    )
    return jax.shard_map(shards, mesh=mesh, in_specs=in_specs, out_specs=out_specs, check_vma=False)
```

```python
from functools import partial

import jax
import jax.numpy as jnp
from jax import lax
from jax.experimental import pallas as pl
from jax.experimental.pallas import tpu as pltpu
from jax.sharding import PartitionSpec as P

norm_eps = 1e-06
gelu_scale = 0.7978845608028654
gelu_cube = 0.044715
FF_STEP = 256

masked = -1e30
UNIT = 128
CHUNK = 256
GROUP = 16
MAX_CHUNKS = 4
TOGETHER = 4


def dot_nn(left, right):
    return lax.dot_general(left, right, (((1,), (0,)), ((), ())), preferred_element_type=jnp.float32)


def dot_nt(left, right):
    return lax.dot_general(left, right, (((1,), (1,)), ((), ())), preferred_element_type=jnp.float32)


def spread_heads(rows, lane_head, quad, heads_per_quad):
    part = rows[:, quad * CHUNK : (quad + 1) * CHUNK]
    zero = jnp.zeros_like(part)
    return jnp.concatenate([jnp.where(lane_head == head, part, zero) for head in range(heads_per_quad)], axis=0)


def own_lanes(wide, lane_head, heads_per_quad):
    total = jnp.where(lane_head == 0, wide[:UNIT], 0.0)
    for head in range(1, heads_per_quad):
        total = total + jnp.where(lane_head == head, wide[head * UNIT : (head + 1) * UNIT], 0.0)
    return total


def part_of(sums, group):
    start = group % TOGETHER * CHUNK
    return sums[:, start : start + CHUNK]


def allowed_keys(chunk, group, blocks):
    key = lax.broadcasted_iota(jnp.int32, (GROUP, CHUNK), 1) - (UNIT + CHUNK * chunk)
    row = lax.broadcasted_iota(jnp.int32, (GROUP, CHUNK), 0) + GROUP * group
    return (key <= row) & (key >= (1 - blocks) * UNIT)


def twice(rows):
    return jnp.concatenate([rows, rows], axis=-1)


def put_groups(ref, quad, per_quad, term):
    low = term.astype(jnp.bfloat16)
    for head in range(per_quad):
        rows = slice((quad * per_quad + head) * GROUP, (quad * per_quad + head + 1) * GROUP)
        for group in range(UNIT // GROUP):
            start = head * UNIT + group * GROUP
            ref[rows, group * CHUNK : (group + 1) * CHUNK] = low[start : start + GROUP]


def fwd_kernel(heads, blocks_ref, q_ref, k_ref, v_ref, mix_ref, att_ref, score_out, prob_out, mixed_out,
               qx, score, prob, mixed, logit, top, norm, total, sems):
    micro, inner, per_row = (pl.program_id(0), pl.program_id(1), pl.num_programs(1))
    blocks = blocks_ref[micro * per_row + inner]
    chunks = (blocks + 1) // 2
    last_unit = k_ref.shape[0] - per_row + inner + 1
    quads = q_ref.shape[3] // CHUNK
    per_quad = heads // quads
    groups = UNIT // GROUP
    wide = heads * GROUP
    lane_head = lax.broadcasted_iota(jnp.int32, (UNIT, CHUNK), 1) // (CHUNK // per_quad)
    for quad in range(quads):
        qx[quad] = spread_heads(q_ref[0, 0], lane_head, quad, per_quad)
    total[...] = jnp.zeros_like(total)
    top[...] = jnp.full_like(top, masked)
    norm[...] = jnp.zeros_like(norm)

    def keys(ref, chunk, quad):
        units = pl.ds(last_unit - 2 * (chunk + 1), 2)
        return ref[units, 0, :, quad * CHUNK : (quad + 1) * CHUNK].reshape(CHUNK, CHUNK)

    step = micro * per_row + inner

    def keep(at, chunk, kind):
        source, target = ((score, score_out), (prob, prob_out), (mixed, mixed_out))[kind]
        place = target.at[at % per_row, at // per_row, chunk]
        return pltpu.make_async_copy(source.at[chunk], place, sems.at[kind, chunk])

    def finish(at):
        @pl.loop(0, (blocks_ref[at] + 1) // 2)
        def _(chunk):
            for kind in range(3):
                keep(at, chunk, kind).wait()

    @pl.when(step > 0)
    def _():
        finish(step - 1)

    @pl.loop(0, chunks)
    def _(chunk):
        for quad in range(quads):
            put_groups(score.at[chunk], quad, per_quad, dot_nt(qx[quad], keys(k_ref, chunk, quad)))
        keep(step, chunk, 0).start()
        for group in range(groups):
            if group % TOGETHER == 0:
                mixes = dot_nn(mix_ref[0], score[chunk, :, group * CHUNK : (group + TOGETHER) * CHUNK])
            l = part_of(mixes, group)
            l = jnp.where(allowed_keys(chunk, group, blocks)[None], l.reshape(heads, GROUP, CHUNK), masked)
            l = l.reshape(wide, CHUNK)
            logit[chunk, group] = l
            old = top[group]
            new = jnp.maximum(old, jnp.maximum(l[:, :UNIT], l[:, UNIT:]))
            terms = jnp.exp(l[:, :UNIT] - new) + jnp.exp(l[:, UNIT:] - new)
            norm[group] = norm[group] * jnp.exp(old - new) + terms
            top[group] = new

    for group in range(groups):
        lanes = top[group]
        high = jnp.broadcast_to(jnp.max(lanes, axis=-1, keepdims=True), lanes.shape)
        whole = jnp.sum(norm[group] * jnp.exp(lanes - high), axis=-1, keepdims=True)
        top[group] = high + jnp.log(jnp.broadcast_to(whole, lanes.shape))

    @pl.loop(0, chunks)
    def _(chunk):
        for group in range(groups):
            p = jnp.exp(logit[chunk, group] - twice(top[group])).astype(jnp.bfloat16)
            prob[chunk, :, group * CHUNK : (group + 1) * CHUNK] = p
        for first in range(0, groups, TOGETHER):
            sums = dot_nn(mix_ref[2], prob[chunk, :, first * CHUNK : (first + TOGETHER) * CHUNK])
            for group in range(first, first + TOGETHER):
                a = part_of(sums, group).astype(jnp.bfloat16)
                mixed[chunk, :, GROUP * group : GROUP * (group + 1), :] = a.reshape(heads, GROUP, CHUNK)
        keep(step, chunk, 1).start()
        keep(step, chunk, 2).start()
        for quad in range(quads):
            a = mixed[chunk, quad * per_quad : (quad + 1) * per_quad].reshape(per_quad * UNIT, CHUNK)
            o = own_lanes(dot_nn(a, keys(v_ref, chunk, quad)), lane_head, per_quad)
            total[:, quad * CHUNK : (quad + 1) * CHUNK] += o

    att_ref[0, 0] = total[...].astype(jnp.bfloat16)

    @pl.when(step == pl.num_programs(0) * per_row - 1)
    def _():
        finish(step)


def attention_specs(q, k, heads):
    per_row, micros, _, width = q.shape
    wide = heads * GROUP
    return (
        pl.BlockSpec((1, 1, UNIT, width), lambda m, u, _: (u, m, 0, 0)),
        pl.BlockSpec((k.shape[0], 1, UNIT, width), lambda m, u, _: (0, m, 0, 0)),
        pl.BlockSpec((4, wide, wide), lambda m, u, _: (0, 0, 0)),
    )


def kept_shapes(heads):
    wide = heads * GROUP
    flat = (MAX_CHUNKS, wide, UNIT // GROUP * CHUNK)
    return (flat, flat, (MAX_CHUNKS, heads, UNIT, CHUNK))


def attention_fwd(blocks, q, k, v, mixes, heads):
    per_row, micros, _, width = q.shape
    wide = heads * GROUP
    groups = UNIT // GROUP
    quads = width // CHUNK
    unit_spec, kv_spec, mix_spec = attention_specs(q, k, heads)
    kept = kept_shapes(heads)
    anywhere = pl.BlockSpec(memory_space=pl.ANY)
    return pl.pallas_call(
        partial(fwd_kernel, heads),
        grid_spec=pltpu.PrefetchScalarGridSpec(
            num_scalar_prefetch=1,
            grid=(micros, per_row),
            in_specs=[unit_spec, kv_spec, kv_spec, mix_spec],
            out_specs=[unit_spec, anywhere, anywhere, anywhere],
            scratch_shapes=[pltpu.VMEM((quads, heads // quads * UNIT, CHUNK), jnp.bfloat16)]
            + [pltpu.VMEM(shape, jnp.bfloat16) for shape in kept]
            + [
                pltpu.VMEM((MAX_CHUNKS, groups, wide, CHUNK), jnp.float32),
                pltpu.VMEM((groups, wide, UNIT), jnp.float32),
                pltpu.VMEM((groups, wide, UNIT), jnp.float32),
                pltpu.VMEM((UNIT, width), jnp.float32),
                pltpu.SemaphoreType.DMA((3, MAX_CHUNKS)),
            ],
        ),
        out_shape=[jax.ShapeDtypeStruct(q.shape, jnp.bfloat16)]
        + [jax.ShapeDtypeStruct((per_row, micros) + shape, jnp.bfloat16) for shape in kept],
        compiler_params=pltpu.CompilerParams(vmem_limit_bytes=50 * 1024 * 1024),
        cost_estimate=pl.CostEstimate(flops=20_000_000_000, bytes_accessed=30_000_000, transcendentals=0),
        name="attention_fwd",
    )(blocks, q, k, v, mixes)


def bwd_kernel(heads, blocks_ref, q_ref, k_ref, v_ref, do_ref, mix_ref, score_in, prob_in, mixed_in,
               dq_ref, dk_ref, dv_ref, gl_ref, gp_ref,
               qxt, dox, doxt, score, prob, mixed, grad_prob, grad_mixed, grad_logit, grad_score,
               delta, dq_total, dk_total, dv_total, sems):
    micro, inner, per_row = (pl.program_id(0), pl.program_id(1), pl.num_programs(1))
    step = micro * per_row + inner
    slot = step % 2
    blocks = blocks_ref[step]
    chunks = (blocks + 1) // 2
    key_units = k_ref.shape[0]
    last_unit = key_units - per_row + inner + 1
    quads = q_ref.shape[3] // CHUNK
    per_quad = heads // quads
    groups = UNIT // GROUP
    wide = heads * GROUP
    lane_head = lax.broadcasted_iota(jnp.int32, (UNIT, CHUNK), 1) // (CHUNK // per_quad)
    row_head = lax.broadcasted_iota(jnp.int32, (CHUNK, UNIT), 0) // (CHUNK // per_quad)
    lowest = key_units
    for other in range(key_units - 7):
        its_chunks = (blocks_ref[micro * per_row + other] + 1) // 2
        lowest = jnp.minimum(lowest, key_units - per_row + other + 1 - 2 * its_chunks)

    def fetch(at, chunk, kind):
        source, target = ((score_in, score), (prob_in, prob), (mixed_in, mixed))[kind]
        place = source.at[at % per_row, at // per_row, chunk]
        return pltpu.make_async_copy(place, target.at[at % 2, chunk], sems.at[kind, at % 2, chunk])

    def fetch_all(at):
        @pl.loop(0, (blocks_ref[at] + 1) // 2)
        def _(chunk):
            for kind in (1, 2, 0):
                fetch(at, chunk, kind).start()

    @pl.when(step == 0)
    def _():
        fetch_all(0)
        gl_ref[...] = jnp.zeros_like(gl_ref)
        gp_ref[...] = jnp.zeros_like(gp_ref)

    @pl.when(step + 1 < pl.num_programs(0) * per_row)
    def _():
        fetch_all(step + 1)

    @pl.when(inner == 0)
    def _():
        @pl.loop(lowest, key_units)
        def _(key_unit):
            dk_total[key_unit] = jnp.zeros_like(dk_total[key_unit])
            dv_total[key_unit] = jnp.zeros_like(dv_total[key_unit])

    def spread_turned(rows, quad):
        turned = rows[:, quad * CHUNK : (quad + 1) * CHUNK].T
        zero = jnp.zeros_like(turned)
        return jnp.concatenate([jnp.where(row_head == head, turned, zero) for head in range(per_quad)], axis=1)

    for quad in range(quads):
        qxt[quad] = spread_turned(q_ref[0, 0], quad)
        dox[quad] = spread_heads(do_ref[0, 0], lane_head, quad, per_quad)
        doxt[quad] = spread_turned(do_ref[0, 0], quad)
    dq_total[...] = jnp.zeros_like(dq_total)
    delta[...] = jnp.zeros_like(delta)

    def keys(ref, chunk, quad):
        units = pl.ds(last_unit - 2 * (chunk + 1), 2)
        return ref[units, 0, :, quad * CHUNK : (quad + 1) * CHUNK].reshape(CHUNK, CHUNK)

    def add_to(total, chunk, quad, term):
        first = last_unit - 2 * (chunk + 1)
        lanes = slice(quad * CHUNK, (quad + 1) * CHUNK)
        total[first, lanes, :] += term[:, :UNIT]
        total[first + 1, lanes, :] += term[:, UNIT:]

    @pl.loop(0, chunks)
    def _(chunk):
        for quad in range(quads):
            put_groups(grad_mixed, quad, per_quad, dot_nt(dox[quad], keys(v_ref, chunk, quad)))
        fetch(step, chunk, 1).wait()
        for group in range(groups):
            cols = slice(group * CHUNK, (group + 1) * CHUNK)
            if group % TOGETHER == 0:
                sums = dot_nn(mix_ref[3], grad_mixed[:, group * CHUNK : (group + TOGETHER) * CHUNK])
            dp = part_of(sums, group)
            grad_prob[chunk, :, cols] = dp.astype(grad_prob.dtype)
            term = prob[slot, chunk, :, cols].astype(jnp.float32) * dp
            delta[group] += term[:, :UNIT] + term[:, UNIT:]
        gp_ref[...] += dot_nt(prob[slot, chunk], grad_mixed[...])
        fetch(step, chunk, 2).wait()
        for quad in range(quads):
            a = mixed[slot, chunk, quad * per_quad : (quad + 1) * per_quad].reshape(per_quad * UNIT, CHUNK)
            add_to(dv_total, chunk, quad, dot_nn(doxt[quad], a))

    for group in range(groups):
        delta[group] = jnp.broadcast_to(jnp.sum(delta[group], axis=-1, keepdims=True), (wide, UNIT))

    @pl.loop(0, chunks)
    def _(chunk):
        for group in range(groups):
            cols = slice(group * CHUNK, (group + 1) * CHUNK)
            dp = grad_prob[chunk, :, cols].astype(jnp.float32) - twice(delta[group])
            dl = (prob[slot, chunk, :, cols].astype(jnp.float32) * dp).astype(jnp.bfloat16)
            grad_logit[:, cols] = dl
        for first in range(0, groups, TOGETHER):
            sums = dot_nn(mix_ref[1], grad_logit[:, first * CHUNK : (first + TOGETHER) * CHUNK])
            for group in range(first, first + TOGETHER):
                ds = part_of(sums, group).astype(jnp.bfloat16)
                grad_score[:, GROUP * group : GROUP * (group + 1), :] = ds.reshape(heads, GROUP, CHUNK)
        fetch(step, chunk, 0).wait()
        gl_ref[...] += dot_nt(score[slot, chunk], grad_logit[...])
        for quad in range(quads):
            ds = grad_score[quad * per_quad : (quad + 1) * per_quad].reshape(per_quad * UNIT, CHUNK)
            dq = own_lanes(dot_nn(ds, keys(k_ref, chunk, quad)), lane_head, per_quad)
            dq_total[:, quad * CHUNK : (quad + 1) * CHUNK] += dq
            add_to(dk_total, chunk, quad, dot_nn(qxt[quad], ds))

    dq_ref[0, 0] = (dq_total[...] * 0.125).astype(jnp.bfloat16)

    @pl.when(inner == per_row - 1)
    def _():
        @pl.loop(0, lowest)
        def _(key_unit):
            dk_ref[key_unit, 0] = jnp.zeros_like(dk_ref[key_unit, 0])
            dv_ref[key_unit, 0] = jnp.zeros_like(dv_ref[key_unit, 0])

        @pl.loop(lowest, key_units)
        def _(key_unit):
            dk_ref[key_unit, 0] = dk_total[key_unit].astype(jnp.bfloat16).T
            dv_ref[key_unit, 0] = dv_total[key_unit].astype(jnp.bfloat16).T


def attention_bwd(blocks, q, k, v, grad_out, kept, mixes, heads):
    per_row, micros, _, width = q.shape
    key_units = k.shape[0]
    wide = heads * GROUP
    groups = UNIT // GROUP
    quads = width // CHUNK
    turned = (quads, CHUNK, heads // quads * UNIT)
    unit_spec, kv_spec, mix_spec = attention_specs(q, k, heads)
    sum_spec = pl.BlockSpec((wide, wide), lambda m, u, _: (0, 0))
    anywhere = pl.BlockSpec(memory_space=pl.ANY)
    return pl.pallas_call(
        partial(bwd_kernel, heads),
        grid_spec=pltpu.PrefetchScalarGridSpec(
            num_scalar_prefetch=1,
            grid=(micros, per_row),
            in_specs=[unit_spec, kv_spec, kv_spec, unit_spec, mix_spec] + [anywhere] * 3,
            out_specs=[unit_spec, kv_spec, kv_spec, sum_spec, sum_spec],
            scratch_shapes=[
                pltpu.VMEM(turned, jnp.bfloat16),
                pltpu.VMEM((quads, heads // quads * UNIT, CHUNK), jnp.bfloat16),
                pltpu.VMEM(turned, jnp.bfloat16),
            ]
            + [pltpu.VMEM((2,) + shape, jnp.bfloat16) for shape in kept_shapes(heads)]
            + [
                pltpu.VMEM((MAX_CHUNKS, wide, groups * CHUNK), jnp.bfloat16),
                pltpu.VMEM((wide, groups * CHUNK), jnp.bfloat16),
                pltpu.VMEM((wide, groups * CHUNK), jnp.bfloat16),
                pltpu.VMEM((heads, UNIT, CHUNK), jnp.bfloat16),
                pltpu.VMEM((groups, wide, UNIT), jnp.float32),
                pltpu.VMEM((UNIT, width), jnp.float32),
                pltpu.VMEM((key_units, width, UNIT), jnp.float32),
                pltpu.VMEM((key_units, width, UNIT), jnp.float32),
                pltpu.SemaphoreType.DMA((3, 2, MAX_CHUNKS)),
            ],
        ),
        out_shape=[
            jax.ShapeDtypeStruct(q.shape, jnp.bfloat16),
            jax.ShapeDtypeStruct(k.shape, jnp.bfloat16),
            jax.ShapeDtypeStruct(v.shape, jnp.bfloat16),
            jax.ShapeDtypeStruct((wide, wide), jnp.float32),
            jax.ShapeDtypeStruct((wide, wide), jnp.float32),
        ],
        compiler_params=pltpu.CompilerParams(vmem_limit_bytes=58 * 1024 * 1024),
        cost_estimate=pl.CostEstimate(flops=45_000_000_000, bytes_accessed=40_000_000, transcendentals=0),
        name="attention_bwd",
    )(blocks, q, k, v, grad_out, mixes, *kept)


def piece_bases(key_units, per_row):
    sizes = [1] + [per_row] * ((key_units - 1) // per_row)
    return [(sum(sizes[:at]), size) for at, size in enumerate(sizes)]


def project_kernel(low_ref, *refs):
    pieces, (w_q, w_k, w_v, q_ref, k_ref, v_ref) = (refs[:-6], refs[-6:])
    key_units, width = (k_ref.shape[0], k_ref.shape[3])
    per_row = q_ref.shape[0]
    low = low_ref[pl.program_id(0)]

    for piece, (base, size) in zip(pieces, piece_bases(key_units, per_row)):
        @pl.when(base + size > low)
        def _():
            rows = piece[:, 0].reshape(size * UNIT, width)
            k_ref[base : base + size, 0] = dot_nn(rows, w_k[...]).astype(jnp.bfloat16).reshape(size, UNIT, width)
            v_ref[base : base + size, 0] = dot_nn(rows, w_v[...]).astype(jnp.bfloat16).reshape(size, UNIT, width)

    rows = pieces[-1][:, 0].reshape(per_row * UNIT, width)
    query = dot_nn(rows, w_q[...]).astype(jnp.bfloat16) * jnp.bfloat16(0.125)
    q_ref[:, 0] = query.reshape(per_row, UNIT, width)


def project(low, pieces, weights):
    micros, width = pieces[0].shape[1], pieces[0].shape[3]
    key_units = sum(piece.shape[0] for piece in pieces)
    per_row = pieces[-1].shape[0]

    def spec(units):
        return pl.BlockSpec((units, 1, UNIT, width), lambda m, _: (0, m, 0, 0))

    weight_spec = pl.BlockSpec((width, width), lambda m, _: (0, 0))
    shapes = [(units, micros, UNIT, width) for units in (per_row, key_units, key_units)]
    return pl.pallas_call(
        project_kernel,
        grid_spec=pltpu.PrefetchScalarGridSpec(
            num_scalar_prefetch=1,
            grid=(micros,),
            in_specs=[spec(piece.shape[0]) for piece in pieces] + [weight_spec] * 3,
            out_specs=[spec(shape[0]) for shape in shapes],
        ),
        out_shape=[jax.ShapeDtypeStruct(shape, jnp.bfloat16) for shape in shapes],
        compiler_params=pltpu.CompilerParams(vmem_limit_bytes=44 * 1024 * 1024),
        cost_estimate=pl.CostEstimate(flops=6_000_000_000, bytes_accessed=15_000_000, transcendentals=0),
        name="project",
    )(low, *pieces, *weights)


def project_back_kernel(low_ref, dq_ref, dk_ref, dv_ref, w_q, w_k, w_v, *outs):
    key_units, width = (dk_ref.shape[0], dk_ref.shape[3])
    per_row = dq_ref.shape[0]
    low = low_ref[pl.program_id(0)]
    bases = piece_bases(key_units, per_row)

    def from_keys(base, size):
        rows = slice(base, base + size)
        key_term = dot_nt(dk_ref[rows, 0].reshape(size * UNIT, width), w_k[...])
        return key_term + dot_nt(dv_ref[rows, 0].reshape(size * UNIT, width), w_v[...])

    for out, (base, size) in zip(outs[:-1], bases[:-1]):
        @pl.when(base + size > low)
        def _():
            out[:, 0] = from_keys(base, size).astype(jnp.bfloat16).reshape(size, UNIT, width)

        @pl.when(base + size <= low)
        def _():
            out[...] = jnp.zeros_like(out)

    own = from_keys(*bases[-1]) + dot_nt(dq_ref[:, 0].reshape(per_row * UNIT, width), w_q[...])
    outs[-1][:, 0] = own.reshape(per_row, UNIT, width)


def project_back(low, grad_query, grad_key, grad_value, weights):
    per_row, micros, _, width = grad_query.shape
    key_units = grad_key.shape[0]

    def spec(units):
        return pl.BlockSpec((units, 1, UNIT, width), lambda m, _: (0, m, 0, 0))

    weight_spec = pl.BlockSpec((width, width), lambda m, _: (0, 0))
    sizes = [size for _, size in piece_bases(key_units, per_row)]
    shapes = [(size, micros, UNIT, width) for size in sizes]
    kinds = [jnp.bfloat16] * (len(sizes) - 1) + [jnp.float32]
    return pl.pallas_call(
        project_back_kernel,
        grid_spec=pltpu.PrefetchScalarGridSpec(
            num_scalar_prefetch=1,
            grid=(micros,),
            in_specs=[spec(per_row), spec(key_units), spec(key_units)] + [weight_spec] * 3,
            out_specs=[spec(size) for size in sizes],
        ),
        out_shape=[jax.ShapeDtypeStruct(shape, kind) for shape, kind in zip(shapes, kinds)],
        compiler_params=pltpu.CompilerParams(vmem_limit_bytes=44 * 1024 * 1024),
        cost_estimate=pl.CostEstimate(flops=6_000_000_000, bytes_accessed=15_000_000, transcendentals=0),
        name="project_back",
    )(low, grad_query, grad_key, grad_value, *weights)


def weigh_kernel(low_ref, dq_ref, dk_ref, dv_ref, *refs):
    pieces, (grad_ref, total) = (refs[:-2], refs[-2:])
    key_units, width = (dk_ref.shape[0], dk_ref.shape[3])
    per_row = dq_ref.shape[0]
    micro = pl.program_id(0)
    low = low_ref[micro]
    bases = piece_bases(key_units, per_row)

    @pl.when(micro == 0)
    def _():
        total[...] = jnp.zeros_like(total)

    def keys(ref, base, size):
        return ref[base : base + size, 0].reshape(size * UNIT, width)

    for piece, (base, size) in zip(pieces, bases):
        @pl.when(base + size > low)
        def _():
            turned = piece[:, 0].reshape(size * UNIT, width).T
            total[1] += dot_nn(turned, keys(dk_ref, base, size))
            total[2] += dot_nn(turned, keys(dv_ref, base, size))
            if base + size == key_units:
                total[0] += dot_nn(turned, keys(dq_ref, 0, per_row))

    @pl.when(micro == pl.num_programs(0) - 1)
    def _():
        grad_ref[...] = total[...].astype(jnp.bfloat16)


def weigh(low, grad_query, grad_key, grad_value, pieces):
    per_row, micros, _, width = grad_query.shape
    key_units = grad_key.shape[0]

    def spec(units):
        return pl.BlockSpec((units, 1, UNIT, width), lambda m, _: (0, m, 0, 0))

    sizes = [size for _, size in piece_bases(key_units, per_row)]
    return pl.pallas_call(
        weigh_kernel,
        grid_spec=pltpu.PrefetchScalarGridSpec(
            num_scalar_prefetch=1,
            grid=(micros,),
            in_specs=[spec(size) for size in [per_row, key_units, key_units] + sizes],
            out_specs=pl.BlockSpec((3, width, width), lambda m, _: (0, 0, 0)),
            scratch_shapes=[pltpu.VMEM((3, width, width), jnp.float32)],
        ),
        out_shape=jax.ShapeDtypeStruct((3, width, width), jnp.bfloat16),
        compiler_params=pltpu.CompilerParams(vmem_limit_bytes=48 * 1024 * 1024),
        cost_estimate=pl.CostEstimate(flops=12_000_000_000, bytes_accessed=14_000_000, transcendentals=0),
        name="weigh",
    )(low, grad_query, grad_key, grad_value, *pieces)


def feed_kernel(x_ref, att_ref, w_o_ref, gain_ref, up_ref, down_ref, cot_ref,
                mid_ref, out_ref, grad_hidden_ref, grad_up_ref, grad_down_ref,
                hidden, turned, out_total, back_total):
    step = pl.program_id(0)

    @pl.when(step == 0)
    def _():
        middle = x_ref[...].astype(jnp.float32) + dot_nn(att_ref[...], w_o_ref[...])
        mid_ref[...] = middle
        inv_rms = lax.rsqrt(jnp.mean(middle * middle, axis=-1, keepdims=True) + norm_eps)
        rows = (middle * inv_rms * gain_ref[...]).astype(jnp.bfloat16)
        hidden[...] = rows
        turned[...] = rows.T
        out_total[...] = jnp.zeros_like(out_total)
        back_total[...] = jnp.zeros_like(back_total)

    for start in range(0, up_ref.shape[2], FF_STEP):
        cols = slice(start, start + FF_STEP)
        up = dot_nn(hidden[...], up_ref[0, :, cols])
        square = up * up
        bent = jnp.tanh(gelu_scale * up * (1.0 + gelu_cube * square))
        half = 0.5 + 0.5 * bent
        slope = half + 0.5 * up * (1.0 - bent * bent) * (gelu_scale * (1.0 + 3.0 * gelu_cube * square))
        active = (up * half).astype(jnp.bfloat16)
        grad_up = (dot_nt(cot_ref[...], down_ref[cols, :]) * slope).astype(jnp.bfloat16)
        out_total[...] += dot_nn(active, down_ref[cols, :])
        back_total[...] += dot_nt(grad_up, up_ref[0, :, cols])
        grad_down_ref[cols, :] = dot_nn(active.T, cot_ref[...]).astype(jnp.bfloat16)
        grad_up_ref[0, :, cols] = dot_nn(turned[...], grad_up).astype(jnp.bfloat16)

    @pl.when(step == pl.num_programs(0) - 1)
    def _():
        out_ref[...] = (mid_ref[...] + out_total[...]).astype(jnp.bfloat16)
        grad_hidden_ref[...] = back_total[...]


def feed_forward(rows, attended, w_o, gain, w_up, w_down, cot):
    tokens, width = rows.shape
    pieces = w_up.shape[0]
    whole = pl.BlockSpec((tokens, width), lambda i: (0, 0))
    up_spec = pl.BlockSpec((1, width, width), lambda i: (i, 0, 0))
    down_spec = pl.BlockSpec((width, width), lambda i: (i, 0))
    f32, bf16 = (jnp.float32, jnp.bfloat16)
    return pl.pallas_call(
        feed_kernel,
        grid=(pieces,),
        in_specs=[
            whole,
            whole,
            pl.BlockSpec((width, width), lambda i: (0, 0)),
            pl.BlockSpec((1, width), lambda i: (0, 0)),
            up_spec,
            down_spec,
            whole,
        ],
        out_specs=[whole, whole, whole, up_spec, down_spec],
        out_shape=[
            jax.ShapeDtypeStruct((tokens, width), f32),
            jax.ShapeDtypeStruct((tokens, width), bf16),
            jax.ShapeDtypeStruct((tokens, width), f32),
            jax.ShapeDtypeStruct(w_up.shape, bf16),
            jax.ShapeDtypeStruct(w_down.shape, bf16),
        ],
        scratch_shapes=[
            pltpu.VMEM((tokens, width), bf16),
            pltpu.VMEM((width, tokens), bf16),
            pltpu.VMEM((tokens, width), f32),
            pltpu.VMEM((tokens, width), f32),
        ],
        compiler_params=pltpu.CompilerParams(vmem_limit_bytes=48 * 1024 * 1024),
        cost_estimate=pl.CostEstimate(flops=16_000_000_000, bytes_accessed=30_000_000, transcendentals=0),
        name="feed_forward",
    )(rows, attended, w_o, gain, w_up, w_down, cot)


def spread_mixes(mix_logits, mix_weights):
    heads = mix_logits.shape[0]
    wide = heads * GROUP
    place = jnp.arange(wide, dtype=jnp.int32)
    pick = (place[:, None] // GROUP == jnp.arange(heads, dtype=jnp.int32)[None, :]).astype(mix_logits.dtype)
    same_row = (place[:, None] % GROUP == place[None, :] % GROUP)[None]
    tables = jnp.stack([mix_logits.T, mix_logits, mix_weights.T, mix_weights]).reshape(4 * heads, heads)
    across = jnp.dot(tables, pick.T, preferred_element_type=jnp.float32).astype(mix_logits.dtype)
    down = jnp.einsum("wh,bhx->bwx", pick, across.reshape(4, heads, wide), preferred_element_type=jnp.float32)
    return jnp.where(same_row, down, 0.0).astype(mix_logits.dtype)


def fold_mix(wide, heads):
    place = jnp.arange(heads * GROUP, dtype=jnp.int32)
    pick = (place[:, None] // GROUP == jnp.arange(heads, dtype=jnp.int32)[None, :]).astype(jnp.float32)
    same_row = place[:, None] % GROUP == place[None, :] % GROUP
    down = jnp.dot(pick.T, jnp.where(same_row, wide, 0.0), precision=lax.Precision.HIGHEST)
    return jnp.dot(down, pick, precision=lax.Precision.HIGHEST)


def from_behind(value, steps):
    count = lax.axis_size("dev")
    first, last = (max(0, -steps), min(count, count - steps))
    return lax.ppermute(value, "dev", [(source, source + steps) for source in range(first, last)])


def with_sibling(value):
    count = lax.axis_size("dev")
    return lax.ppermute(value, "dev", [(source, source ^ 1) for source in range(count)])


def earlier_rows(own):
    size = own.shape[0]
    first_core = lax.axis_index("dev") % 2 == 0
    two, four = (from_behind(own, 2), from_behind(own, 4))
    give = jnp.concatenate([jnp.where(first_core, own, two), jnp.where(first_core, two, four)], axis=0)
    came = with_sibling(give)
    return [four[size - 1 :], came[size:], two, came[:size], own]


def return_rows(four, two, came, beside):
    size = two.shape[0]
    first_core = lax.axis_index("dev") % 2 == 0
    came = came.astype(jnp.float32)
    one, three = (came[:size], came[size:])
    give_two = two.astype(jnp.float32) + jnp.where(first_core, three, one)
    padded = jnp.pad(four.astype(jnp.float32), ((size - four.shape[0], 0), (0, 0), (0, 0), (0, 0)))
    give_four = padded + jnp.where(first_core, 0.0, three)
    back_two = from_behind(give_two.astype(jnp.bfloat16), -2)
    back_two, give_four, beside = lax.optimization_barrier((back_two, give_four.astype(jnp.bfloat16), beside))
    back_four = from_behind(give_four, -4)
    return ((jnp.where(first_core, one, 0.0), back_two, back_four), beside)


def seq_starts(lengths_row, query_rows):
    seq_ends = jnp.cumsum(lengths_row)
    starts = seq_ends - lengths_row
    return jnp.max(jnp.where(starts[None, :] <= query_rows[:, None], starts[None, :], 0), axis=1)


def normalize(values, gain_vec):
    inv_rms = lax.rsqrt(jnp.mean(values * values, axis=-1, keepdims=True) + norm_eps)
    normed = values * inv_rms
    return (normed, inv_rms, (normed * gain_vec.astype(jnp.float32)).astype(jnp.bfloat16))


def norm_back(grad_hidden, normed, inv_rms, gain_vec):
    grad_gain = jnp.sum(grad_hidden * normed, axis=0)
    grad_normed = grad_hidden * gain_vec.astype(jnp.float32)
    inner_mean = jnp.mean(grad_normed * normed, axis=-1, keepdims=True)
    return (inv_rms * (grad_normed - normed * inner_mean), grad_gain)


def matmul(left, right):
    return jnp.dot(left, right, preferred_element_type=jnp.float32)


def matmul_left_t(left, right):
    return lax.dot_general(left, right, (((0,), (0,)), ((), ())), preferred_element_type=jnp.float32)


def matmul_right_t(left, right):
    return lax.dot_general(left, right, (((1,), (1,)), ((), ())), preferred_element_type=jnp.float32)


def exchange(value):
    return lax.all_to_all(value, "dev", split_axis=0, concat_axis=0, tiled=True)


def split_ids(tok_ids, own_rows):
    owner = tok_ids // own_rows
    place = jnp.arange(tok_ids.shape[0], dtype=jnp.int32)
    same = tok_ids[:, None] == tok_ids[None, :]
    repeated = jnp.any(same & (place[None, :] < place[:, None]), axis=1)
    before = (owner[:, None] == owner[None, :]) & (tok_ids[None, :] < tok_ids[:, None]) & ~repeated[None, :]
    return (owner, tok_ids % own_rows, jnp.sum(before, axis=1, dtype=jnp.int32))


def ask_round(ids, index, own_rows, stride, room):
    count = lax.axis_size("dev")
    owner, local, rank = ids
    here = rank - index * room
    slot = jnp.where((here >= 0) & (here < room), owner * stride + here, -1)
    chosen = slot[None, :] == jnp.arange(count * stride, dtype=jnp.int32)[:, None]
    wanted = jnp.max(jnp.where(chosen, local[None, :], -1), axis=1).reshape(count, stride)
    rounds = jnp.broadcast_to(jnp.max(rank) // room + 1, (count, stride))
    return (jnp.concatenate([wanted, rounds], axis=1), chosen.astype(jnp.bfloat16))


def hear_round(message, own_rows, stride):
    asked = exchange(message)
    pick = asked[:, :stride].reshape(-1, 1) == jnp.arange(own_rows, dtype=jnp.int32)[None, :]
    return (pick.astype(jnp.bfloat16), jnp.max(asked[:, stride:]))


def plan_round(ids, index, own_rows, stride, room):
    message, chosen = ask_round(ids, index, own_rows, stride, room)
    pick, _ = hear_round(message, own_rows, stride)
    return (chosen, pick)


def answer(embedding, chosen, pick, stride, extra_row, beside=None):
    count = lax.axis_size("dev")
    rows = matmul(pick, embedding).astype(jnp.bfloat16).reshape(count, stride, -1)
    if extra_row is not None:
        is_extra = (jnp.arange(stride, dtype=jnp.int32) == stride - 1)[None, :, None]
        rows = jnp.where(is_extra, extra_row[None, None, :], rows)
    rows, beside = lax.optimization_barrier((rows.reshape(count * stride, -1), beside))
    got = exchange(rows)
    extra = got.reshape(count, stride, -1)[:, stride - 1]
    return (matmul_left_t(chosen, got).astype(jnp.bfloat16), extra, beside)


def lookup(embedding, ids, message, chosen, extra_row, stride, room, beside):
    own_rows = embedding.shape[0]
    pick, rounds = hear_round(message, own_rows, stride)
    first, extra, beside = answer(embedding, chosen, pick, stride, extra_row, beside)

    def more(carry):
        index, rows = carry
        again, its_pick = plan_round(ids, index, own_rows, stride, room)
        return (index + 1, rows + answer(embedding, again, its_pick, stride, None)[0])

    _, rows = lax.while_loop(lambda carry: carry[0] < rounds, more, (jnp.int32(1), first))
    return (rows, extra, beside, ids, chosen, pick, rounds)


def send_grads(grad_low, chosen, pick, stride, extra_rows, beside=None):
    count = lax.axis_size("dev")
    summed = matmul(chosen, grad_low).astype(jnp.bfloat16).reshape(count, stride, -1)
    if extra_rows is not None:
        place = jnp.arange(stride, dtype=jnp.int32)[None, :, None]
        high, low = extra_rows
        summed = jnp.where(place == stride - 2, high[:, None, :], summed)
        summed = jnp.where(place == stride - 1, low[:, None, :], summed)
    summed, beside = lax.optimization_barrier((summed.reshape(count * stride, -1), beside))
    got = exchange(summed)
    return (matmul_left_t(pick, got), got.reshape(count, stride, -1)[:, stride - 2 :], beside)


def table_back(grad_rows, extra_rows, plan, own_rows, stride, room, beside):
    ids, chosen, pick, rounds = plan
    grad_low = grad_rows.astype(jnp.bfloat16)
    first, extra, beside = send_grads(grad_low, chosen, pick, stride, extra_rows, beside)

    def more(carry):
        index, total = carry
        again, its_pick = plan_round(ids, index, own_rows, stride, room)
        return (index + 1, total + send_grads(grad_low, again, its_pick, stride, None)[0])

    _, total = lax.while_loop(lambda carry: carry[0] < rounds, more, (jnp.int32(1), first))
    return (total, jnp.sum(extra.astype(jnp.float32), axis=(0, 1)), beside)


def double(held, bit, axis):
    count = lax.axis_size("dev")
    low = ((lax.axis_index("dev") >> bit) & 1) == 0
    came = lax.ppermute(held, "dev", [(source, source ^ (1 << bit)) for source in range(count)])
    return jnp.stack([jnp.where(low, held, came), jnp.where(low, came, held)], axis=axis)


def spread_z(shard, first, last):
    bits = lax.axis_size("dev").bit_length() - 1
    for done in range(first, min(last, bits - 3)):
        shard = double(shard, bits - 1 - done, done)
    return shard


def spread_plane(held):
    at, half = (lax.axis_size("dev").bit_length() - 4, held.shape[-1] // 2)
    left = double(double(held[..., :half], 2, at), 1, at + 1)
    right = double(double(held[..., half:], 1, at), 2, at)
    return (left, right)


def spread_cores(halves):
    whole = jnp.concatenate(halves, axis=-1)
    return double(whole, 0, lax.axis_size("dev").bit_length() - 2)


def gather_late(pieces, part, up_cols):
    width = pieces[0].shape[1]
    whole = lax.all_gather(jnp.concatenate(pieces, axis=0), "dev", axis=0)
    middle = part * (1 + up_cols)
    up = whole[:, part:middle].reshape(-1, up_cols, part, width).swapaxes(0, 1)
    return (whole[:, :part].reshape(-1, width), up.reshape(up_cols, -1, width), whole[:, middle:].reshape(-1, width))


def split_rows(summed, sizes):
    pieces, start = ([], 0)
    for size in sizes:
        pieces.append(summed[start : start + size])
        start += size
    return pieces


def swap_parts(held, bit):
    count = lax.axis_size("dev")
    mine = (lax.axis_index("dev") >> bit) & 1
    keep = lax.dynamic_index_in_dim(held, mine, 0, keepdims=False)
    give = lax.dynamic_index_in_dim(held, 1 - mine, 0, keepdims=False)
    return (keep, lax.ppermute(give, "dev", [(source, source ^ (1 << bit)) for source in range(count)]))


def join_parts(parts, last=False):
    total = parts[0].astype(jnp.float32) + parts[1].astype(jnp.float32)
    return total if last else total.astype(jnp.bfloat16)


def swap_halves(held, bit, last=False):
    return join_parts(swap_parts(held, bit), last)


def middle_bits():
    return list(range(1, lax.axis_size("dev").bit_length() - 2))


def sum_cores(term):
    count, pieces, rows, width = term.shape
    grid = term.reshape(count // 2, 2, pieces, rows, width)
    return swap_halves(grid.swapaxes(0, 1), 0).reshape(count // 2, pieces * rows, width)


def cut_thirds(held):
    _, rows, width = held.shape
    middle = middle_bits()
    bits = len(middle) + 1
    grid = held.reshape((2,) * bits + (rows, width))
    thirds = []
    for turn in range(3):
        shift = turn % len(middle)
        order = middle[shift:] + middle[:shift] + [bits]
        axes = [bits - bit for bit in order]
        part = grid[..., turn * (width // 3) : (turn + 1) * (width // 3)]
        thirds.append(part.transpose(axes + [bits, bits + 1]))
    return thirds


def sum_stage(thirds, stage):
    middle = middle_bits()
    return [swap_halves(third, middle[(turn + stage) % len(middle)]) for turn, third in enumerate(thirds)]


def sum_stages(thirds, first):
    for stage in range(first, len(middle_bits())):
        thirds = sum_stage(thirds, stage)
    return thirds


def sum_last(groups):
    whole = [jnp.concatenate(thirds, axis=-1) for thirds in groups]
    return swap_halves(jnp.concatenate(whole, axis=1), len(middle_bits()) + 1, True)


def split_low(values):
    high = lax.reduce_precision(values, 8, 7)
    return (high.astype(jnp.bfloat16), (values - high).astype(jnp.bfloat16))


def low_units(blocks):
    per_row = blocks.shape[1]
    place = 8 + jnp.arange(per_row, dtype=jnp.int32)[None, :]
    return jnp.min(place - 2 * ((blocks + 1) // 2), axis=1).astype(jnp.int32)


def by_unit(array):
    cut = array.reshape((array.shape[0], array.shape[1] // UNIT, UNIT) + array.shape[2:])
    return cut.swapaxes(0, 1)


def by_row(array, micros):
    cut = array.reshape(-1, micros, UNIT, array.shape[-1])
    return cut.swapaxes(0, 1).reshape(micros, -1, array.shape[-1])


def shards(
    token_ids,
    lengths,
    embedding,
    norm1_gain,
    w_query,
    w_key,
    w_value,
    w_out,
    mix_logits,
    mix_weights,
    norm2_gain,
    w_up,
    w_down,
    cotangent,
):
    count = lax.axis_size("dev")
    me = lax.axis_index("dev")
    micros, row_count = token_ids.shape
    own_rows, width = embedding.shape
    heads = mix_logits.shape[0]
    part = norm1_gain.shape[0]
    per_row = row_count // UNIT
    tokens = micros * row_count
    tok_ids = by_unit(token_ids).reshape(-1)
    stride = max(16, 1024 // count)
    room = stride - 2

    unit_rows = me * row_count + UNIT * jnp.arange(per_row, dtype=jnp.int32)
    begins = jnp.stack([seq_starts(lengths[micro], unit_rows) for micro in range(micros)])
    blocks = ((unit_rows[None, :] - begins) // UNIT + 1).reshape(-1).astype(jnp.int32)

    lows = low_units(blocks.reshape(micros, per_row))
    mixes = spread_mixes(mix_logits, mix_weights)

    up_cols = w_up.shape[1] // width
    up_pieces = [w_up[:, col * width : (col + 1) * width] for col in range(up_cols)]
    first_weights = spread_z(jnp.stack([w_query, w_key, w_value]), 0, 1)
    weight_pieces = [w_out] + up_pieces + [w_down]
    ids = split_ids(tok_ids, own_rows)
    message, chosen = ask_round(ids, 0, own_rows, stride, room)
    message, first_weights, weight_pieces = lax.optimization_barrier((message, first_weights, weight_pieces))
    first_weights = spread_plane(spread_z(first_weights, 1, 99))
    w_o, w_u, w_d = gather_late(weight_pieces, part, up_cols)
    gains_row = jnp.concatenate([norm1_gain, norm2_gain, jnp.zeros((width - 2 * part,), jnp.bfloat16)])
    picked, gains, first_weights, *plan = lookup(
        embedding, ids, message, chosen, gains_row, stride, room, first_weights
    )
    gain_one = gains[:, :part].reshape(-1)
    gain_two = gains[:, part : 2 * part].reshape(-1)
    inputs = picked.astype(jnp.float32)

    normed_one, inv_one, hidden_one = normalize(inputs, gain_one)
    own_hidden = hidden_one.reshape(per_row, micros, UNIT, width)
    pieces = earlier_rows(own_hidden)
    first_weights = spread_cores(first_weights).reshape(count, 3, part, width)
    w_q, w_k, w_v = (first_weights[:, at].reshape(-1, width) for at in range(3))
    query, key, value = project(lows, pieces, (w_q, w_k, w_v))
    attended, *kept = attention_fwd(blocks, query, key, value, mixes, heads)
    attended = attended.reshape(tokens, width)

    grad_rows = by_unit(cotangent).reshape(tokens, width)
    gain_row = gain_two.astype(jnp.float32)[None, :]
    middle, output, grad_hidden_two, grad_up, grad_down = feed_forward(
        picked, attended, w_o, gain_row, w_u, w_d, grad_rows
    )
    inv_two = lax.rsqrt(jnp.mean(middle * middle, axis=-1, keepdims=True) + norm_eps)
    normed_two = middle * inv_two
    grad_mid_norm, grad_gain_two = norm_back(grad_hidden_two, normed_two, inv_two, gain_two)
    grad_middle = grad_rows.astype(jnp.float32) + grad_mid_norm
    grad_branch = grad_middle.astype(jnp.bfloat16)
    grad_wout = matmul_left_t(attended, grad_branch)
    grad_att = matmul_right_t(grad_branch, w_o).astype(jnp.bfloat16).reshape(own_hidden.shape)
    up_rows = grad_up.reshape(up_cols, count, part, width).swapaxes(0, 1).reshape(count, -1, width)
    stack = jnp.concatenate([grad_down.reshape(count, -1, width), up_rows], axis=1).reshape(-1, width)
    stack, grad_att = lax.optimization_barrier((stack, grad_att))
    late_sums = lax.psum_scatter(stack, "dev", scatter_dimension=0, tiled=True).astype(jnp.float32)

    def tail(pieces, query, key, value, grad_att, kept, grad_wout):
        grad_query, grad_key, grad_value, wide_logit, wide_prob = attention_bwd(
            blocks, query, key, value, grad_att, kept, mixes, heads
        )
        *terms, grad_own = project_back(lows, grad_query, grad_key, grad_value, (w_q, w_k, w_v))
        came = with_sibling(jnp.concatenate([terms[3], terms[1]], axis=0))
        came, grads, hidden = lax.optimization_barrier((came, (grad_query, grad_key, grad_value), pieces))
        grad_qkv = weigh(lows, *grads, hidden)
        backs, grad_qkv = return_rows(terms[0], terms[2], came, grad_qkv)
        early_terms = jnp.concatenate([grad_qkv, grad_wout.astype(jnp.bfloat16)[None]], axis=0)
        early = cut_thirds(sum_cores(early_terms.reshape(4, count, part, width).swapaxes(0, 1)))
        backs, early = lax.optimization_barrier((backs, early))
        grad_own = grad_own + backs[0] + backs[1].astype(jnp.float32) + backs[2].astype(jnp.float32)
        early = sum_stage(early, 0)
        grad_hidden_one = grad_own.reshape(tokens, width)
        grad_in_norm, grad_gain_one = norm_back(grad_hidden_one, normed_one, inv_one, gain_one)
        grad_inputs = grad_middle + grad_in_norm

        mix_terms = jnp.concatenate([fold_mix(wide_logit, heads).reshape(-1), fold_mix(wide_prob, heads).reshape(-1)])
        mix_size = mix_terms.shape[0]
        small = jnp.concatenate(
            [
                grad_gain_one.reshape(count, part),
                grad_gain_two.reshape(count, part),
                jnp.broadcast_to(mix_terms[None, :], (count, mix_size)),
                jnp.zeros((count, width - 2 * part - mix_size), jnp.float32),
            ],
            axis=1,
        )
        table_grad, small_sum, early = table_back(grad_inputs, split_low(small), plan, own_rows, stride, room, early)
        return (grad_inputs, table_grad, small_sum, sum_last([sum_stages(early, 1)]))

    def no_tail(*operands):
        sizes = ((tokens, width), (own_rows, width), (width,), (4 * part, width))
        return tuple(jnp.zeros(size, jnp.float32) for size in sizes)

    grad_inputs, table_grad, small_sum, early_sums = lax.cond(
        plan[-1] > 0, tail, no_tail, pieces, query, key, value, grad_att, kept, grad_wout
    )
    early_sums = split_rows(early_sums, [part] * 4)
    late_sums = split_rows(late_sums, [w_down.shape[0]] + [part] * up_cols)
    mix_size = 2 * heads * heads
    mixes = small_sum[2 * part : 2 * part + mix_size].reshape(2, heads, heads)
    return (
        by_row(output, micros),
        by_row(grad_inputs, micros),
        table_grad,
        small_sum[:part],
        *early_sums,
        mixes[0],
        mixes[1],
        small_sum[part : 2 * part],
        jnp.concatenate(late_sums[1:], axis=1),
        late_sums[0],
    )


def solution(mesh):
    in_specs = (
        P(None, "dev"),
        P(),
        P("dev", None),
        P("dev"),
        P("dev", None),
        P("dev", None),
        P("dev", None),
        P("dev", None),
        P(),
        P(),
        P("dev"),
        P("dev", None),
        P("dev", None),
        P(None, "dev", None),
    )
    out_specs = (
        P(None, "dev", None),
        P(None, "dev", None),
        P("dev", None),
        P("dev"),
        P("dev", None),
        P("dev", None),
        P("dev", None),
        P("dev", None),
        P(),
        P(),
        P("dev"),
        P("dev", None),
        P("dev", None),
    )
    return jax.shard_map(shards, mesh=mesh, in_specs=in_specs, out_specs=out_specs, check_vma=False)
```

```python
from functools import partial

import jax
import jax.numpy as jnp
from jax import lax
from jax.experimental import pallas as pl
from jax.experimental.pallas import tpu as pltpu
from jax.sharding import PartitionSpec as P

norm_eps = 1e-06
gelu_scale = 0.7978845608028654
gelu_cube = 0.044715
FF_STEP = 256

masked = -1e30
UNIT = 128
CHUNK = 256
GROUP = 16
MAX_CHUNKS = 4
TOGETHER = 4


def dot_nn(left, right):
    return lax.dot_general(left, right, (((1,), (0,)), ((), ())), preferred_element_type=jnp.float32)


def dot_nt(left, right):
    return lax.dot_general(left, right, (((1,), (1,)), ((), ())), preferred_element_type=jnp.float32)


def spread_heads(rows, lane_head, quad, heads_per_quad):
    part = rows[:, quad * CHUNK : (quad + 1) * CHUNK]
    zero = jnp.zeros_like(part)
    return jnp.concatenate([jnp.where(lane_head == head, part, zero) for head in range(heads_per_quad)], axis=0)


def own_lanes(wide, lane_head, heads_per_quad):
    total = jnp.where(lane_head == 0, wide[:UNIT], 0.0)
    for head in range(1, heads_per_quad):
        total = total + jnp.where(lane_head == head, wide[head * UNIT : (head + 1) * UNIT], 0.0)
    return total


def part_of(sums, group):
    start = group % TOGETHER * CHUNK
    return sums[:, start : start + CHUNK]


def allowed_keys(chunk, group, blocks):
    key = lax.broadcasted_iota(jnp.int32, (GROUP, CHUNK), 1) - (UNIT + CHUNK * chunk)
    row = lax.broadcasted_iota(jnp.int32, (GROUP, CHUNK), 0) + GROUP * group
    return (key <= row) & (key >= (1 - blocks) * UNIT)


def twice(rows):
    return jnp.concatenate([rows, rows], axis=-1)


def put_groups(ref, quad, per_quad, term):
    low = term.astype(jnp.bfloat16)
    for head in range(per_quad):
        rows = slice((quad * per_quad + head) * GROUP, (quad * per_quad + head + 1) * GROUP)
        for group in range(UNIT // GROUP):
            start = head * UNIT + group * GROUP
            ref[rows, group * CHUNK : (group + 1) * CHUNK] = low[start : start + GROUP]


def fwd_kernel(heads, blocks_ref, q_ref, k_ref, v_ref, mix_ref, att_ref, score_out, prob_out, mixed_out,
               qx, score, prob, mixed, logit, top, norm, total, sems):
    micro, inner, per_row = (pl.program_id(0), pl.program_id(1), pl.num_programs(1))
    blocks = blocks_ref[micro * per_row + inner]
    chunks = (blocks + 1) // 2
    last_unit = k_ref.shape[0] - per_row + inner + 1
    quads = q_ref.shape[3] // CHUNK
    per_quad = heads // quads
    groups = UNIT // GROUP
    wide = heads * GROUP
    lane_head = lax.broadcasted_iota(jnp.int32, (UNIT, CHUNK), 1) // (CHUNK // per_quad)
    for quad in range(quads):
        qx[quad] = spread_heads(q_ref[0, 0], lane_head, quad, per_quad)
    total[...] = jnp.zeros_like(total)
    top[...] = jnp.full_like(top, masked)
    norm[...] = jnp.zeros_like(norm)

    def keys(ref, chunk, quad):
        units = pl.ds(last_unit - 2 * (chunk + 1), 2)
        return ref[units, 0, :, quad * CHUNK : (quad + 1) * CHUNK].reshape(CHUNK, CHUNK)

    step = micro * per_row + inner

    def keep(at, chunk, kind):
        source, target = ((score, score_out), (prob, prob_out), (mixed, mixed_out))[kind]
        place = target.at[at % per_row, at // per_row, chunk]
        return pltpu.make_async_copy(source.at[chunk], place, sems.at[kind, chunk])

    def finish(at):
        @pl.loop(0, (blocks_ref[at] + 1) // 2)
        def _(chunk):
            for kind in range(3):
                keep(at, chunk, kind).wait()

    @pl.when(step > 0)
    def _():
        finish(step - 1)

    @pl.loop(0, chunks)
    def _(chunk):
        for quad in range(quads):
            put_groups(score.at[chunk], quad, per_quad, dot_nt(qx[quad], keys(k_ref, chunk, quad)))
        keep(step, chunk, 0).start()
        for group in range(groups):
            if group % TOGETHER == 0:
                mixes = dot_nn(mix_ref[0], score[chunk, :, group * CHUNK : (group + TOGETHER) * CHUNK])
            l = part_of(mixes, group)
            l = jnp.where(allowed_keys(chunk, group, blocks)[None], l.reshape(heads, GROUP, CHUNK), masked)
            l = l.reshape(wide, CHUNK)
            logit[chunk, group] = l
            old = top[group]
            new = jnp.maximum(old, jnp.maximum(l[:, :UNIT], l[:, UNIT:]))
            terms = jnp.exp(l[:, :UNIT] - new) + jnp.exp(l[:, UNIT:] - new)
            norm[group] = norm[group] * jnp.exp(old - new) + terms
            top[group] = new

    for group in range(groups):
        lanes = top[group]
        high = jnp.broadcast_to(jnp.max(lanes, axis=-1, keepdims=True), lanes.shape)
        whole = jnp.sum(norm[group] * jnp.exp(lanes - high), axis=-1, keepdims=True)
        top[group] = high + jnp.log(jnp.broadcast_to(whole, lanes.shape))

    @pl.loop(0, chunks)
    def _(chunk):
        for group in range(groups):
            p = jnp.exp(logit[chunk, group] - twice(top[group])).astype(jnp.bfloat16)
            prob[chunk, :, group * CHUNK : (group + 1) * CHUNK] = p
        for first in range(0, groups, TOGETHER):
            sums = dot_nn(mix_ref[2], prob[chunk, :, first * CHUNK : (first + TOGETHER) * CHUNK])
            for group in range(first, first + TOGETHER):
                a = part_of(sums, group).astype(jnp.bfloat16)
                mixed[chunk, :, GROUP * group : GROUP * (group + 1), :] = a.reshape(heads, GROUP, CHUNK)
        keep(step, chunk, 1).start()
        keep(step, chunk, 2).start()
        for quad in range(quads):
            a = mixed[chunk, quad * per_quad : (quad + 1) * per_quad].reshape(per_quad * UNIT, CHUNK)
            o = own_lanes(dot_nn(a, keys(v_ref, chunk, quad)), lane_head, per_quad)
            total[:, quad * CHUNK : (quad + 1) * CHUNK] += o

    att_ref[0, 0] = total[...].astype(jnp.bfloat16)

    @pl.when(step == pl.num_programs(0) * per_row - 1)
    def _():
        finish(step)


def attention_specs(q, k, heads):
    per_row, micros, _, width = q.shape
    wide = heads * GROUP
    return (
        pl.BlockSpec((1, 1, UNIT, width), lambda m, u, _: (u, m, 0, 0)),
        pl.BlockSpec((k.shape[0], 1, UNIT, width), lambda m, u, _: (0, m, 0, 0)),
        pl.BlockSpec((4, wide, wide), lambda m, u, _: (0, 0, 0)),
    )


def kept_shapes(heads):
    wide = heads * GROUP
    flat = (MAX_CHUNKS, wide, UNIT // GROUP * CHUNK)
    return (flat, flat, (MAX_CHUNKS, heads, UNIT, CHUNK))


def attention_fwd(blocks, q, k, v, mixes, heads):
    per_row, micros, _, width = q.shape
    wide = heads * GROUP
    groups = UNIT // GROUP
    quads = width // CHUNK
    unit_spec, kv_spec, mix_spec = attention_specs(q, k, heads)
    kept = kept_shapes(heads)
    anywhere = pl.BlockSpec(memory_space=pl.ANY)
    return pl.pallas_call(
        partial(fwd_kernel, heads),
        grid_spec=pltpu.PrefetchScalarGridSpec(
            num_scalar_prefetch=1,
            grid=(micros, per_row),
            in_specs=[unit_spec, kv_spec, kv_spec, mix_spec],
            out_specs=[unit_spec, anywhere, anywhere, anywhere],
            scratch_shapes=[pltpu.VMEM((quads, heads // quads * UNIT, CHUNK), jnp.bfloat16)]
            + [pltpu.VMEM(shape, jnp.bfloat16) for shape in kept]
            + [
                pltpu.VMEM((MAX_CHUNKS, groups, wide, CHUNK), jnp.float32),
                pltpu.VMEM((groups, wide, UNIT), jnp.float32),
                pltpu.VMEM((groups, wide, UNIT), jnp.float32),
                pltpu.VMEM((UNIT, width), jnp.float32),
                pltpu.SemaphoreType.DMA((3, MAX_CHUNKS)),
            ],
        ),
        out_shape=[jax.ShapeDtypeStruct(q.shape, jnp.bfloat16)]
        + [jax.ShapeDtypeStruct((per_row, micros) + shape, jnp.bfloat16) for shape in kept],
        compiler_params=pltpu.CompilerParams(vmem_limit_bytes=50 * 1024 * 1024),
        cost_estimate=pl.CostEstimate(flops=20_000_000_000, bytes_accessed=30_000_000, transcendentals=0),
        name="attention_fwd",
    )(blocks, q, k, v, mixes)


def bwd_kernel(heads, micro, blocks_ref, q_ref, k_ref, v_ref, do_ref, mix_ref, score_in, prob_in, mixed_in,
               dq_ref, dk_ref, dv_ref, gl_ref, gp_ref,
               qxt, dox, doxt, score, prob, mixed, grad_prob, grad_mixed, grad_logit, grad_score,
               delta, dq_total, dk_total, dv_total, sems):
    inner, per_row = (pl.program_id(0), pl.num_programs(0))
    step = micro * per_row + inner
    slot = step % 2
    blocks = blocks_ref[step]
    chunks = (blocks + 1) // 2
    key_units = k_ref.shape[0]
    last_unit = key_units - per_row + inner + 1
    quads = q_ref.shape[3] // CHUNK
    per_quad = heads // quads
    groups = UNIT // GROUP
    wide = heads * GROUP
    lane_head = lax.broadcasted_iota(jnp.int32, (UNIT, CHUNK), 1) // (CHUNK // per_quad)
    row_head = lax.broadcasted_iota(jnp.int32, (CHUNK, UNIT), 0) // (CHUNK // per_quad)
    lowest = key_units
    for other in range(key_units - 7):
        its_chunks = (blocks_ref[micro * per_row + other] + 1) // 2
        lowest = jnp.minimum(lowest, key_units - per_row + other + 1 - 2 * its_chunks)

    def fetch(at, chunk, kind):
        source, target = ((score_in, score), (prob_in, prob), (mixed_in, mixed))[kind]
        place = source.at[at % per_row, at // per_row, chunk]
        return pltpu.make_async_copy(place, target.at[at % 2, chunk], sems.at[kind, at % 2, chunk])

    def fetch_all(at):
        @pl.loop(0, (blocks_ref[at] + 1) // 2)
        def _(chunk):
            for kind in (1, 2, 0):
                fetch(at, chunk, kind).start()

    @pl.when(inner == 0)
    def _():
        fetch_all(step)
        gl_ref[...] = jnp.zeros_like(gl_ref)
        gp_ref[...] = jnp.zeros_like(gp_ref)

    @pl.when(inner + 1 < per_row)
    def _():
        fetch_all(step + 1)

    @pl.when(inner == 0)
    def _():
        @pl.loop(lowest, key_units)
        def _(key_unit):
            dk_total[key_unit] = jnp.zeros_like(dk_total[key_unit])
            dv_total[key_unit] = jnp.zeros_like(dv_total[key_unit])

    def spread_turned(rows, quad):
        turned = rows[:, quad * CHUNK : (quad + 1) * CHUNK].T
        zero = jnp.zeros_like(turned)
        return jnp.concatenate([jnp.where(row_head == head, turned, zero) for head in range(per_quad)], axis=1)

    for quad in range(quads):
        qxt[quad] = spread_turned(q_ref[0, 0], quad)
        dox[quad] = spread_heads(do_ref[0, 0], lane_head, quad, per_quad)
        doxt[quad] = spread_turned(do_ref[0, 0], quad)
    dq_total[...] = jnp.zeros_like(dq_total)
    delta[...] = jnp.zeros_like(delta)

    def keys(ref, chunk, quad):
        units = pl.ds(last_unit - 2 * (chunk + 1), 2)
        return ref[units, 0, :, quad * CHUNK : (quad + 1) * CHUNK].reshape(CHUNK, CHUNK)

    def add_to(total, chunk, quad, term):
        first = last_unit - 2 * (chunk + 1)
        lanes = slice(quad * CHUNK, (quad + 1) * CHUNK)
        total[first, lanes, :] += term[:, :UNIT]
        total[first + 1, lanes, :] += term[:, UNIT:]

    @pl.loop(0, chunks)
    def _(chunk):
        for quad in range(quads):
            put_groups(grad_mixed, quad, per_quad, dot_nt(dox[quad], keys(v_ref, chunk, quad)))
        fetch(step, chunk, 1).wait()
        for group in range(groups):
            cols = slice(group * CHUNK, (group + 1) * CHUNK)
            if group % TOGETHER == 0:
                sums = dot_nn(mix_ref[3], grad_mixed[:, group * CHUNK : (group + TOGETHER) * CHUNK])
            dp = part_of(sums, group)
            grad_prob[chunk, :, cols] = dp.astype(grad_prob.dtype)
            term = prob[slot, chunk, :, cols].astype(jnp.float32) * dp
            delta[group] += term[:, :UNIT] + term[:, UNIT:]
        gp_ref[...] += dot_nt(prob[slot, chunk], grad_mixed[...])
        fetch(step, chunk, 2).wait()
        for quad in range(quads):
            a = mixed[slot, chunk, quad * per_quad : (quad + 1) * per_quad].reshape(per_quad * UNIT, CHUNK)
            add_to(dv_total, chunk, quad, dot_nn(doxt[quad], a))

    for group in range(groups):
        delta[group] = jnp.broadcast_to(jnp.sum(delta[group], axis=-1, keepdims=True), (wide, UNIT))

    @pl.loop(0, chunks)
    def _(chunk):
        for group in range(groups):
            cols = slice(group * CHUNK, (group + 1) * CHUNK)
            dp = grad_prob[chunk, :, cols].astype(jnp.float32) - twice(delta[group])
            dl = (prob[slot, chunk, :, cols].astype(jnp.float32) * dp).astype(jnp.bfloat16)
            grad_logit[:, cols] = dl
        for first in range(0, groups, TOGETHER):
            sums = dot_nn(mix_ref[1], grad_logit[:, first * CHUNK : (first + TOGETHER) * CHUNK])
            for group in range(first, first + TOGETHER):
                ds = part_of(sums, group).astype(jnp.bfloat16)
                grad_score[:, GROUP * group : GROUP * (group + 1), :] = ds.reshape(heads, GROUP, CHUNK)
        fetch(step, chunk, 0).wait()
        gl_ref[...] += dot_nt(score[slot, chunk], grad_logit[...])
        for quad in range(quads):
            ds = grad_score[quad * per_quad : (quad + 1) * per_quad].reshape(per_quad * UNIT, CHUNK)
            dq = own_lanes(dot_nn(ds, keys(k_ref, chunk, quad)), lane_head, per_quad)
            dq_total[:, quad * CHUNK : (quad + 1) * CHUNK] += dq
            add_to(dk_total, chunk, quad, dot_nn(qxt[quad], ds))

    dq_ref[0, 0] = (dq_total[...] * 0.125).astype(jnp.bfloat16)

    @pl.when(inner == per_row - 1)
    def _():
        @pl.loop(0, lowest)
        def _(key_unit):
            dk_ref[key_unit, 0] = jnp.zeros_like(dk_ref[key_unit, 0])
            dv_ref[key_unit, 0] = jnp.zeros_like(dv_ref[key_unit, 0])

        @pl.loop(lowest, key_units)
        def _(key_unit):
            dk_ref[key_unit, 0] = dk_total[key_unit].astype(jnp.bfloat16).T
            dv_ref[key_unit, 0] = dv_total[key_unit].astype(jnp.bfloat16).T


def attention_bwd(blocks, q, k, v, grad_out, kept, mixes, heads, micro):
    per_row, _, _, width = q.shape
    key_units = k.shape[0]
    wide = heads * GROUP
    groups = UNIT // GROUP
    quads = width // CHUNK
    turned = (quads, CHUNK, heads // quads * UNIT)

    def rows_of(units, at, where):
        return pl.BlockSpec((units, 1, UNIT, width), lambda u, _: (u * where, at, 0, 0))

    sum_spec = pl.BlockSpec((wide, wide), lambda u, _: (0, 0))
    mix_spec = pl.BlockSpec((4, wide, wide), lambda u, _: (0, 0, 0))
    unit_spec, kv_spec = (rows_of(1, micro, 1), rows_of(key_units, micro, 0))
    unit_out, kv_out = (rows_of(1, 0, 1), rows_of(key_units, 0, 0))
    anywhere = pl.BlockSpec(memory_space=pl.ANY)
    return pl.pallas_call(
        partial(bwd_kernel, heads, micro),
        grid_spec=pltpu.PrefetchScalarGridSpec(
            num_scalar_prefetch=1,
            grid=(per_row,),
            in_specs=[unit_spec, kv_spec, kv_spec, unit_spec, mix_spec] + [anywhere] * 3,
            out_specs=[unit_out, kv_out, kv_out, sum_spec, sum_spec],
            scratch_shapes=[
                pltpu.VMEM(turned, jnp.bfloat16),
                pltpu.VMEM((quads, heads // quads * UNIT, CHUNK), jnp.bfloat16),
                pltpu.VMEM(turned, jnp.bfloat16),
            ]
            + [pltpu.VMEM((2,) + shape, jnp.bfloat16) for shape in kept_shapes(heads)]
            + [
                pltpu.VMEM((MAX_CHUNKS, wide, groups * CHUNK), jnp.bfloat16),
                pltpu.VMEM((wide, groups * CHUNK), jnp.bfloat16),
                pltpu.VMEM((wide, groups * CHUNK), jnp.bfloat16),
                pltpu.VMEM((heads, UNIT, CHUNK), jnp.bfloat16),
                pltpu.VMEM((groups, wide, UNIT), jnp.float32),
                pltpu.VMEM((UNIT, width), jnp.float32),
                pltpu.VMEM((key_units, width, UNIT), jnp.float32),
                pltpu.VMEM((key_units, width, UNIT), jnp.float32),
                pltpu.SemaphoreType.DMA((3, 2, MAX_CHUNKS)),
            ],
        ),
        out_shape=[
            jax.ShapeDtypeStruct((per_row, 1, UNIT, width), jnp.bfloat16),
            jax.ShapeDtypeStruct((key_units, 1, UNIT, width), jnp.bfloat16),
            jax.ShapeDtypeStruct((key_units, 1, UNIT, width), jnp.bfloat16),
            jax.ShapeDtypeStruct((wide, wide), jnp.float32),
            jax.ShapeDtypeStruct((wide, wide), jnp.float32),
        ],
        compiler_params=pltpu.CompilerParams(vmem_limit_bytes=58 * 1024 * 1024),
        cost_estimate=pl.CostEstimate(flops=30_000_000_000, bytes_accessed=20_000_000, transcendentals=0),
        name="attention_bwd",
    )(blocks, q, k, v, grad_out, mixes, *kept)


def piece_bases(key_units, per_row):
    sizes = [1] + [per_row] * ((key_units - 1) // per_row)
    return [(sum(sizes[:at]), size) for at, size in enumerate(sizes)]


def project_kernel(low_ref, *refs):
    pieces, (w_q, w_k, w_v, q_ref, k_ref, v_ref) = (refs[:-6], refs[-6:])
    key_units, width = (k_ref.shape[0], k_ref.shape[3])
    per_row = q_ref.shape[0]
    low = low_ref[pl.program_id(0)]

    for piece, (base, size) in zip(pieces, piece_bases(key_units, per_row)):
        @pl.when(base + size > low)
        def _():
            rows = piece[:, 0].reshape(size * UNIT, width)
            k_ref[base : base + size, 0] = dot_nn(rows, w_k[...]).astype(jnp.bfloat16).reshape(size, UNIT, width)
            v_ref[base : base + size, 0] = dot_nn(rows, w_v[...]).astype(jnp.bfloat16).reshape(size, UNIT, width)

    rows = pieces[-1][:, 0].reshape(per_row * UNIT, width)
    query = dot_nn(rows, w_q[...]).astype(jnp.bfloat16) * jnp.bfloat16(0.125)
    q_ref[:, 0] = query.reshape(per_row, UNIT, width)


def project(low, pieces, weights):
    micros, width = pieces[0].shape[1], pieces[0].shape[3]
    key_units = sum(piece.shape[0] for piece in pieces)
    per_row = pieces[-1].shape[0]

    def spec(units):
        return pl.BlockSpec((units, 1, UNIT, width), lambda m, _: (0, m, 0, 0))

    weight_spec = pl.BlockSpec((width, width), lambda m, _: (0, 0))
    shapes = [(units, micros, UNIT, width) for units in (per_row, key_units, key_units)]
    return pl.pallas_call(
        project_kernel,
        grid_spec=pltpu.PrefetchScalarGridSpec(
            num_scalar_prefetch=1,
            grid=(micros,),
            in_specs=[spec(piece.shape[0]) for piece in pieces] + [weight_spec] * 3,
            out_specs=[spec(shape[0]) for shape in shapes],
        ),
        out_shape=[jax.ShapeDtypeStruct(shape, jnp.bfloat16) for shape in shapes],
        compiler_params=pltpu.CompilerParams(vmem_limit_bytes=44 * 1024 * 1024),
        cost_estimate=pl.CostEstimate(flops=6_000_000_000, bytes_accessed=15_000_000, transcendentals=0),
        name="project",
    )(low, *pieces, *weights)


def project_back_kernel(low_ref, dq_ref, dk_ref, dv_ref, w_q, w_k, w_v, *outs):
    key_units, width = (dk_ref.shape[0], dk_ref.shape[3])
    per_row = dq_ref.shape[0]
    low = low_ref[pl.program_id(0)]
    bases = piece_bases(key_units, per_row)

    def from_keys(base, size):
        rows = slice(base, base + size)
        key_term = dot_nt(dk_ref[rows, 0].reshape(size * UNIT, width), w_k[...])
        return key_term + dot_nt(dv_ref[rows, 0].reshape(size * UNIT, width), w_v[...])

    for out, (base, size) in zip(outs[:-1], bases[:-1]):
        @pl.when(base + size > low)
        def _():
            out[:, 0] = from_keys(base, size).astype(jnp.bfloat16).reshape(size, UNIT, width)

        @pl.when(base + size <= low)
        def _():
            out[...] = jnp.zeros_like(out)

    own = from_keys(*bases[-1]) + dot_nt(dq_ref[:, 0].reshape(per_row * UNIT, width), w_q[...])
    outs[-1][:, 0] = own.reshape(per_row, UNIT, width)


def project_back(low, grad_query, grad_key, grad_value, weights):
    per_row, micros, _, width = grad_query.shape
    key_units = grad_key.shape[0]

    def spec(units):
        return pl.BlockSpec((units, 1, UNIT, width), lambda m, _: (0, m, 0, 0))

    weight_spec = pl.BlockSpec((width, width), lambda m, _: (0, 0))
    sizes = [size for _, size in piece_bases(key_units, per_row)]
    shapes = [(size, micros, UNIT, width) for size in sizes]
    kinds = [jnp.bfloat16] * (len(sizes) - 1) + [jnp.float32]
    return pl.pallas_call(
        project_back_kernel,
        grid_spec=pltpu.PrefetchScalarGridSpec(
            num_scalar_prefetch=1,
            grid=(micros,),
            in_specs=[spec(per_row), spec(key_units), spec(key_units)] + [weight_spec] * 3,
            out_specs=[spec(size) for size in sizes],
        ),
        out_shape=[jax.ShapeDtypeStruct(shape, kind) for shape, kind in zip(shapes, kinds)],
        compiler_params=pltpu.CompilerParams(vmem_limit_bytes=44 * 1024 * 1024),
        cost_estimate=pl.CostEstimate(flops=6_000_000_000, bytes_accessed=15_000_000, transcendentals=0),
        name="project_back",
    )(low, grad_query, grad_key, grad_value, *weights)


def weigh_kernel(micros, low_ref, *refs):
    grads, pieces, (grad_ref, total) = (refs[: 3 * micros], refs[3 * micros : -2], refs[-2:])
    key_units, width = (grads[1].shape[0], grads[1].shape[3])
    per_row = grads[0].shape[0]
    bases = piece_bases(key_units, per_row)
    total[...] = jnp.zeros_like(total)

    def keys(ref, base, size):
        return ref[base : base + size, 0].reshape(size * UNIT, width)

    for micro in range(micros):
        dq_ref, dk_ref, dv_ref = grads[3 * micro : 3 * micro + 3]
        for piece, (base, size) in zip(pieces, bases):
            @pl.when(base + size > low_ref[micro])
            def _():
                turned = piece[:, micro].reshape(size * UNIT, width).T
                total[1] += dot_nn(turned, keys(dk_ref, base, size))
                total[2] += dot_nn(turned, keys(dv_ref, base, size))
                if base + size == key_units:
                    total[0] += dot_nn(turned, keys(dq_ref, 0, per_row))

    grad_ref[...] = total[...].astype(jnp.bfloat16)


def weigh(low, grads, pieces):
    width = pieces[0].shape[3]
    operands = [term for terms in grads for term in terms] + list(pieces)

    def spec(shape):
        return pl.BlockSpec(shape, lambda i, _: (0,) * len(shape))

    return pl.pallas_call(
        partial(weigh_kernel, len(grads)),
        grid_spec=pltpu.PrefetchScalarGridSpec(
            num_scalar_prefetch=1,
            grid=(1,),
            in_specs=[spec(operand.shape) for operand in operands],
            out_specs=spec((3, width, width)),
            scratch_shapes=[pltpu.VMEM((3, width, width), jnp.float32)],
        ),
        out_shape=jax.ShapeDtypeStruct((3, width, width), jnp.bfloat16),
        compiler_params=pltpu.CompilerParams(vmem_limit_bytes=56 * 1024 * 1024),
        cost_estimate=pl.CostEstimate(flops=12_000_000_000, bytes_accessed=14_000_000, transcendentals=0),
        name="weigh",
    )(low, *operands)


def feed_kernel(x_ref, att_ref, w_o_ref, gain_ref, up_ref, down_ref, cot_ref,
                mid_ref, out_ref, grad_hidden_ref, grad_up_ref, grad_down_ref,
                hidden, turned, out_total, back_total):
    step = pl.program_id(0)

    @pl.when(step == 0)
    def _():
        middle = x_ref[...].astype(jnp.float32) + dot_nn(att_ref[...], w_o_ref[...])
        mid_ref[...] = middle
        inv_rms = lax.rsqrt(jnp.mean(middle * middle, axis=-1, keepdims=True) + norm_eps)
        rows = (middle * inv_rms * gain_ref[...]).astype(jnp.bfloat16)
        hidden[...] = rows
        turned[...] = rows.T
        out_total[...] = jnp.zeros_like(out_total)
        back_total[...] = jnp.zeros_like(back_total)

    for start in range(0, up_ref.shape[2], FF_STEP):
        cols = slice(start, start + FF_STEP)
        up = dot_nn(hidden[...], up_ref[0, :, cols])
        square = up * up
        bent = jnp.tanh(gelu_scale * up * (1.0 + gelu_cube * square))
        half = 0.5 + 0.5 * bent
        slope = half + 0.5 * up * (1.0 - bent * bent) * (gelu_scale * (1.0 + 3.0 * gelu_cube * square))
        active = (up * half).astype(jnp.bfloat16)
        grad_up = (dot_nt(cot_ref[...], down_ref[cols, :]) * slope).astype(jnp.bfloat16)
        out_total[...] += dot_nn(active, down_ref[cols, :])
        back_total[...] += dot_nt(grad_up, up_ref[0, :, cols])
        grad_down_ref[cols, :] = dot_nn(active.T, cot_ref[...]).astype(jnp.bfloat16)
        grad_up_ref[0, :, cols] = dot_nn(turned[...], grad_up).astype(jnp.bfloat16)

    @pl.when(step == pl.num_programs(0) - 1)
    def _():
        out_ref[...] = (mid_ref[...] + out_total[...]).astype(jnp.bfloat16)
        grad_hidden_ref[...] = back_total[...]


def feed_forward(rows, attended, w_o, gain, w_up, w_down, cot):
    tokens, width = rows.shape
    pieces = w_up.shape[0]
    whole = pl.BlockSpec((tokens, width), lambda i: (0, 0))
    up_spec = pl.BlockSpec((1, width, width), lambda i: (i, 0, 0))
    down_spec = pl.BlockSpec((width, width), lambda i: (i, 0))
    f32, bf16 = (jnp.float32, jnp.bfloat16)
    return pl.pallas_call(
        feed_kernel,
        grid=(pieces,),
        in_specs=[
            whole,
            whole,
            pl.BlockSpec((width, width), lambda i: (0, 0)),
            pl.BlockSpec((1, width), lambda i: (0, 0)),
            up_spec,
            down_spec,
            whole,
        ],
        out_specs=[whole, whole, whole, up_spec, down_spec],
        out_shape=[
            jax.ShapeDtypeStruct((tokens, width), f32),
            jax.ShapeDtypeStruct((tokens, width), bf16),
            jax.ShapeDtypeStruct((tokens, width), f32),
            jax.ShapeDtypeStruct(w_up.shape, bf16),
            jax.ShapeDtypeStruct(w_down.shape, bf16),
        ],
        scratch_shapes=[
            pltpu.VMEM((tokens, width), bf16),
            pltpu.VMEM((width, tokens), bf16),
            pltpu.VMEM((tokens, width), f32),
            pltpu.VMEM((tokens, width), f32),
        ],
        compiler_params=pltpu.CompilerParams(vmem_limit_bytes=48 * 1024 * 1024),
        cost_estimate=pl.CostEstimate(flops=16_000_000_000, bytes_accessed=30_000_000, transcendentals=0),
        name="feed_forward",
    )(rows, attended, w_o, gain, w_up, w_down, cot)


def spread_mixes(mix_logits, mix_weights):
    heads = mix_logits.shape[0]
    wide = heads * GROUP
    place = jnp.arange(wide, dtype=jnp.int32)
    pick = (place[:, None] // GROUP == jnp.arange(heads, dtype=jnp.int32)[None, :]).astype(mix_logits.dtype)
    same_row = (place[:, None] % GROUP == place[None, :] % GROUP)[None]
    tables = jnp.stack([mix_logits.T, mix_logits, mix_weights.T, mix_weights]).reshape(4 * heads, heads)
    across = jnp.dot(tables, pick.T, preferred_element_type=jnp.float32).astype(mix_logits.dtype)
    down = jnp.einsum("wh,bhx->bwx", pick, across.reshape(4, heads, wide), preferred_element_type=jnp.float32)
    return jnp.where(same_row, down, 0.0).astype(mix_logits.dtype)


def fold_mix(wide, heads):
    place = jnp.arange(heads * GROUP, dtype=jnp.int32)
    pick = (place[:, None] // GROUP == jnp.arange(heads, dtype=jnp.int32)[None, :]).astype(jnp.float32)
    same_row = place[:, None] % GROUP == place[None, :] % GROUP
    down = jnp.dot(pick.T, jnp.where(same_row, wide, 0.0), precision=lax.Precision.HIGHEST)
    return jnp.dot(down, pick, precision=lax.Precision.HIGHEST)


def from_behind(value, steps):
    count = lax.axis_size("dev")
    first, last = (max(0, -steps), min(count, count - steps))
    return lax.ppermute(value, "dev", [(source, source + steps) for source in range(first, last)])


def with_sibling(value):
    count = lax.axis_size("dev")
    return lax.ppermute(value, "dev", [(source, source ^ 1) for source in range(count)])


def earlier_rows(own):
    size = own.shape[0]
    first_core = lax.axis_index("dev") % 2 == 0
    two, four = (from_behind(own, 2), from_behind(own, 4))
    give = jnp.concatenate([jnp.where(first_core, own, two), jnp.where(first_core, two, four)], axis=0)
    came = with_sibling(give)
    return [four[size - 1 :], came[size:], two, came[:size], own]


def give_rows(four, two, came):
    size = two.shape[0]
    first_core = lax.axis_index("dev") % 2 == 0
    came = came.astype(jnp.float32)
    one, three = (came[:size], came[size:])
    give_two = two.astype(jnp.float32) + jnp.where(first_core, three, one)
    padded = jnp.pad(four.astype(jnp.float32), ((size - four.shape[0], 0), (0, 0), (0, 0), (0, 0)))
    give_four = padded + jnp.where(first_core, 0.0, three)
    return (jnp.where(first_core, one, 0.0), give_two.astype(jnp.bfloat16), give_four.astype(jnp.bfloat16))


def return_rows(four, two, came):
    kept, give_two, give_four = give_rows(four, two, came)
    return (kept, from_behind(give_two, -2), from_behind(give_four, -4))


def return_in_turn(four, two, came, beside):
    kept, give_two, give_four = give_rows(four, two, came)
    back_two, give_four, beside = lax.optimization_barrier((from_behind(give_two, -2), give_four, beside))
    return ((kept, back_two, from_behind(give_four, -4)), beside)


def seq_starts(lengths_row, query_rows):
    seq_ends = jnp.cumsum(lengths_row)
    starts = seq_ends - lengths_row
    return jnp.max(jnp.where(starts[None, :] <= query_rows[:, None], starts[None, :], 0), axis=1)


def normalize(values, gain_vec):
    inv_rms = lax.rsqrt(jnp.mean(values * values, axis=-1, keepdims=True) + norm_eps)
    normed = values * inv_rms
    return (normed, inv_rms, (normed * gain_vec.astype(jnp.float32)).astype(jnp.bfloat16))


def norm_back(grad_hidden, normed, inv_rms, gain_vec):
    grad_gain = jnp.sum(grad_hidden * normed, axis=0)
    grad_normed = grad_hidden * gain_vec.astype(jnp.float32)
    inner_mean = jnp.mean(grad_normed * normed, axis=-1, keepdims=True)
    return (inv_rms * (grad_normed - normed * inner_mean), grad_gain)


def matmul(left, right):
    return jnp.dot(left, right, preferred_element_type=jnp.float32)


def matmul_left_t(left, right):
    return lax.dot_general(left, right, (((0,), (0,)), ((), ())), preferred_element_type=jnp.float32)


def matmul_right_t(left, right):
    return lax.dot_general(left, right, (((1,), (1,)), ((), ())), preferred_element_type=jnp.float32)


def exchange(value):
    return lax.all_to_all(value, "dev", split_axis=0, concat_axis=0, tiled=True)


def split_ids(tok_ids, own_rows):
    owner = tok_ids // own_rows
    place = jnp.arange(tok_ids.shape[0], dtype=jnp.int32)
    same = tok_ids[:, None] == tok_ids[None, :]
    repeated = jnp.any(same & (place[None, :] < place[:, None]), axis=1)
    before = (owner[:, None] == owner[None, :]) & (tok_ids[None, :] < tok_ids[:, None]) & ~repeated[None, :]
    return (owner, tok_ids % own_rows, jnp.sum(before, axis=1, dtype=jnp.int32))


def ask_round(ids, index, own_rows, stride, room):
    count = lax.axis_size("dev")
    owner, local, rank = ids
    here = rank - index * room
    slot = jnp.where((here >= 0) & (here < room), owner * stride + here, -1)
    chosen = slot[None, :] == jnp.arange(count * stride, dtype=jnp.int32)[:, None]
    wanted = jnp.max(jnp.where(chosen, local[None, :], -1), axis=1).reshape(count, stride)
    rounds = jnp.broadcast_to(jnp.max(rank) // room + 1, (count, stride))
    return (jnp.concatenate([wanted, rounds], axis=1), chosen.astype(jnp.bfloat16))


def hear_round(message, own_rows, stride):
    asked = exchange(message)
    pick = asked[:, :stride].reshape(-1, 1) == jnp.arange(own_rows, dtype=jnp.int32)[None, :]
    return (pick.astype(jnp.bfloat16), jnp.max(asked[:, stride:]))


def plan_round(ids, index, own_rows, stride, room):
    message, chosen = ask_round(ids, index, own_rows, stride, room)
    pick, _ = hear_round(message, own_rows, stride)
    return (chosen, pick)


def answer(embedding, chosen, pick, stride, extra_row, beside=None):
    count = lax.axis_size("dev")
    rows = matmul(pick, embedding).astype(jnp.bfloat16).reshape(count, stride, -1)
    if extra_row is not None:
        is_extra = (jnp.arange(stride, dtype=jnp.int32) == stride - 1)[None, :, None]
        rows = jnp.where(is_extra, extra_row[None, None, :], rows)
    rows, beside = lax.optimization_barrier((rows.reshape(count * stride, -1), beside))
    got = exchange(rows)
    extra = got.reshape(count, stride, -1)[:, stride - 1]
    return (matmul_left_t(chosen, got).astype(jnp.bfloat16), extra, beside)


def lookup(embedding, ids, message, chosen, extra_row, stride, room, beside):
    own_rows = embedding.shape[0]
    pick, rounds = hear_round(message, own_rows, stride)
    first, extra, beside = answer(embedding, chosen, pick, stride, extra_row, beside)

    def more(carry):
        index, rows = carry
        again, its_pick = plan_round(ids, index, own_rows, stride, room)
        return (index + 1, rows + answer(embedding, again, its_pick, stride, None)[0])

    _, rows = lax.while_loop(lambda carry: carry[0] < rounds, more, (jnp.int32(1), first))
    return (rows, extra, beside, ids, chosen, pick, rounds)


def send_grads(grad_low, chosen, pick, stride, extra_rows, beside=None):
    count = lax.axis_size("dev")
    summed = matmul(chosen, grad_low).astype(jnp.bfloat16).reshape(count, stride, -1)
    if extra_rows is not None:
        place = jnp.arange(stride, dtype=jnp.int32)[None, :, None]
        high, low = extra_rows
        summed = jnp.where(place == stride - 2, high[:, None, :], summed)
        summed = jnp.where(place == stride - 1, low[:, None, :], summed)
    summed, beside = lax.optimization_barrier((summed.reshape(count * stride, -1), beside))
    got = exchange(summed)
    return (matmul_left_t(pick, got), got.reshape(count, stride, -1)[:, stride - 2 :], beside)


def table_back(grad_rows, extra_rows, plan, own_rows, stride, room, beside):
    ids, chosen, pick, rounds = plan
    grad_low = grad_rows.astype(jnp.bfloat16)
    first, extra, beside = send_grads(grad_low, chosen, pick, stride, extra_rows, beside)

    def more(carry):
        index, total = carry
        again, its_pick = plan_round(ids, index, own_rows, stride, room)
        return (index + 1, total + send_grads(grad_low, again, its_pick, stride, None)[0])

    _, total = lax.while_loop(lambda carry: carry[0] < rounds, more, (jnp.int32(1), first))
    return (total, jnp.sum(extra.astype(jnp.float32), axis=(0, 1)), beside)


def double(held, bit, axis):
    count = lax.axis_size("dev")
    low = ((lax.axis_index("dev") >> bit) & 1) == 0
    came = lax.ppermute(held, "dev", [(source, source ^ (1 << bit)) for source in range(count)])
    return jnp.stack([jnp.where(low, held, came), jnp.where(low, came, held)], axis=axis)


def spread_z(shard, first, last):
    bits = lax.axis_size("dev").bit_length() - 1
    for done in range(first, min(last, bits - 3)):
        shard = double(shard, bits - 1 - done, done)
    return shard


def spread_plane(held):
    at, half = (lax.axis_size("dev").bit_length() - 4, held.shape[-1] // 2)
    left = double(double(held[..., :half], 2, at), 1, at + 1)
    right = double(double(held[..., half:], 1, at), 2, at)
    return (left, right)


def spread_cores(halves):
    whole = jnp.concatenate(halves, axis=-1)
    return double(whole, 0, lax.axis_size("dev").bit_length() - 2)


def gather_late(stack, part, up_cols):
    width = stack.shape[1]
    whole = lax.all_gather(stack, "dev", axis=0)
    middle = part * (1 + up_cols)
    up = whole[:, part:middle].reshape(-1, up_cols, part, width).swapaxes(0, 1)
    return (whole[:, :part].reshape(-1, width), up.reshape(up_cols, -1, width), whole[:, middle:].reshape(-1, width))


def split_rows(summed, sizes):
    pieces, start = ([], 0)
    for size in sizes:
        pieces.append(summed[start : start + size])
        start += size
    return pieces


def swap_parts(held, bit):
    count = lax.axis_size("dev")
    mine = (lax.axis_index("dev") >> bit) & 1
    keep = lax.dynamic_index_in_dim(held, mine, 0, keepdims=False)
    give = lax.dynamic_index_in_dim(held, 1 - mine, 0, keepdims=False)
    return (keep, lax.ppermute(give, "dev", [(source, source ^ (1 << bit)) for source in range(count)]))


def join_parts(parts, last=False):
    total = parts[0].astype(jnp.float32) + parts[1].astype(jnp.float32)
    return total if last else total.astype(jnp.bfloat16)


def swap_halves(held, bit, last=False):
    return join_parts(swap_parts(held, bit), last)


def middle_bits():
    return list(range(1, lax.axis_size("dev").bit_length() - 2))


def sum_cores(term):
    count, pieces, rows, width = term.shape
    grid = term.reshape(count // 2, 2, pieces, rows, width)
    return swap_halves(grid.swapaxes(0, 1), 0).reshape(count // 2, pieces * rows, width)


def cut_thirds(held):
    _, rows, width = held.shape
    middle = middle_bits()
    bits = len(middle) + 1
    grid = held.reshape((2,) * bits + (rows, width))
    thirds = []
    for turn in range(3):
        shift = turn % len(middle)
        order = middle[shift:] + middle[:shift] + [bits]
        axes = [bits - bit for bit in order]
        part = grid[..., turn * (width // 3) : (turn + 1) * (width // 3)]
        thirds.append(part.transpose(axes + [bits, bits + 1]))
    return thirds


def sum_stage(thirds, stage):
    middle = middle_bits()
    return [swap_halves(third, middle[(turn + stage) % len(middle)]) for turn, third in enumerate(thirds)]


def sum_stages(thirds, first):
    for stage in range(first, len(middle_bits())):
        thirds = sum_stage(thirds, stage)
    return thirds


def sum_last(groups):
    whole = [jnp.concatenate(thirds, axis=-1) for thirds in groups]
    return swap_halves(jnp.concatenate(whole, axis=1), len(middle_bits()) + 1, True)


def split_low(values):
    high = lax.reduce_precision(values, 8, 7)
    return (high.astype(jnp.bfloat16), (values - high).astype(jnp.bfloat16))


def low_units(blocks):
    per_row = blocks.shape[1]
    place = 8 + jnp.arange(per_row, dtype=jnp.int32)[None, :]
    return jnp.min(place - 2 * ((blocks + 1) // 2), axis=1).astype(jnp.int32)


def by_unit(array):
    cut = array.reshape((array.shape[0], array.shape[1] // UNIT, UNIT) + array.shape[2:])
    return cut.swapaxes(0, 1)


def by_row(array, micros):
    cut = array.reshape(-1, micros, UNIT, array.shape[-1])
    return cut.swapaxes(0, 1).reshape(micros, -1, array.shape[-1])


def shards(
    token_ids,
    lengths,
    embedding,
    norm1_gain,
    w_query,
    w_key,
    w_value,
    w_out,
    mix_logits,
    mix_weights,
    norm2_gain,
    w_up,
    w_down,
    cotangent,
):
    count = lax.axis_size("dev")
    me = lax.axis_index("dev")
    micros, row_count = token_ids.shape
    own_rows, width = embedding.shape
    heads = mix_logits.shape[0]
    part = norm1_gain.shape[0]
    per_row = row_count // UNIT
    tokens = micros * row_count
    tok_ids = by_unit(token_ids).reshape(-1)
    stride = max(16, 1024 // count)
    room = stride - 2

    unit_rows = me * row_count + UNIT * jnp.arange(per_row, dtype=jnp.int32)
    begins = jnp.stack([seq_starts(lengths[micro], unit_rows) for micro in range(micros)])
    blocks = ((unit_rows[None, :] - begins) // UNIT + 1).reshape(-1).astype(jnp.int32)

    lows = low_units(blocks.reshape(micros, per_row))
    mixes = spread_mixes(mix_logits, mix_weights)

    up_cols = w_up.shape[1] // width
    up_pieces = [w_up[:, col * width : (col + 1) * width] for col in range(up_cols)]
    first_weights = spread_z(jnp.stack([w_query, w_key, w_value]), 0, 1)
    late_stack = jnp.concatenate([w_out] + up_pieces + [w_down], axis=0)
    ids = split_ids(tok_ids, own_rows)
    message, chosen = ask_round(ids, 0, own_rows, stride, room)
    message, first_weights = lax.optimization_barrier((message, first_weights))
    first_weights = spread_plane(spread_z(first_weights, 1, 99))
    gains_row = jnp.concatenate([norm1_gain, norm2_gain, jnp.zeros((width - 2 * part,), jnp.bfloat16)])
    picked, gains, first_weights, *plan = lookup(
        embedding, ids, message, chosen, gains_row, stride, room, first_weights
    )
    gain_one = gains[:, :part].reshape(-1)
    gain_two = gains[:, part : 2 * part].reshape(-1)
    picked, late_stack = lax.optimization_barrier((picked, late_stack))
    w_o, w_u, w_d = gather_late(late_stack, part, up_cols)
    inputs = picked.astype(jnp.float32)

    normed_one, inv_one, hidden_one = normalize(inputs, gain_one)
    own_hidden = hidden_one.reshape(per_row, micros, UNIT, width)
    pieces = earlier_rows(own_hidden)
    first_weights = spread_cores(first_weights).reshape(count, 3, part, width)
    w_q, w_k, w_v = (first_weights[:, at].reshape(-1, width) for at in range(3))
    query, key, value = project(lows, pieces, (w_q, w_k, w_v))
    attended, *kept = attention_fwd(blocks, query, key, value, mixes, heads)
    attended = attended.reshape(tokens, width)

    grad_rows = by_unit(cotangent).reshape(tokens, width)
    gain_row = gain_two.astype(jnp.float32)[None, :]
    middle, output, grad_hidden_two, grad_up, grad_down = feed_forward(
        picked, attended, w_o, gain_row, w_u, w_d, grad_rows
    )
    inv_two = lax.rsqrt(jnp.mean(middle * middle, axis=-1, keepdims=True) + norm_eps)
    normed_two = middle * inv_two
    grad_mid_norm, grad_gain_two = norm_back(grad_hidden_two, normed_two, inv_two, gain_two)
    grad_middle = grad_rows.astype(jnp.float32) + grad_mid_norm
    grad_branch = grad_middle.astype(jnp.bfloat16)
    grad_wout = matmul_left_t(attended, grad_branch)
    grad_att = matmul_right_t(grad_branch, w_o).astype(jnp.bfloat16).reshape(own_hidden.shape)
    up_rows = grad_up.reshape(up_cols, count, part, width).swapaxes(0, 1).reshape(count, -1, width)
    stack = jnp.concatenate([grad_down.reshape(count, -1, width), up_rows], axis=1).reshape(-1, width)
    stack, grad_att = lax.optimization_barrier((stack, grad_att))
    late_sums = lax.psum_scatter(stack, "dev", scatter_dimension=0, tiled=True).astype(jnp.float32)

    def tail(pieces, query, key, value, grad_att, kept, grad_wout):
        grads, owns, wides, ready = ([], [], [], ())
        for micro in range(micros):
            *grad, wide_logit, wide_prob = attention_bwd(
                blocks, query, key, value, grad_att, kept, mixes, heads, micro
            )
            grad, ready = lax.optimization_barrier((grad, ready))
            grads.append(grad)
            owns.append(ready)
            wides.append((wide_logit, wide_prob))
            *terms, grad_own = project_back(lows[micro : micro + 1], *grad, (w_q, w_k, w_v))
            came = with_sibling(jnp.concatenate([terms[3], terms[1]], axis=0))
            if micro + 1 < micros:
                ready = (grad_own, *return_rows(terms[0], terms[2], came))
        came, grads, hidden = lax.optimization_barrier((came, grads, pieces))
        grad_qkv = weigh(lows, grads, hidden)
        backs, grad_qkv = return_in_turn(terms[0], terms[2], came, grad_qkv)
        wide_logit, wide_prob = (sum(wide[kind] for wide in wides) for kind in range(2))
        early_terms = jnp.concatenate([grad_qkv, grad_wout.astype(jnp.bfloat16)[None]], axis=0)
        early = cut_thirds(sum_cores(early_terms.reshape(4, count, part, width).swapaxes(0, 1)))
        backs, early = lax.optimization_barrier((backs, early))
        owns = owns[1:] + [(grad_own, *backs)]
        grad_own = jnp.concatenate([sum(term.astype(jnp.float32) for term in terms) for terms in owns], axis=1)
        early = sum_stage(early, 0)
        grad_hidden_one = grad_own.reshape(tokens, width)
        grad_in_norm, grad_gain_one = norm_back(grad_hidden_one, normed_one, inv_one, gain_one)
        grad_inputs = grad_middle + grad_in_norm

        mix_terms = jnp.concatenate([fold_mix(wide_logit, heads).reshape(-1), fold_mix(wide_prob, heads).reshape(-1)])
        mix_size = mix_terms.shape[0]
        small = jnp.concatenate(
            [
                grad_gain_one.reshape(count, part),
                grad_gain_two.reshape(count, part),
                jnp.broadcast_to(mix_terms[None, :], (count, mix_size)),
                jnp.zeros((count, width - 2 * part - mix_size), jnp.float32),
            ],
            axis=1,
        )
        table_grad, small_sum, early = table_back(grad_inputs, split_low(small), plan, own_rows, stride, room, early)
        return (grad_inputs, table_grad, small_sum, sum_last([sum_stages(early, 1)]))

    def no_tail(*operands):
        sizes = ((tokens, width), (own_rows, width), (width,), (4 * part, width))
        return tuple(jnp.zeros(size, jnp.float32) for size in sizes)

    grad_inputs, table_grad, small_sum, early_sums = lax.cond(
        plan[-1] > 0, tail, no_tail, pieces, query, key, value, grad_att, kept, grad_wout
    )
    early_sums = split_rows(early_sums, [part] * 4)
    late_sums = split_rows(late_sums, [w_down.shape[0]] + [part] * up_cols)
    mix_size = 2 * heads * heads
    mixes = small_sum[2 * part : 2 * part + mix_size].reshape(2, heads, heads)
    return (
        by_row(output, micros),
        by_row(grad_inputs, micros),
        table_grad,
        small_sum[:part],
        *early_sums,
        mixes[0],
        mixes[1],
        small_sum[part : 2 * part],
        jnp.concatenate(late_sums[1:], axis=1),
        late_sums[0],
    )


def solution(mesh):
    in_specs = (
        P(None, "dev"),
        P(),
        P("dev", None),
        P("dev"),
        P("dev", None),
        P("dev", None),
        P("dev", None),
        P("dev", None),
        P(),
        P(),
        P("dev"),
        P("dev", None),
        P("dev", None),
        P(None, "dev", None),
    )
    out_specs = (
        P(None, "dev", None),
        P(None, "dev", None),
        P("dev", None),
        P("dev"),
        P("dev", None),
        P("dev", None),
        P("dev", None),
        P("dev", None),
        P(),
        P(),
        P("dev"),
        P("dev", None),
        P("dev", None),
    )
    return jax.shard_map(shards, mesh=mesh, in_specs=in_specs, out_specs=out_specs, check_vma=False)
```

```python
from functools import partial

import jax
import jax.numpy as jnp
from jax import lax
from jax.experimental import pallas as pl
from jax.experimental.pallas import tpu as pltpu
from jax.sharding import PartitionSpec as P

norm_eps = 1e-06
gelu_scale = 0.7978845608028654
gelu_cube = 0.044715
FF_STEP = 256

masked = -1e30
UNIT = 128
CHUNK = 256
GROUP = 16
MAX_CHUNKS = 4
TOGETHER = 4


def dot_nn(left, right):
    return lax.dot_general(left, right, (((1,), (0,)), ((), ())), preferred_element_type=jnp.float32)


def dot_nt(left, right):
    return lax.dot_general(left, right, (((1,), (1,)), ((), ())), preferred_element_type=jnp.float32)


def spread_heads(rows, lane_head, quad, heads_per_quad):
    part = rows[:, quad * CHUNK : (quad + 1) * CHUNK]
    zero = jnp.zeros_like(part)
    return jnp.concatenate([jnp.where(lane_head == head, part, zero) for head in range(heads_per_quad)], axis=0)


def own_lanes(wide, lane_head, heads_per_quad):
    total = jnp.where(lane_head == 0, wide[:UNIT], 0.0)
    for head in range(1, heads_per_quad):
        total = total + jnp.where(lane_head == head, wide[head * UNIT : (head + 1) * UNIT], 0.0)
    return total


def part_of(sums, group):
    start = group % TOGETHER * CHUNK
    return sums[:, start : start + CHUNK]


def allowed_keys(chunk, group, blocks):
    key = lax.broadcasted_iota(jnp.int32, (GROUP, CHUNK), 1) - (UNIT + CHUNK * chunk)
    row = lax.broadcasted_iota(jnp.int32, (GROUP, CHUNK), 0) + GROUP * group
    return (key <= row) & (key >= (1 - blocks) * UNIT)


def twice(rows):
    return jnp.concatenate([rows, rows], axis=-1)


def put_groups(ref, quad, per_quad, term):
    low = term.astype(jnp.bfloat16)
    for head in range(per_quad):
        rows = slice((quad * per_quad + head) * GROUP, (quad * per_quad + head + 1) * GROUP)
        for group in range(UNIT // GROUP):
            start = head * UNIT + group * GROUP
            ref[rows, group * CHUNK : (group + 1) * CHUNK] = low[start : start + GROUP]


def fwd_kernel(heads, blocks_ref, q_ref, k_ref, v_ref, mix_ref, att_ref, score_out, prob_out, mixed_out,
               qx, score, prob, mixed, logit, top, norm, total, sems):
    micro, inner, per_row = (pl.program_id(0), pl.program_id(1), pl.num_programs(1))
    blocks = blocks_ref[micro * per_row + inner]
    chunks = (blocks + 1) // 2
    last_unit = k_ref.shape[0] - per_row + inner + 1
    quads = q_ref.shape[3] // CHUNK
    per_quad = heads // quads
    groups = UNIT // GROUP
    wide = heads * GROUP
    lane_head = lax.broadcasted_iota(jnp.int32, (UNIT, CHUNK), 1) // (CHUNK // per_quad)
    for quad in range(quads):
        qx[quad] = spread_heads(q_ref[0, 0], lane_head, quad, per_quad)
    total[...] = jnp.zeros_like(total)
    top[...] = jnp.full_like(top, masked)
    norm[...] = jnp.zeros_like(norm)

    def keys(ref, chunk, quad):
        units = pl.ds(last_unit - 2 * (chunk + 1), 2)
        return ref[units, 0, :, quad * CHUNK : (quad + 1) * CHUNK].reshape(CHUNK, CHUNK)

    step = micro * per_row + inner

    def keep(at, chunk, kind):
        source, target = ((score, score_out), (prob, prob_out), (mixed, mixed_out))[kind]
        place = target.at[at % per_row, at // per_row, chunk]
        return pltpu.make_async_copy(source.at[chunk], place, sems.at[kind, chunk])

    def finish(at):
        @pl.loop(0, (blocks_ref[at] + 1) // 2)
        def _(chunk):
            for kind in range(3):
                keep(at, chunk, kind).wait()

    @pl.when(step > 0)
    def _():
        finish(step - 1)

    @pl.loop(0, chunks)
    def _(chunk):
        for quad in range(quads):
            put_groups(score.at[chunk], quad, per_quad, dot_nt(qx[quad], keys(k_ref, chunk, quad)))
        keep(step, chunk, 0).start()
        for group in range(groups):
            if group % TOGETHER == 0:
                mixes = dot_nn(mix_ref[0], score[chunk, :, group * CHUNK : (group + TOGETHER) * CHUNK])
            l = part_of(mixes, group)
            l = jnp.where(allowed_keys(chunk, group, blocks)[None], l.reshape(heads, GROUP, CHUNK), masked)
            l = l.reshape(wide, CHUNK)
            logit[chunk, group] = l
            old = top[group]
            new = jnp.maximum(old, jnp.maximum(l[:, :UNIT], l[:, UNIT:]))
            terms = jnp.exp(l[:, :UNIT] - new) + jnp.exp(l[:, UNIT:] - new)
            norm[group] = norm[group] * jnp.exp(old - new) + terms
            top[group] = new

    for group in range(groups):
        lanes = top[group]
        high = jnp.broadcast_to(jnp.max(lanes, axis=-1, keepdims=True), lanes.shape)
        whole = jnp.sum(norm[group] * jnp.exp(lanes - high), axis=-1, keepdims=True)
        top[group] = high + jnp.log(jnp.broadcast_to(whole, lanes.shape))

    @pl.loop(0, chunks)
    def _(chunk):
        for group in range(groups):
            p = jnp.exp(logit[chunk, group] - twice(top[group])).astype(jnp.bfloat16)
            prob[chunk, :, group * CHUNK : (group + 1) * CHUNK] = p
        for first in range(0, groups, TOGETHER):
            sums = dot_nn(mix_ref[2], prob[chunk, :, first * CHUNK : (first + TOGETHER) * CHUNK])
            for group in range(first, first + TOGETHER):
                a = part_of(sums, group).astype(jnp.bfloat16)
                mixed[chunk, :, GROUP * group : GROUP * (group + 1), :] = a.reshape(heads, GROUP, CHUNK)
        keep(step, chunk, 1).start()
        keep(step, chunk, 2).start()
        for quad in range(quads):
            a = mixed[chunk, quad * per_quad : (quad + 1) * per_quad].reshape(per_quad * UNIT, CHUNK)
            o = own_lanes(dot_nn(a, keys(v_ref, chunk, quad)), lane_head, per_quad)
            total[:, quad * CHUNK : (quad + 1) * CHUNK] += o

    att_ref[0, 0] = total[...].astype(jnp.bfloat16)

    @pl.when(step == pl.num_programs(0) * per_row - 1)
    def _():
        finish(step)


def attention_specs(q, k, heads):
    per_row, micros, _, width = q.shape
    wide = heads * GROUP
    return (
        pl.BlockSpec((1, 1, UNIT, width), lambda m, u, _: (u, m, 0, 0)),
        pl.BlockSpec((k.shape[0], 1, UNIT, width), lambda m, u, _: (0, m, 0, 0)),
        pl.BlockSpec((4, wide, wide), lambda m, u, _: (0, 0, 0)),
    )


def kept_shapes(heads):
    wide = heads * GROUP
    flat = (MAX_CHUNKS, wide, UNIT // GROUP * CHUNK)
    return (flat, flat, (MAX_CHUNKS, heads, UNIT, CHUNK))


def attention_fwd(blocks, q, k, v, mixes, heads):
    per_row, micros, _, width = q.shape
    wide = heads * GROUP
    groups = UNIT // GROUP
    quads = width // CHUNK
    unit_spec, kv_spec, mix_spec = attention_specs(q, k, heads)
    kept = kept_shapes(heads)
    anywhere = pl.BlockSpec(memory_space=pl.ANY)
    return pl.pallas_call(
        partial(fwd_kernel, heads),
        grid_spec=pltpu.PrefetchScalarGridSpec(
            num_scalar_prefetch=1,
            grid=(micros, per_row),
            in_specs=[unit_spec, kv_spec, kv_spec, mix_spec],
            out_specs=[unit_spec, anywhere, anywhere, anywhere],
            scratch_shapes=[pltpu.VMEM((quads, heads // quads * UNIT, CHUNK), jnp.bfloat16)]
            + [pltpu.VMEM(shape, jnp.bfloat16) for shape in kept]
            + [
                pltpu.VMEM((MAX_CHUNKS, groups, wide, CHUNK), jnp.float32),
                pltpu.VMEM((groups, wide, UNIT), jnp.float32),
                pltpu.VMEM((groups, wide, UNIT), jnp.float32),
                pltpu.VMEM((UNIT, width), jnp.float32),
                pltpu.SemaphoreType.DMA((3, MAX_CHUNKS)),
            ],
        ),
        out_shape=[jax.ShapeDtypeStruct(q.shape, jnp.bfloat16)]
        + [jax.ShapeDtypeStruct((per_row, micros) + shape, jnp.bfloat16) for shape in kept],
        compiler_params=pltpu.CompilerParams(vmem_limit_bytes=50 * 1024 * 1024),
        cost_estimate=pl.CostEstimate(flops=20_000_000_000, bytes_accessed=30_000_000, transcendentals=0),
        name="attention_fwd",
    )(blocks, q, k, v, mixes)


def bwd_kernel(heads, micro, blocks_ref, q_ref, k_ref, v_ref, do_ref, mix_ref, score_in, prob_in, mixed_in,
               dq_ref, dk_ref, dv_ref, gl_ref, gp_ref,
               qxt, dox, doxt, score, prob, mixed, grad_prob, grad_mixed, grad_logit, grad_score,
               delta, dq_total, dk_total, dv_total, sems):
    inner, per_row = (pl.program_id(0), pl.num_programs(0))
    step = micro * per_row + inner
    slot = step % 2
    blocks = blocks_ref[step]
    chunks = (blocks + 1) // 2
    key_units = k_ref.shape[0]
    last_unit = key_units - per_row + inner + 1
    quads = q_ref.shape[3] // CHUNK
    per_quad = heads // quads
    groups = UNIT // GROUP
    wide = heads * GROUP
    lane_head = lax.broadcasted_iota(jnp.int32, (UNIT, CHUNK), 1) // (CHUNK // per_quad)
    row_head = lax.broadcasted_iota(jnp.int32, (CHUNK, UNIT), 0) // (CHUNK // per_quad)
    lowest = key_units
    for other in range(key_units - 7):
        its_chunks = (blocks_ref[micro * per_row + other] + 1) // 2
        lowest = jnp.minimum(lowest, key_units - per_row + other + 1 - 2 * its_chunks)

    def fetch(at, chunk, kind):
        source, target = ((score_in, score), (prob_in, prob), (mixed_in, mixed))[kind]
        place = source.at[at % per_row, at // per_row, chunk]
        return pltpu.make_async_copy(place, target.at[at % 2, chunk], sems.at[kind, at % 2, chunk])

    def fetch_all(at):
        @pl.loop(0, (blocks_ref[at] + 1) // 2)
        def _(chunk):
            for kind in (1, 2, 0):
                fetch(at, chunk, kind).start()

    @pl.when(inner == 0)
    def _():
        fetch_all(step)
        gl_ref[...] = jnp.zeros_like(gl_ref)
        gp_ref[...] = jnp.zeros_like(gp_ref)

    @pl.when(inner + 1 < per_row)
    def _():
        fetch_all(step + 1)

    @pl.when(inner == 0)
    def _():
        @pl.loop(lowest, key_units)
        def _(key_unit):
            dk_total[key_unit] = jnp.zeros_like(dk_total[key_unit])
            dv_total[key_unit] = jnp.zeros_like(dv_total[key_unit])

    def spread_turned(rows, quad):
        turned = rows[:, quad * CHUNK : (quad + 1) * CHUNK].T
        zero = jnp.zeros_like(turned)
        return jnp.concatenate([jnp.where(row_head == head, turned, zero) for head in range(per_quad)], axis=1)

    for quad in range(quads):
        qxt[quad] = spread_turned(q_ref[0, 0], quad)
        dox[quad] = spread_heads(do_ref[0, 0], lane_head, quad, per_quad)
        doxt[quad] = spread_turned(do_ref[0, 0], quad)
    dq_total[...] = jnp.zeros_like(dq_total)
    delta[...] = jnp.zeros_like(delta)

    def keys(ref, chunk, quad):
        units = pl.ds(last_unit - 2 * (chunk + 1), 2)
        return ref[units, 0, :, quad * CHUNK : (quad + 1) * CHUNK].reshape(CHUNK, CHUNK)

    def add_to(total, chunk, quad, term):
        first = last_unit - 2 * (chunk + 1)
        lanes = slice(quad * CHUNK, (quad + 1) * CHUNK)
        total[first, lanes, :] += term[:, :UNIT]
        total[first + 1, lanes, :] += term[:, UNIT:]

    @pl.loop(0, chunks)
    def _(chunk):
        for quad in range(quads):
            put_groups(grad_mixed, quad, per_quad, dot_nt(dox[quad], keys(v_ref, chunk, quad)))
        fetch(step, chunk, 1).wait()
        for group in range(groups):
            cols = slice(group * CHUNK, (group + 1) * CHUNK)
            if group % TOGETHER == 0:
                sums = dot_nn(mix_ref[3], grad_mixed[:, group * CHUNK : (group + TOGETHER) * CHUNK])
            dp = part_of(sums, group)
            grad_prob[chunk, :, cols] = dp.astype(grad_prob.dtype)
            term = prob[slot, chunk, :, cols].astype(jnp.float32) * dp
            delta[group] += term[:, :UNIT] + term[:, UNIT:]
        gp_ref[...] += dot_nt(prob[slot, chunk], grad_mixed[...])
        fetch(step, chunk, 2).wait()
        for quad in range(quads):
            a = mixed[slot, chunk, quad * per_quad : (quad + 1) * per_quad].reshape(per_quad * UNIT, CHUNK)
            add_to(dv_total, chunk, quad, dot_nn(doxt[quad], a))

    for group in range(groups):
        delta[group] = jnp.broadcast_to(jnp.sum(delta[group], axis=-1, keepdims=True), (wide, UNIT))

    @pl.loop(0, chunks)
    def _(chunk):
        for group in range(groups):
            cols = slice(group * CHUNK, (group + 1) * CHUNK)
            dp = grad_prob[chunk, :, cols].astype(jnp.float32) - twice(delta[group])
            dl = (prob[slot, chunk, :, cols].astype(jnp.float32) * dp).astype(jnp.bfloat16)
            grad_logit[:, cols] = dl
        for first in range(0, groups, TOGETHER):
            sums = dot_nn(mix_ref[1], grad_logit[:, first * CHUNK : (first + TOGETHER) * CHUNK])
            for group in range(first, first + TOGETHER):
                ds = part_of(sums, group).astype(jnp.bfloat16)
                grad_score[:, GROUP * group : GROUP * (group + 1), :] = ds.reshape(heads, GROUP, CHUNK)
        fetch(step, chunk, 0).wait()
        gl_ref[...] += dot_nt(score[slot, chunk], grad_logit[...])
        for quad in range(quads):
            ds = grad_score[quad * per_quad : (quad + 1) * per_quad].reshape(per_quad * UNIT, CHUNK)
            dq = own_lanes(dot_nn(ds, keys(k_ref, chunk, quad)), lane_head, per_quad)
            dq_total[:, quad * CHUNK : (quad + 1) * CHUNK] += dq
            add_to(dk_total, chunk, quad, dot_nn(qxt[quad], ds))

    dq_ref[0, 0] = (dq_total[...] * 0.125).astype(jnp.bfloat16)

    @pl.when(inner == per_row - 1)
    def _():
        @pl.loop(0, lowest)
        def _(key_unit):
            dk_ref[key_unit, 0] = jnp.zeros_like(dk_ref[key_unit, 0])
            dv_ref[key_unit, 0] = jnp.zeros_like(dv_ref[key_unit, 0])

        @pl.loop(lowest, key_units)
        def _(key_unit):
            dk_ref[key_unit, 0] = dk_total[key_unit].astype(jnp.bfloat16).T
            dv_ref[key_unit, 0] = dv_total[key_unit].astype(jnp.bfloat16).T


def attention_bwd(blocks, q, k, v, grad_out, kept, mixes, heads, micro):
    per_row, _, _, width = q.shape
    key_units = k.shape[0]
    wide = heads * GROUP
    groups = UNIT // GROUP
    quads = width // CHUNK
    turned = (quads, CHUNK, heads // quads * UNIT)

    def rows_of(units, at, where):
        return pl.BlockSpec((units, 1, UNIT, width), lambda u, _: (u * where, at, 0, 0))

    sum_spec = pl.BlockSpec((wide, wide), lambda u, _: (0, 0))
    mix_spec = pl.BlockSpec((4, wide, wide), lambda u, _: (0, 0, 0))
    unit_spec, kv_spec = (rows_of(1, micro, 1), rows_of(key_units, micro, 0))
    unit_out, kv_out = (rows_of(1, 0, 1), rows_of(key_units, 0, 0))
    anywhere = pl.BlockSpec(memory_space=pl.ANY)
    return pl.pallas_call(
        partial(bwd_kernel, heads, micro),
        grid_spec=pltpu.PrefetchScalarGridSpec(
            num_scalar_prefetch=1,
            grid=(per_row,),
            in_specs=[unit_spec, kv_spec, kv_spec, unit_spec, mix_spec] + [anywhere] * 3,
            out_specs=[unit_out, kv_out, kv_out, sum_spec, sum_spec],
            scratch_shapes=[
                pltpu.VMEM(turned, jnp.bfloat16),
                pltpu.VMEM((quads, heads // quads * UNIT, CHUNK), jnp.bfloat16),
                pltpu.VMEM(turned, jnp.bfloat16),
            ]
            + [pltpu.VMEM((2,) + shape, jnp.bfloat16) for shape in kept_shapes(heads)]
            + [
                pltpu.VMEM((MAX_CHUNKS, wide, groups * CHUNK), jnp.bfloat16),
                pltpu.VMEM((wide, groups * CHUNK), jnp.bfloat16),
                pltpu.VMEM((wide, groups * CHUNK), jnp.bfloat16),
                pltpu.VMEM((heads, UNIT, CHUNK), jnp.bfloat16),
                pltpu.VMEM((groups, wide, UNIT), jnp.float32),
                pltpu.VMEM((UNIT, width), jnp.float32),
                pltpu.VMEM((key_units, width, UNIT), jnp.float32),
                pltpu.VMEM((key_units, width, UNIT), jnp.float32),
                pltpu.SemaphoreType.DMA((3, 2, MAX_CHUNKS)),
            ],
        ),
        out_shape=[
            jax.ShapeDtypeStruct((per_row, 1, UNIT, width), jnp.bfloat16),
            jax.ShapeDtypeStruct((key_units, 1, UNIT, width), jnp.bfloat16),
            jax.ShapeDtypeStruct((key_units, 1, UNIT, width), jnp.bfloat16),
            jax.ShapeDtypeStruct((wide, wide), jnp.float32),
            jax.ShapeDtypeStruct((wide, wide), jnp.float32),
        ],
        compiler_params=pltpu.CompilerParams(vmem_limit_bytes=58 * 1024 * 1024),
        cost_estimate=pl.CostEstimate(flops=30_000_000_000, bytes_accessed=20_000_000, transcendentals=0),
        name="attention_bwd",
    )(blocks, q, k, v, grad_out, mixes, *kept)


def piece_bases(key_units, per_row):
    sizes = [1] + [per_row] * ((key_units - 1) // per_row)
    return [(sum(sizes[:at]), size) for at, size in enumerate(sizes)]


def project_kernel(low_ref, *refs):
    pieces, (w_q, w_k, w_v, q_ref, k_ref, v_ref) = (refs[:-6], refs[-6:])
    key_units, width = (k_ref.shape[0], k_ref.shape[3])
    per_row = q_ref.shape[0]
    low = low_ref[pl.program_id(0)]

    for piece, (base, size) in zip(pieces, piece_bases(key_units, per_row)):
        @pl.when(base + size > low)
        def _():
            rows = piece[:, 0].reshape(size * UNIT, width)
            k_ref[base : base + size, 0] = dot_nn(rows, w_k[...]).astype(jnp.bfloat16).reshape(size, UNIT, width)
            v_ref[base : base + size, 0] = dot_nn(rows, w_v[...]).astype(jnp.bfloat16).reshape(size, UNIT, width)

    rows = pieces[-1][:, 0].reshape(per_row * UNIT, width)
    query = dot_nn(rows, w_q[...]).astype(jnp.bfloat16) * jnp.bfloat16(0.125)
    q_ref[:, 0] = query.reshape(per_row, UNIT, width)


def project(low, pieces, weights):
    micros, width = pieces[0].shape[1], pieces[0].shape[3]
    key_units = sum(piece.shape[0] for piece in pieces)
    per_row = pieces[-1].shape[0]

    def spec(units):
        return pl.BlockSpec((units, 1, UNIT, width), lambda m, _: (0, m, 0, 0))

    weight_spec = pl.BlockSpec((width, width), lambda m, _: (0, 0))
    shapes = [(units, micros, UNIT, width) for units in (per_row, key_units, key_units)]
    return pl.pallas_call(
        project_kernel,
        grid_spec=pltpu.PrefetchScalarGridSpec(
            num_scalar_prefetch=1,
            grid=(micros,),
            in_specs=[spec(piece.shape[0]) for piece in pieces] + [weight_spec] * 3,
            out_specs=[spec(shape[0]) for shape in shapes],
        ),
        out_shape=[jax.ShapeDtypeStruct(shape, jnp.bfloat16) for shape in shapes],
        compiler_params=pltpu.CompilerParams(vmem_limit_bytes=44 * 1024 * 1024),
        cost_estimate=pl.CostEstimate(flops=6_000_000_000, bytes_accessed=15_000_000, transcendentals=0),
        name="project",
    )(low, *pieces, *weights)


def project_back_kernel(low_ref, dq_ref, dk_ref, dv_ref, w_q, w_k, w_v, *outs):
    key_units, width = (dk_ref.shape[0], dk_ref.shape[3])
    per_row = dq_ref.shape[0]
    low = low_ref[pl.program_id(0)]
    bases = piece_bases(key_units, per_row)

    def from_keys(base, size):
        rows = slice(base, base + size)
        key_term = dot_nt(dk_ref[rows, 0].reshape(size * UNIT, width), w_k[...])
        return key_term + dot_nt(dv_ref[rows, 0].reshape(size * UNIT, width), w_v[...])

    for out, (base, size) in zip(outs[:-1], bases[:-1]):
        @pl.when(base + size > low)
        def _():
            out[:, 0] = from_keys(base, size).astype(jnp.bfloat16).reshape(size, UNIT, width)

        @pl.when(base + size <= low)
        def _():
            out[...] = jnp.zeros_like(out)

    own = from_keys(*bases[-1]) + dot_nt(dq_ref[:, 0].reshape(per_row * UNIT, width), w_q[...])
    outs[-1][:, 0] = own.reshape(per_row, UNIT, width)


def project_back(low, grad_query, grad_key, grad_value, weights):
    per_row, micros, _, width = grad_query.shape
    key_units = grad_key.shape[0]

    def spec(units):
        return pl.BlockSpec((units, 1, UNIT, width), lambda m, _: (0, m, 0, 0))

    weight_spec = pl.BlockSpec((width, width), lambda m, _: (0, 0))
    sizes = [size for _, size in piece_bases(key_units, per_row)]
    shapes = [(size, micros, UNIT, width) for size in sizes]
    kinds = [jnp.bfloat16] * (len(sizes) - 1) + [jnp.float32]
    return pl.pallas_call(
        project_back_kernel,
        grid_spec=pltpu.PrefetchScalarGridSpec(
            num_scalar_prefetch=1,
            grid=(micros,),
            in_specs=[spec(per_row), spec(key_units), spec(key_units)] + [weight_spec] * 3,
            out_specs=[spec(size) for size in sizes],
        ),
        out_shape=[jax.ShapeDtypeStruct(shape, kind) for shape, kind in zip(shapes, kinds)],
        compiler_params=pltpu.CompilerParams(vmem_limit_bytes=44 * 1024 * 1024),
        cost_estimate=pl.CostEstimate(flops=6_000_000_000, bytes_accessed=15_000_000, transcendentals=0),
        name="project_back",
    )(low, grad_query, grad_key, grad_value, *weights)


def weigh_kernel(micros, low_ref, *refs):
    grads, pieces, (grad_ref, total) = (refs[: 3 * micros], refs[3 * micros : -2], refs[-2:])
    key_units, width = (grads[1].shape[0], grads[1].shape[3])
    per_row = grads[0].shape[0]
    bases = piece_bases(key_units, per_row)
    total[...] = jnp.zeros_like(total)

    def keys(ref, base, size):
        return ref[base : base + size, 0].reshape(size * UNIT, width)

    for micro in range(micros):
        dq_ref, dk_ref, dv_ref = grads[3 * micro : 3 * micro + 3]
        for piece, (base, size) in zip(pieces, bases):
            @pl.when(base + size > low_ref[micro])
            def _():
                turned = piece[:, micro].reshape(size * UNIT, width).T
                total[1] += dot_nn(turned, keys(dk_ref, base, size))
                total[2] += dot_nn(turned, keys(dv_ref, base, size))
                if base + size == key_units:
                    total[0] += dot_nn(turned, keys(dq_ref, 0, per_row))

    grad_ref[...] = total[...].astype(jnp.bfloat16)


def weigh(low, grads, pieces):
    width = pieces[0].shape[3]
    operands = [term for terms in grads for term in terms] + list(pieces)

    def spec(shape):
        return pl.BlockSpec(shape, lambda i, _: (0,) * len(shape))

    return pl.pallas_call(
        partial(weigh_kernel, len(grads)),
        grid_spec=pltpu.PrefetchScalarGridSpec(
            num_scalar_prefetch=1,
            grid=(1,),
            in_specs=[spec(operand.shape) for operand in operands],
            out_specs=spec((3, width, width)),
            scratch_shapes=[pltpu.VMEM((3, width, width), jnp.float32)],
        ),
        out_shape=jax.ShapeDtypeStruct((3, width, width), jnp.bfloat16),
        compiler_params=pltpu.CompilerParams(vmem_limit_bytes=56 * 1024 * 1024),
        cost_estimate=pl.CostEstimate(flops=12_000_000_000, bytes_accessed=14_000_000, transcendentals=0),
        name="weigh",
    )(low, *operands)


def feed_kernel(x_ref, att_ref, w_o_ref, gain_ref, up_ref, down_ref, cot_ref,
                mid_ref, out_ref, grad_hidden_ref, grad_up_ref, grad_down_ref,
                hidden, turned, out_total, back_total):
    step = pl.program_id(0)

    @pl.when(step == 0)
    def _():
        middle = x_ref[...].astype(jnp.float32) + dot_nn(att_ref[...], w_o_ref[...])
        mid_ref[...] = middle
        inv_rms = lax.rsqrt(jnp.mean(middle * middle, axis=-1, keepdims=True) + norm_eps)
        rows = (middle * inv_rms * gain_ref[...]).astype(jnp.bfloat16)
        hidden[...] = rows
        turned[...] = rows.T
        out_total[...] = jnp.zeros_like(out_total)
        back_total[...] = jnp.zeros_like(back_total)

    down_rows = down_ref[...].reshape(up_ref.shape[1:])
    for start in range(0, up_ref.shape[2], FF_STEP):
        cols = slice(start, start + FF_STEP)
        down = down_rows[cols]
        up = dot_nn(hidden[...], up_ref[0, :, cols])
        square = up * up
        bent = jnp.tanh(gelu_scale * up * (1.0 + gelu_cube * square))
        half = 0.5 + 0.5 * bent
        slope = half + 0.5 * up * (1.0 - bent * bent) * (gelu_scale * (1.0 + 3.0 * gelu_cube * square))
        active = (up * half).astype(jnp.bfloat16)
        grad_up = (dot_nt(cot_ref[...], down) * slope).astype(jnp.bfloat16)
        out_total[...] += dot_nn(active, down)
        back_total[...] += dot_nt(grad_up, up_ref[0, :, cols])
        grad_down_ref[cols, :] = dot_nn(active.T, cot_ref[...]).astype(jnp.bfloat16)
        grad_up_ref[0, :, cols] = dot_nn(turned[...], grad_up).astype(jnp.bfloat16)

    @pl.when(step == pl.num_programs(0) - 1)
    def _():
        out_ref[...] = (mid_ref[...] + out_total[...]).astype(jnp.bfloat16)
        grad_hidden_ref[...] = back_total[...]


def feed_forward(rows, attended, w_o, gain, w_up, w_late, cot):
    tokens, width = rows.shape
    pieces = w_up.shape[0]
    whole = pl.BlockSpec((tokens, width), lambda i: (0, 0))
    up_spec = pl.BlockSpec((1, width, width), lambda i: (i, 0, 0))
    down_spec = pl.BlockSpec((width, width), lambda i: (i, 0))
    devices = w_late.shape[0] // pieces
    late_spec = pl.BlockSpec((devices, width // devices, width), lambda i: (i, 0, 0))
    f32, bf16 = (jnp.float32, jnp.bfloat16)
    return pl.pallas_call(
        feed_kernel,
        grid=(pieces,),
        in_specs=[
            whole,
            whole,
            pl.BlockSpec((width, width), lambda i: (0, 0)),
            pl.BlockSpec((1, width), lambda i: (0, 0)),
            up_spec,
            late_spec,
            whole,
        ],
        out_specs=[whole, whole, whole, up_spec, down_spec],
        out_shape=[
            jax.ShapeDtypeStruct((tokens, width), f32),
            jax.ShapeDtypeStruct((tokens, width), bf16),
            jax.ShapeDtypeStruct((tokens, width), f32),
            jax.ShapeDtypeStruct(w_up.shape, bf16),
            jax.ShapeDtypeStruct((pieces * width, width), bf16),
        ],
        scratch_shapes=[
            pltpu.VMEM((tokens, width), bf16),
            pltpu.VMEM((width, tokens), bf16),
            pltpu.VMEM((tokens, width), f32),
            pltpu.VMEM((tokens, width), f32),
        ],
        compiler_params=pltpu.CompilerParams(vmem_limit_bytes=48 * 1024 * 1024),
        cost_estimate=pl.CostEstimate(flops=16_000_000_000, bytes_accessed=30_000_000, transcendentals=0),
        name="feed_forward",
    )(rows, attended, w_o, gain, w_up, w_late, cot)


def spread_mixes(mix_logits, mix_weights):
    heads = mix_logits.shape[0]
    wide = heads * GROUP
    place = jnp.arange(wide, dtype=jnp.int32)
    pick = (place[:, None] // GROUP == jnp.arange(heads, dtype=jnp.int32)[None, :]).astype(mix_logits.dtype)
    same_row = (place[:, None] % GROUP == place[None, :] % GROUP)[None]
    tables = jnp.stack([mix_logits.T, mix_logits, mix_weights.T, mix_weights]).reshape(4 * heads, heads)
    across = jnp.dot(tables, pick.T, preferred_element_type=jnp.float32).astype(mix_logits.dtype)
    down = jnp.einsum("wh,bhx->bwx", pick, across.reshape(4, heads, wide), preferred_element_type=jnp.float32)
    return jnp.where(same_row, down, 0.0).astype(mix_logits.dtype)


def fold_mix(wide, heads):
    place = jnp.arange(heads * GROUP, dtype=jnp.int32)
    pick = (place[:, None] // GROUP == jnp.arange(heads, dtype=jnp.int32)[None, :]).astype(jnp.float32)
    same_row = place[:, None] % GROUP == place[None, :] % GROUP
    down = jnp.dot(pick.T, jnp.where(same_row, wide, 0.0), precision=lax.Precision.HIGHEST)
    return jnp.dot(down, pick, precision=lax.Precision.HIGHEST)


def from_behind(value, steps):
    count = lax.axis_size("dev")
    first, last = (max(0, -steps), min(count, count - steps))
    return lax.ppermute(value, "dev", [(source, source + steps) for source in range(first, last)])


def with_sibling(value):
    count = lax.axis_size("dev")
    return lax.ppermute(value, "dev", [(source, source ^ 1) for source in range(count)])


def earlier_rows(own):
    size = own.shape[0]
    first_core = lax.axis_index("dev") % 2 == 0
    two, four = (from_behind(own, 2), from_behind(own, 4))
    give = jnp.concatenate([jnp.where(first_core, own, two), jnp.where(first_core, two, four)], axis=0)
    came = with_sibling(give)
    return [four[size - 1 :], came[size:], two, came[:size], own]


def give_rows(four, two, came):
    size = two.shape[0]
    first_core = lax.axis_index("dev") % 2 == 0
    came = came.astype(jnp.float32)
    one, three = (came[:size], came[size:])
    give_two = two.astype(jnp.float32) + jnp.where(first_core, three, one)
    padded = jnp.pad(four.astype(jnp.float32), ((size - four.shape[0], 0), (0, 0), (0, 0), (0, 0)))
    give_four = padded + jnp.where(first_core, 0.0, three)
    return (jnp.where(first_core, one, 0.0), give_two.astype(jnp.bfloat16), give_four.astype(jnp.bfloat16))


def return_rows(four, two, came):
    kept, give_two, give_four = give_rows(four, two, came)
    return (kept, from_behind(give_two, -2), from_behind(give_four, -4))


def return_in_turn(four, two, came, beside):
    kept, give_two, give_four = give_rows(four, two, came)
    back_two, give_four, beside = lax.optimization_barrier((from_behind(give_two, -2), give_four, beside))
    return ((kept, back_two, from_behind(give_four, -4)), beside)


def seq_starts(lengths_row, query_rows):
    seq_ends = jnp.cumsum(lengths_row)
    starts = seq_ends - lengths_row
    return jnp.max(jnp.where(starts[None, :] <= query_rows[:, None], starts[None, :], 0), axis=1)


def normalize(values, gain_vec):
    inv_rms = lax.rsqrt(jnp.mean(values * values, axis=-1, keepdims=True) + norm_eps)
    normed = values * inv_rms
    return (normed, inv_rms, (normed * gain_vec.astype(jnp.float32)).astype(jnp.bfloat16))


def norm_back(grad_hidden, normed, inv_rms, gain_vec):
    grad_gain = jnp.sum(grad_hidden * normed, axis=0)
    grad_normed = grad_hidden * gain_vec.astype(jnp.float32)
    inner_mean = jnp.mean(grad_normed * normed, axis=-1, keepdims=True)
    return (inv_rms * (grad_normed - normed * inner_mean), grad_gain)


def matmul(left, right):
    return jnp.dot(left, right, preferred_element_type=jnp.float32)


def matmul_left_t(left, right):
    return lax.dot_general(left, right, (((0,), (0,)), ((), ())), preferred_element_type=jnp.float32)


def matmul_right_t(left, right):
    return lax.dot_general(left, right, (((1,), (1,)), ((), ())), preferred_element_type=jnp.float32)


def exchange(value):
    return lax.all_to_all(value, "dev", split_axis=0, concat_axis=0, tiled=True)


def split_ids(tok_ids, own_rows):
    owner = tok_ids // own_rows
    place = jnp.arange(tok_ids.shape[0], dtype=jnp.int32)
    same = tok_ids[:, None] == tok_ids[None, :]
    repeated = jnp.any(same & (place[None, :] < place[:, None]), axis=1)
    before = (owner[:, None] == owner[None, :]) & (tok_ids[None, :] < tok_ids[:, None]) & ~repeated[None, :]
    return (owner, tok_ids % own_rows, jnp.sum(before, axis=1, dtype=jnp.int32))


def ask_round(ids, index, own_rows, stride, room):
    count = lax.axis_size("dev")
    owner, local, rank = ids
    here = rank - index * room
    slot = jnp.where((here >= 0) & (here < room), owner * stride + here, -1)
    chosen = slot[None, :] == jnp.arange(count * stride, dtype=jnp.int32)[:, None]
    wanted = jnp.max(jnp.where(chosen, local[None, :], -1), axis=1).reshape(count, stride)
    rounds = jnp.broadcast_to(jnp.max(rank) // room + 1, (count, stride))
    return (jnp.concatenate([wanted, rounds], axis=1), chosen.astype(jnp.bfloat16))


def hear_round(message, own_rows, stride):
    asked = exchange(message)
    pick = asked[:, :stride].reshape(-1, 1) == jnp.arange(own_rows, dtype=jnp.int32)[None, :]
    return (pick.astype(jnp.bfloat16), jnp.max(asked[:, stride:]))


def plan_round(ids, index, own_rows, stride, room):
    message, chosen = ask_round(ids, index, own_rows, stride, room)
    pick, _ = hear_round(message, own_rows, stride)
    return (chosen, pick)


def answer(embedding, chosen, pick, stride, extra_row, beside=None):
    count = lax.axis_size("dev")
    rows = matmul(pick, embedding).astype(jnp.bfloat16).reshape(count, stride, -1)
    if extra_row is not None:
        is_extra = (jnp.arange(stride, dtype=jnp.int32) == stride - 1)[None, :, None]
        rows = jnp.where(is_extra, extra_row[None, None, :], rows)
    rows, beside = lax.optimization_barrier((rows.reshape(count * stride, -1), beside))
    got = exchange(rows)
    extra = got.reshape(count, stride, -1)[:, stride - 1]
    return (matmul_left_t(chosen, got).astype(jnp.bfloat16), extra, beside)


def lookup(embedding, ids, message, chosen, extra_row, stride, room, beside):
    own_rows = embedding.shape[0]
    pick, rounds = hear_round(message, own_rows, stride)
    first, extra, beside = answer(embedding, chosen, pick, stride, extra_row, beside)

    def more(carry):
        index, rows = carry
        again, its_pick = plan_round(ids, index, own_rows, stride, room)
        return (index + 1, rows + answer(embedding, again, its_pick, stride, None)[0])

    _, rows = lax.while_loop(lambda carry: carry[0] < rounds, more, (jnp.int32(1), first))
    return (rows, extra, beside, ids, chosen, pick, rounds)


def send_grads(grad_low, chosen, pick, stride, beside=None):
    count = lax.axis_size("dev")
    summed = matmul(chosen, grad_low).astype(jnp.bfloat16)
    summed, beside = lax.optimization_barrier((summed, beside))
    got = exchange(summed)
    return (matmul_left_t(pick, got), got.reshape(count, stride, -1)[:, stride - 2 :], beside)


def table_back(grad_rows, extra_rows, plan, own_rows, stride, room, beside):
    ids, chosen, pick, rounds = plan
    count = lax.axis_size("dev")
    grad_low = grad_rows.astype(jnp.bfloat16)
    slot = jnp.arange(count * stride, dtype=jnp.int32)[:, None]
    owner = jnp.arange(count, dtype=jnp.int32)[None, :] * stride
    places = [(slot == owner + at).astype(jnp.bfloat16) for at in (stride - 2, stride - 1)]
    whole = jnp.concatenate([grad_low, *extra_rows], axis=0)
    both = jnp.concatenate([chosen, *places], axis=1)
    first, extra, beside = send_grads(whole, both, pick, stride, beside)

    def more(carry):
        index, total = carry
        again, its_pick = plan_round(ids, index, own_rows, stride, room)
        return (index + 1, total + send_grads(grad_low, again, its_pick, stride)[0])

    def rest(start):
        return lax.while_loop(lambda carry: carry[0] < rounds, more, (jnp.int32(1), start))[1]

    total = lax.cond(rounds > 1, rest, lambda start: start, first)
    return (total, jnp.sum(extra.astype(jnp.float32), axis=(0, 1)), beside)


def double(held, bit, axis):
    count = lax.axis_size("dev")
    low = ((lax.axis_index("dev") >> bit) & 1) == 0
    came = lax.ppermute(held, "dev", [(source, source ^ (1 << bit)) for source in range(count)])
    return jnp.stack([jnp.where(low, held, came), jnp.where(low, came, held)], axis=axis)


def spread_z(shard, first, last):
    bits = lax.axis_size("dev").bit_length() - 1
    for done in range(first, min(last, bits - 3)):
        shard = double(shard, bits - 1 - done, done)
    return shard


def spread_plane(held):
    at, half = (lax.axis_size("dev").bit_length() - 4, held.shape[-1] // 2)
    left = double(double(held[..., :half], 2, at), 1, at + 1)
    right = double(double(held[..., half:], 1, at), 2, at)
    return (left, right)


def spread_cores(halves):
    whole = jnp.concatenate(halves, axis=-1)
    return double(whole, 0, lax.axis_size("dev").bit_length() - 2)


def gather_late(stack, part, up_cols):
    width = stack.shape[1]
    down = stack.shape[0] - part * (1 + up_cols)
    whole = lax.all_gather(stack, "dev", axis=0)
    up = whole[:, down + part :].reshape(-1, up_cols, part, width).swapaxes(0, 1)
    late = whole if down % 32 == 0 else whole[:, :down].reshape(up_cols, width, width)
    return (whole[:, down : down + part].reshape(-1, width), up.reshape(up_cols, -1, width), late)


def split_rows(summed, sizes):
    pieces, start = ([], 0)
    for size in sizes:
        pieces.append(summed[start : start + size])
        start += size
    return pieces


def swap_parts(held, bit):
    count = lax.axis_size("dev")
    mine = (lax.axis_index("dev") >> bit) & 1
    keep = lax.dynamic_index_in_dim(held, mine, 0, keepdims=False)
    give = lax.dynamic_index_in_dim(held, 1 - mine, 0, keepdims=False)
    return (keep, lax.ppermute(give, "dev", [(source, source ^ (1 << bit)) for source in range(count)]))


def join_parts(parts, last=False):
    total = parts[0].astype(jnp.float32) + parts[1].astype(jnp.float32)
    return total if last else total.astype(jnp.bfloat16)


def swap_halves(held, bit, last=False):
    return join_parts(swap_parts(held, bit), last)


def middle_bits():
    return list(range(1, lax.axis_size("dev").bit_length() - 2))


def sum_cores(term):
    count, pieces, rows, width = term.shape
    grid = term.reshape(count // 2, 2, pieces, rows, width)
    return swap_halves(grid.swapaxes(0, 1), 0).reshape(count // 2, pieces * rows, width)


def cut_thirds(held):
    _, rows, width = held.shape
    middle = middle_bits()
    bits = len(middle) + 1
    grid = held.reshape((2,) * bits + (rows, width))
    thirds = []
    for turn in range(3):
        shift = turn % len(middle)
        order = middle[shift:] + middle[:shift] + [bits]
        axes = [bits - bit for bit in order]
        part = grid[..., turn * (width // 3) : (turn + 1) * (width // 3)]
        thirds.append(part.transpose(axes + [bits, bits + 1]))
    return thirds


def sum_stage(thirds, stage):
    middle = middle_bits()
    return [swap_halves(third, middle[(turn + stage) % len(middle)]) for turn, third in enumerate(thirds)]


def sum_stages(thirds, first):
    for stage in range(first, len(middle_bits())):
        thirds = sum_stage(thirds, stage)
    return thirds


def sum_last(groups):
    whole = [jnp.concatenate(thirds, axis=-1) for thirds in groups]
    return swap_halves(jnp.concatenate(whole, axis=1), len(middle_bits()) + 1, True)


def split_low(values):
    high = lax.reduce_precision(values, 8, 7)
    return (high.astype(jnp.bfloat16), (values - high).astype(jnp.bfloat16))


def low_units(blocks):
    per_row = blocks.shape[1]
    place = 8 + jnp.arange(per_row, dtype=jnp.int32)[None, :]
    return jnp.min(place - 2 * ((blocks + 1) // 2), axis=1).astype(jnp.int32)


def by_unit(array):
    cut = array.reshape((array.shape[0], array.shape[1] // UNIT, UNIT) + array.shape[2:])
    return cut.swapaxes(0, 1)


def by_row(array, micros):
    cut = array.reshape(-1, micros, UNIT, array.shape[-1])
    return cut.swapaxes(0, 1).reshape(micros, -1, array.shape[-1])


def shards(
    token_ids,
    lengths,
    embedding,
    norm1_gain,
    w_query,
    w_key,
    w_value,
    w_out,
    mix_logits,
    mix_weights,
    norm2_gain,
    w_up,
    w_down,
    cotangent,
):
    count = lax.axis_size("dev")
    me = lax.axis_index("dev")
    micros, row_count = token_ids.shape
    own_rows, width = embedding.shape
    heads = mix_logits.shape[0]
    part = norm1_gain.shape[0]
    per_row = row_count // UNIT
    tokens = micros * row_count
    tok_ids = by_unit(token_ids).reshape(-1)
    stride = max(16, 1024 // count)
    room = stride - 2

    unit_rows = me * row_count + UNIT * jnp.arange(per_row, dtype=jnp.int32)
    begins = jnp.stack([seq_starts(lengths[micro], unit_rows) for micro in range(micros)])
    blocks = ((unit_rows[None, :] - begins) // UNIT + 1).reshape(-1).astype(jnp.int32)

    lows = low_units(blocks.reshape(micros, per_row))
    mixes = spread_mixes(mix_logits, mix_weights)

    up_cols = w_up.shape[1] // width
    up_pieces = [w_up[:, col * width : (col + 1) * width] for col in range(up_cols)]
    first_weights = spread_z(jnp.stack([w_query, w_key, w_value]), 0, 1)
    late_stack = jnp.concatenate([w_down, w_out] + up_pieces, axis=0)
    ids = split_ids(tok_ids, own_rows)
    message, chosen = ask_round(ids, 0, own_rows, stride, room)
    message, first_weights = lax.optimization_barrier((message, first_weights))
    first_weights = spread_plane(spread_z(first_weights, 1, 99))
    gains_row = jnp.concatenate([norm1_gain, norm2_gain, jnp.zeros((width - 2 * part,), jnp.bfloat16)])
    picked, gains, first_weights, *plan = lookup(
        embedding, ids, message, chosen, gains_row, stride, room, first_weights
    )
    gain_one = gains[:, :part].reshape(-1)
    gain_two = gains[:, part : 2 * part].reshape(-1)
    picked, late_stack = lax.optimization_barrier((picked, late_stack))
    w_o, w_u, w_d = gather_late(late_stack, part, up_cols)
    inputs = picked.astype(jnp.float32)

    normed_one, inv_one, hidden_one = normalize(inputs, gain_one)
    own_hidden = hidden_one.reshape(per_row, micros, UNIT, width)
    pieces = earlier_rows(own_hidden)
    first_weights = spread_cores(first_weights).reshape(count, 3, part, width)
    w_q, w_k, w_v = (first_weights[:, at].reshape(-1, width) for at in range(3))
    query, key, value = project(lows, pieces, (w_q, w_k, w_v))
    attended, *kept = attention_fwd(blocks, query, key, value, mixes, heads)
    attended = attended.reshape(tokens, width)

    grad_rows = by_unit(cotangent).reshape(tokens, width)
    gain_row = gain_two.astype(jnp.float32)[None, :]
    middle, output, grad_hidden_two, grad_up, grad_down = feed_forward(
        picked, attended, w_o, gain_row, w_u, w_d, grad_rows
    )
    inv_two = lax.rsqrt(jnp.mean(middle * middle, axis=-1, keepdims=True) + norm_eps)
    normed_two = middle * inv_two
    grad_mid_norm, grad_gain_two = norm_back(grad_hidden_two, normed_two, inv_two, gain_two)
    grad_middle = grad_rows.astype(jnp.float32) + grad_mid_norm
    grad_branch = grad_middle.astype(jnp.bfloat16)
    grad_att = matmul_right_t(grad_branch, w_o).astype(jnp.bfloat16).reshape(own_hidden.shape)
    up_rows = grad_up.reshape(up_cols, count, part, width).swapaxes(0, 1).reshape(count, -1, width)
    stack = jnp.concatenate([grad_down.reshape(count, -1, width), up_rows], axis=1).reshape(-1, width)
    stack, grad_att = lax.optimization_barrier((stack, grad_att))
    late_sums = lax.psum_scatter(stack, "dev", scatter_dimension=0, tiled=True).astype(jnp.float32)

    def tail(pieces, query, key, value, grad_att, kept, attended, grad_branch):
        grads, owns, wides, ready = ([], [], [], ())
        for micro in range(micros):
            *grad, wide_logit, wide_prob = attention_bwd(
                blocks, query, key, value, grad_att, kept, mixes, heads, micro
            )
            grad, ready = lax.optimization_barrier((grad, ready))
            grads.append(grad)
            owns.append(ready)
            wides.append((wide_logit, wide_prob))
            *terms, grad_own = project_back(lows[micro : micro + 1], *grad, (w_q, w_k, w_v))
            came = with_sibling(jnp.concatenate([terms[3], terms[1]], axis=0))
            if micro + 1 < micros:
                ready = (grad_own, *return_rows(terms[0], terms[2], came))
        came, grads, hidden, attended = lax.optimization_barrier((came, grads, pieces, attended))
        grad_wout = matmul_left_t(attended, grad_branch)
        grad_qkv = weigh(lows, grads, hidden)
        grad_wout = grad_wout.astype(jnp.bfloat16)[None]
        backs, (grad_qkv, grad_wout) = return_in_turn(terms[0], terms[2], came, (grad_qkv, grad_wout))
        wide_logit, wide_prob = (sum(wide[kind] for wide in wides) for kind in range(2))
        early_terms = jnp.concatenate([grad_qkv, grad_wout], axis=0)
        early = cut_thirds(sum_cores(early_terms.reshape(4, count, part, width).swapaxes(0, 1)))
        backs, early = lax.optimization_barrier((backs, early))
        owns = owns[1:] + [(grad_own, *backs)]
        grad_own = jnp.concatenate([sum(term.astype(jnp.float32) for term in terms) for terms in owns], axis=1)
        grad_hidden_one = grad_own.reshape(tokens, width)
        grad_in_norm, grad_gain_one = norm_back(grad_hidden_one, normed_one, inv_one, gain_one)
        grad_inputs = grad_middle + grad_in_norm

        mix_terms = jnp.concatenate([fold_mix(wide_logit, heads).reshape(-1), fold_mix(wide_prob, heads).reshape(-1)])
        mix_size = mix_terms.shape[0]
        small = jnp.concatenate(
            [
                grad_gain_one.reshape(count, part),
                grad_gain_two.reshape(count, part),
                jnp.broadcast_to(mix_terms[None, :], (count, mix_size)),
                jnp.zeros((count, width - 2 * part - mix_size), jnp.float32),
            ],
            axis=1,
        )
        table_grad, small_sum, early = table_back(grad_inputs, split_low(small), plan, own_rows, stride, room, early)
        return (by_row(grad_inputs, micros), table_grad, small_sum, sum_last([sum_stages(early, 0)]))

    def no_tail(*operands):
        sizes = ((micros, row_count, width), (own_rows, width), (width,), (4 * part, width))
        return tuple(jnp.zeros(size, jnp.float32) for size in sizes)

    grad_inputs, table_grad, small_sum, early_sums = lax.cond(
        plan[-1] > 0, tail, no_tail, pieces, query, key, value, grad_att, kept, attended, grad_branch
    )
    early_sums = split_rows(early_sums, [part] * 4)
    late_sums = split_rows(late_sums, [w_down.shape[0]] + [part] * up_cols)
    mix_size = 2 * heads * heads
    mixes = small_sum[2 * part : 2 * part + mix_size].reshape(2, heads, heads)
    return (
        by_row(output, micros),
        grad_inputs,
        table_grad,
        small_sum[:part],
        *early_sums,
        mixes[0],
        mixes[1],
        small_sum[part : 2 * part],
        jnp.concatenate(late_sums[1:], axis=1),
        late_sums[0],
    )


def solution(mesh):
    in_specs = (
        P(None, "dev"),
        P(),
        P("dev", None),
        P("dev"),
        P("dev", None),
        P("dev", None),
        P("dev", None),
        P("dev", None),
        P(),
        P(),
        P("dev"),
        P("dev", None),
        P("dev", None),
        P(None, "dev", None),
    )
    out_specs = (
        P(None, "dev", None),
        P(None, "dev", None),
        P("dev", None),
        P("dev"),
        P("dev", None),
        P("dev", None),
        P("dev", None),
        P("dev", None),
        P(),
        P(),
        P("dev"),
        P("dev", None),
        P("dev", None),
    )
    return jax.shard_map(shards, mesh=mesh, in_specs=in_specs, out_specs=out_specs, check_vma=False)
```

```python
from functools import partial

import jax
import jax.numpy as jnp
from jax import lax
from jax.experimental import pallas as pl
from jax.experimental.pallas import tpu as pltpu
from jax.sharding import PartitionSpec as P

norm_eps = 1e-06
gelu_scale = 0.7978845608028654
gelu_cube = 0.044715
FF_STEP = 256

masked = -1e30
UNIT = 128
CHUNK = 256
GROUP = 16
MAX_CHUNKS = 4
TOGETHER = 4


def dot_nn(left, right):
    return lax.dot_general(left, right, (((1,), (0,)), ((), ())), preferred_element_type=jnp.float32)


def dot_nt(left, right):
    return lax.dot_general(left, right, (((1,), (1,)), ((), ())), preferred_element_type=jnp.float32)


def spread_heads(rows, lane_head, quad, heads_per_quad):
    part = rows[:, quad * CHUNK : (quad + 1) * CHUNK]
    zero = jnp.zeros_like(part)
    return jnp.concatenate([jnp.where(lane_head == head, part, zero) for head in range(heads_per_quad)], axis=0)


def own_lanes(wide, lane_head, heads_per_quad):
    total = jnp.where(lane_head == 0, wide[:UNIT], 0.0)
    for head in range(1, heads_per_quad):
        total = total + jnp.where(lane_head == head, wide[head * UNIT : (head + 1) * UNIT], 0.0)
    return total


def part_of(sums, group):
    start = group % TOGETHER * CHUNK
    return sums[:, start : start + CHUNK]


def allowed_keys(chunk, group, blocks):
    key = lax.broadcasted_iota(jnp.int32, (GROUP, CHUNK), 1) - (UNIT + CHUNK * chunk)
    row = lax.broadcasted_iota(jnp.int32, (GROUP, CHUNK), 0) + GROUP * group
    return (key <= row) & (key >= (1 - blocks) * UNIT)


def twice(rows):
    return jnp.concatenate([rows, rows], axis=-1)


def put_groups(ref, quad, per_quad, term):
    low = term.astype(jnp.bfloat16)
    for head in range(per_quad):
        rows = slice((quad * per_quad + head) * GROUP, (quad * per_quad + head + 1) * GROUP)
        for group in range(UNIT // GROUP):
            start = head * UNIT + group * GROUP
            ref[rows, group * CHUNK : (group + 1) * CHUNK] = low[start : start + GROUP]


def fwd_kernel(heads, blocks_ref, q_ref, k_ref, v_ref, mix_ref, att_ref, score_out, prob_out, mixed_out,
               qx, score, prob, mixed, logit, top, norm, total, sems):
    micro, inner, per_row = (pl.program_id(0), pl.program_id(1), pl.num_programs(1))
    blocks = blocks_ref[micro * per_row + inner]
    chunks = (blocks + 1) // 2
    last_unit = k_ref.shape[0] - per_row + inner + 1
    quads = q_ref.shape[3] // CHUNK
    per_quad = heads // quads
    groups = UNIT // GROUP
    wide = heads * GROUP
    lane_head = lax.broadcasted_iota(jnp.int32, (UNIT, CHUNK), 1) // (CHUNK // per_quad)
    for quad in range(quads):
        qx[quad] = spread_heads(q_ref[0, 0], lane_head, quad, per_quad)
    total[...] = jnp.zeros_like(total)
    top[...] = jnp.full_like(top, masked)
    norm[...] = jnp.zeros_like(norm)

    def keys(ref, chunk, quad):
        units = pl.ds(last_unit - 2 * (chunk + 1), 2)
        return ref[units, 0, :, quad * CHUNK : (quad + 1) * CHUNK].reshape(CHUNK, CHUNK)

    step = micro * per_row + inner

    def keep(at, chunk, kind):
        source, target = ((score, score_out), (prob, prob_out), (mixed, mixed_out))[kind]
        place = target.at[at % per_row, at // per_row, chunk]
        return pltpu.make_async_copy(source.at[chunk], place, sems.at[kind, chunk])

    def finish(at):
        @pl.loop(0, (blocks_ref[at] + 1) // 2)
        def _(chunk):
            for kind in range(3):
                keep(at, chunk, kind).wait()

    @pl.when(step > 0)
    def _():
        finish(step - 1)

    @pl.loop(0, chunks)
    def _(chunk):
        for quad in range(quads):
            put_groups(score.at[chunk], quad, per_quad, dot_nt(qx[quad], keys(k_ref, chunk, quad)))
        keep(step, chunk, 0).start()
        for group in range(groups):
            if group % TOGETHER == 0:
                mixes = dot_nn(mix_ref[0], score[chunk, :, group * CHUNK : (group + TOGETHER) * CHUNK])
            l = part_of(mixes, group)
            l = jnp.where(allowed_keys(chunk, group, blocks)[None], l.reshape(heads, GROUP, CHUNK), masked)
            l = l.reshape(wide, CHUNK)
            logit[chunk, group] = l
            old = top[group]
            new = jnp.maximum(old, jnp.maximum(l[:, :UNIT], l[:, UNIT:]))
            terms = jnp.exp(l[:, :UNIT] - new) + jnp.exp(l[:, UNIT:] - new)
            norm[group] = norm[group] * jnp.exp(old - new) + terms
            top[group] = new

    for group in range(groups):
        lanes = top[group]
        high = jnp.broadcast_to(jnp.max(lanes, axis=-1, keepdims=True), lanes.shape)
        whole = jnp.sum(norm[group] * jnp.exp(lanes - high), axis=-1, keepdims=True)
        top[group] = high + jnp.log(jnp.broadcast_to(whole, lanes.shape))

    @pl.loop(0, chunks)
    def _(chunk):
        for group in range(groups):
            p = jnp.exp(logit[chunk, group] - twice(top[group])).astype(jnp.bfloat16)
            prob[chunk, :, group * CHUNK : (group + 1) * CHUNK] = p
        for first in range(0, groups, TOGETHER):
            sums = dot_nn(mix_ref[2], prob[chunk, :, first * CHUNK : (first + TOGETHER) * CHUNK])
            for group in range(first, first + TOGETHER):
                a = part_of(sums, group).astype(jnp.bfloat16)
                mixed[chunk, :, GROUP * group : GROUP * (group + 1), :] = a.reshape(heads, GROUP, CHUNK)
        keep(step, chunk, 1).start()
        keep(step, chunk, 2).start()
        for quad in range(quads):
            a = mixed[chunk, quad * per_quad : (quad + 1) * per_quad].reshape(per_quad * UNIT, CHUNK)
            o = own_lanes(dot_nn(a, keys(v_ref, chunk, quad)), lane_head, per_quad)
            total[:, quad * CHUNK : (quad + 1) * CHUNK] += o

    att_ref[0, 0] = total[...].astype(jnp.bfloat16)

    @pl.when(step == pl.num_programs(0) * per_row - 1)
    def _():
        finish(step)


def attention_specs(q, k, heads):
    per_row, micros, _, width = q.shape
    wide = heads * GROUP
    return (
        pl.BlockSpec((1, 1, UNIT, width), lambda m, u, _: (u, m, 0, 0)),
        pl.BlockSpec((k.shape[0], 1, UNIT, width), lambda m, u, _: (0, m, 0, 0)),
        pl.BlockSpec((4, wide, wide), lambda m, u, _: (0, 0, 0)),
    )


def kept_shapes(heads):
    wide = heads * GROUP
    flat = (MAX_CHUNKS, wide, UNIT // GROUP * CHUNK)
    return (flat, flat, (MAX_CHUNKS, heads, UNIT, CHUNK))


def attention_fwd(blocks, q, k, v, mixes, heads):
    per_row, micros, _, width = q.shape
    wide = heads * GROUP
    groups = UNIT // GROUP
    quads = width // CHUNK
    unit_spec, kv_spec, mix_spec = attention_specs(q, k, heads)
    kept = kept_shapes(heads)
    anywhere = pl.BlockSpec(memory_space=pl.ANY)
    return pl.pallas_call(
        partial(fwd_kernel, heads),
        grid_spec=pltpu.PrefetchScalarGridSpec(
            num_scalar_prefetch=1,
            grid=(micros, per_row),
            in_specs=[unit_spec, kv_spec, kv_spec, mix_spec],
            out_specs=[unit_spec, anywhere, anywhere, anywhere],
            scratch_shapes=[pltpu.VMEM((quads, heads // quads * UNIT, CHUNK), jnp.bfloat16)]
            + [pltpu.VMEM(shape, jnp.bfloat16) for shape in kept]
            + [
                pltpu.VMEM((MAX_CHUNKS, groups, wide, CHUNK), jnp.float32),
                pltpu.VMEM((groups, wide, UNIT), jnp.float32),
                pltpu.VMEM((groups, wide, UNIT), jnp.float32),
                pltpu.VMEM((UNIT, width), jnp.float32),
                pltpu.SemaphoreType.DMA((3, MAX_CHUNKS)),
            ],
        ),
        out_shape=[jax.ShapeDtypeStruct(q.shape, jnp.bfloat16)]
        + [jax.ShapeDtypeStruct((per_row, micros) + shape, jnp.bfloat16) for shape in kept],
        compiler_params=pltpu.CompilerParams(vmem_limit_bytes=50 * 1024 * 1024),
        cost_estimate=pl.CostEstimate(flops=20_000_000_000, bytes_accessed=30_000_000, transcendentals=0),
        name="attention_fwd",
    )(blocks, q, k, v, mixes)


def bwd_kernel(heads, blocks_ref, q_ref, k_ref, v_ref, do_ref, mix_ref, score_in, prob_in, mixed_in,
               dq_ref, dk_ref, dv_ref, gl_ref, gp_ref,
               qxt, dox, doxt, score, prob, mixed, grad_prob, grad_mixed, grad_logit, grad_score,
               delta, dq_total, dk_total, dv_total, sems):
    micro, inner, per_row = (pl.program_id(0), pl.program_id(1), pl.num_programs(1))
    step = micro * per_row + inner
    slot = step % 2
    blocks = blocks_ref[step]
    chunks = (blocks + 1) // 2
    key_units = k_ref.shape[0]
    last_unit = key_units - per_row + inner + 1
    quads = q_ref.shape[3] // CHUNK
    per_quad = heads // quads
    groups = UNIT // GROUP
    wide = heads * GROUP
    lane_head = lax.broadcasted_iota(jnp.int32, (UNIT, CHUNK), 1) // (CHUNK // per_quad)
    row_head = lax.broadcasted_iota(jnp.int32, (CHUNK, UNIT), 0) // (CHUNK // per_quad)
    lowest = key_units
    for other in range(key_units - 7):
        its_chunks = (blocks_ref[micro * per_row + other] + 1) // 2
        lowest = jnp.minimum(lowest, key_units - per_row + other + 1 - 2 * its_chunks)

    def fetch(at, chunk, kind):
        source, target = ((score_in, score), (prob_in, prob), (mixed_in, mixed))[kind]
        place = source.at[at % per_row, at // per_row, chunk]
        return pltpu.make_async_copy(place, target.at[at % 2, chunk], sems.at[kind, at % 2, chunk])

    def fetch_all(at):
        @pl.loop(0, (blocks_ref[at] + 1) // 2)
        def _(chunk):
            for kind in (1, 2, 0):
                fetch(at, chunk, kind).start()

    @pl.when(step == 0)
    def _():
        fetch_all(0)
        gl_ref[...] = jnp.zeros_like(gl_ref)
        gp_ref[...] = jnp.zeros_like(gp_ref)

    @pl.when(step + 1 < pl.num_programs(0) * per_row)
    def _():
        fetch_all(step + 1)

    @pl.when(inner == 0)
    def _():
        @pl.loop(lowest, key_units)
        def _(key_unit):
            dk_total[key_unit] = jnp.zeros_like(dk_total[key_unit])
            dv_total[key_unit] = jnp.zeros_like(dv_total[key_unit])

    def spread_turned(rows, quad):
        turned = rows[:, quad * CHUNK : (quad + 1) * CHUNK].T
        zero = jnp.zeros_like(turned)
        return jnp.concatenate([jnp.where(row_head == head, turned, zero) for head in range(per_quad)], axis=1)

    for quad in range(quads):
        qxt[quad] = spread_turned(q_ref[0, 0], quad)
        dox[quad] = spread_heads(do_ref[0, 0], lane_head, quad, per_quad)
        doxt[quad] = spread_turned(do_ref[0, 0], quad)
    dq_total[...] = jnp.zeros_like(dq_total)
    delta[...] = jnp.zeros_like(delta)

    def keys(ref, chunk, quad):
        units = pl.ds(last_unit - 2 * (chunk + 1), 2)
        return ref[units, 0, :, quad * CHUNK : (quad + 1) * CHUNK].reshape(CHUNK, CHUNK)

    def add_to(total, chunk, quad, term):
        first = last_unit - 2 * (chunk + 1)
        lanes = slice(quad * CHUNK, (quad + 1) * CHUNK)
        total[first, lanes, :] += term[:, :UNIT]
        total[first + 1, lanes, :] += term[:, UNIT:]

    @pl.loop(0, chunks)
    def _(chunk):
        for quad in range(quads):
            put_groups(grad_mixed, quad, per_quad, dot_nt(dox[quad], keys(v_ref, chunk, quad)))
        fetch(step, chunk, 1).wait()
        for group in range(groups):
            cols = slice(group * CHUNK, (group + 1) * CHUNK)
            if group % TOGETHER == 0:
                sums = dot_nn(mix_ref[3], grad_mixed[:, group * CHUNK : (group + TOGETHER) * CHUNK])
            dp = part_of(sums, group)
            grad_prob[chunk, :, cols] = dp.astype(grad_prob.dtype)
            term = prob[slot, chunk, :, cols].astype(jnp.float32) * dp
            delta[group] += term[:, :UNIT] + term[:, UNIT:]
        gp_ref[...] += dot_nt(prob[slot, chunk], grad_mixed[...])
        fetch(step, chunk, 2).wait()
        for quad in range(quads):
            a = mixed[slot, chunk, quad * per_quad : (quad + 1) * per_quad].reshape(per_quad * UNIT, CHUNK)
            add_to(dv_total, chunk, quad, dot_nn(doxt[quad], a))

    for group in range(groups):
        delta[group] = jnp.broadcast_to(jnp.sum(delta[group], axis=-1, keepdims=True), (wide, UNIT))

    @pl.loop(0, chunks)
    def _(chunk):
        for group in range(groups):
            cols = slice(group * CHUNK, (group + 1) * CHUNK)
            dp = grad_prob[chunk, :, cols].astype(jnp.float32) - twice(delta[group])
            dl = (prob[slot, chunk, :, cols].astype(jnp.float32) * dp).astype(jnp.bfloat16)
            grad_logit[:, cols] = dl
        for first in range(0, groups, TOGETHER):
            sums = dot_nn(mix_ref[1], grad_logit[:, first * CHUNK : (first + TOGETHER) * CHUNK])
            for group in range(first, first + TOGETHER):
                ds = part_of(sums, group).astype(jnp.bfloat16)
                grad_score[:, GROUP * group : GROUP * (group + 1), :] = ds.reshape(heads, GROUP, CHUNK)
        fetch(step, chunk, 0).wait()
        gl_ref[...] += dot_nt(score[slot, chunk], grad_logit[...])
        for quad in range(quads):
            ds = grad_score[quad * per_quad : (quad + 1) * per_quad].reshape(per_quad * UNIT, CHUNK)
            dq = own_lanes(dot_nn(ds, keys(k_ref, chunk, quad)), lane_head, per_quad)
            dq_total[:, quad * CHUNK : (quad + 1) * CHUNK] += dq
            add_to(dk_total, chunk, quad, dot_nn(qxt[quad], ds))

    dq_ref[0, 0] = (dq_total[...] * 0.125).astype(jnp.bfloat16)

    @pl.when(inner == per_row - 1)
    def _():
        @pl.loop(0, lowest)
        def _(key_unit):
            dk_ref[key_unit, 0] = jnp.zeros_like(dk_ref[key_unit, 0])
            dv_ref[key_unit, 0] = jnp.zeros_like(dv_ref[key_unit, 0])

        @pl.loop(lowest, key_units)
        def _(key_unit):
            dk_ref[key_unit, 0] = dk_total[key_unit].astype(jnp.bfloat16).T
            dv_ref[key_unit, 0] = dv_total[key_unit].astype(jnp.bfloat16).T


def attention_bwd(blocks, q, k, v, grad_out, kept, mixes, heads):
    per_row, micros, _, width = q.shape
    key_units = k.shape[0]
    wide = heads * GROUP
    groups = UNIT // GROUP
    quads = width // CHUNK
    turned = (quads, CHUNK, heads // quads * UNIT)
    unit_spec, kv_spec, mix_spec = attention_specs(q, k, heads)
    sum_spec = pl.BlockSpec((wide, wide), lambda m, u, _: (0, 0))
    anywhere = pl.BlockSpec(memory_space=pl.ANY)
    return pl.pallas_call(
        partial(bwd_kernel, heads),
        grid_spec=pltpu.PrefetchScalarGridSpec(
            num_scalar_prefetch=1,
            grid=(micros, per_row),
            in_specs=[unit_spec, kv_spec, kv_spec, unit_spec, mix_spec] + [anywhere] * 3,
            out_specs=[unit_spec, kv_spec, kv_spec, sum_spec, sum_spec],
            scratch_shapes=[
                pltpu.VMEM(turned, jnp.bfloat16),
                pltpu.VMEM((quads, heads // quads * UNIT, CHUNK), jnp.bfloat16),
                pltpu.VMEM(turned, jnp.bfloat16),
            ]
            + [pltpu.VMEM((2,) + shape, jnp.bfloat16) for shape in kept_shapes(heads)]
            + [
                pltpu.VMEM((MAX_CHUNKS, wide, groups * CHUNK), jnp.bfloat16),
                pltpu.VMEM((wide, groups * CHUNK), jnp.bfloat16),
                pltpu.VMEM((wide, groups * CHUNK), jnp.bfloat16),
                pltpu.VMEM((heads, UNIT, CHUNK), jnp.bfloat16),
                pltpu.VMEM((groups, wide, UNIT), jnp.float32),
                pltpu.VMEM((UNIT, width), jnp.float32),
                pltpu.VMEM((key_units, width, UNIT), jnp.float32),
                pltpu.VMEM((key_units, width, UNIT), jnp.float32),
                pltpu.SemaphoreType.DMA((3, 2, MAX_CHUNKS)),
            ],
        ),
        out_shape=[
            jax.ShapeDtypeStruct(q.shape, jnp.bfloat16),
            jax.ShapeDtypeStruct(k.shape, jnp.bfloat16),
            jax.ShapeDtypeStruct(v.shape, jnp.bfloat16),
            jax.ShapeDtypeStruct((wide, wide), jnp.float32),
            jax.ShapeDtypeStruct((wide, wide), jnp.float32),
        ],
        compiler_params=pltpu.CompilerParams(vmem_limit_bytes=58 * 1024 * 1024),
        cost_estimate=pl.CostEstimate(flops=45_000_000_000, bytes_accessed=40_000_000, transcendentals=0),
        name="attention_bwd",
    )(blocks, q, k, v, grad_out, mixes, *kept)


def piece_bases(key_units, per_row):
    sizes = [1] + [per_row] * ((key_units - 1) // per_row)
    return [(sum(sizes[:at]), size) for at, size in enumerate(sizes)]


def project_kernel(low_ref, *refs):
    pieces, (w_q, w_k, w_v, q_ref, k_ref, v_ref) = (refs[:-6], refs[-6:])
    key_units, width = (k_ref.shape[0], k_ref.shape[3])
    per_row = q_ref.shape[0]
    low = low_ref[pl.program_id(0)]

    for piece, (base, size) in zip(pieces, piece_bases(key_units, per_row)):
        @pl.when(base + size > low)
        def _():
            rows = piece[:, 0].reshape(size * UNIT, width)
            k_ref[base : base + size, 0] = dot_nn(rows, w_k[...]).astype(jnp.bfloat16).reshape(size, UNIT, width)
            v_ref[base : base + size, 0] = dot_nn(rows, w_v[...]).astype(jnp.bfloat16).reshape(size, UNIT, width)

    rows = pieces[-1][:, 0].reshape(per_row * UNIT, width)
    query = dot_nn(rows, w_q[...]).astype(jnp.bfloat16) * jnp.bfloat16(0.125)
    q_ref[:, 0] = query.reshape(per_row, UNIT, width)


def project(low, pieces, weights):
    micros, width = pieces[0].shape[1], pieces[0].shape[3]
    key_units = sum(piece.shape[0] for piece in pieces)
    per_row = pieces[-1].shape[0]

    def spec(units):
        return pl.BlockSpec((units, 1, UNIT, width), lambda m, _: (0, m, 0, 0))

    weight_spec = pl.BlockSpec((width, width), lambda m, _: (0, 0))
    shapes = [(units, micros, UNIT, width) for units in (per_row, key_units, key_units)]
    return pl.pallas_call(
        project_kernel,
        grid_spec=pltpu.PrefetchScalarGridSpec(
            num_scalar_prefetch=1,
            grid=(micros,),
            in_specs=[spec(piece.shape[0]) for piece in pieces] + [weight_spec] * 3,
            out_specs=[spec(shape[0]) for shape in shapes],
        ),
        out_shape=[jax.ShapeDtypeStruct(shape, jnp.bfloat16) for shape in shapes],
        compiler_params=pltpu.CompilerParams(vmem_limit_bytes=44 * 1024 * 1024),
        cost_estimate=pl.CostEstimate(flops=6_000_000_000, bytes_accessed=15_000_000, transcendentals=0),
        name="project",
    )(low, *pieces, *weights)


def project_back_kernel(low_ref, dq_ref, dk_ref, dv_ref, w_q, w_k, w_v, *outs):
    key_units, width = (dk_ref.shape[0], dk_ref.shape[3])
    per_row = dq_ref.shape[0]
    low = low_ref[pl.program_id(0)]
    bases = piece_bases(key_units, per_row)

    def from_keys(base, size):
        rows = slice(base, base + size)
        key_term = dot_nt(dk_ref[rows, 0].reshape(size * UNIT, width), w_k[...])
        return key_term + dot_nt(dv_ref[rows, 0].reshape(size * UNIT, width), w_v[...])

    for out, (base, size) in zip(outs[:-1], bases[:-1]):
        @pl.when(base + size > low)
        def _():
            out[:, 0] = from_keys(base, size).astype(jnp.bfloat16).reshape(size, UNIT, width)

        @pl.when(base + size <= low)
        def _():
            out[...] = jnp.zeros_like(out)

    own = from_keys(*bases[-1]) + dot_nt(dq_ref[:, 0].reshape(per_row * UNIT, width), w_q[...])
    outs[-1][:, 0] = own.reshape(per_row, UNIT, width)


def project_back(low, grad_query, grad_key, grad_value, weights):
    per_row, micros, _, width = grad_query.shape
    key_units = grad_key.shape[0]

    def spec(units):
        return pl.BlockSpec((units, 1, UNIT, width), lambda m, _: (0, m, 0, 0))

    weight_spec = pl.BlockSpec((width, width), lambda m, _: (0, 0))
    sizes = [size for _, size in piece_bases(key_units, per_row)]
    shapes = [(size, micros, UNIT, width) for size in sizes]
    kinds = [jnp.bfloat16] * (len(sizes) - 1) + [jnp.float32]
    return pl.pallas_call(
        project_back_kernel,
        grid_spec=pltpu.PrefetchScalarGridSpec(
            num_scalar_prefetch=1,
            grid=(micros,),
            in_specs=[spec(per_row), spec(key_units), spec(key_units)] + [weight_spec] * 3,
            out_specs=[spec(size) for size in sizes],
        ),
        out_shape=[jax.ShapeDtypeStruct(shape, kind) for shape, kind in zip(shapes, kinds)],
        compiler_params=pltpu.CompilerParams(vmem_limit_bytes=44 * 1024 * 1024),
        cost_estimate=pl.CostEstimate(flops=6_000_000_000, bytes_accessed=15_000_000, transcendentals=0),
        name="project_back",
    )(low, grad_query, grad_key, grad_value, *weights)


def weigh_kernel(low_ref, dq_ref, dk_ref, dv_ref, att_ref, branch_ref, *refs):
    pieces, (grad_ref, total) = (refs[:-2], refs[-2:])
    key_units, width = (dk_ref.shape[0], dk_ref.shape[3])
    per_row = dq_ref.shape[0]
    micro = pl.program_id(0)
    low = low_ref[micro]
    bases = piece_bases(key_units, per_row)

    @pl.when(micro == 0)
    def _():
        total[0:3] = jnp.zeros_like(total[0:3])
        total[3] = dot_nn(att_ref[...].T, branch_ref[...])

    def keys(ref, base, size):
        return ref[base : base + size, 0].reshape(size * UNIT, width)

    for piece, (base, size) in zip(pieces, bases):
        @pl.when(base + size > low)
        def _():
            turned = piece[:, 0].reshape(size * UNIT, width).T
            total[1] += dot_nn(turned, keys(dk_ref, base, size))
            total[2] += dot_nn(turned, keys(dv_ref, base, size))
            if base + size == key_units:
                total[0] += dot_nn(turned, keys(dq_ref, 0, per_row))

    @pl.when(micro == pl.num_programs(0) - 1)
    def _():
        grad_ref[...] = total[...].astype(jnp.bfloat16)


def weigh(low, grad_query, grad_key, grad_value, attended, branch, pieces):
    per_row, micros, _, width = grad_query.shape
    key_units = grad_key.shape[0]

    def spec(units):
        return pl.BlockSpec((units, 1, UNIT, width), lambda m, _: (0, m, 0, 0))

    sizes = [size for _, size in piece_bases(key_units, per_row)]
    return pl.pallas_call(
        weigh_kernel,
        grid_spec=pltpu.PrefetchScalarGridSpec(
            num_scalar_prefetch=1,
            grid=(micros,),
            in_specs=[spec(size) for size in (per_row, key_units, key_units)]
            + [pl.BlockSpec(attended.shape, lambda m, _: (0, 0))] * 2
            + [spec(size) for size in sizes],
            out_specs=pl.BlockSpec((4, width, width), lambda m, _: (0, 0, 0)),
            scratch_shapes=[pltpu.VMEM((4, width, width), jnp.float32)],
        ),
        out_shape=jax.ShapeDtypeStruct((4, width, width), jnp.bfloat16),
        compiler_params=pltpu.CompilerParams(vmem_limit_bytes=48 * 1024 * 1024),
        cost_estimate=pl.CostEstimate(flops=12_000_000_000, bytes_accessed=14_000_000, transcendentals=0),
        name="weigh",
    )(low, grad_query, grad_key, grad_value, attended, branch, *pieces)


def feed_kernel(x_ref, att_ref, w_o_ref, gain_ref, up_ref, down_ref, cot_ref,
                mid_ref, out_ref, grad_hidden_ref, grad_up_ref, grad_down_ref,
                hidden, turned, out_total, back_total):
    step = pl.program_id(0)

    @pl.when(step == 0)
    def _():
        middle = x_ref[...].astype(jnp.float32) + dot_nn(att_ref[...], w_o_ref[...])
        mid_ref[...] = middle
        inv_rms = lax.rsqrt(jnp.mean(middle * middle, axis=-1, keepdims=True) + norm_eps)
        rows = (middle * inv_rms * gain_ref[...]).astype(jnp.bfloat16)
        hidden[...] = rows
        turned[...] = rows.T
        out_total[...] = jnp.zeros_like(out_total)
        back_total[...] = jnp.zeros_like(back_total)

    down_rows = down_ref[...].reshape(up_ref.shape[1:])
    for start in range(0, up_ref.shape[2], FF_STEP):
        cols = slice(start, start + FF_STEP)
        down = down_rows[cols]
        up = dot_nn(hidden[...], up_ref[0, :, cols])
        square = up * up
        bent = jnp.tanh(gelu_scale * up * (1.0 + gelu_cube * square))
        half = 0.5 + 0.5 * bent
        slope = half + 0.5 * up * (1.0 - bent * bent) * (gelu_scale * (1.0 + 3.0 * gelu_cube * square))
        active = (up * half).astype(jnp.bfloat16)
        grad_up = (dot_nt(cot_ref[...], down) * slope).astype(jnp.bfloat16)
        out_total[...] += dot_nn(active, down)
        back_total[...] += dot_nt(grad_up, up_ref[0, :, cols])
        grad_down_ref[cols, :] = dot_nn(active.T, cot_ref[...]).astype(jnp.bfloat16)
        grad_up_ref[0, :, cols] = dot_nn(turned[...], grad_up).astype(jnp.bfloat16)

    @pl.when(step == pl.num_programs(0) - 1)
    def _():
        out_ref[...] = (mid_ref[...] + out_total[...]).astype(jnp.bfloat16)
        grad_hidden_ref[...] = back_total[...]


def feed_forward(rows, attended, w_o, gain, w_up, w_late, cot):
    tokens, width = rows.shape
    pieces = w_up.shape[0]
    whole = pl.BlockSpec((tokens, width), lambda i: (0, 0))
    up_spec = pl.BlockSpec((1, width, width), lambda i: (i, 0, 0))
    down_spec = pl.BlockSpec((width, width), lambda i: (i, 0))
    devices = w_late.shape[0] // pieces
    late_spec = pl.BlockSpec((devices, width // devices, width), lambda i: (i, 0, 0))
    f32, bf16 = (jnp.float32, jnp.bfloat16)
    return pl.pallas_call(
        feed_kernel,
        grid=(pieces,),
        in_specs=[
            whole,
            whole,
            pl.BlockSpec((width, width), lambda i: (0, 0)),
            pl.BlockSpec((1, width), lambda i: (0, 0)),
            up_spec,
            late_spec,
            whole,
        ],
        out_specs=[whole, whole, whole, up_spec, down_spec],
        out_shape=[
            jax.ShapeDtypeStruct((tokens, width), f32),
            jax.ShapeDtypeStruct((tokens, width), bf16),
            jax.ShapeDtypeStruct((tokens, width), f32),
            jax.ShapeDtypeStruct(w_up.shape, bf16),
            jax.ShapeDtypeStruct((pieces * width, width), bf16),
        ],
        scratch_shapes=[
            pltpu.VMEM((tokens, width), bf16),
            pltpu.VMEM((width, tokens), bf16),
            pltpu.VMEM((tokens, width), f32),
            pltpu.VMEM((tokens, width), f32),
        ],
        compiler_params=pltpu.CompilerParams(vmem_limit_bytes=48 * 1024 * 1024),
        cost_estimate=pl.CostEstimate(flops=16_000_000_000, bytes_accessed=30_000_000, transcendentals=0),
        name="feed_forward",
    )(rows, attended, w_o, gain, w_up, w_late, cot)


def spread_mixes(mix_logits, mix_weights):
    heads = mix_logits.shape[0]
    wide = heads * GROUP
    place = jnp.arange(wide, dtype=jnp.int32)
    pick = (place[:, None] // GROUP == jnp.arange(heads, dtype=jnp.int32)[None, :]).astype(mix_logits.dtype)
    same_row = (place[:, None] % GROUP == place[None, :] % GROUP)[None]
    tables = jnp.stack([mix_logits.T, mix_logits, mix_weights.T, mix_weights]).reshape(4 * heads, heads)
    across = jnp.dot(tables, pick.T, preferred_element_type=jnp.float32).astype(mix_logits.dtype)
    down = jnp.einsum("wh,bhx->bwx", pick, across.reshape(4, heads, wide), preferred_element_type=jnp.float32)
    return jnp.where(same_row, down, 0.0).astype(mix_logits.dtype)


def fold_mix(wide, heads):
    place = jnp.arange(heads * GROUP, dtype=jnp.int32)
    pick = (place[:, None] // GROUP == jnp.arange(heads, dtype=jnp.int32)[None, :]).astype(jnp.float32)
    same_row = place[:, None] % GROUP == place[None, :] % GROUP
    down = jnp.dot(pick.T, jnp.where(same_row, wide, 0.0), precision=lax.Precision.HIGHEST)
    return jnp.dot(down, pick, precision=lax.Precision.HIGHEST)


def from_behind(value, steps):
    count = lax.axis_size("dev")
    first, last = (max(0, -steps), min(count, count - steps))
    return lax.ppermute(value, "dev", [(source, source + steps) for source in range(first, last)])


def with_sibling(value):
    count = lax.axis_size("dev")
    return lax.ppermute(value, "dev", [(source, source ^ 1) for source in range(count)])


def earlier_rows(own):
    size = own.shape[0]
    first_core = lax.axis_index("dev") % 2 == 0
    two, four = (from_behind(own, 2), from_behind(own, 4))
    give = jnp.concatenate([jnp.where(first_core, own, two), jnp.where(first_core, two, four)], axis=0)
    came = with_sibling(give)
    return [four[size - 1 :], came[size:], two, came[:size], own]


def return_rows(four, two, came):
    size = two.shape[0]
    first_core = lax.axis_index("dev") % 2 == 0
    came = came.astype(jnp.float32)
    one, three = (came[:size], came[size:])
    give_two = two.astype(jnp.float32) + jnp.where(first_core, three, one)
    padded = jnp.pad(four.astype(jnp.float32), ((size - four.shape[0], 0), (0, 0), (0, 0), (0, 0)))
    give_four = padded + jnp.where(first_core, 0.0, three)
    back_two = from_behind(give_two.astype(jnp.bfloat16), -2)
    back_four = from_behind(give_four.astype(jnp.bfloat16), -4)
    return (jnp.where(first_core, one, 0.0), back_two, back_four)


def seq_starts(lengths_row, query_rows):
    seq_ends = jnp.cumsum(lengths_row)
    starts = seq_ends - lengths_row
    return jnp.max(jnp.where(starts[None, :] <= query_rows[:, None], starts[None, :], 0), axis=1)


def normalize(values, gain_vec):
    inv_rms = lax.rsqrt(jnp.mean(values * values, axis=-1, keepdims=True) + norm_eps)
    normed = values * inv_rms
    return (normed, inv_rms, (normed * gain_vec.astype(jnp.float32)).astype(jnp.bfloat16))


def norm_back(grad_hidden, normed, inv_rms, gain_vec):
    grad_gain = jnp.sum(grad_hidden * normed, axis=0)
    grad_normed = grad_hidden * gain_vec.astype(jnp.float32)
    inner_mean = jnp.mean(grad_normed * normed, axis=-1, keepdims=True)
    return (inv_rms * (grad_normed - normed * inner_mean), grad_gain)


def matmul(left, right):
    return jnp.dot(left, right, preferred_element_type=jnp.float32)


def matmul_left_t(left, right):
    return lax.dot_general(left, right, (((0,), (0,)), ((), ())), preferred_element_type=jnp.float32)


def matmul_right_t(left, right):
    return lax.dot_general(left, right, (((1,), (1,)), ((), ())), preferred_element_type=jnp.float32)


def exchange(value):
    return lax.all_to_all(value, "dev", split_axis=0, concat_axis=0, tiled=True)


def split_ids(tok_ids, own_rows):
    owner = tok_ids // own_rows
    place = jnp.arange(tok_ids.shape[0], dtype=jnp.int32)
    same = tok_ids[:, None] == tok_ids[None, :]
    repeated = jnp.any(same & (place[None, :] < place[:, None]), axis=1)
    before = (owner[:, None] == owner[None, :]) & (tok_ids[None, :] < tok_ids[:, None]) & ~repeated[None, :]
    return (owner, tok_ids % own_rows, jnp.sum(before, axis=1, dtype=jnp.int32))


def ask_round(ids, index, own_rows, stride, room):
    count = lax.axis_size("dev")
    owner, local, rank = ids
    here = rank - index * room
    slot = jnp.where((here >= 0) & (here < room), owner * stride + here, -1)
    chosen = slot[None, :] == jnp.arange(count * stride, dtype=jnp.int32)[:, None]
    wanted = jnp.max(jnp.where(chosen, local[None, :], -1), axis=1).reshape(count, stride)
    rounds = jnp.broadcast_to(jnp.max(rank) // room + 1, (count, stride))
    return (jnp.concatenate([wanted, rounds], axis=1), chosen.astype(jnp.bfloat16))


def hear_round(message, own_rows, stride):
    asked = exchange(message)
    pick = asked[:, :stride].reshape(-1, 1) == jnp.arange(own_rows, dtype=jnp.int32)[None, :]
    return (pick.astype(jnp.bfloat16), jnp.max(asked[:, stride:]))


def plan_round(ids, index, own_rows, stride, room):
    message, chosen = ask_round(ids, index, own_rows, stride, room)
    pick, _ = hear_round(message, own_rows, stride)
    return (chosen, pick)


def answer(embedding, chosen, pick, stride, extra_row, beside=None):
    count = lax.axis_size("dev")
    rows = matmul(pick, embedding).astype(jnp.bfloat16).reshape(count, stride, -1)
    if extra_row is not None:
        is_extra = (jnp.arange(stride, dtype=jnp.int32) == stride - 1)[None, :, None]
        rows = jnp.where(is_extra, extra_row[None, None, :], rows)
    rows, beside = lax.optimization_barrier((rows.reshape(count * stride, -1), beside))
    got = exchange(rows)
    extra = got.reshape(count, stride, -1)[:, stride - 1]
    return (matmul_left_t(chosen, got).astype(jnp.bfloat16), extra, beside)


def lookup(embedding, ids, message, chosen, extra_row, stride, room, beside):
    own_rows = embedding.shape[0]
    pick, rounds = hear_round(message, own_rows, stride)
    first, extra, beside = answer(embedding, chosen, pick, stride, extra_row, beside)

    def more(carry):
        index, rows = carry
        again, its_pick = plan_round(ids, index, own_rows, stride, room)
        return (index + 1, rows + answer(embedding, again, its_pick, stride, None)[0])

    _, rows = lax.while_loop(lambda carry: carry[0] < rounds, more, (jnp.int32(1), first))
    return (rows, extra, beside, ids, chosen, pick, rounds)


def send_grads(grad_low, chosen, pick, stride, beside=None):
    count = lax.axis_size("dev")
    summed = matmul(chosen, grad_low).astype(jnp.bfloat16)
    summed, beside = lax.optimization_barrier((summed, beside))
    got = exchange(summed)
    return (matmul_left_t(pick, got), got.reshape(count, stride, -1)[:, stride - 2 :], beside)


def table_back(grad_rows, extra_rows, plan, own_rows, stride, room, beside):
    ids, chosen, pick, rounds = plan
    count = lax.axis_size("dev")
    grad_low = grad_rows.astype(jnp.bfloat16)
    slot = jnp.arange(count * stride, dtype=jnp.int32)[:, None]
    owner = jnp.arange(count, dtype=jnp.int32)[None, :] * stride
    places = [(slot == owner + at).astype(jnp.bfloat16) for at in (stride - 2, stride - 1)]
    whole = jnp.concatenate([grad_low, *extra_rows], axis=0)
    both = jnp.concatenate([chosen, *places], axis=1)
    first, extra, beside = send_grads(whole, both, pick, stride, beside)

    def more(carry):
        index, total = carry
        again, its_pick = plan_round(ids, index, own_rows, stride, room)
        return (index + 1, total + send_grads(grad_low, again, its_pick, stride)[0])

    def rest(start):
        return lax.while_loop(lambda carry: carry[0] < rounds, more, (jnp.int32(1), start))[1]

    total = lax.cond(rounds > 1, rest, lambda start: start, first)
    return (total, jnp.sum(extra.astype(jnp.float32), axis=(0, 1)), beside)


def double(held, bit, axis):
    count = lax.axis_size("dev")
    low = ((lax.axis_index("dev") >> bit) & 1) == 0
    came = lax.ppermute(held, "dev", [(source, source ^ (1 << bit)) for source in range(count)])
    return jnp.stack([jnp.where(low, held, came), jnp.where(low, came, held)], axis=axis)


def spread_z(shard, first, last):
    bits = lax.axis_size("dev").bit_length() - 1
    for done in range(first, min(last, bits - 3)):
        shard = double(shard, bits - 1 - done, done)
    return shard


def spread_plane(held):
    at, half = (lax.axis_size("dev").bit_length() - 4, held.shape[-1] // 2)
    return (double(held[..., :half], 2, at), double(held[..., half:], 1, at))


def spread_rest(halves):
    at = lax.axis_size("dev").bit_length() - 4
    return (double(halves[0], 1, at + 1), double(halves[1], 2, at))


def spread_cores(halves):
    whole = jnp.concatenate(halves, axis=-1)
    return double(whole, 0, lax.axis_size("dev").bit_length() - 2)


def gather_late(stack, part, up_cols):
    width = stack.shape[1]
    down = stack.shape[0] - part * (1 + up_cols)
    whole = lax.all_gather(stack, "dev", axis=0)
    up = whole[:, down + part :].reshape(-1, up_cols, part, width).swapaxes(0, 1)
    late = whole if down % 32 == 0 else whole[:, :down].reshape(up_cols, width, width)
    return (whole[:, down : down + part].reshape(-1, width), up.reshape(up_cols, -1, width), late)


def split_rows(summed, sizes):
    pieces, start = ([], 0)
    for size in sizes:
        pieces.append(summed[start : start + size])
        start += size
    return pieces


def swap_parts(held, bit):
    count = lax.axis_size("dev")
    mine = (lax.axis_index("dev") >> bit) & 1
    keep = lax.dynamic_index_in_dim(held, mine, 0, keepdims=False)
    give = lax.dynamic_index_in_dim(held, 1 - mine, 0, keepdims=False)
    return (keep, lax.ppermute(give, "dev", [(source, source ^ (1 << bit)) for source in range(count)]))


def join_parts(parts, last=False):
    total = parts[0].astype(jnp.float32) + parts[1].astype(jnp.float32)
    return total if last else total.astype(jnp.bfloat16)


def swap_halves(held, bit, last=False):
    return join_parts(swap_parts(held, bit), last)


def middle_bits():
    return list(range(1, lax.axis_size("dev").bit_length() - 2))


def sum_cores(term):
    count, pieces, rows, width = term.shape
    grid = term.reshape(count // 2, 2, pieces, rows, width)
    return swap_halves(grid.swapaxes(0, 1), 0).reshape(count // 2, pieces * rows, width)


def cut_thirds(held):
    _, rows, width = held.shape
    middle = middle_bits()
    bits = len(middle) + 1
    grid = held.reshape((2,) * bits + (rows, width))
    thirds = []
    for turn in range(3):
        shift = turn % len(middle)
        order = middle[shift:] + middle[:shift] + [bits]
        axes = [bits - bit for bit in order]
        part = grid[..., turn * (width // 3) : (turn + 1) * (width // 3)]
        thirds.append(part.transpose(axes + [bits, bits + 1]))
    return thirds


def sum_stage(thirds, stage):
    middle = middle_bits()
    return [swap_halves(third, middle[(turn + stage) % len(middle)]) for turn, third in enumerate(thirds)]


def sum_stages(thirds, first):
    for stage in range(first, len(middle_bits())):
        thirds = sum_stage(thirds, stage)
    return thirds


def sum_last(groups):
    whole = [jnp.concatenate(thirds, axis=-1) for thirds in groups]
    return swap_halves(jnp.concatenate(whole, axis=1), len(middle_bits()) + 1, True)


def split_low(values):
    high = lax.reduce_precision(values, 8, 7)
    return (high.astype(jnp.bfloat16), (values - high).astype(jnp.bfloat16))


def low_units(blocks):
    per_row = blocks.shape[1]
    place = 8 + jnp.arange(per_row, dtype=jnp.int32)[None, :]
    return jnp.min(place - 2 * ((blocks + 1) // 2), axis=1).astype(jnp.int32)


def by_unit(array):
    cut = array.reshape((array.shape[0], array.shape[1] // UNIT, UNIT) + array.shape[2:])
    return cut.swapaxes(0, 1)


def by_row(array, micros):
    cut = array.reshape(-1, micros, UNIT, array.shape[-1])
    return cut.swapaxes(0, 1).reshape(micros, -1, array.shape[-1])


def shards(
    token_ids,
    lengths,
    embedding,
    norm1_gain,
    w_query,
    w_key,
    w_value,
    w_out,
    mix_logits,
    mix_weights,
    norm2_gain,
    w_up,
    w_down,
    cotangent,
):
    count = lax.axis_size("dev")
    me = lax.axis_index("dev")
    micros, row_count = token_ids.shape
    own_rows, width = embedding.shape
    heads = mix_logits.shape[0]
    part = norm1_gain.shape[0]
    per_row = row_count // UNIT
    tokens = micros * row_count
    tok_ids = by_unit(token_ids).reshape(-1)
    stride = max(16, 1024 // count)
    room = stride - 2

    unit_rows = me * row_count + UNIT * jnp.arange(per_row, dtype=jnp.int32)
    begins = jnp.stack([seq_starts(lengths[micro], unit_rows) for micro in range(micros)])
    blocks = ((unit_rows[None, :] - begins) // UNIT + 1).reshape(-1).astype(jnp.int32)

    lows = low_units(blocks.reshape(micros, per_row))
    mixes = spread_mixes(mix_logits, mix_weights)

    up_cols = w_up.shape[1] // width
    up_pieces = [w_up[:, col * width : (col + 1) * width] for col in range(up_cols)]
    first_weights = spread_z(jnp.stack([w_query, w_key, w_value]), 0, 1)
    late_stack = jnp.concatenate([w_down, w_out] + up_pieces, axis=0)
    ids = split_ids(tok_ids, own_rows)
    message, chosen = ask_round(ids, 0, own_rows, stride, room)
    message, first_weights = lax.optimization_barrier((message, first_weights))
    first_weights = spread_plane(spread_z(first_weights, 1, 99))
    gains_row = jnp.concatenate([norm1_gain, norm2_gain, jnp.zeros((width - 2 * part,), jnp.bfloat16)])
    picked, gains, (first_weights, late_stack), *plan = lookup(
        embedding, ids, message, chosen, gains_row, stride, room, (first_weights, late_stack)
    )
    w_o, w_u, w_d = gather_late(late_stack, part, up_cols)
    gain_one = gains[:, :part].reshape(-1)
    gain_two = gains[:, part : 2 * part].reshape(-1)
    inputs = picked.astype(jnp.float32)

    normed_one, inv_one, hidden_one = normalize(inputs, gain_one)
    own_hidden = hidden_one.reshape(per_row, micros, UNIT, width)
    pieces = earlier_rows(own_hidden)
    first_weights = spread_cores(spread_rest(first_weights)).reshape(count, 3, part, width)
    w_q, w_k, w_v = (first_weights[:, at].reshape(-1, width) for at in range(3))
    query, key, value = project(lows, pieces, (w_q, w_k, w_v))
    attended, *kept = attention_fwd(blocks, query, key, value, mixes, heads)
    attended = attended.reshape(tokens, width)

    grad_rows = by_unit(cotangent).reshape(tokens, width)
    gain_row = gain_two.astype(jnp.float32)[None, :]
    middle, output, grad_hidden_two, grad_up, grad_down = feed_forward(
        picked, attended, w_o, gain_row, w_u, w_d, grad_rows
    )
    inv_two = lax.rsqrt(jnp.mean(middle * middle, axis=-1, keepdims=True) + norm_eps)
    normed_two = middle * inv_two
    grad_mid_norm, grad_gain_two = norm_back(grad_hidden_two, normed_two, inv_two, gain_two)
    grad_middle = grad_rows.astype(jnp.float32) + grad_mid_norm
    grad_branch = grad_middle.astype(jnp.bfloat16)
    grad_att = matmul_right_t(grad_branch, w_o).astype(jnp.bfloat16).reshape(own_hidden.shape)
    up_rows = grad_up.reshape(up_cols, count, part, width).swapaxes(0, 1).reshape(count, -1, width)
    stack = jnp.concatenate([grad_down.reshape(count, -1, width), up_rows], axis=1).reshape(-1, width)
    stack, grad_att = lax.optimization_barrier((stack, grad_att))
    late_sums = lax.psum_scatter(stack, "dev", scatter_dimension=0, tiled=True).astype(jnp.float32)

    def tail(pieces, query, key, value, grad_att, kept, attended, grad_branch):
        grad_query, grad_key, grad_value, wide_logit, wide_prob = attention_bwd(
            blocks, query, key, value, grad_att, kept, mixes, heads
        )
        *terms, grad_own = project_back(lows, grad_query, grad_key, grad_value, (w_q, w_k, w_v))
        came = with_sibling(jnp.concatenate([terms[3], terms[1]], axis=0))
        grads, wides = ((grad_query, grad_key, grad_value), (wide_logit, wide_prob))
        came, grads, wides, hidden, attended = lax.optimization_barrier((came, grads, wides, pieces, attended))
        backs = return_rows(terms[0], terms[2], came)
        early_terms = weigh(lows, *grads, attended, grad_branch, hidden)
        mix_terms = jnp.concatenate([fold_mix(wide, heads).reshape(-1) for wide in wides])
        backs, early_terms, mix_terms = lax.optimization_barrier((backs, early_terms, mix_terms))
        early = cut_thirds(sum_cores(early_terms.reshape(4, count, part, width).swapaxes(0, 1)))
        grad_own = grad_own + backs[0] + backs[1].astype(jnp.float32) + backs[2].astype(jnp.float32)
        grad_hidden_one = grad_own.reshape(tokens, width)
        grad_in_norm, grad_gain_one = norm_back(grad_hidden_one, normed_one, inv_one, gain_one)
        grad_inputs = grad_middle + grad_in_norm

        mix_size = mix_terms.shape[0]
        small = jnp.concatenate(
            [
                grad_gain_one.reshape(count, part),
                grad_gain_two.reshape(count, part),
                jnp.broadcast_to(mix_terms[None, :], (count, mix_size)),
                jnp.zeros((count, width - 2 * part - mix_size), jnp.float32),
            ],
            axis=1,
        )
        table_grad, small_sum, early = table_back(grad_inputs, split_low(small), plan, own_rows, stride, room, early)
        return (by_row(grad_inputs, micros), table_grad, small_sum, sum_last([sum_stages(early, 0)]))

    def no_tail(*operands):
        sizes = ((micros, row_count, width), (own_rows, width), (width,), (4 * part, width))
        return tuple(jnp.zeros(size, jnp.float32) for size in sizes)

    grad_inputs, table_grad, small_sum, early_sums = lax.cond(
        plan[-1] > 0, tail, no_tail, pieces, query, key, value, grad_att, kept, attended, grad_branch
    )
    early_sums = split_rows(early_sums, [part] * 4)
    late_sums = split_rows(late_sums, [w_down.shape[0]] + [part] * up_cols)
    mix_size = 2 * heads * heads
    mixes = small_sum[2 * part : 2 * part + mix_size].reshape(2, heads, heads)
    return (
        by_row(output, micros),
        grad_inputs,
        table_grad,
        small_sum[:part],
        *early_sums,
        mixes[0],
        mixes[1],
        small_sum[part : 2 * part],
        jnp.concatenate(late_sums[1:], axis=1),
        late_sums[0],
    )


def solution(mesh):
    in_specs = (
        P(None, "dev"),
        P(),
        P("dev", None),
        P("dev"),
        P("dev", None),
        P("dev", None),
        P("dev", None),
        P("dev", None),
        P(),
        P(),
        P("dev"),
        P("dev", None),
        P("dev", None),
        P(None, "dev", None),
    )
    out_specs = (
        P(None, "dev", None),
        P(None, "dev", None),
        P("dev", None),
        P("dev"),
        P("dev", None),
        P("dev", None),
        P("dev", None),
        P("dev", None),
        P(),
        P(),
        P("dev"),
        P("dev", None),
        P("dev", None),
    )
    return jax.shard_map(shards, mesh=mesh, in_specs=in_specs, out_specs=out_specs, check_vma=False)
```

```python
from functools import partial

import jax
import jax.numpy as jnp
from jax import lax
from jax.experimental import pallas as pl
from jax.experimental.pallas import tpu as pltpu
from jax.sharding import PartitionSpec as P

norm_eps = 1e-06
gelu_scale = 0.7978845608028654
gelu_cube = 0.044715
FF_STEP = 256

masked = -1e30
UNIT = 128
CHUNK = 256
GROUP = 16
MAX_CHUNKS = 4
TOGETHER = 4


def dot_nn(left, right):
    return lax.dot_general(left, right, (((1,), (0,)), ((), ())), preferred_element_type=jnp.float32)


def dot_nt(left, right):
    return lax.dot_general(left, right, (((1,), (1,)), ((), ())), preferred_element_type=jnp.float32)


def spread_heads(rows, lane_head, quad, heads_per_quad):
    part = rows[:, quad * CHUNK : (quad + 1) * CHUNK]
    zero = jnp.zeros_like(part)
    return jnp.concatenate([jnp.where(lane_head == head, part, zero) for head in range(heads_per_quad)], axis=0)


def own_lanes(wide, lane_head, heads_per_quad):
    total = jnp.where(lane_head == 0, wide[:UNIT], 0.0)
    for head in range(1, heads_per_quad):
        total = total + jnp.where(lane_head == head, wide[head * UNIT : (head + 1) * UNIT], 0.0)
    return total


def part_of(sums, group):
    start = group % TOGETHER * CHUNK
    return sums[:, start : start + CHUNK]


def allowed_keys(chunk, group, blocks):
    key = lax.broadcasted_iota(jnp.int32, (GROUP, CHUNK), 1) - (UNIT + CHUNK * chunk)
    row = lax.broadcasted_iota(jnp.int32, (GROUP, CHUNK), 0) + GROUP * group
    return (key <= row) & (key >= (1 - blocks) * UNIT)


def twice(rows):
    return jnp.concatenate([rows, rows], axis=-1)


def put_groups(ref, quad, per_quad, term):
    low = term.astype(jnp.bfloat16)
    for head in range(per_quad):
        rows = slice((quad * per_quad + head) * GROUP, (quad * per_quad + head + 1) * GROUP)
        for group in range(UNIT // GROUP):
            start = head * UNIT + group * GROUP
            ref[rows, group * CHUNK : (group + 1) * CHUNK] = low[start : start + GROUP]


def fwd_kernel(heads, blocks_ref, q_ref, k_ref, v_ref, mix_ref, att_ref, score_out, prob_out, mixed_out,
               qx, score, prob, mixed, logit, top, norm, total, sems):
    micro, inner, per_row = (pl.program_id(0), pl.program_id(1), pl.num_programs(1))
    blocks = blocks_ref[micro * per_row + inner]
    chunks = (blocks + 1) // 2
    last_unit = k_ref.shape[0] - per_row + inner + 1
    quads = q_ref.shape[3] // CHUNK
    per_quad = heads // quads
    groups = UNIT // GROUP
    wide = heads * GROUP
    lane_head = lax.broadcasted_iota(jnp.int32, (UNIT, CHUNK), 1) // (CHUNK // per_quad)
    for quad in range(quads):
        qx[quad] = spread_heads(q_ref[0, 0], lane_head, quad, per_quad)
    total[...] = jnp.zeros_like(total)
    top[...] = jnp.full_like(top, masked)
    norm[...] = jnp.zeros_like(norm)

    def keys(ref, chunk, quad):
        units = pl.ds(last_unit - 2 * (chunk + 1), 2)
        return ref[units, 0, :, quad * CHUNK : (quad + 1) * CHUNK].reshape(CHUNK, CHUNK)

    step = micro * per_row + inner

    def keep(at, chunk, kind):
        source, target = ((score, score_out), (prob, prob_out), (mixed, mixed_out))[kind]
        place = target.at[at % per_row, at // per_row, chunk]
        return pltpu.make_async_copy(source.at[chunk], place, sems.at[kind, chunk])

    def finish(at):
        @pl.loop(0, (blocks_ref[at] + 1) // 2)
        def _(chunk):
            for kind in range(3):
                keep(at, chunk, kind).wait()

    @pl.when(step > 0)
    def _():
        finish(step - 1)

    @pl.loop(0, chunks)
    def _(chunk):
        for quad in range(quads):
            put_groups(score.at[chunk], quad, per_quad, dot_nt(qx[quad], keys(k_ref, chunk, quad)))
        keep(step, chunk, 0).start()
        for group in range(groups):
            if group % TOGETHER == 0:
                mixes = dot_nn(mix_ref[0], score[chunk, :, group * CHUNK : (group + TOGETHER) * CHUNK])
            l = part_of(mixes, group)
            l = jnp.where(allowed_keys(chunk, group, blocks)[None], l.reshape(heads, GROUP, CHUNK), masked)
            l = l.reshape(wide, CHUNK)
            logit[chunk, group] = l
            old = top[group]
            new = jnp.maximum(old, jnp.maximum(l[:, :UNIT], l[:, UNIT:]))
            terms = jnp.exp(l[:, :UNIT] - new) + jnp.exp(l[:, UNIT:] - new)
            norm[group] = norm[group] * jnp.exp(old - new) + terms
            top[group] = new

    for group in range(groups):
        lanes = top[group]
        high = jnp.broadcast_to(jnp.max(lanes, axis=-1, keepdims=True), lanes.shape)
        whole = jnp.sum(norm[group] * jnp.exp(lanes - high), axis=-1, keepdims=True)
        top[group] = high + jnp.log(jnp.broadcast_to(whole, lanes.shape))

    @pl.loop(0, chunks)
    def _(chunk):
        for group in range(groups):
            p = jnp.exp(logit[chunk, group] - twice(top[group])).astype(jnp.bfloat16)
            prob[chunk, :, group * CHUNK : (group + 1) * CHUNK] = p
        for first in range(0, groups, TOGETHER):
            sums = dot_nn(mix_ref[2], prob[chunk, :, first * CHUNK : (first + TOGETHER) * CHUNK])
            for group in range(first, first + TOGETHER):
                a = part_of(sums, group).astype(jnp.bfloat16)
                mixed[chunk, :, GROUP * group : GROUP * (group + 1), :] = a.reshape(heads, GROUP, CHUNK)
        keep(step, chunk, 1).start()
        keep(step, chunk, 2).start()
        for quad in range(quads):
            a = mixed[chunk, quad * per_quad : (quad + 1) * per_quad].reshape(per_quad * UNIT, CHUNK)
            o = own_lanes(dot_nn(a, keys(v_ref, chunk, quad)), lane_head, per_quad)
            total[:, quad * CHUNK : (quad + 1) * CHUNK] += o

    att_ref[0, 0] = total[...].astype(jnp.bfloat16)

    @pl.when(step == pl.num_programs(0) * per_row - 1)
    def _():
        finish(step)


def attention_specs(q, k, heads):
    per_row, micros, _, width = q.shape
    wide = heads * GROUP
    return (
        pl.BlockSpec((1, 1, UNIT, width), lambda m, u, _: (u, m, 0, 0)),
        pl.BlockSpec((k.shape[0], 1, UNIT, width), lambda m, u, _: (0, m, 0, 0)),
        pl.BlockSpec((4, wide, wide), lambda m, u, _: (0, 0, 0)),
    )


def kept_shapes(heads):
    wide = heads * GROUP
    flat = (MAX_CHUNKS, wide, UNIT // GROUP * CHUNK)
    return (flat, flat, (MAX_CHUNKS, heads, UNIT, CHUNK))


def attention_fwd(blocks, q, k, v, mixes, heads):
    per_row, micros, _, width = q.shape
    wide = heads * GROUP
    groups = UNIT // GROUP
    quads = width // CHUNK
    unit_spec, kv_spec, mix_spec = attention_specs(q, k, heads)
    kept = kept_shapes(heads)
    anywhere = pl.BlockSpec(memory_space=pl.ANY)
    return pl.pallas_call(
        partial(fwd_kernel, heads),
        grid_spec=pltpu.PrefetchScalarGridSpec(
            num_scalar_prefetch=1,
            grid=(micros, per_row),
            in_specs=[unit_spec, kv_spec, kv_spec, mix_spec],
            out_specs=[unit_spec, anywhere, anywhere, anywhere],
            scratch_shapes=[pltpu.VMEM((quads, heads // quads * UNIT, CHUNK), jnp.bfloat16)]
            + [pltpu.VMEM(shape, jnp.bfloat16) for shape in kept]
            + [
                pltpu.VMEM((MAX_CHUNKS, groups, wide, CHUNK), jnp.float32),
                pltpu.VMEM((groups, wide, UNIT), jnp.float32),
                pltpu.VMEM((groups, wide, UNIT), jnp.float32),
                pltpu.VMEM((UNIT, width), jnp.float32),
                pltpu.SemaphoreType.DMA((3, MAX_CHUNKS)),
            ],
        ),
        out_shape=[jax.ShapeDtypeStruct(q.shape, jnp.bfloat16)]
        + [jax.ShapeDtypeStruct((per_row, micros) + shape, jnp.bfloat16) for shape in kept],
        compiler_params=pltpu.CompilerParams(vmem_limit_bytes=50 * 1024 * 1024),
        cost_estimate=pl.CostEstimate(flops=20_000_000_000, bytes_accessed=30_000_000, transcendentals=0),
        name="attention_fwd",
    )(blocks, q, k, v, mixes)


def bwd_kernel(heads, blocks_ref, q_ref, k_ref, v_ref, do_ref, mix_ref, score_in, prob_in, mixed_in,
               dq_ref, dk_ref, dv_ref, gl_ref, gp_ref,
               qxt, dox, doxt, score, prob, mixed, grad_prob, grad_mixed, grad_logit, grad_score,
               delta, dq_total, dk_total, dv_total, sems):
    micro, inner, per_row = (pl.program_id(0), pl.program_id(1), pl.num_programs(1))
    step = micro * per_row + inner
    slot = step % 2
    blocks = blocks_ref[step]
    chunks = (blocks + 1) // 2
    key_units = k_ref.shape[0]
    last_unit = key_units - per_row + inner + 1
    quads = q_ref.shape[3] // CHUNK
    per_quad = heads // quads
    groups = UNIT // GROUP
    wide = heads * GROUP
    lane_head = lax.broadcasted_iota(jnp.int32, (UNIT, CHUNK), 1) // (CHUNK // per_quad)
    row_head = lax.broadcasted_iota(jnp.int32, (CHUNK, UNIT), 0) // (CHUNK // per_quad)
    lowest = key_units
    for other in range(key_units - 7):
        its_chunks = (blocks_ref[micro * per_row + other] + 1) // 2
        lowest = jnp.minimum(lowest, key_units - per_row + other + 1 - 2 * its_chunks)

    def fetch(at, chunk, kind):
        source, target = ((score_in, score), (prob_in, prob), (mixed_in, mixed))[kind]
        place = source.at[at % per_row, at // per_row, chunk]
        return pltpu.make_async_copy(place, target.at[at % 2, chunk], sems.at[kind, at % 2, chunk])

    def fetch_all(at):
        @pl.loop(0, (blocks_ref[at] + 1) // 2)
        def _(chunk):
            for kind in (1, 2, 0):
                fetch(at, chunk, kind).start()

    @pl.when(step == 0)
    def _():
        fetch_all(0)
        gl_ref[...] = jnp.zeros_like(gl_ref)
        gp_ref[...] = jnp.zeros_like(gp_ref)

    @pl.when(step + 1 < pl.num_programs(0) * per_row)
    def _():
        fetch_all(step + 1)

    @pl.when(inner == 0)
    def _():
        @pl.loop(lowest, key_units)
        def _(key_unit):
            dk_total[key_unit] = jnp.zeros_like(dk_total[key_unit])
            dv_total[key_unit] = jnp.zeros_like(dv_total[key_unit])

    def spread_turned(rows, quad):
        turned = rows[:, quad * CHUNK : (quad + 1) * CHUNK].T
        zero = jnp.zeros_like(turned)
        return jnp.concatenate([jnp.where(row_head == head, turned, zero) for head in range(per_quad)], axis=1)

    for quad in range(quads):
        qxt[quad] = spread_turned(q_ref[0, 0], quad)
        dox[quad] = spread_heads(do_ref[0, 0], lane_head, quad, per_quad)
        doxt[quad] = spread_turned(do_ref[0, 0], quad)
    dq_total[...] = jnp.zeros_like(dq_total)
    delta[...] = jnp.zeros_like(delta)

    def keys(ref, chunk, quad):
        units = pl.ds(last_unit - 2 * (chunk + 1), 2)
        return ref[units, 0, :, quad * CHUNK : (quad + 1) * CHUNK].reshape(CHUNK, CHUNK)

    def add_to(total, chunk, quad, term):
        first = last_unit - 2 * (chunk + 1)
        lanes = slice(quad * CHUNK, (quad + 1) * CHUNK)
        total[first, lanes, :] += term[:, :UNIT]
        total[first + 1, lanes, :] += term[:, UNIT:]

    @pl.loop(0, chunks)
    def _(chunk):
        for quad in range(quads):
            put_groups(grad_mixed, quad, per_quad, dot_nt(dox[quad], keys(v_ref, chunk, quad)))
        fetch(step, chunk, 1).wait()
        for group in range(groups):
            cols = slice(group * CHUNK, (group + 1) * CHUNK)
            if group % TOGETHER == 0:
                sums = dot_nn(mix_ref[3], grad_mixed[:, group * CHUNK : (group + TOGETHER) * CHUNK])
            dp = part_of(sums, group)
            grad_prob[chunk, :, cols] = dp.astype(grad_prob.dtype)
            term = prob[slot, chunk, :, cols].astype(jnp.float32) * dp
            delta[group] += term[:, :UNIT] + term[:, UNIT:]
        gp_ref[...] += dot_nt(prob[slot, chunk], grad_mixed[...])
        fetch(step, chunk, 2).wait()
        for quad in range(quads):
            a = mixed[slot, chunk, quad * per_quad : (quad + 1) * per_quad].reshape(per_quad * UNIT, CHUNK)
            add_to(dv_total, chunk, quad, dot_nn(doxt[quad], a))

    for group in range(groups):
        delta[group] = jnp.broadcast_to(jnp.sum(delta[group], axis=-1, keepdims=True), (wide, UNIT))

    @pl.loop(0, chunks)
    def _(chunk):
        for group in range(groups):
            cols = slice(group * CHUNK, (group + 1) * CHUNK)
            dp = grad_prob[chunk, :, cols].astype(jnp.float32) - twice(delta[group])
            dl = (prob[slot, chunk, :, cols].astype(jnp.float32) * dp).astype(jnp.bfloat16)
            grad_logit[:, cols] = dl
        for first in range(0, groups, TOGETHER):
            sums = dot_nn(mix_ref[1], grad_logit[:, first * CHUNK : (first + TOGETHER) * CHUNK])
            for group in range(first, first + TOGETHER):
                ds = part_of(sums, group).astype(jnp.bfloat16)
                grad_score[:, GROUP * group : GROUP * (group + 1), :] = ds.reshape(heads, GROUP, CHUNK)
        fetch(step, chunk, 0).wait()
        gl_ref[...] += dot_nt(score[slot, chunk], grad_logit[...])
        for quad in range(quads):
            ds = grad_score[quad * per_quad : (quad + 1) * per_quad].reshape(per_quad * UNIT, CHUNK)
            dq = own_lanes(dot_nn(ds, keys(k_ref, chunk, quad)), lane_head, per_quad)
            dq_total[:, quad * CHUNK : (quad + 1) * CHUNK] += dq
            add_to(dk_total, chunk, quad, dot_nn(qxt[quad], ds))

    dq_ref[0, 0] = (dq_total[...] * 0.125).astype(jnp.bfloat16)

    @pl.when(inner == per_row - 1)
    def _():
        @pl.loop(0, lowest)
        def _(key_unit):
            dk_ref[key_unit, 0] = jnp.zeros_like(dk_ref[key_unit, 0])
            dv_ref[key_unit, 0] = jnp.zeros_like(dv_ref[key_unit, 0])

        @pl.loop(lowest, key_units)
        def _(key_unit):
            dk_ref[key_unit, 0] = dk_total[key_unit].astype(jnp.bfloat16).T
            dv_ref[key_unit, 0] = dv_total[key_unit].astype(jnp.bfloat16).T


def attention_bwd(blocks, q, k, v, grad_out, kept, mixes, heads):
    per_row, micros, _, width = q.shape
    key_units = k.shape[0]
    wide = heads * GROUP
    groups = UNIT // GROUP
    quads = width // CHUNK
    turned = (quads, CHUNK, heads // quads * UNIT)
    unit_spec, kv_spec, mix_spec = attention_specs(q, k, heads)
    sum_spec = pl.BlockSpec((wide, wide), lambda m, u, _: (0, 0))
    anywhere = pl.BlockSpec(memory_space=pl.ANY)
    return pl.pallas_call(
        partial(bwd_kernel, heads),
        grid_spec=pltpu.PrefetchScalarGridSpec(
            num_scalar_prefetch=1,
            grid=(micros, per_row),
            in_specs=[unit_spec, kv_spec, kv_spec, unit_spec, mix_spec] + [anywhere] * 3,
            out_specs=[unit_spec, kv_spec, kv_spec, sum_spec, sum_spec],
            scratch_shapes=[
                pltpu.VMEM(turned, jnp.bfloat16),
                pltpu.VMEM((quads, heads // quads * UNIT, CHUNK), jnp.bfloat16),
                pltpu.VMEM(turned, jnp.bfloat16),
            ]
            + [pltpu.VMEM((2,) + shape, jnp.bfloat16) for shape in kept_shapes(heads)]
            + [
                pltpu.VMEM((MAX_CHUNKS, wide, groups * CHUNK), jnp.bfloat16),
                pltpu.VMEM((wide, groups * CHUNK), jnp.bfloat16),
                pltpu.VMEM((wide, groups * CHUNK), jnp.bfloat16),
                pltpu.VMEM((heads, UNIT, CHUNK), jnp.bfloat16),
                pltpu.VMEM((groups, wide, UNIT), jnp.float32),
                pltpu.VMEM((UNIT, width), jnp.float32),
                pltpu.VMEM((key_units, width, UNIT), jnp.float32),
                pltpu.VMEM((key_units, width, UNIT), jnp.float32),
                pltpu.SemaphoreType.DMA((3, 2, MAX_CHUNKS)),
            ],
        ),
        out_shape=[
            jax.ShapeDtypeStruct(q.shape, jnp.bfloat16),
            jax.ShapeDtypeStruct(k.shape, jnp.bfloat16),
            jax.ShapeDtypeStruct(v.shape, jnp.bfloat16),
            jax.ShapeDtypeStruct((wide, wide), jnp.float32),
            jax.ShapeDtypeStruct((wide, wide), jnp.float32),
        ],
        compiler_params=pltpu.CompilerParams(vmem_limit_bytes=58 * 1024 * 1024),
        cost_estimate=pl.CostEstimate(flops=45_000_000_000, bytes_accessed=40_000_000, transcendentals=0),
        name="attention_bwd",
    )(blocks, q, k, v, grad_out, mixes, *kept)


def piece_bases(key_units, per_row):
    sizes = [1] + [per_row] * ((key_units - 1) // per_row)
    return [(sum(sizes[:at]), size) for at, size in enumerate(sizes)]


def project_kernel(low_ref, *refs):
    pieces, (w_q, w_k, w_v, q_ref, k_ref, v_ref) = (refs[:-6], refs[-6:])
    key_units, width = (k_ref.shape[0], k_ref.shape[3])
    per_row = q_ref.shape[0]
    low = low_ref[pl.program_id(0)]

    for piece, (base, size) in zip(pieces, piece_bases(key_units, per_row)):
        @pl.when(base + size > low)
        def _():
            rows = piece[:, 0].reshape(size * UNIT, width)
            k_ref[base : base + size, 0] = dot_nn(rows, w_k[...]).astype(jnp.bfloat16).reshape(size, UNIT, width)
            v_ref[base : base + size, 0] = dot_nn(rows, w_v[...]).astype(jnp.bfloat16).reshape(size, UNIT, width)

    rows = pieces[-1][:, 0].reshape(per_row * UNIT, width)
    query = dot_nn(rows, w_q[...]).astype(jnp.bfloat16) * jnp.bfloat16(0.125)
    q_ref[:, 0] = query.reshape(per_row, UNIT, width)


def project(low, pieces, weights):
    micros, width = pieces[0].shape[1], pieces[0].shape[3]
    key_units = sum(piece.shape[0] for piece in pieces)
    per_row = pieces[-1].shape[0]

    def spec(units):
        return pl.BlockSpec((units, 1, UNIT, width), lambda m, _: (0, m, 0, 0))

    weight_spec = pl.BlockSpec((width, width), lambda m, _: (0, 0))
    shapes = [(units, micros, UNIT, width) for units in (per_row, key_units, key_units)]
    return pl.pallas_call(
        project_kernel,
        grid_spec=pltpu.PrefetchScalarGridSpec(
            num_scalar_prefetch=1,
            grid=(micros,),
            in_specs=[spec(piece.shape[0]) for piece in pieces] + [weight_spec] * 3,
            out_specs=[spec(shape[0]) for shape in shapes],
        ),
        out_shape=[jax.ShapeDtypeStruct(shape, jnp.bfloat16) for shape in shapes],
        compiler_params=pltpu.CompilerParams(vmem_limit_bytes=44 * 1024 * 1024),
        cost_estimate=pl.CostEstimate(flops=6_000_000_000, bytes_accessed=15_000_000, transcendentals=0),
        name="project",
    )(low, *pieces, *weights)


def project_back_kernel(low_ref, dq_ref, dk_ref, dv_ref, w_q, w_k, w_v, *outs):
    key_units, width = (dk_ref.shape[0], dk_ref.shape[3])
    per_row = dq_ref.shape[0]
    low = low_ref[pl.program_id(0)]
    bases = piece_bases(key_units, per_row)

    def from_keys(base, size):
        rows = slice(base, base + size)
        key_term = dot_nt(dk_ref[rows, 0].reshape(size * UNIT, width), w_k[...])
        return key_term + dot_nt(dv_ref[rows, 0].reshape(size * UNIT, width), w_v[...])

    for out, (base, size) in zip(outs[:-1], bases[:-1]):
        @pl.when(base + size > low)
        def _():
            out[:, 0] = from_keys(base, size).astype(jnp.bfloat16).reshape(size, UNIT, width)

        @pl.when(base + size <= low)
        def _():
            out[...] = jnp.zeros_like(out)

    own = from_keys(*bases[-1]) + dot_nt(dq_ref[:, 0].reshape(per_row * UNIT, width), w_q[...])
    outs[-1][:, 0] = own.reshape(per_row, UNIT, width)


def project_back(low, grad_query, grad_key, grad_value, weights):
    per_row, micros, _, width = grad_query.shape
    key_units = grad_key.shape[0]

    def spec(units):
        return pl.BlockSpec((units, 1, UNIT, width), lambda m, _: (0, m, 0, 0))

    weight_spec = pl.BlockSpec((width, width), lambda m, _: (0, 0))
    sizes = [size for _, size in piece_bases(key_units, per_row)]
    shapes = [(size, micros, UNIT, width) for size in sizes]
    kinds = [jnp.bfloat16] * (len(sizes) - 1) + [jnp.float32]
    return pl.pallas_call(
        project_back_kernel,
        grid_spec=pltpu.PrefetchScalarGridSpec(
            num_scalar_prefetch=1,
            grid=(micros,),
            in_specs=[spec(per_row), spec(key_units), spec(key_units)] + [weight_spec] * 3,
            out_specs=[spec(size) for size in sizes],
        ),
        out_shape=[jax.ShapeDtypeStruct(shape, kind) for shape, kind in zip(shapes, kinds)],
        compiler_params=pltpu.CompilerParams(vmem_limit_bytes=44 * 1024 * 1024),
        cost_estimate=pl.CostEstimate(flops=6_000_000_000, bytes_accessed=15_000_000, transcendentals=0),
        name="project_back",
    )(low, grad_query, grad_key, grad_value, *weights)


def weigh_kernel(low_ref, dq_ref, dk_ref, dv_ref, att_ref, branch_ref, *refs):
    pieces, (grad_ref, total) = (refs[:-2], refs[-2:])
    key_units, width = (dk_ref.shape[0], dk_ref.shape[3])
    per_row = dq_ref.shape[0]
    micro = pl.program_id(0)
    low = low_ref[micro]
    bases = piece_bases(key_units, per_row)

    @pl.when(micro == 0)
    def _():
        total[0:3] = jnp.zeros_like(total[0:3])
        total[3] = dot_nn(att_ref[...].T, branch_ref[...])

    def keys(ref, base, size):
        return ref[base : base + size, 0].reshape(size * UNIT, width)

    for piece, (base, size) in zip(pieces, bases):
        @pl.when(base + size > low)
        def _():
            turned = piece[:, 0].reshape(size * UNIT, width).T
            total[1] += dot_nn(turned, keys(dk_ref, base, size))
            total[2] += dot_nn(turned, keys(dv_ref, base, size))
            if base + size == key_units:
                total[0] += dot_nn(turned, keys(dq_ref, 0, per_row))

    @pl.when(micro == pl.num_programs(0) - 1)
    def _():
        grad_ref[...] = total[...].astype(jnp.bfloat16)


def weigh(low, grad_query, grad_key, grad_value, attended, branch, pieces):
    per_row, micros, _, width = grad_query.shape
    key_units = grad_key.shape[0]

    def spec(units):
        return pl.BlockSpec((units, 1, UNIT, width), lambda m, _: (0, m, 0, 0))

    sizes = [size for _, size in piece_bases(key_units, per_row)]
    return pl.pallas_call(
        weigh_kernel,
        grid_spec=pltpu.PrefetchScalarGridSpec(
            num_scalar_prefetch=1,
            grid=(micros,),
            in_specs=[spec(size) for size in (per_row, key_units, key_units)]
            + [pl.BlockSpec(attended.shape, lambda m, _: (0, 0))] * 2
            + [spec(size) for size in sizes],
            out_specs=pl.BlockSpec((4, width, width), lambda m, _: (0, 0, 0)),
            scratch_shapes=[pltpu.VMEM((4, width, width), jnp.float32)],
        ),
        out_shape=jax.ShapeDtypeStruct((4, width, width), jnp.bfloat16),
        compiler_params=pltpu.CompilerParams(vmem_limit_bytes=48 * 1024 * 1024),
        cost_estimate=pl.CostEstimate(flops=12_000_000_000, bytes_accessed=14_000_000, transcendentals=0),
        name="weigh",
    )(low, grad_query, grad_key, grad_value, attended, branch, *pieces)


def feed_kernel(x_ref, att_ref, w_o_ref, gain_ref, up_ref, down_ref, cot_ref,
                out_ref, grad_mid_ref, branch_ref, grad_att_ref, grad_gain_ref, grad_up_ref, grad_down_ref,
                middle_ref, hidden, turned, out_total, back_total):
    step = pl.program_id(0)

    @pl.when(step == 0)
    def _():
        middle = x_ref[...].astype(jnp.float32) + dot_nn(att_ref[...], w_o_ref[...])
        middle_ref[...] = middle
        inv_rms = lax.rsqrt(jnp.mean(middle * middle, axis=-1, keepdims=True) + norm_eps)
        rows = (middle * inv_rms * gain_ref[...]).astype(jnp.bfloat16)
        hidden[...] = rows
        turned[...] = rows.T
        out_total[...] = jnp.zeros_like(out_total)
        back_total[...] = jnp.zeros_like(back_total)

    down_rows = down_ref[...].reshape(up_ref.shape[1:])
    for start in range(0, up_ref.shape[2], FF_STEP):
        cols = slice(start, start + FF_STEP)
        down = down_rows[cols]
        up = dot_nn(hidden[...], up_ref[0, :, cols])
        square = up * up
        bent = jnp.tanh(gelu_scale * up * (1.0 + gelu_cube * square))
        half = 0.5 + 0.5 * bent
        slope = half + 0.5 * up * (1.0 - bent * bent) * (gelu_scale * (1.0 + 3.0 * gelu_cube * square))
        active = (up * half).astype(jnp.bfloat16)
        grad_up = (dot_nt(cot_ref[...], down) * slope).astype(jnp.bfloat16)
        out_total[...] += dot_nn(active, down)
        back_total[...] += dot_nt(grad_up, up_ref[0, :, cols])
        grad_down_ref[cols, :] = dot_nn(active.T, cot_ref[...]).astype(jnp.bfloat16)
        grad_up_ref[0, :, cols] = dot_nn(turned[...], grad_up).astype(jnp.bfloat16)

    @pl.when(step == pl.num_programs(0) - 1)
    def _():
        middle = middle_ref[...]
        out_ref[...] = (middle + out_total[...]).astype(jnp.bfloat16)
        inv_rms = lax.rsqrt(jnp.mean(middle * middle, axis=-1, keepdims=True) + norm_eps)
        normed = middle * inv_rms
        grad_hidden = back_total[...]
        grad_gain_ref[...] = jnp.sum(grad_hidden * normed, axis=0, keepdims=True)
        grad_normed = grad_hidden * gain_ref[...]
        inner_mean = jnp.mean(grad_normed * normed, axis=-1, keepdims=True)
        grad_mid = cot_ref[...].astype(jnp.float32) + inv_rms * (grad_normed - normed * inner_mean)
        grad_mid_ref[...] = grad_mid
        branch = grad_mid.astype(jnp.bfloat16)
        branch_ref[...] = branch
        grad_att_ref[...] = dot_nt(branch, w_o_ref[...]).astype(jnp.bfloat16)


def feed_forward(rows, attended, w_o, gain, w_up, w_late, cot):
    tokens, width = rows.shape
    pieces = w_up.shape[0]
    whole = pl.BlockSpec((tokens, width), lambda i: (0, 0))
    up_spec = pl.BlockSpec((1, width, width), lambda i: (i, 0, 0))
    down_spec = pl.BlockSpec((width, width), lambda i: (i, 0))
    devices = w_late.shape[0] // pieces
    late_spec = pl.BlockSpec((devices, width // devices, width), lambda i: (i, 0, 0))
    f32, bf16 = (jnp.float32, jnp.bfloat16)
    return pl.pallas_call(
        feed_kernel,
        grid=(pieces,),
        in_specs=[
            whole,
            whole,
            pl.BlockSpec((width, width), lambda i: (0, 0)),
            pl.BlockSpec((1, width), lambda i: (0, 0)),
            up_spec,
            late_spec,
            whole,
        ],
        out_specs=[whole, whole, whole, whole, pl.BlockSpec((1, width), lambda i: (0, 0)), up_spec, down_spec],
        out_shape=[
            jax.ShapeDtypeStruct((tokens, width), bf16),
            jax.ShapeDtypeStruct((tokens, width), f32),
            jax.ShapeDtypeStruct((tokens, width), bf16),
            jax.ShapeDtypeStruct((tokens, width), bf16),
            jax.ShapeDtypeStruct((1, width), f32),
            jax.ShapeDtypeStruct(w_up.shape, bf16),
            jax.ShapeDtypeStruct((pieces * width, width), bf16),
        ],
        scratch_shapes=[
            pltpu.VMEM((tokens, width), f32),
            pltpu.VMEM((tokens, width), bf16),
            pltpu.VMEM((width, tokens), bf16),
            pltpu.VMEM((tokens, width), f32),
            pltpu.VMEM((tokens, width), f32),
        ],
        compiler_params=pltpu.CompilerParams(vmem_limit_bytes=48 * 1024 * 1024),
        cost_estimate=pl.CostEstimate(flops=16_000_000_000, bytes_accessed=30_000_000, transcendentals=0),
        name="feed_forward",
    )(rows, attended, w_o, gain, w_up, w_late, cot)


def spread_mixes(mix_logits, mix_weights):
    heads = mix_logits.shape[0]
    wide = heads * GROUP
    place = jnp.arange(wide, dtype=jnp.int32)
    pick = (place[:, None] // GROUP == jnp.arange(heads, dtype=jnp.int32)[None, :]).astype(mix_logits.dtype)
    same_row = (place[:, None] % GROUP == place[None, :] % GROUP)[None]
    tables = jnp.stack([mix_logits.T, mix_logits, mix_weights.T, mix_weights]).reshape(4 * heads, heads)
    across = jnp.dot(tables, pick.T, preferred_element_type=jnp.float32).astype(mix_logits.dtype)
    down = jnp.einsum("wh,bhx->bwx", pick, across.reshape(4, heads, wide), preferred_element_type=jnp.float32)
    return jnp.where(same_row, down, 0.0).astype(mix_logits.dtype)


def fold_mix(wide, heads):
    place = jnp.arange(heads * GROUP, dtype=jnp.int32)
    pick = (place[:, None] // GROUP == jnp.arange(heads, dtype=jnp.int32)[None, :]).astype(jnp.float32)
    same_row = place[:, None] % GROUP == place[None, :] % GROUP
    down = jnp.dot(pick.T, jnp.where(same_row, wide, 0.0), precision=lax.Precision.HIGHEST)
    return jnp.dot(down, pick, precision=lax.Precision.HIGHEST)


def from_behind(value, steps):
    count = lax.axis_size("dev")
    first, last = (max(0, -steps), min(count, count - steps))
    return lax.ppermute(value, "dev", [(source, source + steps) for source in range(first, last)])


def with_sibling(value):
    count = lax.axis_size("dev")
    return lax.ppermute(value, "dev", [(source, source ^ 1) for source in range(count)])


def earlier_rows(own):
    size = own.shape[0]
    first_core = lax.axis_index("dev") % 2 == 0
    two, four = (from_behind(own, 2), from_behind(own, 4))
    give = jnp.concatenate([jnp.where(first_core, own, two), jnp.where(first_core, two, four)], axis=0)
    came = with_sibling(give)
    return [four[size - 1 :], came[size:], two, came[:size], own]


def give_rows(four, two, came):
    size = two.shape[0]
    first_core = lax.axis_index("dev") % 2 == 0
    came = came.astype(jnp.float32)
    one, three = (came[:size], came[size:])
    give_two = two.astype(jnp.float32) + jnp.where(first_core, three, one)
    padded = jnp.pad(four.astype(jnp.float32), ((size - four.shape[0], 0), (0, 0), (0, 0), (0, 0)))
    give_four = padded + jnp.where(first_core, 0.0, three)
    return (jnp.where(first_core, one, 0.0), give_two.astype(jnp.bfloat16), give_four.astype(jnp.bfloat16))


def seq_starts(lengths_row, query_rows):
    seq_ends = jnp.cumsum(lengths_row)
    starts = seq_ends - lengths_row
    return jnp.max(jnp.where(starts[None, :] <= query_rows[:, None], starts[None, :], 0), axis=1)


def normalize(values, gain_vec):
    inv_rms = lax.rsqrt(jnp.mean(values * values, axis=-1, keepdims=True) + norm_eps)
    normed = values * inv_rms
    return (normed, inv_rms, (normed * gain_vec.astype(jnp.float32)).astype(jnp.bfloat16))


def norm_back(grad_hidden, normed, inv_rms, gain_vec):
    grad_gain = jnp.sum(grad_hidden * normed, axis=0)
    grad_normed = grad_hidden * gain_vec.astype(jnp.float32)
    inner_mean = jnp.mean(grad_normed * normed, axis=-1, keepdims=True)
    return (inv_rms * (grad_normed - normed * inner_mean), grad_gain)


def matmul(left, right):
    return jnp.dot(left, right, preferred_element_type=jnp.float32)


def matmul_left_t(left, right):
    return lax.dot_general(left, right, (((0,), (0,)), ((), ())), preferred_element_type=jnp.float32)


def matmul_right_t(left, right):
    return lax.dot_general(left, right, (((1,), (1,)), ((), ())), preferred_element_type=jnp.float32)


def exchange(value):
    return lax.all_to_all(value, "dev", split_axis=0, concat_axis=0, tiled=True)


def split_ids(tok_ids, own_rows):
    owner = tok_ids // own_rows
    place = jnp.arange(tok_ids.shape[0], dtype=jnp.int32)
    same = tok_ids[:, None] == tok_ids[None, :]
    repeated = jnp.any(same & (place[None, :] < place[:, None]), axis=1)
    before = (owner[:, None] == owner[None, :]) & (tok_ids[None, :] < tok_ids[:, None]) & ~repeated[None, :]
    return (owner, tok_ids % own_rows, jnp.sum(before, axis=1, dtype=jnp.int32))


def ask_round(ids, index, own_rows, stride, room):
    count = lax.axis_size("dev")
    owner, local, rank = ids
    here = rank - index * room
    slot = jnp.where((here >= 0) & (here < room), owner * stride + here, -1)
    chosen = slot[None, :] == jnp.arange(count * stride, dtype=jnp.int32)[:, None]
    wanted = jnp.max(jnp.where(chosen, local[None, :], -1), axis=1).reshape(count, stride)
    rounds = jnp.broadcast_to(jnp.max(rank) // room + 1, (count, stride))
    return (jnp.concatenate([wanted, rounds], axis=1), chosen.astype(jnp.bfloat16))


def hear_round(message, own_rows, stride):
    asked = exchange(message)
    pick = asked[:, :stride].reshape(-1, 1) == jnp.arange(own_rows, dtype=jnp.int32)[None, :]
    return (pick.astype(jnp.bfloat16), jnp.max(asked[:, stride:]))


def plan_round(ids, index, own_rows, stride, room):
    message, chosen = ask_round(ids, index, own_rows, stride, room)
    pick, _ = hear_round(message, own_rows, stride)
    return (chosen, pick)


def answer(embedding, chosen, pick, stride, extra_row, beside=None):
    count = lax.axis_size("dev")
    rows = matmul(pick, embedding).astype(jnp.bfloat16).reshape(count, stride, -1)
    if extra_row is not None:
        is_extra = (jnp.arange(stride, dtype=jnp.int32) == stride - 1)[None, :, None]
        rows = jnp.where(is_extra, extra_row[None, None, :], rows)
    rows, beside = lax.optimization_barrier((rows.reshape(count * stride, -1), beside))
    got = exchange(rows)
    extra = got.reshape(count, stride, -1)[:, stride - 1]
    return (matmul_left_t(chosen, got).astype(jnp.bfloat16), extra, beside)


def lookup(embedding, ids, message, chosen, extra_row, stride, room, beside):
    own_rows = embedding.shape[0]
    pick, rounds = hear_round(message, own_rows, stride)
    first, extra, beside = answer(embedding, chosen, pick, stride, extra_row, beside)

    def more(carry):
        index, rows = carry
        again, its_pick = plan_round(ids, index, own_rows, stride, room)
        return (index + 1, rows + answer(embedding, again, its_pick, stride, None)[0])

    _, rows = lax.while_loop(lambda carry: carry[0] < rounds, more, (jnp.int32(1), first))
    return (rows, extra, beside, ids, chosen, pick, rounds)


def send_grads(grad_low, chosen, pick, stride, beside=None):
    count = lax.axis_size("dev")
    summed = matmul(chosen, grad_low).astype(jnp.bfloat16)
    summed, beside = lax.optimization_barrier((summed, beside))
    got = exchange(summed)
    return (matmul_left_t(pick, got), got.reshape(count, stride, -1)[:, stride - 2 :], beside)


def table_back(grad_rows, extra_rows, plan, own_rows, stride, room, beside):
    ids, chosen, pick, rounds = plan
    count = lax.axis_size("dev")
    grad_low = grad_rows.astype(jnp.bfloat16)
    slot = jnp.arange(count * stride, dtype=jnp.int32)[:, None]
    owner = jnp.arange(count, dtype=jnp.int32)[None, :] * stride
    places = [(slot == owner + at).astype(jnp.bfloat16) for at in (stride - 2, stride - 1)]
    whole = jnp.concatenate([grad_low, *extra_rows], axis=0)
    both = jnp.concatenate([chosen, *places], axis=1)
    first, extra, beside = send_grads(whole, both, pick, stride, beside)

    def more(carry):
        index, total = carry
        again, its_pick = plan_round(ids, index, own_rows, stride, room)
        return (index + 1, total + send_grads(grad_low, again, its_pick, stride)[0])

    beside = sum_stages(beside, 0)
    first, beside = lax.optimization_barrier((first, beside))

    def rest(start):
        return lax.while_loop(lambda carry: carry[0] < rounds, more, (jnp.int32(1), start))[1]

    total = lax.cond(rounds > 1, rest, lambda start: start, first)
    return (total, jnp.sum(extra.astype(jnp.float32), axis=(0, 1)), beside)


def pair_up(held, bit):
    count = lax.axis_size("dev")
    return (held, lax.ppermute(held, "dev", [(source, source ^ (1 << bit)) for source in range(count)]))


def put_together(pair, bit, axis):
    low = ((lax.axis_index("dev") >> bit) & 1) == 0
    held, came = pair
    return jnp.stack([jnp.where(low, held, came), jnp.where(low, came, held)], axis=axis)


def double(held, bit, axis):
    return put_together(pair_up(held, bit), bit, axis)


def spread_z(shard, first, last):
    bits = lax.axis_size("dev").bit_length() - 1
    for done in range(first, min(last, bits - 3)):
        shard = double(shard, bits - 1 - done, done)
    return shard


def spread_plane(held):
    at, half = (lax.axis_size("dev").bit_length() - 4, held.shape[-1] // 2)
    return (double(held[..., :half], 2, at), double(held[..., half:], 1, at))


def spread_rest(halves):
    return (pair_up(halves[0], 1), pair_up(halves[1], 2))


def finish_rest(pairs):
    at = lax.axis_size("dev").bit_length() - 4
    return (put_together(pairs[0], 1, at + 1), put_together(pairs[1], 2, at))


def spread_cores(halves):
    whole = jnp.concatenate(halves, axis=-1)
    return double(whole, 0, lax.axis_size("dev").bit_length() - 2)


def gather_late(stack, part, up_cols):
    width = stack.shape[1]
    down = stack.shape[0] - part * up_cols
    whole = lax.all_gather(stack, "dev", axis=0)
    starts = [down + part * col for col in range(up_cols)]
    up = jnp.stack([whole[:, start : start + part].reshape(-1, width) for start in starts])
    return (up, whole if down % 32 == 0 else whole[:, :down].reshape(up_cols, width, width))


def split_rows(summed, sizes):
    pieces, start = ([], 0)
    for size in sizes:
        pieces.append(summed[start : start + size])
        start += size
    return pieces


def swap_parts(held, bit):
    count = lax.axis_size("dev")
    mine = (lax.axis_index("dev") >> bit) & 1
    keep = lax.dynamic_index_in_dim(held, mine, 0, keepdims=False)
    give = lax.dynamic_index_in_dim(held, 1 - mine, 0, keepdims=False)
    return (keep, lax.ppermute(give, "dev", [(source, source ^ (1 << bit)) for source in range(count)]))


def join_parts(parts, last=False):
    total = parts[0].astype(jnp.float32) + parts[1].astype(jnp.float32)
    return total if last else total.astype(jnp.bfloat16)


def swap_halves(held, bit, last=False):
    return join_parts(swap_parts(held, bit), last)


def middle_bits():
    return list(range(1, lax.axis_size("dev").bit_length() - 2))


def sum_cores(term):
    count, pieces, rows, width = term.shape
    grid = term.reshape(count // 2, 2, pieces, rows, width)
    return swap_halves(grid.swapaxes(0, 1), 0).reshape(count // 2, pieces * rows, width)


def cut_thirds(held):
    _, rows, width = held.shape
    middle = middle_bits()
    bits = len(middle) + 1
    grid = held.reshape((2,) * bits + (rows, width))
    thirds = []
    for turn in range(3):
        shift = turn % len(middle)
        order = middle[shift:] + middle[:shift] + [bits]
        axes = [bits - bit for bit in order]
        part = grid[..., turn * (width // 3) : (turn + 1) * (width // 3)]
        thirds.append(part.transpose(axes + [bits, bits + 1]))
    return thirds


def sum_stage(thirds, stage):
    middle = middle_bits()
    return [swap_halves(third, middle[(turn + stage) % len(middle)]) for turn, third in enumerate(thirds)]


def sum_stages(thirds, first):
    for stage in range(first, len(middle_bits())):
        thirds = sum_stage(thirds, stage)
    return thirds


def sum_last(groups):
    whole = [jnp.concatenate(thirds, axis=-1) for thirds in groups]
    return swap_halves(jnp.concatenate(whole, axis=1), len(middle_bits()) + 1, True)


def split_low(values):
    high = lax.reduce_precision(values, 8, 7)
    return (high.astype(jnp.bfloat16), (values - high).astype(jnp.bfloat16))


def low_units(blocks):
    per_row = blocks.shape[1]
    place = 8 + jnp.arange(per_row, dtype=jnp.int32)[None, :]
    return jnp.min(place - 2 * ((blocks + 1) // 2), axis=1).astype(jnp.int32)


def by_unit(array):
    cut = array.reshape((array.shape[0], array.shape[1] // UNIT, UNIT) + array.shape[2:])
    return cut.swapaxes(0, 1)


def by_row(array, micros):
    cut = array.reshape(-1, micros, UNIT, array.shape[-1])
    return cut.swapaxes(0, 1).reshape(micros, -1, array.shape[-1])


def shards(
    token_ids,
    lengths,
    embedding,
    norm1_gain,
    w_query,
    w_key,
    w_value,
    w_out,
    mix_logits,
    mix_weights,
    norm2_gain,
    w_up,
    w_down,
    cotangent,
):
    count = lax.axis_size("dev")
    me = lax.axis_index("dev")
    micros, row_count = token_ids.shape
    own_rows, width = embedding.shape
    heads = mix_logits.shape[0]
    part = norm1_gain.shape[0]
    per_row = row_count // UNIT
    tokens = micros * row_count
    tok_ids = by_unit(token_ids).reshape(-1)
    stride = max(16, 1024 // count)
    room = stride - 2

    unit_rows = me * row_count + UNIT * jnp.arange(per_row, dtype=jnp.int32)
    begins = jnp.stack([seq_starts(lengths[micro], unit_rows) for micro in range(micros)])
    blocks = ((unit_rows[None, :] - begins) // UNIT + 1).reshape(-1).astype(jnp.int32)

    lows = low_units(blocks.reshape(micros, per_row))
    mixes = spread_mixes(mix_logits, mix_weights)

    up_cols = w_up.shape[1] // width
    up_pieces = [w_up[:, col * width : (col + 1) * width] for col in range(up_cols)]
    first_weights = spread_z(jnp.stack([w_query, w_key, w_value, w_out]), 0, 1)
    late_stack = jnp.concatenate([w_down] + up_pieces, axis=0)
    ids = split_ids(tok_ids, own_rows)
    message, chosen = ask_round(ids, 0, own_rows, stride, room)
    message, first_weights = lax.optimization_barrier((message, first_weights))
    first_weights = spread_plane(spread_z(first_weights, 1, 99))
    gains_row = jnp.concatenate([norm1_gain, norm2_gain, jnp.zeros((width - 2 * part,), jnp.bfloat16)])
    picked, gains, (first_weights, mixes), *plan = lookup(
        embedding, ids, message, chosen, gains_row, stride, room, (first_weights, mixes)
    )
    first_weights = spread_rest(first_weights)
    picked, late_stack, first_weights = lax.optimization_barrier((picked, late_stack, first_weights))
    w_u, w_d = gather_late(late_stack, part, up_cols)
    gain_one = gains[:, :part].reshape(-1)
    gain_two = gains[:, part : 2 * part].reshape(-1)
    inputs = picked.astype(jnp.float32)

    normed_one, inv_one, hidden_one = normalize(inputs, gain_one)
    own_hidden = hidden_one.reshape(per_row, micros, UNIT, width)
    pieces = earlier_rows(own_hidden)
    first_weights = spread_cores(finish_rest(first_weights)).reshape(count, 4, part, width)
    w_q, w_k, w_v, w_o = (first_weights[:, at].reshape(-1, width) for at in range(4))
    query, key, value = project(lows, pieces, (w_q, w_k, w_v))
    attended, *kept = attention_fwd(blocks, query, key, value, mixes, heads)
    attended = attended.reshape(tokens, width)

    grad_rows = by_unit(cotangent).reshape(tokens, width)
    gain_row = gain_two.astype(jnp.float32)[None, :]
    output, grad_middle, grad_branch, grad_att, grad_gain_two, grad_up, grad_down = feed_forward(
        picked, attended, w_o, gain_row, w_u, w_d, grad_rows
    )
    grad_att = grad_att.reshape(own_hidden.shape)
    up_rows = grad_up.reshape(up_cols, count, part, width).swapaxes(0, 1).reshape(count, -1, width)
    stack = jnp.concatenate([grad_down.reshape(count, -1, width), up_rows], axis=1).reshape(-1, width)
    stack, grad_att = lax.optimization_barrier((stack, grad_att))
    late_sums = lax.psum_scatter(stack, "dev", scatter_dimension=0, tiled=True).astype(jnp.float32)

    def tail(pieces, query, key, value, grad_att, kept, attended, grad_branch):
        grad_query, grad_key, grad_value, wide_logit, wide_prob = attention_bwd(
            blocks, query, key, value, grad_att, kept, mixes, heads
        )
        *terms, grad_own = project_back(lows, grad_query, grad_key, grad_value, (w_q, w_k, w_v))
        came = with_sibling(jnp.concatenate([terms[3], terms[1]], axis=0))
        grads, wides = ((grad_query, grad_key, grad_value), (wide_logit, wide_prob))
        came, grads, wides, hidden, attended = lax.optimization_barrier((came, grads, wides, pieces, attended))
        kept_rows, give_two, give_four = give_rows(terms[0], terms[2], came)
        back_two = from_behind(give_two, -2)
        early_terms = weigh(lows, *grads, attended, grad_branch, hidden)
        mix_terms = jnp.concatenate([fold_mix(wide, heads).reshape(-1) for wide in wides])
        back_two, early_terms, give_four, mix_terms = lax.optimization_barrier(
            (back_two, early_terms, give_four, mix_terms)
        )
        back_four = from_behind(give_four, -4)
        early = cut_thirds(sum_cores(early_terms.reshape(4, count, part, width).swapaxes(0, 1)))
        back_four, early = lax.optimization_barrier((back_four, early))
        backs = (kept_rows, back_two, back_four)
        grad_own = grad_own + backs[0] + backs[1].astype(jnp.float32) + backs[2].astype(jnp.float32)
        grad_hidden_one = grad_own.reshape(tokens, width)
        grad_in_norm, grad_gain_one = norm_back(grad_hidden_one, normed_one, inv_one, gain_one)
        grad_inputs = grad_middle + grad_in_norm

        mix_size = mix_terms.shape[0]
        small = jnp.concatenate(
            [
                grad_gain_one.reshape(count, part),
                grad_gain_two.reshape(count, part),
                jnp.broadcast_to(mix_terms[None, :], (count, mix_size)),
                jnp.zeros((count, width - 2 * part - mix_size), jnp.float32),
            ],
            axis=1,
        )
        table_grad, small_sum, early = table_back(grad_inputs, split_low(small), plan, own_rows, stride, room, early)
        return (by_row(grad_inputs, micros), table_grad, small_sum, sum_last([early]))

    def no_tail(*operands):
        sizes = ((micros, row_count, width), (own_rows, width), (width,), (4 * part, width))
        return tuple(jnp.zeros(size, jnp.float32) for size in sizes)

    grad_inputs, table_grad, small_sum, early_sums = lax.cond(
        plan[-1] > 0, tail, no_tail, pieces, query, key, value, grad_att, kept, attended, grad_branch
    )
    early_sums = split_rows(early_sums, [part] * 4)
    late_sums = split_rows(late_sums, [w_down.shape[0]] + [part] * up_cols)
    mix_size = 2 * heads * heads
    mixes = small_sum[2 * part : 2 * part + mix_size].reshape(2, heads, heads)
    return (
        by_row(output, micros),
        grad_inputs,
        table_grad,
        small_sum[:part],
        *early_sums,
        mixes[0],
        mixes[1],
        small_sum[part : 2 * part],
        jnp.concatenate(late_sums[1:], axis=1),
        late_sums[0],
    )


def solution(mesh):
    in_specs = (
        P(None, "dev"),
        P(),
        P("dev", None),
        P("dev"),
        P("dev", None),
        P("dev", None),
        P("dev", None),
        P("dev", None),
        P(),
        P(),
        P("dev"),
        P("dev", None),
        P("dev", None),
        P(None, "dev", None),
    )
    out_specs = (
        P(None, "dev", None),
        P(None, "dev", None),
        P("dev", None),
        P("dev"),
        P("dev", None),
        P("dev", None),
        P("dev", None),
        P("dev", None),
        P(),
        P(),
        P("dev"),
        P("dev", None),
        P("dev", None),
    )
    return jax.shard_map(shards, mesh=mesh, in_specs=in_specs, out_specs=out_specs, check_vma=False)
```

```python
from functools import partial

import jax
import jax.numpy as jnp
from jax import lax
from jax.experimental import pallas as pl
from jax.experimental.pallas import tpu as pltpu
from jax.sharding import PartitionSpec as P

norm_eps = 1e-06
gelu_scale = 0.7978845608028654
gelu_cube = 0.044715
FF_STEP = 256

masked = -1e30
UNIT = 128
CHUNK = 256
GROUP = 16
MAX_CHUNKS = 4
TOGETHER = 4


def dot_nn(left, right):
    return lax.dot_general(left, right, (((1,), (0,)), ((), ())), preferred_element_type=jnp.float32)


def dot_nt(left, right):
    return lax.dot_general(left, right, (((1,), (1,)), ((), ())), preferred_element_type=jnp.float32)


def spread_heads(rows, lane_head, quad, heads_per_quad):
    part = rows[:, quad * CHUNK : (quad + 1) * CHUNK]
    zero = jnp.zeros_like(part)
    return jnp.concatenate([jnp.where(lane_head == head, part, zero) for head in range(heads_per_quad)], axis=0)


def own_lanes(wide, lane_head, heads_per_quad):
    total = jnp.where(lane_head == 0, wide[:UNIT], 0.0)
    for head in range(1, heads_per_quad):
        total = total + jnp.where(lane_head == head, wide[head * UNIT : (head + 1) * UNIT], 0.0)
    return total


def part_of(sums, group):
    start = group % TOGETHER * CHUNK
    return sums[:, start : start + CHUNK]


def allowed_keys(chunk, group, blocks):
    key = lax.broadcasted_iota(jnp.int32, (GROUP, CHUNK), 1) - (UNIT + CHUNK * chunk)
    row = lax.broadcasted_iota(jnp.int32, (GROUP, CHUNK), 0) + GROUP * group
    return (key <= row) & (key >= (1 - blocks) * UNIT)


def twice(rows):
    return jnp.concatenate([rows, rows], axis=-1)


def put_groups(ref, quad, per_quad, term):
    low = term.astype(jnp.bfloat16)
    for head in range(per_quad):
        rows = slice((quad * per_quad + head) * GROUP, (quad * per_quad + head + 1) * GROUP)
        for group in range(UNIT // GROUP):
            start = head * UNIT + group * GROUP
            ref[rows, group * CHUNK : (group + 1) * CHUNK] = low[start : start + GROUP]


def fwd_kernel(heads, blocks_ref, q_ref, k_ref, v_ref, mix_ref, att_ref, score_out, prob_out, mixed_out,
               qx, score, prob, mixed, logit, top, norm, total, sems):
    micro, inner, per_row = (pl.program_id(0), pl.program_id(1), pl.num_programs(1))
    blocks = blocks_ref[micro * per_row + inner]
    chunks = (blocks + 1) // 2
    last_unit = k_ref.shape[0] - per_row + inner + 1
    quads = q_ref.shape[3] // CHUNK
    per_quad = heads // quads
    groups = UNIT // GROUP
    wide = heads * GROUP
    lane_head = lax.broadcasted_iota(jnp.int32, (UNIT, CHUNK), 1) // (CHUNK // per_quad)
    for quad in range(quads):
        qx[quad] = spread_heads(q_ref[0, 0], lane_head, quad, per_quad)
    total[...] = jnp.zeros_like(total)
    top[...] = jnp.full_like(top, masked)
    norm[...] = jnp.zeros_like(norm)

    def keys(ref, chunk, quad):
        units = pl.ds(last_unit - 2 * (chunk + 1), 2)
        return ref[units, 0, :, quad * CHUNK : (quad + 1) * CHUNK].reshape(CHUNK, CHUNK)

    step = micro * per_row + inner

    def keep(at, chunk, kind):
        source, target = ((score, score_out), (prob, prob_out), (mixed, mixed_out))[kind]
        place = target.at[at % per_row, at // per_row, chunk]
        return pltpu.make_async_copy(source.at[chunk], place, sems.at[kind, chunk])

    def finish(at):
        @pl.loop(0, (blocks_ref[at] + 1) // 2)
        def _(chunk):
            for kind in range(3):
                keep(at, chunk, kind).wait()

    @pl.when(step > 0)
    def _():
        finish(step - 1)

    @pl.loop(0, chunks)
    def _(chunk):
        for quad in range(quads):
            put_groups(score.at[chunk], quad, per_quad, dot_nt(qx[quad], keys(k_ref, chunk, quad)))
        keep(step, chunk, 0).start()
        for group in range(groups):
            if group % TOGETHER == 0:
                mixes = dot_nn(mix_ref[0], score[chunk, :, group * CHUNK : (group + TOGETHER) * CHUNK])
            l = part_of(mixes, group)
            l = jnp.where(allowed_keys(chunk, group, blocks)[None], l.reshape(heads, GROUP, CHUNK), masked)
            l = l.reshape(wide, CHUNK)
            logit[chunk, group] = l
            old = top[group]
            new = jnp.maximum(old, jnp.maximum(l[:, :UNIT], l[:, UNIT:]))
            terms = jnp.exp(l[:, :UNIT] - new) + jnp.exp(l[:, UNIT:] - new)
            norm[group] = norm[group] * jnp.exp(old - new) + terms
            top[group] = new

    for group in range(groups):
        lanes = top[group]
        high = jnp.broadcast_to(jnp.max(lanes, axis=-1, keepdims=True), lanes.shape)
        whole = jnp.sum(norm[group] * jnp.exp(lanes - high), axis=-1, keepdims=True)
        top[group] = high + jnp.log(jnp.broadcast_to(whole, lanes.shape))

    @pl.loop(0, chunks)
    def _(chunk):
        for group in range(groups):
            p = jnp.exp(logit[chunk, group] - twice(top[group])).astype(jnp.bfloat16)
            prob[chunk, :, group * CHUNK : (group + 1) * CHUNK] = p
        for first in range(0, groups, TOGETHER):
            sums = dot_nn(mix_ref[2], prob[chunk, :, first * CHUNK : (first + TOGETHER) * CHUNK])
            for group in range(first, first + TOGETHER):
                a = part_of(sums, group).astype(jnp.bfloat16)
                mixed[chunk, :, GROUP * group : GROUP * (group + 1), :] = a.reshape(heads, GROUP, CHUNK)
        keep(step, chunk, 1).start()
        keep(step, chunk, 2).start()
        for quad in range(quads):
            a = mixed[chunk, quad * per_quad : (quad + 1) * per_quad].reshape(per_quad * UNIT, CHUNK)
            o = own_lanes(dot_nn(a, keys(v_ref, chunk, quad)), lane_head, per_quad)
            total[:, quad * CHUNK : (quad + 1) * CHUNK] += o

    att_ref[0, 0] = total[...].astype(jnp.bfloat16)

    @pl.when(step == pl.num_programs(0) * per_row - 1)
    def _():
        finish(step)


def attention_specs(q, k, heads):
    per_row, micros, _, width = q.shape
    wide = heads * GROUP
    return (
        pl.BlockSpec((1, 1, UNIT, width), lambda m, u, _: (u, m, 0, 0)),
        pl.BlockSpec((k.shape[0], 1, UNIT, width), lambda m, u, _: (0, m, 0, 0)),
        pl.BlockSpec((4, wide, wide), lambda m, u, _: (0, 0, 0)),
    )


def kept_shapes(heads):
    wide = heads * GROUP
    flat = (MAX_CHUNKS, wide, UNIT // GROUP * CHUNK)
    return (flat, flat, (MAX_CHUNKS, heads, UNIT, CHUNK))


def attention_fwd(blocks, q, k, v, mixes, heads):
    per_row, micros, _, width = q.shape
    wide = heads * GROUP
    groups = UNIT // GROUP
    quads = width // CHUNK
    unit_spec, kv_spec, mix_spec = attention_specs(q, k, heads)
    kept = kept_shapes(heads)
    anywhere = pl.BlockSpec(memory_space=pl.ANY)
    return pl.pallas_call(
        partial(fwd_kernel, heads),
        grid_spec=pltpu.PrefetchScalarGridSpec(
            num_scalar_prefetch=1,
            grid=(micros, per_row),
            in_specs=[unit_spec, kv_spec, kv_spec, mix_spec],
            out_specs=[unit_spec, anywhere, anywhere, anywhere],
            scratch_shapes=[pltpu.VMEM((quads, heads // quads * UNIT, CHUNK), jnp.bfloat16)]
            + [pltpu.VMEM(shape, jnp.bfloat16) for shape in kept]
            + [
                pltpu.VMEM((MAX_CHUNKS, groups, wide, CHUNK), jnp.float32),
                pltpu.VMEM((groups, wide, UNIT), jnp.float32),
                pltpu.VMEM((groups, wide, UNIT), jnp.float32),
                pltpu.VMEM((UNIT, width), jnp.float32),
                pltpu.SemaphoreType.DMA((3, MAX_CHUNKS)),
            ],
        ),
        out_shape=[jax.ShapeDtypeStruct(q.shape, jnp.bfloat16)]
        + [jax.ShapeDtypeStruct((per_row, micros) + shape, jnp.bfloat16) for shape in kept],
        compiler_params=pltpu.CompilerParams(vmem_limit_bytes=50 * 1024 * 1024),
        cost_estimate=pl.CostEstimate(flops=20_000_000_000, bytes_accessed=30_000_000, transcendentals=0),
        name="attention_fwd",
    )(blocks, q, k, v, mixes)


def bwd_kernel(heads, blocks_ref, q_ref, k_ref, v_ref, do_ref, mix_ref, score_in, prob_in, mixed_in,
               dq_ref, dk_ref, dv_ref, gl_ref, gp_ref,
               qxt, dox, doxt, score, prob, mixed, grad_prob, grad_mixed, grad_logit, grad_score,
               delta, dq_total, dk_total, dv_total, sems):
    micro, inner, per_row = (pl.program_id(0), pl.program_id(1), pl.num_programs(1))
    step = micro * per_row + inner
    slot = step % 2
    blocks = blocks_ref[step]
    chunks = (blocks + 1) // 2
    key_units = k_ref.shape[0]
    last_unit = key_units - per_row + inner + 1
    quads = q_ref.shape[3] // CHUNK
    per_quad = heads // quads
    groups = UNIT // GROUP
    wide = heads * GROUP
    lane_head = lax.broadcasted_iota(jnp.int32, (UNIT, CHUNK), 1) // (CHUNK // per_quad)
    row_head = lax.broadcasted_iota(jnp.int32, (CHUNK, UNIT), 0) // (CHUNK // per_quad)
    lowest = key_units
    for other in range(key_units - 7):
        its_chunks = (blocks_ref[micro * per_row + other] + 1) // 2
        lowest = jnp.minimum(lowest, key_units - per_row + other + 1 - 2 * its_chunks)

    def fetch(at, chunk, kind):
        source, target = ((score_in, score), (prob_in, prob), (mixed_in, mixed))[kind]
        place = source.at[at % per_row, at // per_row, chunk]
        return pltpu.make_async_copy(place, target.at[at % 2, chunk], sems.at[kind, at % 2, chunk])

    def fetch_all(at):
        @pl.loop(0, (blocks_ref[at] + 1) // 2)
        def _(chunk):
            for kind in (1, 2, 0):
                fetch(at, chunk, kind).start()

    @pl.when(step == 0)
    def _():
        fetch_all(0)
        gl_ref[...] = jnp.zeros_like(gl_ref)
        gp_ref[...] = jnp.zeros_like(gp_ref)

    @pl.when(step + 1 < pl.num_programs(0) * per_row)
    def _():
        fetch_all(step + 1)

    @pl.when(inner == 0)
    def _():
        @pl.loop(lowest, key_units)
        def _(key_unit):
            dk_total[key_unit] = jnp.zeros_like(dk_total[key_unit])
            dv_total[key_unit] = jnp.zeros_like(dv_total[key_unit])

    def spread_turned(rows, quad):
        turned = rows[:, quad * CHUNK : (quad + 1) * CHUNK].T
        zero = jnp.zeros_like(turned)
        return jnp.concatenate([jnp.where(row_head == head, turned, zero) for head in range(per_quad)], axis=1)

    for quad in range(quads):
        qxt[quad] = spread_turned(q_ref[0, 0], quad)
        dox[quad] = spread_heads(do_ref[0, 0], lane_head, quad, per_quad)
        doxt[quad] = spread_turned(do_ref[0, 0], quad)
    dq_total[...] = jnp.zeros_like(dq_total)
    delta[...] = jnp.zeros_like(delta)

    def keys(ref, chunk, quad):
        units = pl.ds(last_unit - 2 * (chunk + 1), 2)
        return ref[units, 0, :, quad * CHUNK : (quad + 1) * CHUNK].reshape(CHUNK, CHUNK)

    def add_to(total, chunk, quad, term):
        first = last_unit - 2 * (chunk + 1)
        lanes = slice(quad * CHUNK, (quad + 1) * CHUNK)
        total[first, lanes, :] += term[:, :UNIT]
        total[first + 1, lanes, :] += term[:, UNIT:]

    @pl.loop(0, chunks)
    def _(chunk):
        for quad in range(quads):
            put_groups(grad_mixed, quad, per_quad, dot_nt(dox[quad], keys(v_ref, chunk, quad)))
        fetch(step, chunk, 1).wait()
        for group in range(groups):
            cols = slice(group * CHUNK, (group + 1) * CHUNK)
            if group % TOGETHER == 0:
                sums = dot_nn(mix_ref[3], grad_mixed[:, group * CHUNK : (group + TOGETHER) * CHUNK])
            dp = part_of(sums, group)
            grad_prob[chunk, :, cols] = dp.astype(grad_prob.dtype)
            term = prob[slot, chunk, :, cols].astype(jnp.float32) * dp
            delta[group] += term[:, :UNIT] + term[:, UNIT:]
        gp_ref[...] += dot_nt(prob[slot, chunk], grad_mixed[...])
        fetch(step, chunk, 2).wait()
        for quad in range(quads):
            a = mixed[slot, chunk, quad * per_quad : (quad + 1) * per_quad].reshape(per_quad * UNIT, CHUNK)
            add_to(dv_total, chunk, quad, dot_nn(doxt[quad], a))

    for group in range(groups):
        delta[group] = jnp.broadcast_to(jnp.sum(delta[group], axis=-1, keepdims=True), (wide, UNIT))

    @pl.loop(0, chunks)
    def _(chunk):
        for group in range(groups):
            cols = slice(group * CHUNK, (group + 1) * CHUNK)
            dp = grad_prob[chunk, :, cols].astype(jnp.float32) - twice(delta[group])
            dl = (prob[slot, chunk, :, cols].astype(jnp.float32) * dp).astype(jnp.bfloat16)
            grad_logit[:, cols] = dl
        for first in range(0, groups, TOGETHER):
            sums = dot_nn(mix_ref[1], grad_logit[:, first * CHUNK : (first + TOGETHER) * CHUNK])
            for group in range(first, first + TOGETHER):
                ds = part_of(sums, group).astype(jnp.bfloat16)
                grad_score[:, GROUP * group : GROUP * (group + 1), :] = ds.reshape(heads, GROUP, CHUNK)
        fetch(step, chunk, 0).wait()
        gl_ref[...] += dot_nt(score[slot, chunk], grad_logit[...])
        for quad in range(quads):
            ds = grad_score[quad * per_quad : (quad + 1) * per_quad].reshape(per_quad * UNIT, CHUNK)
            dq = own_lanes(dot_nn(ds, keys(k_ref, chunk, quad)), lane_head, per_quad)
            dq_total[:, quad * CHUNK : (quad + 1) * CHUNK] += dq
            add_to(dk_total, chunk, quad, dot_nn(qxt[quad], ds))

    dq_ref[0, 0] = (dq_total[...] * 0.125).astype(jnp.bfloat16)

    @pl.when(inner == per_row - 1)
    def _():
        @pl.loop(0, lowest)
        def _(key_unit):
            dk_ref[key_unit, 0] = jnp.zeros_like(dk_ref[key_unit, 0])
            dv_ref[key_unit, 0] = jnp.zeros_like(dv_ref[key_unit, 0])

        @pl.loop(lowest, key_units)
        def _(key_unit):
            dk_ref[key_unit, 0] = dk_total[key_unit].astype(jnp.bfloat16).T
            dv_ref[key_unit, 0] = dv_total[key_unit].astype(jnp.bfloat16).T


def attention_bwd(blocks, q, k, v, grad_out, kept, mixes, heads):
    per_row, micros, _, width = q.shape
    key_units = k.shape[0]
    wide = heads * GROUP
    groups = UNIT // GROUP
    quads = width // CHUNK
    turned = (quads, CHUNK, heads // quads * UNIT)
    unit_spec, kv_spec, mix_spec = attention_specs(q, k, heads)
    sum_spec = pl.BlockSpec((wide, wide), lambda m, u, _: (0, 0))
    anywhere = pl.BlockSpec(memory_space=pl.ANY)
    return pl.pallas_call(
        partial(bwd_kernel, heads),
        grid_spec=pltpu.PrefetchScalarGridSpec(
            num_scalar_prefetch=1,
            grid=(micros, per_row),
            in_specs=[unit_spec, kv_spec, kv_spec, unit_spec, mix_spec] + [anywhere] * 3,
            out_specs=[unit_spec, kv_spec, kv_spec, sum_spec, sum_spec],
            scratch_shapes=[
                pltpu.VMEM(turned, jnp.bfloat16),
                pltpu.VMEM((quads, heads // quads * UNIT, CHUNK), jnp.bfloat16),
                pltpu.VMEM(turned, jnp.bfloat16),
            ]
            + [pltpu.VMEM((2,) + shape, jnp.bfloat16) for shape in kept_shapes(heads)]
            + [
                pltpu.VMEM((MAX_CHUNKS, wide, groups * CHUNK), jnp.bfloat16),
                pltpu.VMEM((wide, groups * CHUNK), jnp.bfloat16),
                pltpu.VMEM((wide, groups * CHUNK), jnp.bfloat16),
                pltpu.VMEM((heads, UNIT, CHUNK), jnp.bfloat16),
                pltpu.VMEM((groups, wide, UNIT), jnp.float32),
                pltpu.VMEM((UNIT, width), jnp.float32),
                pltpu.VMEM((key_units, width, UNIT), jnp.float32),
                pltpu.VMEM((key_units, width, UNIT), jnp.float32),
                pltpu.SemaphoreType.DMA((3, 2, MAX_CHUNKS)),
            ],
        ),
        out_shape=[
            jax.ShapeDtypeStruct(q.shape, jnp.bfloat16),
            jax.ShapeDtypeStruct(k.shape, jnp.bfloat16),
            jax.ShapeDtypeStruct(v.shape, jnp.bfloat16),
            jax.ShapeDtypeStruct((wide, wide), jnp.float32),
            jax.ShapeDtypeStruct((wide, wide), jnp.float32),
        ],
        compiler_params=pltpu.CompilerParams(vmem_limit_bytes=58 * 1024 * 1024),
        cost_estimate=pl.CostEstimate(flops=45_000_000_000, bytes_accessed=40_000_000, transcendentals=0),
        name="attention_bwd",
    )(blocks, q, k, v, grad_out, mixes, *kept)


def piece_bases(key_units, per_row):
    sizes = [1] + [per_row] * ((key_units - 1) // per_row)
    return [(sum(sizes[:at]), size) for at, size in enumerate(sizes)]


def project_kernel(low_ref, *refs):
    pieces, (w_q, w_k, w_v, q_ref, k_ref, v_ref) = (refs[:-6], refs[-6:])
    key_units, width = (k_ref.shape[0], k_ref.shape[3])
    per_row = q_ref.shape[0]
    low = low_ref[pl.program_id(0)]

    for piece, (base, size) in zip(pieces, piece_bases(key_units, per_row)):
        @pl.when(base + size > low)
        def _():
            rows = piece[:, 0].reshape(size * UNIT, width)
            k_ref[base : base + size, 0] = dot_nn(rows, w_k[...]).astype(jnp.bfloat16).reshape(size, UNIT, width)
            v_ref[base : base + size, 0] = dot_nn(rows, w_v[...]).astype(jnp.bfloat16).reshape(size, UNIT, width)

    rows = pieces[-1][:, 0].reshape(per_row * UNIT, width)
    query = dot_nn(rows, w_q[...]).astype(jnp.bfloat16) * jnp.bfloat16(0.125)
    q_ref[:, 0] = query.reshape(per_row, UNIT, width)


def project(low, pieces, weights):
    micros, width = pieces[0].shape[1], pieces[0].shape[3]
    key_units = sum(piece.shape[0] for piece in pieces)
    per_row = pieces[-1].shape[0]

    def spec(units):
        return pl.BlockSpec((units, 1, UNIT, width), lambda m, _: (0, m, 0, 0))

    weight_spec = pl.BlockSpec((width, width), lambda m, _: (0, 0))
    shapes = [(units, micros, UNIT, width) for units in (per_row, key_units, key_units)]
    return pl.pallas_call(
        project_kernel,
        grid_spec=pltpu.PrefetchScalarGridSpec(
            num_scalar_prefetch=1,
            grid=(micros,),
            in_specs=[spec(piece.shape[0]) for piece in pieces] + [weight_spec] * 3,
            out_specs=[spec(shape[0]) for shape in shapes],
        ),
        out_shape=[jax.ShapeDtypeStruct(shape, jnp.bfloat16) for shape in shapes],
        compiler_params=pltpu.CompilerParams(vmem_limit_bytes=60 * 1024 * 1024),
        cost_estimate=pl.CostEstimate(flops=6_000_000_000, bytes_accessed=15_000_000, transcendentals=0),
        name="project",
    )(low, *pieces, *weights)


def project_back_kernel(low_ref, dq_ref, dk_ref, dv_ref, w_q, w_k, w_v, *outs):
    key_units, width = (dk_ref.shape[0], dk_ref.shape[3])
    per_row = dq_ref.shape[0]
    low = low_ref[pl.program_id(0)]
    bases = piece_bases(key_units, per_row)

    def from_keys(base, size):
        rows = slice(base, base + size)
        key_term = dot_nt(dk_ref[rows, 0].reshape(size * UNIT, width), w_k[...])
        return key_term + dot_nt(dv_ref[rows, 0].reshape(size * UNIT, width), w_v[...])

    for out, (base, size) in zip(outs[:-1], bases[:-1]):
        @pl.when(base + size > low)
        def _():
            out[:, 0] = from_keys(base, size).astype(jnp.bfloat16).reshape(size, UNIT, width)

        @pl.when(base + size <= low)
        def _():
            out[...] = jnp.zeros_like(out)

    own = from_keys(*bases[-1]) + dot_nt(dq_ref[:, 0].reshape(per_row * UNIT, width), w_q[...])
    outs[-1][:, 0] = own.reshape(per_row, UNIT, width)


def project_back(low, grad_query, grad_key, grad_value, weights):
    per_row, micros, _, width = grad_query.shape
    key_units = grad_key.shape[0]

    def spec(units):
        return pl.BlockSpec((units, 1, UNIT, width), lambda m, _: (0, m, 0, 0))

    weight_spec = pl.BlockSpec((width, width), lambda m, _: (0, 0))
    sizes = [size for _, size in piece_bases(key_units, per_row)]
    shapes = [(size, micros, UNIT, width) for size in sizes]
    kinds = [jnp.bfloat16] * (len(sizes) - 1) + [jnp.float32]
    return pl.pallas_call(
        project_back_kernel,
        grid_spec=pltpu.PrefetchScalarGridSpec(
            num_scalar_prefetch=1,
            grid=(micros,),
            in_specs=[spec(per_row), spec(key_units), spec(key_units)] + [weight_spec] * 3,
            out_specs=[spec(size) for size in sizes],
        ),
        out_shape=[jax.ShapeDtypeStruct(shape, kind) for shape, kind in zip(shapes, kinds)],
        compiler_params=pltpu.CompilerParams(vmem_limit_bytes=60 * 1024 * 1024),
        cost_estimate=pl.CostEstimate(flops=6_000_000_000, bytes_accessed=15_000_000, transcendentals=0),
        name="project_back",
    )(low, grad_query, grad_key, grad_value, *weights)


def weigh_kernel(low_ref, dq_ref, dk_ref, dv_ref, att_ref, branch_ref, *refs):
    pieces, (grad_ref, total) = (refs[:-2], refs[-2:])
    key_units, width = (dk_ref.shape[0], dk_ref.shape[3])
    per_row = dq_ref.shape[0]
    micro = pl.program_id(0)
    low = low_ref[micro]
    bases = piece_bases(key_units, per_row)

    @pl.when(micro == 0)
    def _():
        total[0:3] = jnp.zeros_like(total[0:3])
        total[3] = dot_nn(att_ref[...].T, branch_ref[...])

    def keys(ref, base, size):
        return ref[base : base + size, 0].reshape(size * UNIT, width)

    for piece, (base, size) in zip(pieces, bases):
        @pl.when(base + size > low)
        def _():
            turned = piece[:, 0].reshape(size * UNIT, width).T
            total[1] += dot_nn(turned, keys(dk_ref, base, size))
            total[2] += dot_nn(turned, keys(dv_ref, base, size))
            if base + size == key_units:
                total[0] += dot_nn(turned, keys(dq_ref, 0, per_row))

    @pl.when(micro == pl.num_programs(0) - 1)
    def _():
        grad_ref[...] = total[...].astype(jnp.bfloat16)


def weigh(low, grad_query, grad_key, grad_value, attended, branch, pieces):
    per_row, micros, _, width = grad_query.shape
    key_units = grad_key.shape[0]

    def spec(units):
        return pl.BlockSpec((units, 1, UNIT, width), lambda m, _: (0, m, 0, 0))

    sizes = [size for _, size in piece_bases(key_units, per_row)]
    return pl.pallas_call(
        weigh_kernel,
        grid_spec=pltpu.PrefetchScalarGridSpec(
            num_scalar_prefetch=1,
            grid=(micros,),
            in_specs=[spec(size) for size in (per_row, key_units, key_units)]
            + [pl.BlockSpec(attended.shape, lambda m, _: (0, 0))] * 2
            + [spec(size) for size in sizes],
            out_specs=pl.BlockSpec((4, width, width), lambda m, _: (0, 0, 0)),
            scratch_shapes=[pltpu.VMEM((4, width, width), jnp.float32)],
        ),
        out_shape=jax.ShapeDtypeStruct((4, width, width), jnp.bfloat16),
        compiler_params=pltpu.CompilerParams(vmem_limit_bytes=60 * 1024 * 1024),
        cost_estimate=pl.CostEstimate(flops=12_000_000_000, bytes_accessed=14_000_000, transcendentals=0),
        name="weigh",
    )(low, grad_query, grad_key, grad_value, attended, branch, *pieces)


def feed_kernel(x_ref, att_ref, w_o_ref, gain_ref, up_ref, down_ref, cot_ref,
                out_ref, grad_mid_ref, branch_ref, grad_att_ref, grad_gain_ref, grad_up_ref, grad_down_ref,
                middle_ref, hidden, turned, out_total, back_total):
    step = pl.program_id(0)

    @pl.when(step == 0)
    def _():
        middle = x_ref[...].astype(jnp.float32) + dot_nn(att_ref[...], w_o_ref[...])
        middle_ref[...] = middle
        inv_rms = lax.rsqrt(jnp.mean(middle * middle, axis=-1, keepdims=True) + norm_eps)
        rows = (middle * inv_rms * gain_ref[...]).astype(jnp.bfloat16)
        hidden[...] = rows
        turned[...] = rows.T
        out_total[...] = jnp.zeros_like(out_total)
        back_total[...] = jnp.zeros_like(back_total)

    down_rows = down_ref[...].reshape(up_ref.shape[1:])
    for start in range(0, up_ref.shape[2], FF_STEP):
        cols = slice(start, start + FF_STEP)
        down = down_rows[cols]
        up = dot_nn(hidden[...], up_ref[0, :, cols])
        square = up * up
        bent = jnp.tanh(gelu_scale * up * (1.0 + gelu_cube * square))
        half = 0.5 + 0.5 * bent
        slope = half + 0.5 * up * (1.0 - bent * bent) * (gelu_scale * (1.0 + 3.0 * gelu_cube * square))
        active = (up * half).astype(jnp.bfloat16)
        grad_up = (dot_nt(cot_ref[...], down) * slope).astype(jnp.bfloat16)
        out_total[...] += dot_nn(active, down)
        back_total[...] += dot_nt(grad_up, up_ref[0, :, cols])
        grad_down_ref[cols, :] = dot_nn(active.T, cot_ref[...]).astype(jnp.bfloat16)
        term = dot_nn(turned[...], grad_up)
        if len(grad_up_ref.shape) == 3:
            grad_up_ref[0, :, cols] = term.astype(jnp.bfloat16)
        else:
            shape = (grad_up_ref.shape[0], grad_up_ref.shape[2], FF_STEP)
            grad_up_ref[:, 0, :, cols] = term.reshape(shape).astype(jnp.bfloat16)

    @pl.when(step == pl.num_programs(0) - 1)
    def _():
        middle = middle_ref[...]
        out_ref[...] = (middle + out_total[...]).astype(jnp.bfloat16)
        inv_rms = lax.rsqrt(jnp.mean(middle * middle, axis=-1, keepdims=True) + norm_eps)
        normed = middle * inv_rms
        grad_hidden = back_total[...]
        grad_gain_ref[...] = jnp.sum(grad_hidden * normed, axis=0, keepdims=True)
        grad_normed = grad_hidden * gain_ref[...]
        inner_mean = jnp.mean(grad_normed * normed, axis=-1, keepdims=True)
        grad_mid = cot_ref[...].astype(jnp.float32) + inv_rms * (grad_normed - normed * inner_mean)
        grad_mid_ref[...] = grad_mid
        branch = grad_mid.astype(jnp.bfloat16)
        branch_ref[...] = branch
        grad_att_ref[...] = dot_nt(branch, w_o_ref[...]).astype(jnp.bfloat16)


def feed_forward(rows, attended, w_o, gain, w_up, w_late, cot, part):
    tokens, width = rows.shape
    pieces = w_up.shape[0]
    whole = pl.BlockSpec((tokens, width), lambda i: (0, 0))
    up_spec = pl.BlockSpec((1, width, width), lambda i: (i, 0, 0))
    down_spec = pl.BlockSpec((width, width), lambda i: (i, 0))
    devices = w_late.shape[0] // pieces
    late_spec = pl.BlockSpec((devices, width // devices, width), lambda i: (i, 0, 0))
    grad_spec, grad_shape = (up_spec, w_up.shape)
    if part % 8 == 0:
        grad_shape = (width // part, pieces, part, width)
        grad_spec = pl.BlockSpec((width // part, 1, part, width), lambda i: (0, i, 0, 0))
    f32, bf16 = (jnp.float32, jnp.bfloat16)
    return pl.pallas_call(
        feed_kernel,
        grid=(pieces,),
        in_specs=[
            whole,
            whole,
            pl.BlockSpec((width, width), lambda i: (0, 0)),
            pl.BlockSpec((1, width), lambda i: (0, 0)),
            up_spec,
            late_spec,
            whole,
        ],
        out_specs=[whole, whole, whole, whole, pl.BlockSpec((1, width), lambda i: (0, 0)), grad_spec, down_spec],
        out_shape=[
            jax.ShapeDtypeStruct((tokens, width), bf16),
            jax.ShapeDtypeStruct((tokens, width), f32),
            jax.ShapeDtypeStruct((tokens, width), bf16),
            jax.ShapeDtypeStruct((tokens, width), bf16),
            jax.ShapeDtypeStruct((1, width), f32),
            jax.ShapeDtypeStruct(grad_shape, bf16),
            jax.ShapeDtypeStruct((pieces * width, width), bf16),
        ],
        scratch_shapes=[
            pltpu.VMEM((tokens, width), f32),
            pltpu.VMEM((tokens, width), bf16),
            pltpu.VMEM((width, tokens), bf16),
            pltpu.VMEM((tokens, width), f32),
            pltpu.VMEM((tokens, width), f32),
        ],
        compiler_params=pltpu.CompilerParams(vmem_limit_bytes=48 * 1024 * 1024),
        cost_estimate=pl.CostEstimate(flops=16_000_000_000, bytes_accessed=30_000_000, transcendentals=0),
        name="feed_forward",
    )(rows, attended, w_o, gain, w_up, w_late, cot)


def spread_mixes(mix_logits, mix_weights):
    heads = mix_logits.shape[0]
    wide = heads * GROUP
    place = jnp.arange(wide, dtype=jnp.int32)
    pick = (place[:, None] // GROUP == jnp.arange(heads, dtype=jnp.int32)[None, :]).astype(mix_logits.dtype)
    same_row = (place[:, None] % GROUP == place[None, :] % GROUP)[None]
    tables = jnp.stack([mix_logits.T, mix_logits, mix_weights.T, mix_weights]).reshape(4 * heads, heads)
    across = jnp.dot(tables, pick.T, preferred_element_type=jnp.float32).astype(mix_logits.dtype)
    down = jnp.einsum("wh,bhx->bwx", pick, across.reshape(4, heads, wide), preferred_element_type=jnp.float32)
    return jnp.where(same_row, down, 0.0).astype(mix_logits.dtype)


def fold_mix(wide, heads):
    place = jnp.arange(heads * GROUP, dtype=jnp.int32)
    pick = (place[:, None] // GROUP == jnp.arange(heads, dtype=jnp.int32)[None, :]).astype(jnp.float32)
    same_row = place[:, None] % GROUP == place[None, :] % GROUP
    down = jnp.dot(pick.T, jnp.where(same_row, wide, 0.0), precision=lax.Precision.HIGHEST)
    return jnp.dot(down, pick, precision=lax.Precision.HIGHEST)


def from_behind(value, steps):
    count = lax.axis_size("dev")
    first, last = (max(0, -steps), min(count, count - steps))
    return lax.ppermute(value, "dev", [(source, source + steps) for source in range(first, last)])


def with_sibling(value):
    count = lax.axis_size("dev")
    return lax.ppermute(value, "dev", [(source, source ^ 1) for source in range(count)])


def earlier_rows(own):
    size = own.shape[0]
    first_core = lax.axis_index("dev") % 2 == 0
    two, four = (from_behind(own, 2), from_behind(own, 4))
    give = jnp.concatenate([jnp.where(first_core, own, two), jnp.where(first_core, two, four)], axis=0)
    came = with_sibling(give)
    return [four[size - 1 :], came[size:], two, came[:size], own]


def give_rows(four, two, came):
    size = two.shape[0]
    first_core = lax.axis_index("dev") % 2 == 0
    came = came.astype(jnp.float32)
    one, three = (came[:size], came[size:])
    give_two = two.astype(jnp.float32) + jnp.where(first_core, three, one)
    padded = jnp.pad(four.astype(jnp.float32), ((size - four.shape[0], 0), (0, 0), (0, 0), (0, 0)))
    give_four = padded + jnp.where(first_core, 0.0, three)
    return (jnp.where(first_core, one, 0.0), give_two.astype(jnp.bfloat16), give_four.astype(jnp.bfloat16))


def seq_starts(lengths_row, query_rows):
    seq_ends = jnp.cumsum(lengths_row)
    starts = seq_ends - lengths_row
    return jnp.max(jnp.where(starts[None, :] <= query_rows[:, None], starts[None, :], 0), axis=1)


def normalize(values, gain_vec):
    inv_rms = lax.rsqrt(jnp.mean(values * values, axis=-1, keepdims=True) + norm_eps)
    normed = values * inv_rms
    return (normed, inv_rms, (normed * gain_vec.astype(jnp.float32)).astype(jnp.bfloat16))


def norm_back(grad_hidden, normed, inv_rms, gain_vec):
    grad_gain = jnp.sum(grad_hidden * normed, axis=0)
    grad_normed = grad_hidden * gain_vec.astype(jnp.float32)
    inner_mean = jnp.mean(grad_normed * normed, axis=-1, keepdims=True)
    return (inv_rms * (grad_normed - normed * inner_mean), grad_gain)


def matmul(left, right):
    return jnp.dot(left, right, preferred_element_type=jnp.float32)


def matmul_left_t(left, right):
    return lax.dot_general(left, right, (((0,), (0,)), ((), ())), preferred_element_type=jnp.float32)


def matmul_right_t(left, right):
    return lax.dot_general(left, right, (((1,), (1,)), ((), ())), preferred_element_type=jnp.float32)


def exchange(value):
    return lax.all_to_all(value, "dev", split_axis=0, concat_axis=0, tiled=True)


def split_ids(tok_ids, own_rows):
    owner = tok_ids // own_rows
    place = jnp.arange(tok_ids.shape[0], dtype=jnp.int32)
    same = tok_ids[:, None] == tok_ids[None, :]
    repeated = jnp.any(same & (place[None, :] < place[:, None]), axis=1)
    before = (owner[:, None] == owner[None, :]) & (tok_ids[None, :] < tok_ids[:, None]) & ~repeated[None, :]
    return (owner, tok_ids % own_rows, jnp.sum(before, axis=1, dtype=jnp.int32))


def ask_round(ids, index, own_rows, stride, room):
    count = lax.axis_size("dev")
    owner, local, rank = ids
    here = rank - index * room
    slot = jnp.where((here >= 0) & (here < room), owner * stride + here, -1)
    chosen = slot[None, :] == jnp.arange(count * stride, dtype=jnp.int32)[:, None]
    wanted = jnp.max(jnp.where(chosen, local[None, :], -1), axis=1).reshape(count, stride)
    rounds = jnp.broadcast_to(jnp.max(rank) // room + 1, (count, stride))
    return (jnp.concatenate([wanted, rounds], axis=1), chosen.astype(jnp.bfloat16))


def hear_round(message, own_rows, stride):
    asked = exchange(message)
    pick = asked[:, :stride].reshape(-1, 1) == jnp.arange(own_rows, dtype=jnp.int32)[None, :]
    return (pick.astype(jnp.bfloat16), jnp.max(asked[:, stride:]))


def plan_round(ids, index, own_rows, stride, room):
    message, chosen = ask_round(ids, index, own_rows, stride, room)
    pick, _ = hear_round(message, own_rows, stride)
    return (chosen, pick)


def answer(embedding, chosen, pick, stride, extra_row, beside=None):
    count = lax.axis_size("dev")
    rows = matmul(pick, embedding).astype(jnp.bfloat16).reshape(count, stride, -1)
    if extra_row is not None:
        is_extra = (jnp.arange(stride, dtype=jnp.int32) == stride - 1)[None, :, None]
        rows = jnp.where(is_extra, extra_row[None, None, :], rows)
    rows, beside = lax.optimization_barrier((rows.reshape(count * stride, -1), beside))
    got = exchange(rows)
    extra = got.reshape(count, stride, -1)[:, stride - 1]
    return (matmul_left_t(chosen, got).astype(jnp.bfloat16), extra, beside)


def lookup(embedding, ids, message, chosen, extra_row, stride, room, beside):
    own_rows = embedding.shape[0]
    pick, rounds = hear_round(message, own_rows, stride)
    first, extra, beside = answer(embedding, chosen, pick, stride, extra_row, beside)

    def more(carry):
        index, rows = carry
        again, its_pick = plan_round(ids, index, own_rows, stride, room)
        return (index + 1, rows + answer(embedding, again, its_pick, stride, None)[0])

    _, rows = lax.while_loop(lambda carry: carry[0] < rounds, more, (jnp.int32(1), first))
    return (rows, extra, beside, ids, chosen, pick, rounds)


def send_grads(grad_low, chosen, pick, stride, beside=None):
    count = lax.axis_size("dev")
    summed = matmul(chosen, grad_low).astype(jnp.bfloat16)
    summed, beside = lax.optimization_barrier((summed, beside))
    got = exchange(summed)
    return (matmul_left_t(pick, got), got.reshape(count, stride, -1)[:, stride - 2 :], beside)


def table_back(grad_rows, extra_rows, plan, own_rows, stride, room, beside):
    ids, chosen, pick, rounds = plan
    count = lax.axis_size("dev")
    grad_low = grad_rows.astype(jnp.bfloat16)
    slot = jnp.arange(count * stride, dtype=jnp.int32)[:, None]
    owner = jnp.arange(count, dtype=jnp.int32)[None, :] * stride
    places = [(slot == owner + at).astype(jnp.bfloat16) for at in (stride - 2, stride - 1)]
    whole = jnp.concatenate([grad_low, *extra_rows], axis=0)
    both = jnp.concatenate([chosen, *places], axis=1)
    nothing = jnp.zeros((own_rows, grad_low.shape[1]), jnp.float32)

    def more(carry):
        index, total = carry
        again, its_pick = plan_round(ids, index, own_rows, stride, room)
        return (index + 1, total + send_grads(grad_low, again, its_pick, stride)[0])

    def rest(start):
        return lax.while_loop(lambda carry: carry[0] < rounds, more, (jnp.int32(1), start))[1]

    more_terms = lax.cond(rounds > 1, rest, lambda start: start, nothing)
    first, extra, beside = send_grads(whole, both, pick, stride, beside)
    beside = sum_stages(beside, 0)
    total, beside = lax.optimization_barrier((first + more_terms, beside))
    return (total, jnp.sum(extra.astype(jnp.float32), axis=(0, 1)), beside)


def pair_up(held, bit):
    count = lax.axis_size("dev")
    return (held, lax.ppermute(held, "dev", [(source, source ^ (1 << bit)) for source in range(count)]))


def put_together(pair, bit, axis):
    low = ((lax.axis_index("dev") >> bit) & 1) == 0
    held, came = pair
    return jnp.stack([jnp.where(low, held, came), jnp.where(low, came, held)], axis=axis)


def double(held, bit, axis):
    return put_together(pair_up(held, bit), bit, axis)


def spread_z(shard, first, last):
    bits = lax.axis_size("dev").bit_length() - 1
    for done in range(first, min(last, bits - 3)):
        shard = double(shard, bits - 1 - done, done)
    return shard


def spread_plane(held):
    at, half = (lax.axis_size("dev").bit_length() - 4, held.shape[-1] // 2)
    return (double(held[..., :half], 2, at), double(held[..., half:], 1, at))


def spread_rest(halves):
    return (pair_up(halves[0], 1), pair_up(halves[1], 2))


def finish_rest(pairs):
    at = lax.axis_size("dev").bit_length() - 4
    return (put_together(pairs[0], 1, at + 1), put_together(pairs[1], 2, at))


def spread_cores(halves):
    whole = jnp.concatenate(halves, axis=-1)
    return double(whole, 0, lax.axis_size("dev").bit_length() - 2)


def gather_late(stack, part, up_cols):
    width = stack.shape[1]
    down = stack.shape[0] - part * up_cols
    whole = lax.all_gather(stack, "dev", axis=0)
    starts = [down + part * col for col in range(up_cols)]
    up = jnp.stack([whole[:, start : start + part].reshape(-1, width) for start in starts])
    return (up, whole if down % 32 == 0 else whole[:, :down].reshape(up_cols, width, width))


def split_rows(summed, sizes):
    pieces, start = ([], 0)
    for size in sizes:
        pieces.append(summed[start : start + size])
        start += size
    return pieces


def swap_parts(held, bit):
    count = lax.axis_size("dev")
    mine = (lax.axis_index("dev") >> bit) & 1
    keep = lax.dynamic_index_in_dim(held, mine, 0, keepdims=False)
    give = lax.dynamic_index_in_dim(held, 1 - mine, 0, keepdims=False)
    return (keep, lax.ppermute(give, "dev", [(source, source ^ (1 << bit)) for source in range(count)]))


def join_parts(parts, last=False):
    total = parts[0].astype(jnp.float32) + parts[1].astype(jnp.float32)
    return total if last else total.astype(jnp.bfloat16)


def swap_halves(held, bit, last=False):
    return join_parts(swap_parts(held, bit), last)


def middle_bits():
    return list(range(1, lax.axis_size("dev").bit_length() - 2))


def sum_cores(term):
    pieces, count, rows, width = term.shape
    grid = term.reshape(pieces, count // 2, 2, rows, width)
    mine = lax.axis_index("dev") & 1
    keep = lax.dynamic_index_in_dim(grid, mine, 2, keepdims=False)
    came = with_sibling(lax.dynamic_index_in_dim(grid, 1 - mine, 2, keepdims=False))
    return join_parts((keep, came))


def cut_thirds(held):
    pieces, _, rows, width = held.shape
    middle = middle_bits()
    bits = len(middle) + 1
    grid = held.reshape((pieces,) + (2,) * bits + (rows, width))
    thirds = []
    for turn in range(3):
        shift = turn % len(middle)
        order = middle[shift:] + middle[:shift] + [bits]
        axes = [bits - bit + 1 for bit in order]
        part = grid[..., turn * (width // 3) : (turn + 1) * (width // 3)]
        part = part.transpose(axes + [0, bits + 1, bits + 2])
        thirds.append(part.reshape((2,) * bits + (pieces * rows, width // 3)))
    return thirds


def sum_stage(thirds, stage):
    middle = middle_bits()
    return [swap_halves(third, middle[(turn + stage) % len(middle)]) for turn, third in enumerate(thirds)]


def sum_stages(thirds, first):
    for stage in range(first, len(middle_bits())):
        thirds = sum_stage(thirds, stage)
    return thirds


def sum_last(groups):
    whole = [jnp.concatenate(thirds, axis=-1) for thirds in groups]
    return swap_halves(jnp.concatenate(whole, axis=1), len(middle_bits()) + 1, True)


def split_low(values):
    high = lax.reduce_precision(values, 8, 7)
    return (high.astype(jnp.bfloat16), (values - high).astype(jnp.bfloat16))


def low_units(blocks):
    per_row = blocks.shape[1]
    place = 8 + jnp.arange(per_row, dtype=jnp.int32)[None, :]
    return jnp.min(place - 2 * ((blocks + 1) // 2), axis=1).astype(jnp.int32)


def by_unit(array):
    cut = array.reshape((array.shape[0], array.shape[1] // UNIT, UNIT) + array.shape[2:])
    return cut.swapaxes(0, 1)


def by_row(array, micros):
    cut = array.reshape(-1, micros, UNIT, array.shape[-1])
    return cut.swapaxes(0, 1).reshape(micros, -1, array.shape[-1])


def shards(
    token_ids,
    lengths,
    embedding,
    norm1_gain,
    w_query,
    w_key,
    w_value,
    w_out,
    mix_logits,
    mix_weights,
    norm2_gain,
    w_up,
    w_down,
    cotangent,
):
    count = lax.axis_size("dev")
    me = lax.axis_index("dev")
    micros, row_count = token_ids.shape
    own_rows, width = embedding.shape
    heads = mix_logits.shape[0]
    part = norm1_gain.shape[0]
    per_row = row_count // UNIT
    tokens = micros * row_count
    tok_ids = by_unit(token_ids).reshape(-1)
    stride = max(16, 1024 // count)
    room = stride - 2

    unit_rows = me * row_count + UNIT * jnp.arange(per_row, dtype=jnp.int32)
    begins = jnp.stack([seq_starts(lengths[micro], unit_rows) for micro in range(micros)])
    blocks = ((unit_rows[None, :] - begins) // UNIT + 1).reshape(-1).astype(jnp.int32)

    lows = low_units(blocks.reshape(micros, per_row))
    mixes = spread_mixes(mix_logits, mix_weights)

    up_cols = w_up.shape[1] // width
    up_pieces = [w_up[:, col * width : (col + 1) * width] for col in range(up_cols)]
    first_weights = spread_z(jnp.stack([w_query, w_key, w_value, w_out]), 0, 1)
    late_stack = jnp.concatenate([w_down] + up_pieces, axis=0)
    ids = split_ids(tok_ids, own_rows)
    message, chosen = ask_round(ids, 0, own_rows, stride, room)
    message, first_weights = lax.optimization_barrier((message, first_weights))
    first_weights = spread_plane(spread_z(first_weights, 1, 99))
    gains_row = jnp.concatenate([norm1_gain, norm2_gain, jnp.zeros((width - 2 * part,), jnp.bfloat16)])
    picked, gains, (first_weights, mixes), *plan = lookup(
        embedding, ids, message, chosen, gains_row, stride, room, (first_weights, mixes)
    )
    first_weights = spread_rest(first_weights)
    picked, late_stack, first_weights = lax.optimization_barrier((picked, late_stack, first_weights))
    w_u, w_d = gather_late(late_stack, part, up_cols)
    gain_one = gains[:, :part].reshape(-1)
    gain_two = gains[:, part : 2 * part].reshape(-1)
    inputs = picked.astype(jnp.float32)

    normed_one, inv_one, hidden_one = normalize(inputs, gain_one)
    own_hidden = hidden_one.reshape(per_row, micros, UNIT, width)
    pieces = earlier_rows(own_hidden)
    first_weights = spread_cores(finish_rest(first_weights)).reshape(count, 4, part, width)
    w_q, w_k, w_v, w_o = (first_weights[:, at].reshape(-1, width) for at in range(4))
    query, key, value = project(lows, pieces, (w_q, w_k, w_v))
    attended, *kept = attention_fwd(blocks, query, key, value, mixes, heads)
    attended = attended.reshape(tokens, width)

    grad_rows = by_unit(cotangent).reshape(tokens, width)
    gain_row = gain_two.astype(jnp.float32)[None, :]
    output, grad_middle, grad_branch, grad_att, grad_gain_two, grad_up, grad_down = feed_forward(
        picked, attended, w_o, gain_row, w_u, w_d, grad_rows, part
    )
    grad_att = grad_att.reshape(own_hidden.shape)
    if grad_up.ndim == 3:
        grad_up = grad_up.reshape(up_cols, count, part, width).swapaxes(0, 1)
    up_rows = grad_up.reshape(count, -1, width)
    stack = jnp.concatenate([grad_down.reshape(count, -1, width), up_rows], axis=1).reshape(-1, width)
    stack, grad_att = lax.optimization_barrier((stack, grad_att))
    late_sums = lax.psum_scatter(stack, "dev", scatter_dimension=0, tiled=True).astype(jnp.float32)

    def tail(pieces, query, key, value, grad_att, kept, attended, grad_branch):
        grad_query, grad_key, grad_value, wide_logit, wide_prob = attention_bwd(
            blocks, query, key, value, grad_att, kept, mixes, heads
        )
        *terms, grad_own = project_back(lows, grad_query, grad_key, grad_value, (w_q, w_k, w_v))
        came = with_sibling(jnp.concatenate([terms[3], terms[1]], axis=0))
        grads, wides = ((grad_query, grad_key, grad_value), (wide_logit, wide_prob))
        came, grads, wides, hidden, attended = lax.optimization_barrier((came, grads, wides, pieces, attended))
        kept_rows, give_two, give_four = give_rows(terms[0], terms[2], came)
        back_two = from_behind(give_two, -2)
        early_terms = weigh(lows, *grads, attended, grad_branch, hidden)
        mix_terms = jnp.concatenate([fold_mix(wide, heads).reshape(-1) for wide in wides])
        back_two, early_terms, give_four, mix_terms = lax.optimization_barrier(
            (back_two, early_terms, give_four, mix_terms)
        )
        back_four = from_behind(give_four, -4)
        early = cut_thirds(sum_cores(early_terms.reshape(4, count, part, width)))
        back_four, early = lax.optimization_barrier((back_four, early))
        backs = (kept_rows, back_two, back_four)
        grad_own = grad_own + backs[0] + backs[1].astype(jnp.float32) + backs[2].astype(jnp.float32)
        grad_hidden_one = grad_own.reshape(tokens, width)
        grad_in_norm, grad_gain_one = norm_back(grad_hidden_one, normed_one, inv_one, gain_one)
        grad_inputs = grad_middle + grad_in_norm

        mix_size = mix_terms.shape[0]
        small = jnp.concatenate(
            [
                grad_gain_one.reshape(count, part),
                grad_gain_two.reshape(count, part),
                jnp.broadcast_to(mix_terms[None, :], (count, mix_size)),
                jnp.zeros((count, width - 2 * part - mix_size), jnp.float32),
            ],
            axis=1,
        )
        table_grad, small_sum, early = table_back(grad_inputs, split_low(small), plan, own_rows, stride, room, early)
        mix_grads = small_sum[2 * part : 2 * part + mix_size].reshape(2, heads, heads)
        smalls = (small_sum[:part], small_sum[part : 2 * part], mix_grads[0], mix_grads[1])
        return (by_row(grad_inputs, micros), table_grad, smalls, split_rows(sum_last([early]), [part] * 4))

    def no_tail(*operands):
        def zeros(*size):
            return jnp.zeros(size, jnp.float32)

        smalls = (zeros(part), zeros(part), zeros(heads, heads), zeros(heads, heads))
        return (zeros(micros, row_count, width), zeros(own_rows, width), smalls, [zeros(part, width)] * 4)

    grad_inputs, table_grad, smalls, early_sums = lax.cond(
        plan[-1] > 0, tail, no_tail, pieces, query, key, value, grad_att, kept, attended, grad_branch
    )
    late_sums = split_rows(late_sums, [w_down.shape[0]] + [part] * up_cols)
    return (
        by_row(output, micros),
        grad_inputs,
        table_grad,
        smalls[0],
        *early_sums,
        smalls[2],
        smalls[3],
        smalls[1],
        jnp.concatenate(late_sums[1:], axis=1),
        late_sums[0],
    )


def solution(mesh):
    in_specs = (
        P(None, "dev"),
        P(),
        P("dev", None),
        P("dev"),
        P("dev", None),
        P("dev", None),
        P("dev", None),
        P("dev", None),
        P(),
        P(),
        P("dev"),
        P("dev", None),
        P("dev", None),
        P(None, "dev", None),
    )
    out_specs = (
        P(None, "dev", None),
        P(None, "dev", None),
        P("dev", None),
        P("dev"),
        P("dev", None),
        P("dev", None),
        P("dev", None),
        P("dev", None),
        P(),
        P(),
        P("dev"),
        P("dev", None),
        P("dev", None),
    )
    return jax.shard_map(shards, mesh=mesh, in_specs=in_specs, out_specs=out_specs, check_vma=False)
```
